32 devices in a mesh: dp: 8 (over z, x), heads: 2 (over y), tensor: 2 (over core).
Axes of the slice: x: 2, y: 2, z: 4, core: 2. Of those that a mesh axis runs over, the one named last changes fastest.
Arguments:
- block_input: float32 [8192, 2048], P(('dp', 'heads', 'tensor')), may hold values from -6 to 6
- cotangent: float32 [8192, 2048], P(('dp', 'heads', 'tensor')), may hold values from -6 to 6
- segments: int32 [8, 1024], P('dp'), may hold values from 0 to 3, never falling along the last dimension, each value on 1 to 800 neighbouring positions
- matrices: float32 [4, 192, 256, 256], P(('heads', 'tensor'), 'dp')
- first_moment: float32 [4, 192, 256, 256], P(('heads', 'tensor'), 'dp')
- second_moment: float32 [4, 192, 256, 256], P(('heads', 'tensor'), 'dp'), as said below
- left_stat: float32 [4, 192, 256, 256], P(('heads', 'tensor'), 'dp'), as said below
- right_stat: float32 [4, 192, 256, 256], P(('heads', 'tensor'), 'dp'), as said below
- left_basis: float32 [4, 192, 256, 256], P(('heads', 'tensor'), 'dp'), as said below
- right_basis: float32 [4, 192, 256, 256], P(('heads', 'tensor'), 'dp'), as said below
- vectors: float32 [26624], replicated
- vec_first: float32 [26624], replicated
- vec_second: float32 [26624], replicated, as said below
Outputs:
- output: float32 [8192, 2048], P(('dp', 'heads', 'tensor'))
- grad_input: float32 [8192, 2048], P(('dp', 'heads', 'tensor'))
- new_matrices: float32 [4, 192, 256, 256], P(('heads', 'tensor'), 'dp')
- new_matrices_low: bfloat16 [4, 192, 256, 256], P(('heads', 'tensor'), 'dp')
- new_first: float32 [4, 192, 256, 256], P(('heads', 'tensor'), 'dp')
- new_second: float32 [4, 192, 256, 256], P(('heads', 'tensor'), 'dp')
- new_left_stat: float32 [4, 192, 256, 256], P(('heads', 'tensor'), 'dp')
- new_right_stat: float32 [4, 192, 256, 256], P(('heads', 'tensor'), 'dp')
- new_left_basis: float32 [4, 192, 256, 256], P(('heads', 'tensor'), 'dp')
- new_right_basis: float32 [4, 192, 256, 256], P(('heads', 'tensor'), 'dp')
- new_vectors: float32 [26624], replicated
- new_vec_first: float32 [26624], replicated
- new_vec_second: float32 [26624], replicated
The draws below stay inside these ranges and needn't reach their ends.
Inputs may be any that keep to these rules, and one draw needn't show every extreme that they name: `segments`: along each sequence the numbers never fall; a segment holds at most 800 tokens, and one holds exactly that many. `left_basis`: every block is orthogonal. `right_basis`: every block is orthogonal. `left_stat`: every block is symmetric positive definite. `right_stat`: every block is symmetric positive definite. `second_moment`: entries are positive. `vec_second`: entries are positive.
All inputs are finite; a program needn't handle non-finite values.
Results may differ from the reference program's by a relative error of at most 0.0094.
Values may be sent and summed in bfloat16 or wider, within the bound.
A program may use at most 384 MiB of HBM per device.

```python
import math
import jax
import jax.numpy as jnp
import numpy as np
from jax import lax

D = 2048
H = 8
HD = 256
RD = 64
FF = 8192
LEN = 1024
STEP = 10
TPW = 4
HPS = 2
FPS = 2048
BLK = 256
NBL = 192
NVEC = 26624
SEQS = 8
TOKENS = 8192


def block_kinds():
    column = jnp.arange(NBL)
    row_blocks = D // BLK
    hidden_blocks = FPS // BLK
    attn_count = HPS * 4 * row_blocks
    part_index = column // row_blocks % 4
    return jnp.where(column < attn_count, jnp.where(part_index == 3, 1, 0), jnp.where(column < attn_count + hidden_blocks * row_blocks, 2, 3))


def by_kind(entries):
    return jnp.array(entries, jnp.float32)[block_kinds()][None, :, None, None]


def gradient_size():
    return TOKENS ** 0.5 * by_kind([1.0, 0.15, 0.3, 0.6])


def log_factor(key, shape):
    return jnp.exp(jax.random.uniform(key, shape, jnp.float32, 0.0, math.log(4.0)))


def orthogonal_draw(key):
    subkeys = jax.random.split(key, TPW * NBL)
    orders = jax.vmap(lambda subkey: jax.random.permutation(subkey, BLK))(subkeys).reshape(TPW, NBL, BLK)
    flips = jnp.where(jax.random.bernoulli(jax.random.fold_in(key, 7), 0.5, (TPW, NBL, 1, BLK)), 1.0, -1.0)
    column = jnp.arange(BLK).astype(jnp.float32)
    scales = jnp.where(column == 0, (1.0 / BLK) ** 0.5, (2.0 / BLK) ** 0.5)
    return scales * jnp.cos(math.pi * (orders[..., None].astype(jnp.float32) + 0.5) * column / BLK) * flips


def statistic_draw(key):
    entries = BLK * gradient_size()[..., 0] ** 2 * log_factor(jax.random.fold_in(key, 1), (TPW, NBL, BLK))
    turn = orthogonal_draw(jax.random.fold_in(key, 2))
    full = jnp.matmul(turn * entries[..., None, :], jnp.swapaxes(turn, -1, -2), precision=lax.Precision.HIGHEST)
    return 0.5 * (full + jnp.swapaxes(full, -1, -2))


def vector_size():
    column = jnp.arange(NVEC)
    return TOKENS ** 0.5 * jnp.where((column >= 8 * D) & (column < 8 * D + FF), 0.3, 1.0)


def draw_matrices(key, part):
    key = jax.random.fold_in(key, 11)
    spread = by_kind([D ** (-0.5), (32.0 / D) ** 0.5, D ** (-0.5), FF ** (-0.5)])
    return jax.random.truncated_normal(key, -3.0, 3.0, (TPW, NBL, BLK, BLK), jnp.float32) * spread


def draw_first_moment(key, part):
    key = jax.random.fold_in(key, 12)
    return 0.111 * jax.random.truncated_normal(key, -3.0, 3.0, (TPW, NBL, BLK, BLK), jnp.float32) * gradient_size()


def draw_second_moment(key, part):
    key = jax.random.fold_in(key, 13)
    return log_factor(key, (TPW, NBL, BLK, BLK)) * (0.05 / 0.95) * gradient_size() ** 2


def draw_left_stat(key, part):
    key = jax.random.fold_in(key, 14)
    return statistic_draw(key)


def draw_right_stat(key, part):
    key = jax.random.fold_in(key, 15)
    return statistic_draw(key)


def draw_left_basis(key, part):
    key = jax.random.fold_in(key, 16)
    return orthogonal_draw(key)


def draw_right_basis(key, part):
    key = jax.random.fold_in(key, 17)
    return orthogonal_draw(key)


def draw_vectors(key, part):
    key = jax.random.fold_in(key, 18)
    column = jnp.arange(NVEC)
    gain_area = (column < D) | (column >= 2 * D) & (column < 3 * D)
    spread = jax.random.uniform(jax.random.fold_in(key, 1), (NVEC,), jnp.float32, -1.0, 1.0)
    shifts = jax.random.truncated_normal(jax.random.fold_in(key, 2), -3.0, 3.0, (NVEC,), jnp.float32)
    return jnp.where(gain_area, 1.0 + 0.15 * spread, 0.2 * shifts)


def draw_vec_first(key, part):
    key = jax.random.fold_in(key, 19)
    return 0.111 * jax.random.truncated_normal(key, -3.0, 3.0, (NVEC,), jnp.float32) * vector_size()


def draw_vec_second(key, part):
    key = jax.random.fold_in(key, 20)
    return log_factor(key, (NVEC,)) * (0.05 / 0.95) * vector_size() ** 2


def block_levels(key, shape, cuts, low, largest):
    loudness, own = 1.0, jax.random.fold_in(key, 6)
    for position, shards_of in cuts:
        steps = jnp.exp(jax.random.uniform(jax.random.fold_in(own, position), (shards_of,), jnp.float32, low / len(cuts), largest / len(cuts)))
        loudness = loudness * jnp.repeat(steps, shape[position] // shards_of).reshape([-1 if axis == position else 1 for axis in range(len(shape))])
    return loudness


def length_profile(number_of, total, limit, lean):
    portions = [(1 << 20) // math.isqrt(rank ** lean) + 1 for rank in range(2, number_of + 1)]
    rest, given = total - limit - (number_of - 1), [1] * (number_of - 1)
    while rest > 0:
        free = [i for i in range(number_of - 1) if given[i] < limit]
        pool, left = sum([portions[i] for i in free]), rest
        for i in free:
            more = min(limit - given[i], max(1, left * portions[i] // pool), rest)
            given[i] = given[i] + more
            rest = rest - more
    return np.array([limit] + given)


def uneven_parts(rng, amount, total, limit, lean):
    if amount == 2:
        one = jax.random.randint(rng, (), max(1, total - limit), min(limit, total - 1) + 1)
        return jnp.stack([one, total - one])
    sizes = jnp.asarray(length_profile(amount, total, limit, lean), jnp.int32)
    pairs = (amount - 1) // 2
    giver, taker = sizes[1:1 + 2 * pairs:2], sizes[2:2 + 2 * pairs:2]
    room = jnp.minimum(giver - 1, limit - taker)
    passed = jax.random.randint(jax.random.fold_in(rng, 1), (pairs,), 0, 1 << 20) % (room + 1)
    sizes = sizes.at[1:1 + 2 * pairs:2].set(giver - passed).at[2:2 + 2 * pairs:2].set(taker + passed)
    return sizes[jax.random.permutation(jax.random.fold_in(rng, 2), amount)]


def scatter_about(rng, shape, deviation, bound, shards=(), kind=jnp.bfloat16):
    level = block_levels(rng, shape, shards, -0.22, 0.18) if shards else 1.0
    drawn = jax.random.normal(rng, shape, jnp.float32) * deviation * level
    return jnp.minimum(jnp.maximum(drawn, -bound), bound).astype(kind)


def setup_inputs(seed: int = 0) -> dict:
    key_of = jax.random.split(jax.random.key(seed), 14)
    block_input = scatter_about(key_of[0], (TOKENS, D), 1.0, 6.0, ((0, 32),), jnp.float32)
    cotangent = scatter_about(key_of[1], (TOKENS, D), 1.0, 6.0, ((0, 32),), jnp.float32)
    segments = jax.vmap(lambda own: jnp.searchsorted(jnp.cumsum(uneven_parts(own, 4, LEN, LEN * 25 // 32, 1)), jnp.arange(LEN), side="right"))(jax.random.split(key_of[2], SEQS)).reshape((SEQS, LEN)).astype(jnp.int32)
    matrices = draw_matrices(jax.random.fold_in(key_of[13], 71), 0)
    first_moment = draw_first_moment(jax.random.fold_in(key_of[13], 71), 0)
    second_moment = draw_second_moment(jax.random.fold_in(key_of[13], 71), 0)
    left_stat = draw_left_stat(jax.random.fold_in(key_of[13], 71), 0)
    right_stat = draw_right_stat(jax.random.fold_in(key_of[13], 71), 0)
    left_basis = draw_left_basis(jax.random.fold_in(key_of[13], 71), 0)
    right_basis = draw_right_basis(jax.random.fold_in(key_of[13], 71), 0)
    vectors = draw_vectors(jax.random.fold_in(key_of[13], 71), 0)
    vec_first = draw_vec_first(jax.random.fold_in(key_of[13], 71), 0)
    vec_second = draw_vec_second(jax.random.fold_in(key_of[13], 71), 0)
    return {"block_input": block_input, "cotangent": cotangent, "segments": segments, "matrices": matrices, "first_moment": first_moment, "second_moment": second_moment, "left_stat": left_stat, "right_stat": right_stat, "left_basis": left_basis, "right_basis": right_basis, "vectors": vectors, "vec_first": vec_first, "vec_second": vec_second}


highest = lax.Precision.HIGHEST
epsilon_norm = 1e-05
epsilon_adam = 1e-08
rope_base = 10000.0
beta_one = 0.9
beta_two = 0.95
beta_stat = 0.95
rate_matrix = 0.05
rate_vector = 0.1
weight_decay = 0.01

@jax.custom_vjp
def low(v):
    return lax.optimization_barrier(v.astype(jnp.bfloat16)).astype(jnp.float32)

@jax.custom_vjp
def low_back(v):
    return v

def low_keep(v):
    return (low(v), None)

def low_pass(kept, grad):
    return (grad,)

def back_keep(v):
    return (v, None)

def back_low(kept, grad):
    return (low(grad),)
low.defvjp(low_keep, low_pass)
low_back.defvjp(back_keep, back_low)

def layer_norm(rows, gain, shift):
    middle = lax.optimization_barrier(jnp.mean(rows, axis=-1, keepdims=True))
    centered = rows - middle
    spread = lax.optimization_barrier(jnp.mean(centered * centered, axis=-1, keepdims=True))
    return centered * lax.rsqrt(spread + epsilon_norm) * gain + shift

def angles(segments):
    seq_count = segments.shape[0]
    column = jnp.arange(LEN, dtype=jnp.int32)[None, :]
    border = jnp.concatenate([jnp.ones((seq_count, 1), jnp.bool_), segments[:, 1:] != segments[:, :-1]], axis=1)
    starts = lax.cummax(jnp.where(border, column, 0).astype(jnp.int32), axis=1)
    places = (column - starts).astype(jnp.float32)
    frequency = 1.0 / rope_base ** (jnp.arange(0, RD, 2).astype(jnp.float32) / RD)
    turns = places[:, :, None] * frequency[None, None, :]
    return (jnp.cos(turns)[:, :, None, :], jnp.sin(turns)[:, :, None, :])

def rotate(part, cosine, sine):
    half_dims = RD // 2
    first_half = part[..., :half_dims]
    second_half = part[..., half_dims:RD]
    return jnp.concatenate([first_half * cosine - second_half * sine, second_half * cosine + first_half * sine, part[..., RD:]], axis=-1)

def split_blocks(blocks):
    row_blocks = D // HD
    hidden_blocks = FPS // HD
    attn_count = HPS * 4 * row_blocks
    up_count = hidden_blocks * row_blocks
    attn_part = blocks[:, :attn_count].reshape(TPW, HPS, 4, row_blocks, HD, HD)
    w_up = blocks[:, attn_count:attn_count + up_count].reshape(TPW, hidden_blocks, row_blocks, HD, HD)
    w_down = blocks[:, attn_count + up_count:].reshape(TPW, hidden_blocks, row_blocks, HD, HD)
    return (attn_part[:, :, :3], attn_part[:, :, 3], w_up, w_down)

def attend_one(queries, keys_rot, values, segment_row):
    column = jnp.arange(LEN)
    allowed = (segment_row[:, None] == segment_row[None, :]) & (column[None, :] <= column[:, None])
    scores = low_back(jnp.einsum('qhd,khd->hqk', queries, keys_rot, precision=highest) * HD ** (-0.5))
    scores = jnp.where(allowed[None], scores, -1e+30)
    probs = jax.nn.softmax(scores, axis=-1)
    return jnp.einsum('hqk,khd->qhd', low(probs), values, precision=highest)

def group_forward(blocks, params, rows, segs):
    w_qkv, w_out, w_up, w_down = split_blocks(low(blocks))
    gain_one = params[0:D]
    shift_one = params[D:2 * D]
    gain_two = params[2 * D:3 * D]
    shift_two = params[3 * D:4 * D]
    bias_qkv = params[4 * D:7 * D]
    bias_out = params[7 * D:8 * D]
    bias_up = params[8 * D:8 * D + FF]
    bias_down = params[8 * D + FF:9 * D + FF]
    tokens_here = rows.shape[0]
    row_blocks = D // HD
    norm_one = low(layer_norm(rows, gain_one, shift_one))
    norm_two = low(layer_norm(rows, gain_two, shift_two))
    projected = jnp.einsum('tbr,phqbrc->tphqc', norm_one.reshape(tokens_here, row_blocks, HD), w_qkv, precision=highest)
    projected = low_back(projected.reshape(tokens_here, H, 3, HD) + bias_qkv.reshape(H, 3, HD))
    shaped = projected.reshape(segs.shape[0], LEN, H, 3, HD)
    cosine, sine = angles(segs)
    queries = low(rotate(shaped[:, :, :, 0], cosine, sine))
    keys_rot = low(rotate(shaped[:, :, :, 1], cosine, sine))
    values = low(shaped[:, :, :, 2])
    attended = lax.map(jax.checkpoint(lambda items: attend_one(items[0], items[1], items[2], items[3])), (queries, keys_rot, values, segs))
    attended = low(low_back(attended)).reshape(tokens_here, TPW, HPS, HD)
    attn_branch = jnp.einsum('tphr,phbrc->tbc', attended, w_out, precision=highest).reshape(tokens_here, D)
    attn_branch = low_back(attn_branch + bias_out)
    pre_act = jnp.einsum('tbr,pkbrc->tpkc', norm_two.reshape(tokens_here, row_blocks, HD), w_up, precision=highest)
    pre_act = low_back(pre_act.reshape(tokens_here, FF) + bias_up)
    act_low = low(jax.nn.gelu(pre_act, approximate=False)).reshape(tokens_here, TPW, FPS // HD, HD)
    mlp_branch = jnp.einsum('tpkr,pkbrc->tbc', act_low, w_down, precision=highest).reshape(tokens_here, D)
    mlp_branch = low_back(mlp_branch + bias_down)
    return rows + attn_branch + mlp_branch

def swap_last(matrix):
    return jnp.swapaxes(matrix, -1, -2)

def basis_step(matrix):
    gram = jnp.matmul(swap_last(matrix), matrix, precision=highest)
    lower_factor = jnp.linalg.cholesky(gram)
    return swap_last(jax.scipy.linalg.solve_triangular(lower_factor, swap_last(matrix), lower=True))

def soap_update(grad, weight, first, second, lstat, rstat, lbasis, rbasis):
    turned = jnp.matmul(jnp.matmul(swap_last(lbasis), grad, precision=highest), rbasis, precision=highest)
    first_new = beta_one * first + (1.0 - beta_one) * turned
    second_new = beta_two * second + (1.0 - beta_two) * turned * turned
    direction = first_new / (1.0 - beta_one ** STEP) / (jnp.sqrt(second_new / (1.0 - beta_two ** STEP)) + epsilon_adam)
    stepped = jnp.matmul(jnp.matmul(lbasis, direction, precision=highest), swap_last(rbasis), precision=highest)
    weight_new = weight - rate_matrix * (stepped + weight_decay * weight)
    lstat_new = beta_stat * lstat + (1.0 - beta_stat) * jnp.matmul(grad, swap_last(grad), precision=highest)
    rstat_new = beta_stat * rstat + (1.0 - beta_stat) * jnp.matmul(swap_last(grad), grad, precision=highest)
    lbasis_new = basis_step(jnp.matmul(lstat_new, lbasis, precision=highest))
    rbasis_new = basis_step(jnp.matmul(rstat_new, rbasis, precision=highest))
    return (weight_new, weight_new.astype(jnp.bfloat16), first_new, second_new, lstat_new, rstat_new, lbasis_new, rbasis_new)

def adam_vector(grad, params, first, second):
    first_new = beta_one * first + (1.0 - beta_one) * grad
    second_new = beta_two * second + (1.0 - beta_two) * grad * grad
    direction = first_new / (1.0 - beta_one ** STEP) / (jnp.sqrt(second_new / (1.0 - beta_two ** STEP)) + epsilon_adam)
    return (params - rate_vector * direction, first_new, second_new)

def reference(block_input, cotangent, segments, matrices, first_moment, second_moment, left_stat, right_stat, left_basis, right_basis, vectors, vec_first, vec_second):

    def forward(blocks, params, rows):
        stacked = rows.reshape(SEQS // 4, 4 * LEN, D)
        seg_groups = segments.reshape(SEQS // 4, 4, LEN)
        result = lax.map(lambda items: jax.checkpoint(group_forward)(blocks, params, items[0], items[1]), (stacked, seg_groups))
        return result.reshape(TOKENS, D)
    output, pull = jax.vjp(forward, matrices, vectors, block_input)
    grad_blocks, grad_vectors, grad_input = pull(cotangent)
    updated = lax.map(lambda items: soap_update(items[0], items[1], items[2], items[3], items[4], items[5], items[6], items[7]), (grad_blocks, matrices, first_moment, second_moment, left_stat, right_stat, left_basis, right_basis))
    new_vectors, new_vec_first, new_vec_second = adam_vector(grad_vectors, vectors, vec_first, vec_second)
    return (output, grad_input, updated[0], updated[1], updated[2], updated[3], updated[4], updated[5], updated[6], updated[7], new_vectors, new_vec_first, new_vec_second)
```

```python
import functools

import jax
import jax.numpy as jnp
from jax import lax
from jax.experimental import pallas as pl
from jax.experimental.pallas import tpu as pltpu
from jax.sharding import PartitionSpec as P

D = 2048
H = 8
HD = 256
RD = 64
FF = 8192
LEN = 1024
STEP = 10


epsilon_norm = 1e-05
epsilon_adam = 1e-08
rope_base = 10000.0
beta_one = 0.9
beta_two = 0.95
beta_stat = 0.95
rate_matrix = 0.05
rate_vector = 0.1
weight_decay = 0.01
PAN = 32
UNROLL = 8
GROUP = 2


def layer_norm(rows, gain, shift):
    middle = jnp.mean(rows, axis=-1, keepdims=True)
    centered = rows - middle
    spread = jnp.mean(centered * centered, axis=-1, keepdims=True)
    inverse = lax.rsqrt(spread + epsilon_norm)
    unit = centered * inverse
    return (unit * gain + shift, unit, inverse)


def norm_back(grad, unit, inverse, gain):
    scaled = grad * gain
    return inverse * (
        scaled
        - jnp.mean(scaled, axis=-1, keepdims=True)
        - unit * jnp.mean(scaled * unit, axis=-1, keepdims=True)
    )


def angles(segments):
    seq_count = segments.shape[0]
    column = jnp.arange(LEN, dtype=jnp.int32)[None, :]
    border = jnp.concatenate(
        [jnp.ones((seq_count, 1), jnp.bool_), segments[:, 1:] != segments[:, :-1]], axis=1
    )
    starts = lax.cummax(jnp.where(border, column, 0), axis=1)
    places = (column - starts).astype(jnp.float32)
    frequency = 1.0 / rope_base ** (jnp.arange(0, RD, 2).astype(jnp.float32) / RD)
    turns = places[:, :, None] * frequency[None, None, :]
    return (jnp.cos(turns)[:, :, None, :], jnp.sin(turns)[:, :, None, :])


def rotate(part, cosine, sine):
    half_dims = RD // 2
    first_half = part[..., :half_dims]
    second_half = part[..., half_dims:RD]
    return jnp.concatenate(
        [
            first_half * cosine - second_half * sine,
            second_half * cosine + first_half * sine,
            part[..., RD:],
        ],
        axis=-1,
    )


def unpack_blocks(blocks, heads_here, row_blocks, hidden_blocks):
    attn_count = heads_here * 4 * row_blocks
    up_count = hidden_blocks * row_blocks
    attn_part = blocks[:attn_count].reshape(heads_here, 4, row_blocks, HD, HD)
    w_up = blocks[attn_count : attn_count + up_count].reshape(hidden_blocks, row_blocks, HD, HD)
    w_down = blocks[attn_count + up_count :].reshape(hidden_blocks, row_blocks, HD, HD)
    return (attn_part[:, :3], attn_part[:, 3], w_up, w_down)


def masked_scores(queries, keys_rot, segment_row):
    column = jnp.arange(LEN)
    allowed = (segment_row[:, None] == segment_row[None, :]) & (column[None, :] <= column[:, None])
    scores = jnp.einsum(
        "qhd,khd->hqk", queries, keys_rot, preferred_element_type=jnp.float32
    ) * HD ** (-0.5)
    return jnp.where(allowed[None], scores, -1e30)


def seq_forward(items):
    queries, keys_rot, values, segment_row = items
    scores = masked_scores(queries, keys_rot, segment_row)
    row_max = jnp.max(scores, axis=-1, keepdims=True)
    powers = jnp.exp(scores - row_max)
    row_total = jnp.sum(powers, axis=-1, keepdims=True)
    probs_low = (powers / row_total).astype(jnp.bfloat16)
    attended = jnp.einsum("hqk,khd->qhd", probs_low, values, preferred_element_type=jnp.float32)
    return (attended, (row_max + jnp.log(row_total))[..., 0])


def seq_backward(items):
    queries, keys_rot, values, segment_row, log_total, grad_attend = items
    scores = masked_scores(queries, keys_rot, segment_row)
    probs = jnp.exp(scores - log_total[..., None])
    grad_probs = jnp.einsum("qhd,khd->hqk", grad_attend, values, preferred_element_type=jnp.float32)
    inner = jnp.sum(probs * grad_probs, axis=-1, keepdims=True)
    grad_scores = (probs * (grad_probs - inner)).astype(jnp.bfloat16)
    grad_queries = jnp.einsum(
        "hqk,khd->qhd", grad_scores, keys_rot, preferred_element_type=jnp.float32
    ) * HD ** (-0.5)
    grad_keys = jnp.einsum(
        "hqk,qhd->khd", grad_scores, queries, preferred_element_type=jnp.float32
    ) * HD ** (-0.5)
    grad_values = jnp.einsum(
        "hqk,qhd->khd", probs.astype(jnp.bfloat16), grad_attend, preferred_element_type=jnp.float32
    )
    return (grad_queries, grad_keys, grad_values)


def gelu_exact(inputs):
    return jax.nn.gelu(inputs, approximate=False)


def dot_nn(a, b):
    return lax.dot_general(a, b, (((1,), (0,)), ((), ())), preferred_element_type=jnp.float32)


def dot_nt(a, b):
    return lax.dot_general(a, b, (((1,), (1,)), ((), ())), preferred_element_type=jnp.float32)


def dot_tn(a, b):
    return lax.dot_general(a, b, (((0,), (0,)), ((), ())), preferred_element_type=jnp.float32)


def split(x):
    high = x.astype(jnp.bfloat16)
    return high, (x - high.astype(jnp.float32)).astype(jnp.bfloat16)


def three(dot, a, b):
    return dot(a[0], b[0]) + (dot(a[0], b[1]) + dot(a[1], b[0]))


def eliminate(diag, mats):
    lane = lax.broadcasted_iota(jnp.int32, (mats, 128), 1)
    rows = []
    for i in range(PAN):
        row = diag[pl.ds(i * mats, mats), :]
        rows.append(jnp.where(lane < PAN, jnp.where(lane == i, 1.0, 0.0), row))

    def entry(row, j):
        return jnp.broadcast_to(row[:, PAN + j : PAN + j + 1], (mats, 128))

    for k in range(0, PAN, 2):
        one, two = rows[k], rows[k + 1]
        cross = entry(one, k + 1)
        inverse = lax.rsqrt(entry(one, k))
        ratio = cross * (inverse * inverse)
        inverse_two = lax.rsqrt(entry(two, k + 1) - ratio * cross)
        two = two - ratio * one
        first, second = one * inverse, two * inverse_two
        diag[pl.ds(k * mats, mats), :] = first
        diag[pl.ds((k + 1) * mats, mats), :] = second
        for i in range(k + 2, PAN):
            of_one = entry(rows[k], i)
            of_two = entry(rows[k + 1], i) - ratio * of_one
            rows[i] = rows[i] - (of_one * inverse) * first - (of_two * inverse_two) * second


def soap_kernel(count, g, w, f, s, ls, rs, lb, rb, ow, owl, of, os, ols, ors, olb, orb, aug, diag):
    step = pl.program_id(0)
    mats = 2 * count
    unroll = UNROLL if mats % UNROLL == 0 else 4
    blocks = range(GROUP)
    grad = [g[i].astype(jnp.bfloat16) for i in blocks]
    left, right = [split(lb[i]) for i in blocks], [split(rb[i]) for i in blocks]
    left_t = [(x.T, y.T) for x, y in left]
    right_t = [(x.T, y.T) for x, y in right]
    grad_t = [x.T for x in grad]
    lnew = [beta_stat * ls[i] + (1.0 - beta_stat) * dot_nn(grad[i], grad_t[i]) for i in blocks]
    rnew = [beta_stat * rs[i] + (1.0 - beta_stat) * dot_nn(grad_t[i], grad[i]) for i in blocks]
    turned = [dot_nn(left_t[i][0], grad[i]) + dot_nn(left_t[i][1], grad[i]) for i in blocks]
    for i in blocks:
        ols[i] = lnew[i]
        ors[i] = rnew[i]
    turned = [three(dot_nn, split(turned[i]), right[i]) for i in blocks]
    sides = [
        three(dot_nn, basis_t, split(stat))
        for i in blocks
        for basis_t, stat in ((left_t[i], lnew[i]), (right_t[i], rnew[i]))
    ]
    first_new = [beta_one * f[i] + (1.0 - beta_one) * turned[i] for i in blocks]
    second_new = [beta_two * s[i] + (1.0 - beta_two) * turned[i] * turned[i] for i in blocks]
    direction = [
        x / (1.0 - beta_one**STEP) / (jnp.sqrt(y / (1.0 - beta_two**STEP)) + epsilon_adam)
        for x, y in zip(first_new, second_new)
    ]
    for i in blocks:
        of[i] = first_new[i]
        os[i] = second_new[i]
    stepped = [three(dot_nn, left[i], split(direction[i])) for i in blocks]
    for i, side in enumerate(sides):
        aug[2 * GROUP * step + i, :, HD:] = side
    grams = [three(dot_nt, x, x) for x in map(split, sides)]
    stepped = [three(dot_nn, split(stepped[i]), right_t[i]) for i in blocks]
    for i, gram in enumerate(grams):
        aug[2 * GROUP * step + i, :, :HD] = gram
    for i in blocks:
        weight = w[i]
        weight_new = weight - rate_matrix * (stepped[i] + weight_decay * weight)
        ow[i] = weight_new
        owl[i] = weight_new.astype(jnp.bfloat16)

    @pl.when(step == count // GROUP - 1)
    def _():
        for p in range(HD // PAN):
            low = p * PAN

            def place(m):
                base = low // 128 * 128
                own = aug[m, low : low + PAN, base : base + 128]
                shift = (PAN - (low - base)) % 128
                if shift:
                    own = pltpu.roll(own, shift, 1)
                diag[pl.ds(m, PAN, stride=mats), :] = own

            if p == 0:

                def start(i, carry):
                    for u in range(unroll):
                        place(i * unroll + u)
                    return carry

                lax.fori_loop(0, mats // unroll, start, 0)
            eliminate(diag, mats)
            low = low + PAN
            edge = low // 128 * 128

            def update(i, carry):
                mine = [i * unroll + u for u in range(unroll)]
                factors = [split(diag[pl.ds(m, PAN, stride=mats), :][:, :PAN]) for m in mine]
                panels = [split(aug[m, low - PAN : low, :]) for m in mine]
                panels = [three(dot_nn, x, y) for x, y in zip(factors, panels)]
                if low == HD:
                    for m, panel in zip(mine, panels):
                        aug[m, low - PAN : low, HD:] = panel[:, HD:]
                    return carry
                parts = [split(panel) for panel in panels]
                lhs = [jnp.concatenate([x[:, :HD], x[:, :HD], y[:, :HD]], axis=0).T for x, y in parts]
                rhs = [jnp.concatenate([x, y, x], axis=0) for x, y in parts]
                rest = [
                    aug[m, low:, edge:] - dot_nn(x[low:], y[:, edge:]) for m, x, y in zip(mine, lhs, rhs)
                ]
                for m, panel, left in zip(mine, panels, rest):
                    aug[m, low - PAN : low, HD:] = panel[:, HD:]
                    aug[m, low:, edge:] = left
                    own = left[:PAN, :128]
                    shift = (PAN - (low - edge)) % 128
                    if shift:
                        own = pltpu.roll(own, shift, 1)
                    diag[pl.ds(m, PAN, stride=mats), :] = own
                return carry

            lax.fori_loop(0, mats // unroll, update, 0)

        def finish(b, carry):
            for side, out in enumerate((olb, orb)):
                out[b] = aug[2 * b + side, :, HD:].T
            return carry

        lax.fori_loop(0, count, finish, 0)


LIMIT = 56 * 2**20


def cost(flops, moved, trans=0):
    return pl.CostEstimate(flops=int(flops), bytes_accessed=int(moved), transcendentals=int(trans))


def turn(rows, cosine, sine):
    head = rows[:, :128]
    lane = lax.broadcasted_iota(jnp.int32, head.shape, 1)
    partner = jnp.where(lane < RD // 2, pltpu.roll(head, 128 - RD // 2, 1), pltpu.roll(head, RD // 2, 1))
    return jnp.concatenate([head * cosine + partner * sine, rows[:, 128:]], axis=1)


def project_kernel(unit, grad, gain, shift, bias, cosine, sine, wq, wk, wv, wo, q, k, v, ga):
    norm = (unit[...].astype(jnp.float32) * gain[...] + shift[...]).astype(jnp.bfloat16)
    q[...] = turn(dot_nn(norm, wq[...]) + bias[0:1, :], cosine[...], sine[...]).astype(jnp.bfloat16)
    k[...] = turn(dot_nn(norm, wk[...]) + bias[1:2, :], cosine[...], sine[...]).astype(jnp.bfloat16)
    v[...] = (dot_nn(norm, wv[...]) + bias[2:3, :]).astype(jnp.bfloat16)
    total = dot_nt(grad[:, :HD], wo[0])
    for b in range(1, D // HD):
        total = total + dot_nt(grad[:, b * HD : (b + 1) * HD], wo[b])
    ga[...] = total.astype(jnp.bfloat16)


def project(unit, grad, gain, shift, bias, cosine, sine, wq, wk, wv, wo):
    tokens = unit.shape[0]
    tile = 512
    rows = pl.BlockSpec((tile, D), lambda i: (i, 0))
    narrow = pl.BlockSpec((tile, HD), lambda i: (i, 0))
    angle = pl.BlockSpec((tile, 128), lambda i: (i, 0))
    line = pl.BlockSpec((1, D), lambda i: (0, 0))
    flat = pl.BlockSpec((D, HD), lambda i: (0, 0))
    return pl.pallas_call(
        project_kernel,
        grid=(tokens // tile,),
        in_specs=[rows, rows, line, line, pl.BlockSpec((3, HD), lambda i: (0, 0)), angle, angle]
        + [flat] * 3
        + [pl.BlockSpec((D // HD, HD, HD), lambda i: (0, 0, 0))],
        out_specs=[narrow] * 4,
        out_shape=[jax.ShapeDtypeStruct((tokens, HD), jnp.bfloat16)] * 4,
        compiler_params=pltpu.CompilerParams(vmem_limit_bytes=LIMIT),
        cost_estimate=cost(8 * tokens * D * HD, 4 * tokens * D + 8 * D * HD),
        name="project",
    )(unit, grad, gain, shift, bias, cosine, sine, wq.reshape(D, HD), wk.reshape(D, HD), wv.reshape(D, HD), wo)


def attention_kernel(q, k, v, ga, seg_row, seg_col, cosine, sine, att, dq, dk, dv, keys, vals):
    tile = 256
    scale = HD ** (-0.5)
    keys[...] = jnp.zeros_like(keys)
    vals[...] = jnp.zeros_like(vals)
    for i in range(LEN // tile):
        here = slice(i * tile, (i + 1) * tile)
        upto = (i + 1) * tile
        scores = dot_nt(q[here, :], k[:upto, :]) * scale
        at = lax.broadcasted_iota(jnp.int32, (tile, upto), 0) + i * tile
        of = lax.broadcasted_iota(jnp.int32, (tile, upto), 1)
        allowed = (seg_col[0, here, :] == seg_row[0, :, :upto]) & (of <= at)
        scores = jnp.where(allowed, scores, -1e30)
        powers = jnp.exp(scores - jnp.max(scores, axis=-1, keepdims=True))
        probs = powers / jnp.sum(powers, axis=-1, keepdims=True)
        low = probs.astype(jnp.bfloat16)
        att[here, :] = dot_nn(low, v[:upto, :]).astype(jnp.bfloat16)
        pull = dot_nt(ga[here, :], v[:upto, :])
        inner = jnp.sum(probs * pull, axis=-1, keepdims=True)
        gs = (probs * (pull - inner)).astype(jnp.bfloat16)
        dq[here, :] = turn(dot_nn(gs, k[:upto, :]) * scale, cosine[here, :], -sine[here, :]).astype(jnp.bfloat16)
        keys[:upto, :] = keys[:upto, :] + dot_tn(gs, q[here, :])
        vals[:upto, :] = vals[:upto, :] + dot_tn(low, ga[here, :])
    dk[...] = turn(keys[...] * scale, cosine[...], -sine[...]).astype(jnp.bfloat16)
    dv[...] = vals[...].astype(jnp.bfloat16)


def attention(q, k, v, ga, segments, cosine, sine):
    tokens = q.shape[0]
    count = tokens // LEN
    narrow = pl.BlockSpec((LEN, HD), lambda i: (i, 0))
    angle = pl.BlockSpec((LEN, 128), lambda i: (i, 0))
    return pl.pallas_call(
        attention_kernel,
        grid=(count,),
        in_specs=[narrow] * 4
        + [pl.BlockSpec((1, 1, LEN), lambda i: (i, 0, 0)), pl.BlockSpec((1, LEN, 1), lambda i: (i, 0, 0))]
        + [angle] * 2,
        out_specs=[narrow] * 4,
        out_shape=[jax.ShapeDtypeStruct((tokens, HD), jnp.bfloat16)] * 4,
        scratch_shapes=[pltpu.VMEM((LEN, HD), jnp.float32)] * 2,
        compiler_params=pltpu.CompilerParams(vmem_limit_bytes=LIMIT),
        cost_estimate=cost(14 * tokens * LEN * HD, 16 * tokens * HD, tokens * LEN),
        name="attention",
    )(q, k, v, ga, segments.reshape(count, 1, LEN), segments.reshape(count, LEN, 1), cosine, sine)


def mlp_kernel(unit, grad, gain, shift, bias, wu, wd, act, pre):
    norm = (unit[...].astype(jnp.float32) * gain[...] + shift[...]).astype(jnp.bfloat16)
    inner = dot_nn(norm, wu[...]) + bias[...]
    pull = dot_nt(grad[:, :HD], wd[0])
    for b in range(1, D // HD):
        pull = pull + dot_nt(grad[:, b * HD : (b + 1) * HD], wd[b])
    share = 0.5 + 0.5 * lax.erf(inner * (0.5**0.5))
    act[...] = (inner * share).astype(jnp.bfloat16)
    slope = share + inner * jnp.exp(-0.5 * inner * inner) * ((2.0 * 3.141592653589793) ** (-0.5))
    pre[...] = (slope * pull).astype(jnp.bfloat16)


def mlp(unit, grad, gain, shift, bias, wu, wd):
    tokens = unit.shape[0]
    tile = 512
    rows = pl.BlockSpec((tile, D), lambda i: (i, 0))
    narrow = pl.BlockSpec((tile, HD), lambda i: (i, 0))
    line = pl.BlockSpec((1, D), lambda i: (0, 0))
    return pl.pallas_call(
        mlp_kernel,
        grid=(tokens // tile,),
        in_specs=[rows, rows, line, line, pl.BlockSpec((1, HD), lambda i: (0, 0))]
        + [pl.BlockSpec((D, HD), lambda i: (0, 0)), pl.BlockSpec((D // HD, HD, HD), lambda i: (0, 0, 0))],
        out_specs=[narrow] * 2,
        out_shape=[jax.ShapeDtypeStruct((tokens, HD), jnp.bfloat16)] * 2,
        compiler_params=pltpu.CompilerParams(vmem_limit_bytes=LIMIT),
        cost_estimate=cost(4 * tokens * D * HD, 4 * tokens * D + 4 * D * HD, 2 * tokens * HD),
        name="mlp",
    )(unit, grad, gain, shift, bias, wu.reshape(D, HD), wd)


def output_kernel(parts, *refs):
    acts, weights, out = refs[:parts], refs[parts : 2 * parts], refs[-1]
    for b in range(D // HD):
        total = dot_nn(acts[0][...], weights[0][b])
        for a, w in zip(acts[1:], weights[1:]):
            total = total + dot_nn(a[...], w[b])
        out[:, b * HD : (b + 1) * HD] = total.astype(jnp.bfloat16)


def output_rows(acts, weights):
    tokens, parts = acts[0].shape[0], len(acts)
    tile = 512
    return pl.pallas_call(
        functools.partial(output_kernel, parts),
        grid=(tokens // tile,),
        in_specs=[pl.BlockSpec((tile, HD), lambda i: (i, 0))] * parts
        + [pl.BlockSpec((D // HD, HD, HD), lambda i: (0, 0, 0))] * parts,
        out_specs=pl.BlockSpec((tile, D), lambda i: (i, 0)),
        out_shape=jax.ShapeDtypeStruct((tokens, D), jnp.bfloat16),
        compiler_params=pltpu.CompilerParams(vmem_limit_bytes=LIMIT),
        cost_estimate=cost(2 * parts * tokens * D * HD, 2 * tokens * D + parts * 2 * D * HD),
        name="output_rows",
    )(*acts, *weights)


def input_kernel(first, second, *refs):
    grads, weights = refs[: first + second], refs[first + second : 2 * (first + second)]
    gain_one, gain_two, out = refs[-3:]

    def summed(low, high, b):
        total = dot_nt(grads[low][...], weights[low][b])
        for i in range(low + 1, high):
            total = total + dot_nt(grads[i][...], weights[i][b])
        return total

    for b in range(D // HD):
        here = slice(b * HD, (b + 1) * HD)
        total = summed(0, first, b) * gain_one[:, here] + summed(first, first + second, b) * gain_two[:, here]
        out[:, here] = total.astype(jnp.bfloat16)


def input_rows(ones, twos, weights, gain_one, gain_two):
    tokens, parts = ones[0].shape[0], len(weights)
    tile = 512
    line = pl.BlockSpec((1, D), lambda i: (0, 0))
    return pl.pallas_call(
        functools.partial(input_kernel, len(ones), len(twos)),
        grid=(tokens // tile,),
        in_specs=[pl.BlockSpec((tile, HD), lambda i: (i, 0))] * parts
        + [pl.BlockSpec((D // HD, HD, HD), lambda i: (0, 0, 0))] * parts
        + [line] * 2,
        out_specs=pl.BlockSpec((tile, D), lambda i: (i, 0)),
        out_shape=jax.ShapeDtypeStruct((tokens, D), jnp.bfloat16),
        compiler_params=pltpu.CompilerParams(vmem_limit_bytes=LIMIT),
        cost_estimate=cost(2 * parts * tokens * D * HD, 2 * tokens * D + parts * 2 * D * HD),
        name="input_rows",
    )(*ones, *twos, *weights, gain_one, gain_two)


def down_grad_kernel(act, grad, out, flipped):
    @pl.when(pl.program_id(0) == 0)
    def _():
        flipped[...] = act[...].T

    out[0] = dot_nn(flipped[...], grad[...]).astype(jnp.bfloat16)


def down_grad(act, grad):
    tokens = act.shape[0]
    return pl.pallas_call(
        down_grad_kernel,
        grid=(D // HD,),
        in_specs=[pl.BlockSpec((tokens, HD), lambda b: (0, 0)), pl.BlockSpec((tokens, HD), lambda b: (0, b))],
        out_specs=pl.BlockSpec((1, HD, HD), lambda b: (b, 0, 0)),
        out_shape=jax.ShapeDtypeStruct((D // HD, HD, HD), jnp.bfloat16),
        scratch_shapes=[pltpu.VMEM((HD, tokens), jnp.bfloat16)],
        compiler_params=pltpu.CompilerParams(vmem_limit_bytes=LIMIT),
        cost_estimate=cost(2 * tokens * D * HD, 2 * tokens * D + 2 * D * HD),
        name="down_grad",
    )(act, grad)


def up_grad_kernel(parts, *refs):
    unit, gain, shift = refs[:3]
    grads, weights = refs[3 : 3 + parts], refs[3 + parts : 3 + 2 * parts]
    outs, (gains, shifts, biases) = refs[3 + 2 * parts : 3 + 3 * parts], refs[3 + 3 * parts : 6 + 3 * parts]
    flipped, column = refs[6 + 3 * parts :]

    @pl.when(pl.program_id(0) == 0)
    def _():
        for i, g in enumerate(grads):
            wide = g[...].astype(jnp.float32)
            flipped[i * HD : (i + 1) * HD, :] = g[...].T
            total = jnp.sum(wide, axis=0, keepdims=True)
            biases[:, i * HD : (i + 1) * HD] = total
            column[i] = jnp.broadcast_to(total, (128, HD)).T

    lines = []
    for i in range(parts):
        turned = dot_nn(flipped[i * HD : (i + 1) * HD, :], unit[...])
        weight = weights[i][0].T.astype(jnp.float32)
        bias = column[i][:, 0:1]
        lines.append(
            (jnp.sum(weight * turned, axis=0, keepdims=True), jnp.sum(weight * bias, axis=0, keepdims=True))
        )
        outs[i][0] = (turned * gain[...] + bias * shift[...]).T.astype(jnp.bfloat16)
    gains[...] = sum(x for x, _ in lines)
    shifts[...] = sum(x for _, x in lines)


def up_grad(unit, gain, shift, grads, weights):
    tokens, parts = unit.shape[0], len(grads)
    line = pl.BlockSpec((1, HD), lambda b: (0, b))
    block = pl.BlockSpec((1, HD, HD), lambda b: (b, 0, 0))
    result = pl.pallas_call(
        functools.partial(up_grad_kernel, parts),
        grid=(D // HD,),
        in_specs=[pl.BlockSpec((tokens, HD), lambda b: (0, b)), line, line]
        + [pl.BlockSpec((tokens, HD), lambda b: (0, 0))] * parts
        + [block] * parts,
        out_specs=[block] * parts + [line, line, pl.BlockSpec((1, parts * HD), lambda b: (0, 0))],
        out_shape=[jax.ShapeDtypeStruct((D // HD, HD, HD), jnp.bfloat16)] * parts
        + [jax.ShapeDtypeStruct((1, D), jnp.float32)] * 2
        + [jax.ShapeDtypeStruct((1, parts * HD), jnp.float32)],
        scratch_shapes=[pltpu.VMEM((parts * HD, tokens), jnp.bfloat16), pltpu.VMEM((parts, HD, 128), jnp.float32)],
        compiler_params=pltpu.CompilerParams(vmem_limit_bytes=LIMIT),
        cost_estimate=cost(2 * parts * tokens * D * HD, 2 * tokens * D + parts * 4 * D * HD),
        name="up_grad",
    )(unit, gain, shift, *grads, *weights)
    return result[:parts], result[parts][0], result[parts + 1][0], result[parts + 2][0]


def soap_part(places, grad, blocks, previous):
    total, count = blocks[0].shape[0], grad.shape[0]
    mats = 2 * count
    own = pl.BlockSpec((GROUP, HD, HD), lambda i, at: (i, 0, 0))
    some = pl.BlockSpec((GROUP, HD, HD), lambda i, at: (at[0] * (count // GROUP) + i, 0, 0))
    whole = pl.BlockSpec((count, HD, HD), lambda i, at: (at[0], 0, 0))
    full = jax.ShapeDtypeStruct((total, HD, HD), jnp.float32)
    shapes = [full, jax.ShapeDtypeStruct((total, HD, HD), jnp.bfloat16)] + [full] * 6
    extra = [] if previous is None else list(previous)

    def body(at, *refs):
        soap_kernel(count, *refs[:8], *refs[8 + len(extra) :])

    return pl.pallas_call(
        body,
        grid_spec=pltpu.PrefetchScalarGridSpec(
            num_scalar_prefetch=1,
            grid=(count // GROUP,),
            in_specs=[own] + [some] * 7 + [pl.BlockSpec(memory_space=pl.ANY)] * len(extra),
            out_specs=[some] * 6 + [whole] * 2,
            scratch_shapes=[
                pltpu.VMEM((mats, HD, 2 * HD), jnp.float32),
                pltpu.VMEM((PAN * mats, 128), jnp.float32),
            ],
        ),
        out_shape=shapes,
        input_output_aliases={9 + i: i for i in range(len(extra))},
        compiler_params=pltpu.CompilerParams(vmem_limit_bytes=LIMIT),
        cost_estimate=cost(count * 40 * 2 * HD**3 * 3, count * 16 * 4 * HD * HD),
        name="soap",
    )(places, grad, *blocks, *extra)


def adam_vector(grad, params, first, second):
    first_new = beta_one * first + (1.0 - beta_one) * grad
    second_new = beta_two * second + (1.0 - beta_two) * grad * grad
    direction = (
        first_new
        / (1.0 - beta_one**STEP)
        / (jnp.sqrt(second_new / (1.0 - beta_two**STEP)) + epsilon_adam)
    )
    return (params - rate_vector * direction, first_new, second_new)


ALL = ("dp", "heads", "tensor")
ORDER = ((0, 1, 2), (1, 2, 0), (2, 0, 1), (2, 0, 1), (0, 1, 2), (0, 2, 1), (2, 0, 1), (2, 0, 1))
SLOTS = ((0, 4, 5, 6), (3, 7, 1, 2))


def places():
    for z in range(4):
        for x in range(2):
            for y in range(2):
                for c in range(2):
                    yield z, x, y, c


def index_of(z, x, y, c):
    return ((z * 2 + x) * 2 + y) * 2 + c


def move(array, target):
    return lax.ppermute(array, ALL, [(index_of(*at), index_of(*target(*at))) for at in places()])


LINES = [[index_of(z, x, y, c) for z in range(4)] for x in range(2) for y in range(2) for c in range(2)]


def over_core(array):
    return move(array, lambda z, x, y, c: (z, x, y, 1 - c))


def over_y(array):
    return move(array, lambda z, x, y, c: (z, x, 1 - y, c))


def over_x(array):
    return move(array, lambda z, x, y, c: (z, 1 - x, y, c))


def over_xy(array):
    return move(array, lambda z, x, y, c: (z, 1 - x, 1 - y, c))


def over_z(array, flip):
    return move(array, lambda z, x, y, c: (z ^ flip, x, y, c))


def gather_rows(rows, x, y, c):
    parts = [rows, over_x(rows), over_y(rows), over_xy(rows)]
    own = jnp.stack(parts)
    other = over_core(own)
    buffer = jnp.zeros((2, 2, 2) + rows.shape, rows.dtype)
    for i, (dx, dy) in enumerate(((0, 0), (1, 0), (0, 1), (1, 1))):
        for core, source in ((c, own), (1 - c, other)):
            buffer = lax.dynamic_update_slice(buffer, source[i][None, None, None], (x ^ dx, y ^ dy, core, 0, 0))
    return buffer.reshape(-1, rows.shape[-1])


def scatter_rows(partial, x, y, c):
    pieces = partial.reshape(2, 2, 2, -1, partial.shape[-1])
    here = lax.dynamic_index_in_dim(pieces, c, 2, keepdims=False)
    there = lax.dynamic_index_in_dim(pieces, 1 - c, 2, keepdims=False)
    pair = (here.astype(jnp.float32) + over_core(there).astype(jnp.float32)).astype(jnp.bfloat16)

    def pick(dx, dy):
        return lax.dynamic_slice(pair, (x ^ dx, y ^ dy, 0, 0), (1, 1) + pair.shape[2:])[0, 0]

    return (
        pick(0, 0).astype(jnp.float32)
        + over_x(pick(1, 0)).astype(jnp.float32)
        + over_y(pick(0, 1)).astype(jnp.float32)
        + over_xy(pick(1, 1)).astype(jnp.float32)
    )


def total_vector(vector):
    for step in (over_core, over_y, over_x, lambda v: over_z(v, 1), lambda v: over_z(v, 2)):
        vector = vector + step(vector)
    return vector


def wide_angles(segments):
    cosine, sine = angles(segments)
    cosine, sine = cosine[:, :, 0], sine[:, :, 0]
    one, zero = jnp.ones(cosine.shape[:2] + (64,), jnp.float32), jnp.zeros(cosine.shape[:2] + (64,), jnp.float32)
    cosine = jnp.concatenate([cosine, cosine, one], axis=-1).reshape(-1, 128)
    sine = jnp.concatenate([-sine, sine, zero], axis=-1).reshape(-1, 128)
    return cosine, sine


def plane_shards(
    block_input,
    cotangent,
    segments,
    matrices,
    first_moment,
    second_moment,
    left_stat,
    right_stat,
    left_basis,
    right_basis,
    vectors,
    vec_first,
    vec_second,
):
    d, y, c = lax.axis_index("dp"), lax.axis_index("heads"), lax.axis_index("tensor")
    x = d % 2
    even = x == 0
    shard = 2 * y + c
    order = jnp.array(ORDER, jnp.int32)[d]
    slots = jnp.array(SLOTS, jnp.int32)[x]
    gain_one, shift_one, gain_two, shift_two = (vectors[i * D : (i + 1) * D] for i in range(4))
    head = shard * 2 + x
    qkv_offset = 4 * D + head * 3 * HD
    bias_qkv = lax.dynamic_slice_in_dim(vectors, qkv_offset, 3 * HD).reshape(3, HD)
    bias_out, bias_down = vectors[7 * D : 8 * D], vectors[8 * D + FF : 9 * D + FF]
    up_offsets = [8 * D + shard * (FF // 4) + slots[s] * HD for s in range(4)]
    bias_up = [lax.dynamic_slice_in_dim(vectors, at, HD).reshape(1, HD) for at in up_offsets]

    def pick(left, right):
        return jnp.where(even, left, right)

    weights = []
    for j in range(3):
        own = lax.dynamic_slice_in_dim(matrices[0], order[j] * 8, 8).astype(jnp.bfloat16)
        weights.append(lax.all_gather(own, ALL, axis=0, axis_index_groups=LINES))
    w = lambda z, j: weights[j][z]
    swap_a = over_x(pick(w(1, 1), w(0, 2)))
    swap_b = over_x(pick(w(1, 2), w(2, 2)))
    swap_c = over_x(w(3, 1))
    swap_d = over_x(w(3, 2))
    w_q, w_k, w_v, w_out = w(0, 0), w(0, 1), pick(w(0, 2), swap_a), pick(swap_a, swap_b)
    w_up = [w(1, 0), w(2, 0), pick(w(2, 1), w(1, 1)), pick(w(2, 2), w(1, 2))]
    w_down = [pick(swap_b, swap_d), w(3, 0), pick(swap_c, w(2, 1)), pick(swap_d, swap_c)]

    middle = jnp.mean(block_input, axis=-1, keepdims=True)
    centered = block_input - middle
    inverse = lax.rsqrt(jnp.mean(centered * centered, axis=-1, keepdims=True) + epsilon_norm)
    unit = centered * inverse
    grad_own = cotangent.astype(jnp.bfloat16)
    units = gather_rows(unit.astype(jnp.bfloat16), x, y, c)
    grads = gather_rows(grad_own, x, y, c)
    segs = jnp.where(even, jnp.concatenate([segments, over_x(segments)]), jnp.concatenate([over_x(segments), segments]))
    cosine, sine = wide_angles(segs)
    g1, s1, g2, s2 = (v.reshape(1, D) for v in (gain_one, shift_one, gain_two, shift_two))

    acts, pres = [None] * 4, [None] * 4
    downs, ups = [None] * 4, [None] * 4
    gain_two_sum = shift_two_sum = 0.0
    bias_up_sum = [None] * 4
    for s in (1, 2, 3, 0):
        acts[s], pres[s] = mlp(units, grads, g2, s2, bias_up[s], w_up[s], w_down[s])
        downs[s] = down_grad(acts[s], grads)
        (ups[s],), gains, shifts, bias_up_sum[s] = up_grad(units, g2, s2, [pres[s]], [w_up[s]])
        gain_two_sum, shift_two_sum = gain_two_sum + gains, shift_two_sum + shifts
    queries, keys_rot, values, pull = project(units, grads, g1, s1, bias_qkv, cosine, sine, w_q, w_k, w_v, w_out)
    attended, *grad_qkv = attention(queries, keys_rot, values, pull, segs, cosine, sine)
    (grad_q, grad_k, grad_v), gain_one_sum, shift_one_sum, bias_qkv_sum = up_grad(
        units, g1, s1, grad_qkv, [w_q, w_k, w_v]
    )
    grad_out = down_grad(attended, grads)

    back_a = over_x(pick(grad_out, grad_v))
    back_b = over_x(pick(downs[0], grad_out))
    back_c = over_x(pick(downs[2], downs[3]))
    back_d = over_x(pick(downs[3], downs[0]))
    sends = (
        (grad_q, ups[0], ups[1], downs[1]),
        (grad_k, pick(back_a, ups[2]), pick(ups[2], downs[2]), back_c),
        (pick(grad_v, back_a), pick(back_b, ups[3]), pick(ups[3], back_b), back_d),
    )
    owned = [
        lax.psum_scatter(jnp.stack(send), ALL, scatter_dimension=0, tiled=False, axis_index_groups=LINES)
        for send in sends
    ]

    summed = scatter_rows(output_rows(acts + [attended], w_down + [w_out]), x, y, c)
    output = block_input + summed + bias_out + bias_down
    e = scatter_rows(input_rows(grad_qkv, pres, [w_q, w_k, w_v] + w_up, g1, g2), x, y, c)
    grad_input = cotangent + inverse * (
        e - jnp.mean(e, axis=-1, keepdims=True) - unit * jnp.mean(e * unit, axis=-1, keepdims=True)
    )

    grad_rows = jnp.sum(grad_own, axis=0, dtype=jnp.float32)
    pieces = jnp.concatenate(
        [
            gain_one_sum,
            shift_one_sum,
            gain_two_sum,
            shift_two_sum,
            jnp.zeros((3 * D,), jnp.float32),
            grad_rows,
            jnp.zeros((FF,), jnp.float32),
            grad_rows,
        ]
    )
    pieces = lax.dynamic_update_slice_in_dim(pieces, bias_qkv_sum, qkv_offset, 0)
    for at, part in zip(up_offsets, bias_up_sum):
        pieces = lax.dynamic_update_slice_in_dim(pieces, part, at, 0)
    grad_vectors = total_vector(pieces)

    blocks = [a[0] for a in (matrices, first_moment, second_moment, left_stat, right_stat, left_basis, right_basis)]
    updated = None
    for j in range(3):
        updated = soap_part(order[j : j + 1], owned[j], blocks, updated)
    new_vectors, new_vec_first, new_vec_second = adam_vector(grad_vectors, vectors, vec_first, vec_second)
    return (output, grad_input, *[u[None] for u in updated], new_vectors, new_vec_first, new_vec_second)


def generic_shards(
    block_input,
    cotangent,
    segments,
    matrices,
    first_moment,
    second_moment,
    left_stat,
    right_stat,
    left_basis,
    right_basis,
    vectors,
    vec_first,
    vec_second,
):
    group_size = lax.axis_size(("heads", "tensor"))
    member = lax.axis_index(("heads", "tensor"))
    heads_here = H // group_size
    hidden_here = FF // group_size
    row_blocks = D // HD
    hidden_blocks = hidden_here // HD
    seq_count = segments.shape[0]
    tokens_here = seq_count * LEN
    own_rows = block_input.shape[0]
    qkv_offset = 4 * D + member * heads_here * 3 * HD
    up_offset = 8 * D + member * hidden_here
    gain_one = vectors[0:D]
    shift_one = vectors[D : 2 * D]
    gain_two = vectors[2 * D : 3 * D]
    shift_two = vectors[3 * D : 4 * D]
    bias_qkv = lax.dynamic_slice_in_dim(vectors, qkv_offset, heads_here * 3 * HD).reshape(
        heads_here, 3, HD
    )
    bias_out = vectors[7 * D : 8 * D]
    bias_up = lax.dynamic_slice_in_dim(vectors, up_offset, hidden_here)
    bias_down = vectors[8 * D + FF : 9 * D + FF]
    gathered = lax.all_gather(matrices.astype(jnp.bfloat16), "dp", axis=1, tiled=True)[0]
    w_qkv, w_out, w_up, w_down = unpack_blocks(gathered, heads_here, row_blocks, hidden_blocks)
    normed_one, unit_one, inverse_one = layer_norm(block_input, gain_one, shift_one)
    normed_two, unit_two, inverse_two = layer_norm(block_input, gain_two, shift_two)
    grad_own = cotangent.astype(jnp.bfloat16)
    norm_one, norm_two, grad_rows = (
        lax.all_gather(normed_one.astype(jnp.bfloat16), ("heads", "tensor"), axis=0, tiled=True),
        lax.all_gather(normed_two.astype(jnp.bfloat16), ("heads", "tensor"), axis=0, tiled=True),
        lax.all_gather(grad_own, ("heads", "tensor"), axis=0, tiled=True),
    )
    norm_one3 = norm_one.reshape(tokens_here, row_blocks, HD)
    norm_two3 = norm_two.reshape(tokens_here, row_blocks, HD)
    projected = (
        jnp.einsum("tbr,hqbrc->thqc", norm_one3, w_qkv, preferred_element_type=jnp.float32)
        + bias_qkv
    )
    shaped = projected.reshape(seq_count, LEN, heads_here, 3, HD)
    cosine, sine = angles(segments)
    queries = rotate(shaped[:, :, :, 0], cosine, sine).astype(jnp.bfloat16)
    keys_rot = rotate(shaped[:, :, :, 1], cosine, sine).astype(jnp.bfloat16)
    values = shaped[:, :, :, 2].astype(jnp.bfloat16)
    attended, log_total = lax.map(seq_forward, (queries, keys_rot, values, segments))
    attend_low = attended.astype(jnp.bfloat16).reshape(tokens_here, heads_here, HD)
    pre_act = (
        jnp.einsum("tbr,kbrc->tkc", norm_two3, w_up, preferred_element_type=jnp.float32).reshape(
            tokens_here, hidden_here
        )
        + bias_up
    )
    act_low = gelu_exact(pre_act).astype(jnp.bfloat16)
    rows_act = act_low.reshape(lax.axis_size(("heads", "tensor")) * own_rows, hidden_blocks, HD)
    first_term = jnp.einsum("thr,hbrc->tbc", attend_low, w_out, preferred_element_type=jnp.float32)
    second_term = jnp.einsum("tkr,kbrc->tbc", rows_act, w_down, preferred_element_type=jnp.float32)
    summed = lax.psum_scatter(
        (first_term + second_term).reshape(lax.axis_size(("heads", "tensor")) * own_rows, D),
        ("heads", "tensor"),
        scatter_dimension=0,
        tiled=True,
    )
    output = block_input + summed + bias_out + bias_down
    regathered = lax.all_gather(matrices.astype(jnp.bfloat16), "dp", axis=1, tiled=True)[0]
    w_qkv, w_out, w_up, w_down = unpack_blocks(regathered, heads_here, row_blocks, hidden_blocks)
    grad_rows3 = grad_rows.reshape(tokens_here, row_blocks, HD)
    act_low3 = act_low.reshape(tokens_here, hidden_blocks, HD)
    grad_act = jnp.einsum(
        "tbc,kbrc->tkr", grad_rows3, w_down, preferred_element_type=jnp.float32
    ).reshape(tokens_here, hidden_here)
    gelu_pull = jax.vjp(gelu_exact, pre_act)[1]
    grad_pre = gelu_pull(grad_act)[0].astype(jnp.bfloat16)
    grad_pre3 = grad_pre.reshape(tokens_here, hidden_blocks, HD)
    grad_attend = jnp.einsum(
        "tbc,hbrc->thr", grad_rows3, w_out, preferred_element_type=jnp.float32
    ).astype(jnp.bfloat16)
    grad_attend = grad_attend.reshape(seq_count, LEN, heads_here, HD)
    grad_queries, grad_keys, grad_values = lax.map(
        seq_backward, (queries, keys_rot, values, segments, log_total, grad_attend)
    )
    grad_raw = jnp.stack(
        [rotate(grad_queries, cosine, -sine), rotate(grad_keys, cosine, -sine), grad_values], axis=3
    )
    grad_raw = grad_raw.astype(jnp.bfloat16).reshape(tokens_here, heads_here, 3, HD)
    rows_up = grad_pre.reshape(lax.axis_size(("heads", "tensor")) * own_rows, hidden_blocks, HD)
    back_one = jnp.einsum(
        "thqc,hqbrc->tbr", grad_raw, w_qkv, preferred_element_type=jnp.float32
    ).reshape(lax.axis_size(("heads", "tensor")) * own_rows, D)
    back_two = jnp.einsum(
        "tkc,kbrc->tbr", rows_up, w_up, preferred_element_type=jnp.float32
    ).reshape(lax.axis_size(("heads", "tensor")) * own_rows, D)
    grad_norms = lax.psum_scatter(
        jnp.stack([back_one, back_two], axis=1),
        ("heads", "tensor"),
        scatter_dimension=0,
        tiled=True,
    )
    grad_norm_one = grad_norms[:, 0]
    grad_norm_two = grad_norms[:, 1]
    grad_input = (
        cotangent
        + norm_back(grad_norm_one, unit_one, inverse_one, gain_one)
        + norm_back(grad_norm_two, unit_two, inverse_two, gain_two)
    )
    grad_bias_rows = jnp.sum(grad_own, axis=0, dtype=jnp.float32)
    pieces = jnp.concatenate(
        [
            jnp.sum(grad_norm_one * unit_one, axis=0),
            jnp.sum(grad_norm_one, axis=0),
            jnp.sum(grad_norm_two * unit_two, axis=0),
            jnp.sum(grad_norm_two, axis=0),
            jnp.zeros((3 * D,), jnp.float32),
            grad_bias_rows,
            jnp.zeros((FF,), jnp.float32),
            grad_bias_rows,
        ]
    )
    pieces = lax.dynamic_update_slice_in_dim(
        pieces, jnp.sum(grad_raw, axis=0, dtype=jnp.float32).reshape(-1), qkv_offset, 0
    )
    pieces = lax.dynamic_update_slice_in_dim(
        pieces, jnp.sum(grad_pre, axis=0, dtype=jnp.float32), up_offset, 0
    )
    grad_vectors = lax.psum(pieces, ("dp", "heads", "tensor"))
    grad_down = jnp.einsum(
        "tkr,tbc->kbrc", act_low3, grad_rows3, preferred_element_type=jnp.float32
    )
    grad_up = jnp.einsum("tbr,tkc->kbrc", norm_two3, grad_pre3, preferred_element_type=jnp.float32)
    grad_out = jnp.einsum(
        "thr,tbc->hbrc", attend_low, grad_rows3, preferred_element_type=jnp.float32
    )
    grad_qkv = jnp.einsum(
        "tbr,thqc->hqbrc", norm_one3, grad_raw, preferred_element_type=jnp.float32
    )
    attn_grads = jnp.concatenate([grad_qkv, grad_out[:, None]], axis=1).reshape(-1, HD, HD)
    all_grads = jnp.concatenate(
        [attn_grads, grad_up.reshape(-1, HD, HD), grad_down.reshape(-1, HD, HD)], axis=0
    )[None]
    owned = lax.psum_scatter(all_grads, "dp", scatter_dimension=1, tiled=True)
    blocks = [a[0] for a in (matrices, first_moment, second_moment, left_stat, right_stat, left_basis, right_basis)]
    updated = [u[None] for u in soap_part(jnp.zeros((1,), jnp.int32), owned[0], blocks, None)]
    new_vectors, new_vec_first, new_vec_second = adam_vector(
        grad_vectors, vectors, vec_first, vec_second
    )
    return (
        output,
        grad_input,
        updated[0],
        updated[1],
        updated[2],
        updated[3],
        updated[4],
        updated[5],
        updated[6],
        updated[7],
        new_vectors,
        new_vec_first,
        new_vec_second,
    )


def solution(mesh):
    in_specs = (
        P(("dp", "heads", "tensor"), None),
        P(("dp", "heads", "tensor"), None),
        P("dp", None),
        P(("heads", "tensor"), "dp", None, None),
        P(("heads", "tensor"), "dp", None, None),
        P(("heads", "tensor"), "dp", None, None),
        P(("heads", "tensor"), "dp", None, None),
        P(("heads", "tensor"), "dp", None, None),
        P(("heads", "tensor"), "dp", None, None),
        P(("heads", "tensor"), "dp", None, None),
        P(),
        P(),
        P(),
    )
    out_specs = (
        P(("dp", "heads", "tensor"), None),
        P(("dp", "heads", "tensor"), None),
        P(("heads", "tensor"), "dp", None, None),
        P(("heads", "tensor"), "dp", None, None),
        P(("heads", "tensor"), "dp", None, None),
        P(("heads", "tensor"), "dp", None, None),
        P(("heads", "tensor"), "dp", None, None),
        P(("heads", "tensor"), "dp", None, None),
        P(("heads", "tensor"), "dp", None, None),
        P(("heads", "tensor"), "dp", None, None),
        P(),
        P(),
        P(),
    )
    plane = dict(mesh.shape) == {"dp": 8, "heads": 2, "tensor": 2}
    shards = plane_shards if plane else generic_shards
    return jax.shard_map(shards, mesh=mesh, in_specs=in_specs, out_specs=out_specs, check_vma=False)
```

```python
import functools

import jax
import jax.numpy as jnp
from jax import lax
from jax.experimental import pallas as pl
from jax.experimental.pallas import tpu as pltpu
from jax.sharding import PartitionSpec as P

D = 2048
H = 8
HD = 256
RD = 64
FF = 8192
LEN = 1024
STEP = 10


epsilon_norm = 1e-05
epsilon_adam = 1e-08
rope_base = 10000.0
beta_one = 0.9
beta_two = 0.95
beta_stat = 0.95
rate_matrix = 0.05
rate_vector = 0.1
weight_decay = 0.01
PAN = 32
UNROLL = 8
GROUP = 2


def layer_norm(rows, gain, shift):
    middle = jnp.mean(rows, axis=-1, keepdims=True)
    centered = rows - middle
    spread = jnp.mean(centered * centered, axis=-1, keepdims=True)
    inverse = lax.rsqrt(spread + epsilon_norm)
    unit = centered * inverse
    return (unit * gain + shift, unit, inverse)


def norm_back(grad, unit, inverse, gain):
    scaled = grad * gain
    return inverse * (
        scaled
        - jnp.mean(scaled, axis=-1, keepdims=True)
        - unit * jnp.mean(scaled * unit, axis=-1, keepdims=True)
    )


def angles(segments):
    seq_count = segments.shape[0]
    column = jnp.arange(LEN, dtype=jnp.int32)[None, :]
    border = jnp.concatenate(
        [jnp.ones((seq_count, 1), jnp.bool_), segments[:, 1:] != segments[:, :-1]], axis=1
    )
    starts = lax.cummax(jnp.where(border, column, 0), axis=1)
    places = (column - starts).astype(jnp.float32)
    frequency = 1.0 / rope_base ** (jnp.arange(0, RD, 2).astype(jnp.float32) / RD)
    turns = places[:, :, None] * frequency[None, None, :]
    return (jnp.cos(turns)[:, :, None, :], jnp.sin(turns)[:, :, None, :])


def rotate(part, cosine, sine):
    half_dims = RD // 2
    first_half = part[..., :half_dims]
    second_half = part[..., half_dims:RD]
    return jnp.concatenate(
        [
            first_half * cosine - second_half * sine,
            second_half * cosine + first_half * sine,
            part[..., RD:],
        ],
        axis=-1,
    )


def unpack_blocks(blocks, heads_here, row_blocks, hidden_blocks):
    attn_count = heads_here * 4 * row_blocks
    up_count = hidden_blocks * row_blocks
    attn_part = blocks[:attn_count].reshape(heads_here, 4, row_blocks, HD, HD)
    w_up = blocks[attn_count : attn_count + up_count].reshape(hidden_blocks, row_blocks, HD, HD)
    w_down = blocks[attn_count + up_count :].reshape(hidden_blocks, row_blocks, HD, HD)
    return (attn_part[:, :3], attn_part[:, 3], w_up, w_down)


def masked_scores(queries, keys_rot, segment_row):
    column = jnp.arange(LEN)
    allowed = (segment_row[:, None] == segment_row[None, :]) & (column[None, :] <= column[:, None])
    scores = jnp.einsum(
        "qhd,khd->hqk", queries, keys_rot, preferred_element_type=jnp.float32
    ) * HD ** (-0.5)
    return jnp.where(allowed[None], scores, -1e30)


def seq_forward(items):
    queries, keys_rot, values, segment_row = items
    scores = masked_scores(queries, keys_rot, segment_row)
    row_max = jnp.max(scores, axis=-1, keepdims=True)
    powers = jnp.exp(scores - row_max)
    row_total = jnp.sum(powers, axis=-1, keepdims=True)
    probs_low = (powers / row_total).astype(jnp.bfloat16)
    attended = jnp.einsum("hqk,khd->qhd", probs_low, values, preferred_element_type=jnp.float32)
    return (attended, (row_max + jnp.log(row_total))[..., 0])


def seq_backward(items):
    queries, keys_rot, values, segment_row, log_total, grad_attend = items
    scores = masked_scores(queries, keys_rot, segment_row)
    probs = jnp.exp(scores - log_total[..., None])
    grad_probs = jnp.einsum("qhd,khd->hqk", grad_attend, values, preferred_element_type=jnp.float32)
    inner = jnp.sum(probs * grad_probs, axis=-1, keepdims=True)
    grad_scores = (probs * (grad_probs - inner)).astype(jnp.bfloat16)
    grad_queries = jnp.einsum(
        "hqk,khd->qhd", grad_scores, keys_rot, preferred_element_type=jnp.float32
    ) * HD ** (-0.5)
    grad_keys = jnp.einsum(
        "hqk,qhd->khd", grad_scores, queries, preferred_element_type=jnp.float32
    ) * HD ** (-0.5)
    grad_values = jnp.einsum(
        "hqk,qhd->khd", probs.astype(jnp.bfloat16), grad_attend, preferred_element_type=jnp.float32
    )
    return (grad_queries, grad_keys, grad_values)


def gelu_exact(inputs):
    return jax.nn.gelu(inputs, approximate=False)


def dot_nn(a, b):
    return lax.dot_general(a, b, (((1,), (0,)), ((), ())), preferred_element_type=jnp.float32)


def dot_nt(a, b):
    return lax.dot_general(a, b, (((1,), (1,)), ((), ())), preferred_element_type=jnp.float32)


def dot_tn(a, b):
    return lax.dot_general(a, b, (((0,), (0,)), ((), ())), preferred_element_type=jnp.float32)


def split(x):
    high = x.astype(jnp.bfloat16)
    return high, (x - high.astype(jnp.float32)).astype(jnp.bfloat16)


def three(dot, a, b):
    return dot(a[0], b[0]) + (dot(a[0], b[1]) + dot(a[1], b[0]))


def eliminate(diag, mats):
    lane = lax.broadcasted_iota(jnp.int32, (mats, 128), 1)
    rows = []
    for i in range(PAN):
        row = diag[pl.ds(i * mats, mats), :]
        rows.append(jnp.where(lane < PAN, jnp.where(lane == i, 1.0, 0.0), row))

    def entry(row, j):
        return jnp.broadcast_to(row[:, PAN + j : PAN + j + 1], (mats, 128))

    for k in range(0, PAN, 2):
        one, two = rows[k], rows[k + 1]
        cross = entry(one, k + 1)
        inverse = lax.rsqrt(entry(one, k))
        ratio = cross * (inverse * inverse)
        inverse_two = lax.rsqrt(entry(two, k + 1) - ratio * cross)
        two = two - ratio * one
        first, second = one * inverse, two * inverse_two
        diag[pl.ds(k * mats, mats), :] = first
        diag[pl.ds((k + 1) * mats, mats), :] = second
        for i in range(k + 2, PAN):
            of_one = entry(rows[k], i)
            of_two = entry(rows[k + 1], i) - ratio * of_one
            rows[i] = rows[i] - (of_one * inverse) * first - (of_two * inverse_two) * second


def soap_kernel(count, g, w, f, s, ls, rs, lb, rb, ow, owl, of, os, ols, ors, olb, orb, aug, diag):
    step = pl.program_id(0)
    mats = 2 * count
    unroll = UNROLL if mats % UNROLL == 0 else 4
    blocks = range(GROUP)
    grad = [g[i].astype(jnp.bfloat16) for i in blocks]
    left, right = [split(lb[i]) for i in blocks], [split(rb[i]) for i in blocks]
    left_t = [(x.T, y.T) for x, y in left]
    right_t = [(x.T, y.T) for x, y in right]
    grad_t = [x.T for x in grad]
    lnew = [beta_stat * ls[i] + (1.0 - beta_stat) * dot_nn(grad[i], grad_t[i]) for i in blocks]
    rnew = [beta_stat * rs[i] + (1.0 - beta_stat) * dot_nn(grad_t[i], grad[i]) for i in blocks]
    turned = [dot_nn(left_t[i][0], grad[i]) + dot_nn(left_t[i][1], grad[i]) for i in blocks]
    for i in blocks:
        ols[i] = lnew[i]
        ors[i] = rnew[i]
    turned = [three(dot_nn, split(turned[i]), right[i]) for i in blocks]
    sides = [
        three(dot_nn, basis_t, split(stat))
        for i in blocks
        for basis_t, stat in ((left_t[i], lnew[i]), (right_t[i], rnew[i]))
    ]
    first_new = [beta_one * f[i] + (1.0 - beta_one) * turned[i] for i in blocks]
    second_new = [beta_two * s[i] + (1.0 - beta_two) * turned[i] * turned[i] for i in blocks]
    direction = [
        x / (1.0 - beta_one**STEP) / (jnp.sqrt(y / (1.0 - beta_two**STEP)) + epsilon_adam)
        for x, y in zip(first_new, second_new)
    ]
    for i in blocks:
        of[i] = first_new[i]
        os[i] = second_new[i]
    stepped = [three(dot_nn, left[i], split(direction[i])) for i in blocks]
    for i, side in enumerate(sides):
        aug[2 * GROUP * step + i, :, HD:] = side
    grams = [three(dot_nt, x, x) for x in map(split, sides)]
    stepped = [three(dot_nn, split(stepped[i]), right_t[i]) for i in blocks]
    for i, gram in enumerate(grams):
        aug[2 * GROUP * step + i, :, :HD] = gram
    for i in blocks:
        weight = w[i]
        weight_new = weight - rate_matrix * (stepped[i] + weight_decay * weight)
        ow[i] = weight_new
        owl[i] = weight_new.astype(jnp.bfloat16)

    @pl.when(step == count // GROUP - 1)
    def _():
        for p in range(HD // PAN):
            low = p * PAN

            def place(m):
                base = low // 128 * 128
                own = aug[m, low : low + PAN, base : base + 128]
                shift = (PAN - (low - base)) % 128
                if shift:
                    own = pltpu.roll(own, shift, 1)
                diag[pl.ds(m, PAN, stride=mats), :] = own

            if p == 0:

                def start(i, carry):
                    for u in range(unroll):
                        place(i * unroll + u)
                    return carry

                lax.fori_loop(0, mats // unroll, start, 0)
            eliminate(diag, mats)
            low = low + PAN
            edge = low // 128 * 128

            def update(i, carry):
                mine = [i * unroll + u for u in range(unroll)]
                factors = [split(diag[pl.ds(m, PAN, stride=mats), :][:, :PAN]) for m in mine]
                panels = [split(aug[m, low - PAN : low, :]) for m in mine]
                panels = [three(dot_nn, x, y) for x, y in zip(factors, panels)]
                if low == HD:
                    for m, panel in zip(mine, panels):
                        aug[m, low - PAN : low, HD:] = panel[:, HD:]
                    return carry
                parts = [split(panel) for panel in panels]
                lhs = [jnp.concatenate([x[:, :HD], x[:, :HD], y[:, :HD]], axis=0).T for x, y in parts]
                rhs = [jnp.concatenate([x, y, x], axis=0) for x, y in parts]
                rest = [
                    aug[m, low:, edge:] - dot_nn(x[low:], y[:, edge:]) for m, x, y in zip(mine, lhs, rhs)
                ]
                for m, panel, left in zip(mine, panels, rest):
                    aug[m, low - PAN : low, HD:] = panel[:, HD:]
                    aug[m, low:, edge:] = left
                    own = left[:PAN, :128]
                    shift = (PAN - (low - edge)) % 128
                    if shift:
                        own = pltpu.roll(own, shift, 1)
                    diag[pl.ds(m, PAN, stride=mats), :] = own
                return carry

            lax.fori_loop(0, mats // unroll, update, 0)

        def finish(b, carry):
            for side, out in enumerate((olb, orb)):
                out[b] = aug[2 * b + side, :, HD:].T
            return carry

        lax.fori_loop(0, count, finish, 0)


LIMIT = 56 * 2**20
SHRINK = 1


def cost(flops, moved, trans=0):
    return pl.CostEstimate(flops=int(flops) // SHRINK, bytes_accessed=int(moved) // SHRINK, transcendentals=0)


def turn(rows, cosine, sine):
    head = rows[:, :128]
    lane = lax.broadcasted_iota(jnp.int32, head.shape, 1)
    partner = jnp.where(lane < RD // 2, pltpu.roll(head, 128 - RD // 2, 1), pltpu.roll(head, RD // 2, 1))
    return jnp.concatenate([head * cosine + partner * sine, rows[:, 128:]], axis=1)


def project_kernel(at, unit, grad, gain, shift, bias, cos_one, cos_two, sin_one, sin_two, wq, wk, wv, wo, q, k, v, ga):
    cosine = jnp.concatenate([cos_one[...], cos_two[...]], axis=0)
    sine = jnp.concatenate([sin_one[...], sin_two[...]], axis=0)
    norm = (unit[...].astype(jnp.float32) * gain[...] + shift[...]).astype(jnp.bfloat16)
    q[...] = turn(dot_nn(norm, wq[...]) + bias[0:1, :], cosine, sine).astype(jnp.bfloat16)
    k[...] = turn(dot_nn(norm, wk[...]) + bias[1:2, :], cosine, sine).astype(jnp.bfloat16)
    v[...] = (dot_nn(norm, wv[...]) + bias[2:3, :]).astype(jnp.bfloat16)
    total = dot_nt(grad[:, :HD], wo[0])
    for b in range(1, D // HD):
        total = total + dot_nt(grad[:, b * HD : (b + 1) * HD], wo[b])
    ga[...] = total.astype(jnp.bfloat16)


def project(places, unit, grad, gain, shift, bias, cosine, sine, wq, wk, wv, wo):
    tokens = unit.shape[0]
    tile = 512
    rows = pl.BlockSpec((tile, D), lambda i, at: (i, 0))
    narrow = pl.BlockSpec((tile, HD), lambda i, at: (i, 0))
    angles_of = [pl.BlockSpec((tile // 2, 128), lambda i, at, u=u: (at[2 * i + u], 0)) for u in range(2)]
    line = pl.BlockSpec((1, D), lambda i, at: (0, 0))
    flat = pl.BlockSpec((D, HD), lambda i, at: (0, 0))
    return pl.pallas_call(
        project_kernel,
        grid_spec=pltpu.PrefetchScalarGridSpec(
            num_scalar_prefetch=1,
            grid=(tokens // tile,),
            in_specs=[rows, rows, line, line, pl.BlockSpec((3, HD), lambda i, at: (0, 0))]
            + angles_of * 2
            + [flat] * 3
            + [pl.BlockSpec((D // HD, HD, HD), lambda i, at: (0, 0, 0))],
            out_specs=[narrow] * 4,
        ),
        out_shape=[jax.ShapeDtypeStruct((tokens, HD), jnp.bfloat16)] * 4,
        compiler_params=pltpu.CompilerParams(vmem_limit_bytes=LIMIT),
        cost_estimate=cost(8 * tokens * D * HD, 4 * tokens * D + 8 * D * HD),
        name="project",
    )(
        places, unit, grad, gain, shift, bias, cosine, cosine, sine, sine,
        wq.reshape(D, HD), wk.reshape(D, HD), wv.reshape(D, HD), wo,
    )


def attention_kernel(at, q, k, v, ga, seg_row, seg_col, cosine, sine, att, dq, dk, dv, kseq, vseq, keys, vals):
    tile = 256
    scale = HD ** (-0.5)
    pieces = LEN // tile
    rows = [pl.ds(at[pl.program_id(0) * pieces + i] * tile, tile) for i in range(pieces)]
    for i in range(pieces):
        kseq[i * tile : (i + 1) * tile, :] = k[rows[i], :]
        vseq[i * tile : (i + 1) * tile, :] = v[rows[i], :]
    keys[...] = jnp.zeros_like(keys)
    vals[...] = jnp.zeros_like(vals)
    for i in range(pieces):
        here = slice(i * tile, (i + 1) * tile)
        upto = (i + 1) * tile
        mine, pulled = q[rows[i], :], ga[rows[i], :]
        scores = dot_nt(mine, kseq[:upto, :]) * scale
        to = lax.broadcasted_iota(jnp.int32, (tile, upto), 0) + i * tile
        of = lax.broadcasted_iota(jnp.int32, (tile, upto), 1)
        allowed = (seg_col[0, here, :] == seg_row[0, :, :upto]) & (of <= to)
        scores = jnp.where(allowed, scores, -1e30)
        powers = jnp.exp(scores - jnp.max(scores, axis=-1, keepdims=True))
        probs = powers / jnp.sum(powers, axis=-1, keepdims=True)
        low = probs.astype(jnp.bfloat16)
        att[rows[i], :] = dot_nn(low, vseq[:upto, :]).astype(jnp.bfloat16)
        pull = dot_nt(pulled, vseq[:upto, :])
        inner = jnp.sum(probs * pull, axis=-1, keepdims=True)
        gs = (probs * (pull - inner)).astype(jnp.bfloat16)
        turned = turn(dot_nn(gs, kseq[:upto, :]) * scale, cosine[here, :], -sine[here, :])
        dq[rows[i], :] = turned.astype(jnp.bfloat16)
        keys[:upto, :] = keys[:upto, :] + dot_tn(gs, mine)
        vals[:upto, :] = vals[:upto, :] + dot_tn(low, pulled)
    for i in range(pieces):
        here = slice(i * tile, (i + 1) * tile)
        turned = turn(keys[here, :] * scale, cosine[here, :], -sine[here, :])
        dk[rows[i], :] = turned.astype(jnp.bfloat16)
        dv[rows[i], :] = vals[here, :].astype(jnp.bfloat16)


def attention(places, q, k, v, ga, segments, cosine, sine):
    tokens = q.shape[0]
    count = tokens // LEN
    whole = pl.BlockSpec((tokens, HD), lambda i, at: (0, 0))
    angle = pl.BlockSpec((LEN, 128), lambda i, at: (i, 0))
    return pl.pallas_call(
        attention_kernel,
        grid_spec=pltpu.PrefetchScalarGridSpec(
            num_scalar_prefetch=1,
            grid=(count,),
            in_specs=[whole] * 4
            + [pl.BlockSpec((1, 1, LEN), lambda i, at: (i, 0, 0)), pl.BlockSpec((1, LEN, 1), lambda i, at: (i, 0, 0))]
            + [angle] * 2,
            out_specs=[whole] * 4,
            scratch_shapes=[pltpu.VMEM((LEN, HD), jnp.bfloat16)] * 2 + [pltpu.VMEM((LEN, HD), jnp.float32)] * 2,
        ),
        out_shape=[jax.ShapeDtypeStruct((tokens, HD), jnp.bfloat16)] * 4,
        compiler_params=pltpu.CompilerParams(vmem_limit_bytes=LIMIT),
        cost_estimate=cost(14 * tokens * LEN * HD, 16 * tokens * HD, tokens * LEN),
        name="attention",
    )(places, q, k, v, ga, segments.reshape(count, 1, LEN), segments.reshape(count, LEN, 1), cosine, sine)


def mlp_kernel(parts, unit, grad, gain, shift, *refs):
    biases, ups, downs, acts, pres = (refs[i * parts : (i + 1) * parts] for i in range(5))
    norm = (unit[...].astype(jnp.float32) * gain[...] + shift[...]).astype(jnp.bfloat16)
    for bias, wu, wd, act, pre in zip(biases, ups, downs, acts, pres):
        inner = dot_nn(norm, wu[...]) + bias[...]
        pull = dot_nt(grad[:, :HD], wd[0])
        for b in range(1, D // HD):
            pull = pull + dot_nt(grad[:, b * HD : (b + 1) * HD], wd[b])
        share = 0.5 + 0.5 * lax.erf(inner * (0.5**0.5))
        act[...] = (inner * share).astype(jnp.bfloat16)
        slope = share + inner * jnp.exp(-0.5 * inner * inner) * ((2.0 * 3.141592653589793) ** (-0.5))
        pre[...] = (slope * pull).astype(jnp.bfloat16)


def mlp(unit, grad, gain, shift, biases, ups, downs):
    tokens, parts = unit.shape[0], len(ups)
    tile = 512
    rows = pl.BlockSpec((tile, D), lambda i: (i, 0))
    narrow = pl.BlockSpec((tile, HD), lambda i: (i, 0))
    line = pl.BlockSpec((1, D), lambda i: (0, 0))
    result = pl.pallas_call(
        functools.partial(mlp_kernel, parts),
        grid=(tokens // tile,),
        in_specs=[rows, rows, line, line]
        + [pl.BlockSpec((1, HD), lambda i: (0, 0))] * parts
        + [pl.BlockSpec((D, HD), lambda i: (0, 0))] * parts
        + [pl.BlockSpec((D // HD, HD, HD), lambda i: (0, 0, 0))] * parts,
        out_specs=[narrow] * (2 * parts),
        out_shape=[jax.ShapeDtypeStruct((tokens, HD), jnp.bfloat16)] * (2 * parts),
        compiler_params=pltpu.CompilerParams(vmem_limit_bytes=LIMIT),
        cost_estimate=cost(4 * parts * tokens * D * HD, 4 * tokens * D + 4 * parts * D * HD, 2 * parts * tokens * HD),
        name="mlp",
    )(unit, grad, gain, shift, *biases, *[u.reshape(D, HD) for u in ups], *downs)
    return result[:parts], result[parts:]


def output_kernel(parts, *refs):
    acts, weights, out = refs[:parts], refs[parts : 2 * parts], refs[-1]
    for b in range(D // HD):
        total = dot_nn(acts[0][...], weights[0][b])
        for a, w in zip(acts[1:], weights[1:]):
            total = total + dot_nn(a[...], w[b])
        out[:, b * HD : (b + 1) * HD] = total.astype(jnp.bfloat16)


def output_rows(acts, weights):
    tokens, parts = acts[0].shape[0], len(acts)
    tile = 512
    return pl.pallas_call(
        functools.partial(output_kernel, parts),
        grid=(tokens // tile,),
        in_specs=[pl.BlockSpec((tile, HD), lambda i: (i, 0))] * parts
        + [pl.BlockSpec((D // HD, HD, HD), lambda i: (0, 0, 0))] * parts,
        out_specs=pl.BlockSpec((tile, D), lambda i: (i, 0)),
        out_shape=jax.ShapeDtypeStruct((tokens, D), jnp.bfloat16),
        compiler_params=pltpu.CompilerParams(vmem_limit_bytes=LIMIT),
        cost_estimate=cost(2 * parts * tokens * D * HD, 2 * tokens * D + parts * 2 * D * HD),
        name="output_rows",
    )(*acts, *weights)


def input_kernel(first, second, *refs):
    grads, weights = refs[: first + second], refs[first + second : 2 * (first + second)]
    gain_one, gain_two, out = refs[-3:]

    def summed(low, high, b):
        total = dot_nt(grads[low][...], weights[low][b])
        for i in range(low + 1, high):
            total = total + dot_nt(grads[i][...], weights[i][b])
        return total

    for b in range(D // HD):
        here = slice(b * HD, (b + 1) * HD)
        total = summed(0, first, b) * gain_one[:, here] + summed(first, first + second, b) * gain_two[:, here]
        out[:, here] = total.astype(jnp.bfloat16)


def input_rows(ones, twos, weights, gain_one, gain_two):
    tokens, parts = ones[0].shape[0], len(weights)
    tile = 512
    line = pl.BlockSpec((1, D), lambda i: (0, 0))
    return pl.pallas_call(
        functools.partial(input_kernel, len(ones), len(twos)),
        grid=(tokens // tile,),
        in_specs=[pl.BlockSpec((tile, HD), lambda i: (i, 0))] * parts
        + [pl.BlockSpec((D // HD, HD, HD), lambda i: (0, 0, 0))] * parts
        + [line] * 2,
        out_specs=pl.BlockSpec((tile, D), lambda i: (i, 0)),
        out_shape=jax.ShapeDtypeStruct((tokens, D), jnp.bfloat16),
        compiler_params=pltpu.CompilerParams(vmem_limit_bytes=LIMIT),
        cost_estimate=cost(2 * parts * tokens * D * HD, 2 * tokens * D + parts * 2 * D * HD),
        name="input_rows",
    )(*ones, *twos, *weights, gain_one, gain_two)


def down_grad_kernel(parts, *refs):
    acts, grad, outs, flipped = refs[:parts], refs[parts], refs[parts + 1 : 2 * parts + 1], refs[-1]

    @pl.when(pl.program_id(0) == 0)
    def _():
        for i, act in enumerate(acts):
            flipped[i * HD : (i + 1) * HD, :] = act[...].T

    for i, out in enumerate(outs):
        out[0] = dot_nn(flipped[i * HD : (i + 1) * HD, :], grad[...]).astype(jnp.bfloat16)


def down_grad(acts, grad):
    tokens, parts = grad.shape[0], len(acts)
    return pl.pallas_call(
        functools.partial(down_grad_kernel, parts),
        grid=(D // HD,),
        in_specs=[pl.BlockSpec((tokens, HD), lambda b: (0, 0))] * parts + [pl.BlockSpec((tokens, HD), lambda b: (0, b))],
        out_specs=[pl.BlockSpec((1, HD, HD), lambda b: (b, 0, 0))] * parts,
        out_shape=[jax.ShapeDtypeStruct((D // HD, HD, HD), jnp.bfloat16)] * parts,
        scratch_shapes=[pltpu.VMEM((parts * HD, tokens), jnp.bfloat16)],
        compiler_params=pltpu.CompilerParams(vmem_limit_bytes=LIMIT),
        cost_estimate=cost(2 * parts * tokens * D * HD, 2 * tokens * D + 4 * parts * D * HD),
        name="down_grad",
    )(*acts, grad)


def up_grad_kernel(parts, *refs):
    unit, gain, shift = refs[:3]
    grads, weights = refs[3 : 3 + parts], refs[3 + parts : 3 + 2 * parts]
    outs, (gains, shifts, biases) = refs[3 + 2 * parts : 3 + 3 * parts], refs[3 + 3 * parts : 6 + 3 * parts]
    flipped, column = refs[6 + 3 * parts :]

    @pl.when(pl.program_id(0) == 0)
    def _():
        for i, g in enumerate(grads):
            wide = g[...].astype(jnp.float32)
            flipped[i * HD : (i + 1) * HD, :] = g[...].T
            total = jnp.sum(wide, axis=0, keepdims=True)
            biases[:, i * HD : (i + 1) * HD] = total
            column[i] = jnp.broadcast_to(total, (128, HD)).T

    lines = []
    for i in range(parts):
        turned = dot_nn(flipped[i * HD : (i + 1) * HD, :], unit[...])
        weight = weights[i][0].T.astype(jnp.float32)
        bias = column[i][:, 0:1]
        lines.append(
            (jnp.sum(weight * turned, axis=0, keepdims=True), jnp.sum(weight * bias, axis=0, keepdims=True))
        )
        outs[i][0] = (turned * gain[...] + bias * shift[...]).T.astype(jnp.bfloat16)
    gains[...] = sum(x for x, _ in lines)
    shifts[...] = sum(x for _, x in lines)


def up_grad(unit, gain, shift, grads, weights):
    tokens, parts = unit.shape[0], len(grads)
    line = pl.BlockSpec((1, HD), lambda b: (0, b))
    block = pl.BlockSpec((1, HD, HD), lambda b: (b, 0, 0))
    result = pl.pallas_call(
        functools.partial(up_grad_kernel, parts),
        grid=(D // HD,),
        in_specs=[pl.BlockSpec((tokens, HD), lambda b: (0, b)), line, line]
        + [pl.BlockSpec((tokens, HD), lambda b: (0, 0))] * parts
        + [block] * parts,
        out_specs=[block] * parts + [line, line, pl.BlockSpec((1, parts * HD), lambda b: (0, 0))],
        out_shape=[jax.ShapeDtypeStruct((D // HD, HD, HD), jnp.bfloat16)] * parts
        + [jax.ShapeDtypeStruct((1, D), jnp.float32)] * 2
        + [jax.ShapeDtypeStruct((1, parts * HD), jnp.float32)],
        scratch_shapes=[pltpu.VMEM((parts * HD, tokens), jnp.bfloat16), pltpu.VMEM((parts, HD, 128), jnp.float32)],
        compiler_params=pltpu.CompilerParams(vmem_limit_bytes=LIMIT),
        cost_estimate=cost(2 * parts * tokens * D * HD, 2 * tokens * D + parts * 4 * D * HD),
        name="up_grad",
    )(unit, gain, shift, *grads, *weights)
    return result[:parts], result[parts][0], result[parts + 1][0], result[parts + 2][0]


def choose_kernel(plan, many, x_at, *refs):
    inputs, outs, sems = refs[:many], refs[many : many + len(plan)], refs[-1]
    for i, out in enumerate(outs):
        for x in range(2):
            which, place = plan[i][x]

            @pl.when(x_at[0] == x)
            def _():
                pltpu.make_async_copy(inputs[which].at[place], out, sems.at[i]).start()

    for i, out in enumerate(outs):
        pltpu.make_async_copy(inputs[0].at[0], out, sems.at[i]).wait()


def choose(x, *wanted):
    arrays, plan = [], []
    for sides in wanted:
        row = []
        for array, place in sides:
            spot = [i for i, a in enumerate(arrays) if a is array]
            if not spot:
                arrays.append(array)
                spot = [len(arrays) - 1]
            row.append((spot[0], place))
        plan.append(row)
    anywhere = pl.BlockSpec(memory_space=pl.ANY)
    shape = arrays[0].shape[1:]
    return pl.pallas_call(
        functools.partial(choose_kernel, plan, len(arrays)),
        in_specs=[pl.BlockSpec(memory_space=pltpu.SMEM)] + [anywhere] * len(arrays),
        out_specs=[pl.BlockSpec(memory_space=pltpu.VMEM)] * len(plan),
        out_shape=[jax.ShapeDtypeStruct(shape, jnp.bfloat16)] * len(plan),
        scratch_shapes=[pltpu.SemaphoreType.DMA((len(plan),))],
        compiler_params=pltpu.CompilerParams(vmem_limit_bytes=LIMIT),
        cost_estimate=cost(0, 4 * len(plan) * D * HD),
        name="choose",
    )(x.reshape(1), *arrays)


MESH = pl.DeviceIdType.MESH
RIGHT = (
    {0: 0, 1: 3, 2: 6},
    {0: 1, 1: 4, 2: 3},
    {0: 2, 1: 0, 2: 4},
    {1: 1, 2: 0},
    {1: 2, 2: 1},
    {1: 5, 2: 2},
    {2: 7},
    {2: 8},
    {2: 5},
)
LEFT = (
    {3: 9, 2: 6, 1: 3},
    {3: 10, 2: 9, 1: 6},
    {3: 11, 2: 10, 1: 9},
    {2: 7, 1: 4},
    {2: 11, 1: 10},
    {2: 8, 1: 7},
    {1: 11},
    {1: 8},
    {1: 5},
)
SWAPS = ((3, 9), (4, 0), (10, 11), (11, 8))
ROLES = {
    "q": (0, 1),
    "k": (1, 2),
    "v": (2, 12),
    "out": (13, 13),
    "up": ((6, 3), (7, 7), (8, 4), (5, 5)),
    "down": ((9, 6), (12, 10), (14, 14), (15, 15)),
}


def layer_kernel(
    own, unit, grad, lines, bias_qkv, bias_up, cosine, sine, seg_row, seg_col,
    held, units_out, grads_out, partial, rows_out, sums, biases,
    units, grads, weight, act, pre, flipped, column, q, k, v, ga, att, dq, dk, dv, kseq, vseq, keys, vals, stage,
    right_send, right_recv, left_send, left_recv, swap_send, swap_recv, row_send, row_recv, local,
):
    d, y, c = lax.axis_index("dp"), lax.axis_index("heads"), lax.axis_index("tensor")
    z, x = d // 2, d % 2
    by_x, by_y, by_core = {"dp": d + 1 - 2 * x}, {"heads": 1 - y}, {"tensor": 1 - c}
    block = unit.shape[0]
    tokens = units.shape[0]

    barrier = pltpu.get_barrier_semaphore()
    for near in (by_x, by_y, by_core):
        pl.semaphore_signal(barrier, inc=1, device_id=near, device_id_type=MESH)

    @pl.when(z < 3)
    def _():
        pl.semaphore_signal(barrier, inc=1, device_id={"dp": d + 2}, device_id_type=MESH)

    @pl.when(z > 0)
    def _():
        pl.semaphore_signal(barrier, inc=1, device_id={"dp": d - 2}, device_id_type=MESH)

    pl.semaphore_wait(barrier, 4 + (z + 1) // 2 % 2)

    def remote(source, target, send, recv, device):
        return pltpu.make_async_remote_copy(
            src_ref=source, dst_ref=target, send_sem=send, recv_sem=recv, device_id=device, device_id_type=MESH
        )

    def hop(table, step, sends, recvs, shift, at):
        place = table[step][at]
        source = own.at[place % 3] if place // 3 == at else held.at[place]
        return remote(source, held.at[place], sends.at[step], recvs.at[step], {"dp": d + 2 * shift})

    ways = ((RIGHT, right_send, right_recv, 1), (LEFT, left_send, left_recv, -1))

    def start(step):
        for table, sends, recvs, shift in ways:
            for at in table[step]:

                @pl.when(z == at)
                def _():
                    hop(table, step, sends, recvs, shift, at).start()

    def arrived(step):
        for table, sends, recvs, shift in ways:
            for at in table[step]:

                @pl.when(z == at + shift)
                def _():
                    hop(table, step, sends, recvs, shift, at).wait_recv()

    def sent(step):
        for table, sends, recvs, shift in ways:
            for at in table[step]:

                @pl.when(z == at)
                def _():
                    hop(table, step, sends, recvs, shift, at).wait_send()

    def pump(step):
        arrived(step)
        if step + 1 < len(RIGHT):
            start(step + 1)

    def swap(i, side):
        return remote(held.at[SWAPS[i][side]], held.at[12 + i], swap_send.at[i], swap_recv.at[i], by_x)

    def start_swap(i):
        for side in range(2):

            @pl.when(x == side)
            def _():
                swap(i, side).start()

    def fetch(role, slot):
        for side in range(2):

            @pl.when(x == side)
            def _():
                pltpu.make_async_copy(held.at[role[side]], weight.at[slot], local.at[slot]).start()

    def fetched(slot):
        pltpu.make_async_copy(held.at[0], weight.at[slot], local.at[slot]).wait()

    start(0)
    first = [pltpu.make_async_copy(unit, units.at[:block], local.at[6]), pltpu.make_async_copy(grad, grads.at[:block], local.at[7])]
    for copy in first:
        copy.start()
    for j in range(3):
        pltpu.make_async_copy(own.at[j], weight.at[j], local.at[j]).start()
    for copy in first:
        copy.wait()

    def send_rows(kind, i, low, high, there, device):
        array = (units, grads)[kind]
        at = kind * 8 + i
        return remote(
            array.at[low:high], array.at[there : there + high - low], row_send.at[at], row_recv.at[at], device
        )

    half = block // 2

    def row_plan(kind):
        return (
            send_rows(kind, 0, 0, block, block, by_x),
            send_rows(kind, 1, 0, block, 2 * block, by_y),
            send_rows(kind, 2, block, block + half, 3 * block, by_y),
            send_rows(kind, 3, 2 * block + half, 3 * block, 3 * block + half, by_x),
            send_rows(kind, 4, 0, block, 4 * block, by_core),
            send_rows(kind, 5, block, 2 * block, 5 * block, by_core),
            send_rows(kind, 6, 2 * block, 3 * block, 6 * block, by_core),
            send_rows(kind, 7, 3 * block, 4 * block, 7 * block, by_core),
        )

    rows = [row_plan(kind) for kind in range(2)]
    for plan in rows:
        plan[0].start()
        plan[1].start()
        plan[4].start()
    for j in range(3):
        pltpu.make_async_copy(own.at[j], weight.at[j], local.at[j]).wait()
        for at in range(4):

            @pl.when(z == at)
            def _():
                pltpu.make_async_copy(weight.at[j], held.at[3 * at + j], local.at[j]).start()

    for j in range(3):
        pltpu.make_async_copy(weight.at[j], held.at[j], local.at[j]).wait()
    pump(0)
    for plan in rows:
        plan[0].wait_recv()
        plan[2].start()
        plan[5].start()
        plan[1].wait_recv()
        plan[3].start()
        plan[6].start()
    pump(1)
    for plan in rows:
        plan[2].wait_recv()
        plan[3].wait_recv()
        plan[7].start()
    pump(2)
    start_swap(0)
    fetch(ROLES["up"][0], 0)
    fetch(ROLES["down"][0], 1)
    for plan in rows:
        for i in range(4, 8):
            plan[i].wait_recv()
        for i in range(8):
            plan[i].wait_send()
    keep = [pltpu.make_async_copy(units, units_out, local.at[6]), pltpu.make_async_copy(grads, grads_out, local.at[7])]
    for copy in keep:
        copy.start()

    tile = 512

    def run_mlp(slot):
        wu, wd = weight.at[0], weight.at[1]

        def body(i, carry):
            here = pl.ds(pl.multiple_of(i * tile, tile), tile)
            norm = (units[here, :].astype(jnp.float32) * lines[2:3, :] + lines[3:4, :]).astype(jnp.bfloat16)
            inner = dot_nn(norm, wu[...].reshape(D, HD)) + bias_up[slot : slot + 1, :]
            pull = dot_nt(grads[here, :HD], wd[0])
            for b in range(1, D // HD):
                pull = pull + dot_nt(grads[here, b * HD : (b + 1) * HD], wd[b])
            share = 0.5 + 0.5 * lax.erf(inner * (0.5**0.5))
            act[here, :] = (inner * share).astype(jnp.bfloat16)
            slope = share + inner * jnp.exp(-0.5 * inner * inner) * ((2.0 * 3.141592653589793) ** (-0.5))
            pre[here, :] = (slope * pull).astype(jnp.bfloat16)
            return carry

        lax.fori_loop(0, tokens // tile, body, 0)

    def save_rows(source, i):
        copy = pltpu.make_async_copy(source, rows_out.at[i], local.at[8 + i])
        copy.start()
        return copy

    def save_stage(i, j):
        copy = pltpu.make_async_copy(stage.at[i], partial.at[j], local.at[16 + j])
        copy.start()
        return copy

    def run_down(source, at):
        flipped[:HD, :] = source[...].T

        def body(b, carry):
            here = pl.ds(pl.multiple_of(b * HD, HD), HD)
            stage[at, b] = dot_nn(flipped[:HD, :], grads[:, here]).astype(jnp.bfloat16)
            return carry

        lax.fori_loop(0, D // HD, body, 0)

    def run_up(sources, places, slots, gain, row, offset):
        for i, source in enumerate(sources):
            wide = source[...]
            flipped[i * HD : (i + 1) * HD, :] = wide.T
            total = jnp.sum(wide.astype(jnp.float32), axis=0, keepdims=True)
            biases[:, offset + i * HD : offset + (i + 1) * HD] = total
            column[i] = jnp.broadcast_to(total, (128, HD)).T

        def body(b, carry):
            here = pl.ds(pl.multiple_of(b * HD, HD), HD)
            gains = shifts = 0.0
            for i, (place, slot) in enumerate(zip(places, slots)):
                turned = dot_nn(flipped[i * HD : (i + 1) * HD, :], units[:, here])
                w = weight[slot, b].T.astype(jnp.float32)
                bias = column[i][:, 0:1]
                gains = gains + jnp.sum(w * turned, axis=0, keepdims=True)
                shifts = shifts + jnp.sum(w * bias, axis=0, keepdims=True)
                result = turned * lines[gain : gain + 1, here] + bias * lines[gain + 1 : gain + 2, here]
                stage[place, b] = result.T.astype(jnp.bfloat16)
            sums[row : row + 1, here] = gains
            sums[row + 1 : row + 2, here] = shifts
            return carry

        lax.fori_loop(0, D // HD, body, 0)

    fetched(0)
    fetched(1)
    run_mlp(0)
    saves = [save_rows(act, 0), save_rows(pre, 1)]
    run_down(act, 0)
    done = save_stage(0, 0)
    pump(3)
    start_swap(1)
    run_up([pre], [1], [0], 2, 2, 3 * HD)
    done_up = save_stage(1, 1)
    pump(4)
    pump(5)

    swap(0, 0).wait_recv()
    swap(1, 0).wait_recv()
    for i, role in enumerate(("q", "k", "v", "out")):
        fetch(ROLES[role], 2 + i)
    for i in range(4):
        fetched(2 + i)

    def project_rows(i, carry):
        here = pl.ds(pl.multiple_of(i * tile, tile), tile)
        turns = []
        for u in range(tile // block):
            r = i * (tile // block) + u
            a = (((x + r % 2) % 2) * 2 + (y + r // 2 % 2) % 2) * 2 + (c + r // 4) % 2
            turns.append(pl.ds(pl.multiple_of(a * block, block), block))
        cos_here = jnp.concatenate([cosine[t, :] for t in turns], axis=0)
        sin_here = jnp.concatenate([sine[t, :] for t in turns], axis=0)
        norm = (units[here, :].astype(jnp.float32) * lines[0:1, :] + lines[1:2, :]).astype(jnp.bfloat16)
        q[here, :] = turn(
            dot_nn(norm, weight[2].reshape(D, HD)) + bias_qkv[0:1, :], cos_here, sin_here
        ).astype(jnp.bfloat16)
        k[here, :] = turn(
            dot_nn(norm, weight[3].reshape(D, HD)) + bias_qkv[1:2, :], cos_here, sin_here
        ).astype(jnp.bfloat16)
        v[here, :] = (dot_nn(norm, weight[4].reshape(D, HD)) + bias_qkv[2:3, :]).astype(jnp.bfloat16)
        total = dot_nt(grads[here, :HD], weight[5, 0])
        for b in range(1, D // HD):
            total = total + dot_nt(grads[here, b * HD : (b + 1) * HD], weight[5, b])
        ga[here, :] = total.astype(jnp.bfloat16)
        return carry

    lax.fori_loop(0, tokens // tile, project_rows, 0)
    pieces = LEN // block

    def attend(s, carry):
        scale = HD ** (-0.5)
        spots = []
        for i in range(pieces):
            a = s * pieces + i
            r = ((c + a % 2) % 2) * 4 + (x + a // 4) % 2 + 2 * ((y + a // 2 % 2) % 2)
            spots.append(pl.ds(pl.multiple_of(r * block, block), block))
        for i in range(pieces):
            kseq[i * block : (i + 1) * block, :] = k[spots[i], :]
            vseq[i * block : (i + 1) * block, :] = v[spots[i], :]
        keys[...] = jnp.zeros_like(keys)
        vals[...] = jnp.zeros_like(vals)
        for i in range(pieces):
            upto = (i + 1) * block
            angle = pl.ds(pl.multiple_of(s * LEN + i * block, block), block)
            mine, pulled = q[spots[i], :], ga[spots[i], :]
            scores = dot_nt(mine, kseq[:upto, :]) * scale
            to = lax.broadcasted_iota(jnp.int32, (block, upto), 0) + i * block
            of = lax.broadcasted_iota(jnp.int32, (block, upto), 1)
            allowed = (seg_col[s, i * block : upto, :] == seg_row[s, :, :upto]) & (of <= to)
            scores = jnp.where(allowed, scores, -1e30)
            powers = jnp.exp(scores - jnp.max(scores, axis=-1, keepdims=True))
            probs = powers / jnp.sum(powers, axis=-1, keepdims=True)
            low = probs.astype(jnp.bfloat16)
            att[spots[i], :] = dot_nn(low, vseq[:upto, :]).astype(jnp.bfloat16)
            pull = dot_nt(pulled, vseq[:upto, :])
            inner = jnp.sum(probs * pull, axis=-1, keepdims=True)
            gs = (probs * (pull - inner)).astype(jnp.bfloat16)
            turned = turn(dot_nn(gs, kseq[:upto, :]) * scale, cosine[angle, :], -sine[angle, :])
            dq[spots[i], :] = turned.astype(jnp.bfloat16)
            keys[:upto, :] = keys[:upto, :] + dot_tn(gs, mine)
            vals[:upto, :] = vals[:upto, :] + dot_tn(low, pulled)
        for i in range(pieces):
            here = slice(i * block, (i + 1) * block)
            angle = pl.ds(pl.multiple_of(s * LEN + i * block, block), block)
            turned = turn(keys[here, :] * scale, cosine[angle, :], -sine[angle, :])
            dk[spots[i], :] = turned.astype(jnp.bfloat16)
            dv[spots[i], :] = vals[here, :].astype(jnp.bfloat16)
        return carry

    lax.fori_loop(0, tokens // LEN, attend, 0)
    pump(6)
    start_swap(2)
    fetch(ROLES["up"][1], 0)
    fetch(ROLES["down"][1], 1)
    for copy in saves:
        copy.wait()
    saves = [save_rows(a, 4 + i) for i, a in enumerate((att, dq, dk, dv))]
    run_up([dq, dk, dv], [2, 3, 4], [2, 3, 4], 0, 0, 0)
    done_qkv = [save_stage(2 + i, 2 + i) for i in range(3)]
    done.wait()
    run_down(att, 0)
    done = save_stage(0, 5)
    pump(7)
    start_swap(3)

    def back(side):
        return remote(stage.at[(0, 4)[side]], partial.at[7], swap_send.at[4], swap_recv.at[4], by_x)

    for side in range(2):

        @pl.when(x == side)
        def _():
            back(side).start()

    fetched(0)
    fetched(1)
    run_mlp(1)
    saves += [save_rows(act, 2), save_rows(pre, 3)]
    done_up.wait()
    run_down(act, 1)
    done_up = save_stage(1, 6)
    arrived(8)
    for step in range(len(RIGHT)):
        sent(step)
    for i in range(4):
        swap(i, 0).wait_send()
    for i in range(2, 4):
        swap(i, 0).wait_recv()
    back(0).wait()
    for copy in saves + done_qkv + keep + [done, done_up]:
        copy.wait()


def layer(own, unit, grad, lines, bias_qkv, bias_up, cosine, sine, segments):
    block = unit.shape[0]
    tokens = 8 * block
    count = tokens // LEN
    anywhere, near = pl.BlockSpec(memory_space=pl.ANY), pl.BlockSpec(memory_space=pltpu.VMEM)
    low, full = jnp.bfloat16, jnp.float32
    group = (D // HD, HD, HD)
    narrow = pltpu.VMEM((tokens, HD), low)
    return pl.pallas_call(
        layer_kernel,
        in_specs=[anywhere] * 3 + [near] * 7,
        out_specs=[anywhere] * 5 + [near] * 2,
        out_shape=[
            jax.ShapeDtypeStruct((16,) + group, low),
            jax.ShapeDtypeStruct((tokens, D), low),
            jax.ShapeDtypeStruct((tokens, D), low),
            jax.ShapeDtypeStruct((8,) + group, low),
            jax.ShapeDtypeStruct((8, tokens, HD), low),
            jax.ShapeDtypeStruct((4, D), full),
            jax.ShapeDtypeStruct((1, 4 * HD), full),
        ],
        scratch_shapes=[
            pltpu.VMEM((tokens, D), low),
            pltpu.VMEM((tokens, D), low),
            pltpu.VMEM((6,) + group, low),
            narrow,
            narrow,
            pltpu.VMEM((3 * HD, tokens), low),
            pltpu.VMEM((3, HD, 128), full),
        ]
        + [narrow] * 8
        + [pltpu.VMEM((LEN, HD), low)] * 2
        + [pltpu.VMEM((LEN, HD), full)] * 2
        + [pltpu.VMEM((5,) + group, low)]
        + [pltpu.SemaphoreType.DMA((9,))] * 4
        + [pltpu.SemaphoreType.DMA((5,))] * 2
        + [pltpu.SemaphoreType.DMA((16,))] * 2
        + [pltpu.SemaphoreType.DMA((24,))],
        compiler_params=pltpu.CompilerParams(
            vmem_limit_bytes=62 * 2**20, collective_id=0, has_side_effects=True
        ),
        cost_estimate=cost(6e10, 1e8),
        name="layer",
    )(
        own, unit, grad, lines, bias_qkv, bias_up, cosine, sine,
        segments.reshape(count, 1, LEN), segments.reshape(count, LEN, 1),
    )


def soap_part(places, grad, blocks, previous):
    total, count = blocks[0].shape[0], grad.shape[0]
    mats = 2 * count
    own = pl.BlockSpec((GROUP, HD, HD), lambda i, at: (i, 0, 0))
    some = pl.BlockSpec((GROUP, HD, HD), lambda i, at: (at[0] * (count // GROUP) + i, 0, 0))
    whole = pl.BlockSpec((count, HD, HD), lambda i, at: (at[0], 0, 0))
    full = jax.ShapeDtypeStruct((total, HD, HD), jnp.float32)
    shapes = [full, jax.ShapeDtypeStruct((total, HD, HD), jnp.bfloat16)] + [full] * 6
    extra = [] if previous is None else list(previous)

    def body(at, *refs):
        soap_kernel(count, *refs[:8], *refs[8 + len(extra) :])

    return pl.pallas_call(
        body,
        grid_spec=pltpu.PrefetchScalarGridSpec(
            num_scalar_prefetch=1,
            grid=(count // GROUP,),
            in_specs=[own] + [some] * 7 + [pl.BlockSpec(memory_space=pl.ANY)] * len(extra),
            out_specs=[some] * 6 + [whole] * 2,
            scratch_shapes=[
                pltpu.VMEM((mats, HD, 2 * HD), jnp.float32),
                pltpu.VMEM((PAN * mats, 128), jnp.float32),
            ],
        ),
        out_shape=shapes,
        input_output_aliases={9 + i: i for i in range(len(extra))},
        compiler_params=pltpu.CompilerParams(vmem_limit_bytes=LIMIT),
        cost_estimate=cost(count * 40 * 2 * HD**3 * 3, count * 16 * 4 * HD * HD),
        name="soap",
    )(places, grad, *blocks, *extra)


def adam_vector(grad, params, first, second):
    first_new = beta_one * first + (1.0 - beta_one) * grad
    second_new = beta_two * second + (1.0 - beta_two) * grad * grad
    direction = (
        first_new
        / (1.0 - beta_one**STEP)
        / (jnp.sqrt(second_new / (1.0 - beta_two**STEP)) + epsilon_adam)
    )
    return (params - rate_vector * direction, first_new, second_new)


ALL = ("dp", "heads", "tensor")
SUMMED = ((1, 0, 2), (1, 0, 2), (0, 1, 2), (0, 1, 2), (0, 1, 2), (2, 0, 1), (2, 0, 1), (2, 0, 1))
ORDER = ((0, 1, 2), (0, 1, 2), (0, 1, 2), (0, 1, 2), (0, 1, 2), (2, 0, 1), (2, 0, 1), (0, 2, 1))
SLOTS = ((4, 5, 6, 0), (1, 7, 2, 3))


def places():
    for z in range(4):
        for x in range(2):
            for y in range(2):
                for c in range(2):
                    yield z, x, y, c


def index_of(z, x, y, c):
    return ((z * 2 + x) * 2 + y) * 2 + c


def move(array, target):
    return lax.ppermute(array, ALL, [(index_of(*at), index_of(*target(*at))) for at in places()])


LINES = [[index_of(z, x, y, c) for z in range(4)] for x in range(2) for y in range(2) for c in range(2)]


def over_core(array):
    return move(array, lambda z, x, y, c: (z, x, y, 1 - c))


def over_y(array):
    return move(array, lambda z, x, y, c: (z, x, 1 - y, c))


def over_x(array):
    return move(array, lambda z, x, y, c: (z, 1 - x, y, c))


def over_xy(array):
    return move(array, lambda z, x, y, c: (z, 1 - x, 1 - y, c))


def over_z(array, flip):
    return move(array, lambda z, x, y, c: (z ^ flip, x, y, c))


def along_z(array, pairs):
    return lax.ppermute(
        array,
        ALL,
        [(index_of(a, x, y, c), index_of(b, x, y, c)) for a, b in pairs for x in range(2) for y in range(2) for c in range(2)],
    )


def gather_rows(rows):
    own = jnp.concatenate([rows, over_x(rows), over_y(rows), over_xy(rows)])
    return jnp.concatenate([own, over_core(own)])


def scatter_rows(partial):
    half = partial.shape[0] // 2
    here, there = partial[:half], partial[half:]
    pair = (here.astype(jnp.float32) + over_core(there).astype(jnp.float32)).astype(jnp.bfloat16)
    own, by_x, by_y, by_xy = (pair[i * half // 4 : (i + 1) * half // 4] for i in range(4))
    return (
        own.astype(jnp.float32)
        + over_x(by_x).astype(jnp.float32)
        + over_y(by_y).astype(jnp.float32)
        + over_xy(by_xy).astype(jnp.float32)
    )


def total_vector(vector):
    for step in (over_core, over_y, over_x, lambda v: over_z(v, 1), lambda v: over_z(v, 2)):
        vector = vector + step(vector)
    return vector


def after(array, *earlier):
    return lax.optimization_barrier((array, *earlier))[0]


def wide_angles(segments):
    cosine, sine = angles(segments)
    cosine, sine = cosine[:, :, 0], sine[:, :, 0]
    one, zero = jnp.ones(cosine.shape[:2] + (64,), jnp.float32), jnp.zeros(cosine.shape[:2] + (64,), jnp.float32)
    cosine = jnp.concatenate([cosine, cosine, one], axis=-1).reshape(-1, 128)
    sine = jnp.concatenate([-sine, sine, zero], axis=-1).reshape(-1, 128)
    return cosine, sine


def plane_shards(
    block_input,
    cotangent,
    segments,
    matrices,
    first_moment,
    second_moment,
    left_stat,
    right_stat,
    left_basis,
    right_basis,
    vectors,
    vec_first,
    vec_second,
):
    d, y, c = lax.axis_index("dp"), lax.axis_index("heads"), lax.axis_index("tensor")
    x = d % 2
    even = x == 0
    shard = 2 * y + c
    order = jnp.array(ORDER, jnp.int32)[d]
    slots = jnp.array(SLOTS, jnp.int32)[x]
    gain_one, shift_one, gain_two, shift_two = (vectors[i * D : (i + 1) * D] for i in range(4))
    head = shard * 2 + x
    qkv_offset = 4 * D + head * 3 * HD
    bias_qkv = lax.dynamic_slice_in_dim(vectors, qkv_offset, 3 * HD).reshape(3, HD)
    bias_out, bias_down = vectors[7 * D : 8 * D], vectors[8 * D + FF : 9 * D + FF]
    up_offsets = [8 * D + shard * (FF // 4) + slots[s] * HD for s in range(4)]
    bias_up = [lax.dynamic_slice_in_dim(vectors, at, HD).reshape(1, HD) for at in up_offsets]

    def pick(left, right):
        return jnp.where(even, left, right)

    middle = jnp.mean(block_input, axis=-1, keepdims=True)
    centered = block_input - middle
    inverse = lax.rsqrt(jnp.mean(centered * centered, axis=-1, keepdims=True) + epsilon_norm)
    unit = centered * inverse
    grad_own = cotangent.astype(jnp.bfloat16)
    segs = jnp.where(even, jnp.concatenate([segments, over_x(segments)]), jnp.concatenate([over_x(segments), segments]))
    cosine, sine = wide_angles(segs)
    g1, s1, g2, s2 = (v.reshape(1, D) for v in (gain_one, shift_one, gain_two, shift_two))
    own = jnp.concatenate([lax.dynamic_slice_in_dim(matrices[0], order[j] * 8, 8) for j in range(3)])
    held, units, grads, partial, rows, sums, biases = layer(
        own.astype(jnp.bfloat16).reshape(3, 8, HD, HD),
        unit.astype(jnp.bfloat16),
        grad_own,
        jnp.concatenate([g1, s1, g2, s2]),
        bias_qkv,
        jnp.concatenate(bias_up[:2]),
        cosine,
        sine,
        segs,
    )

    def role(spots):
        return (held, spots[0]), (held, spots[1])

    w_up, w_down = [None] * 4, [held[14]] * 3 + [held[15]]
    w_q, w_k, w_v, w_out, w_up[0], w_up[1], w_up[2], w_up[3], w_down[0], w_down[1] = choose(
        x,
        *[role(ROLES[n]) for n in ("q", "k", "v", "out")],
        *[role(r) for r in ROLES["up"]],
        *[role(r) for r in ROLES["down"][:2]],
    )
    w_down[2] = held[14]
    acts = [rows[0], rows[2], None, None]
    pres = [rows[1], rows[3], None, None]
    attended, grad_qkv = rows[4], [rows[5], rows[6], rows[7]]
    downs, ups = [partial[0], partial[6], None, None], [partial[1], None, None, None]
    grad_q, grad_k, grad_v, grad_out, back_a = (partial[i] for i in (2, 3, 4, 5, 7))
    bias_qkv_sum = biases[0, : 3 * HD]
    bias_up_sum = [biases[0, 3 * HD :], None, None, None]
    gain_one_sum, shift_one_sum = sums[0], sums[1]
    sums_two = [(sums[2], sums[3])]

    (ups[1],), gains, shifts, bias_up_sum[1] = up_grad(units, g2, s2, [pres[1]], [w_up[1]])
    sums_two.append((gains, shifts))
    (acts[2], acts[3]), (pres[2], pres[3]) = mlp(units, grads, g2, s2, bias_up[2:], w_up[2:], w_down[2:])
    downs[2:] = down_grad(acts[2:], grads)
    ups[2:], gains, shifts, both = up_grad(units, g2, s2, pres[2:], w_up[2:])
    bias_up_sum[2], bias_up_sum[3] = both[:HD], both[HD:]
    sums_two.append((gains, shifts))
    gain_two_sum, shift_two_sum = (sum(v[i] for v in sums_two) for i in range(2))

    back_b = over_x(pick(downs[1], grad_out))
    back_c = over_x(downs[2])
    back_d = over_x(downs[3])
    sends = (
        (pick(grad_k, grad_q), pick(back_a, ups[0]), pick(ups[0], downs[0]), pick(downs[0], downs[1])),
        (pick(grad_q, back_a), pick(back_b, ups[2]), ups[1], pick(back_c, back_b)),
        (pick(grad_v, grad_k), ups[3], pick(ups[2], back_d), pick(back_d, back_c)),
    )
    owned = [
        lax.psum_scatter(jnp.stack(send), ALL, scatter_dimension=0, tiled=False, axis_index_groups=LINES)
        for send in sends
    ]

    summed = scatter_rows(output_rows(acts + [attended], w_down + [w_out]))
    output = block_input + summed + bias_out + bias_down
    e = scatter_rows(input_rows(grad_qkv, pres, [w_q, w_k, w_v] + w_up, g1, g2))
    grad_input = cotangent + inverse * (
        e - jnp.mean(e, axis=-1, keepdims=True) - unit * jnp.mean(e * unit, axis=-1, keepdims=True)
    )

    grad_rows = jnp.sum(grad_own, axis=0, dtype=jnp.float32)
    pieces = jnp.concatenate(
        [
            gain_one_sum,
            shift_one_sum,
            gain_two_sum,
            shift_two_sum,
            jnp.zeros((3 * D,), jnp.float32),
            grad_rows,
            jnp.zeros((FF,), jnp.float32),
            grad_rows,
        ]
    )
    pieces = lax.dynamic_update_slice_in_dim(pieces, bias_qkv_sum, qkv_offset, 0)
    for at, part in zip(up_offsets, bias_up_sum):
        pieces = lax.dynamic_update_slice_in_dim(pieces, part, at, 0)
    grad_vectors = total_vector(pieces)

    blocks = [a[0] for a in (matrices, first_moment, second_moment, left_stat, right_stat, left_basis, right_basis)]
    summed_order = jnp.array(SUMMED, jnp.int32)[d]
    updated = None
    for j in range(3):
        updated = soap_part(summed_order[j : j + 1], owned[j], blocks, updated)
    new_vectors, new_vec_first, new_vec_second = adam_vector(grad_vectors, vectors, vec_first, vec_second)
    return (output, grad_input, *[u[None] for u in updated], new_vectors, new_vec_first, new_vec_second)


def generic_shards(
    block_input,
    cotangent,
    segments,
    matrices,
    first_moment,
    second_moment,
    left_stat,
    right_stat,
    left_basis,
    right_basis,
    vectors,
    vec_first,
    vec_second,
):
    group_size = lax.axis_size(("heads", "tensor"))
    member = lax.axis_index(("heads", "tensor"))
    heads_here = H // group_size
    hidden_here = FF // group_size
    row_blocks = D // HD
    hidden_blocks = hidden_here // HD
    seq_count = segments.shape[0]
    tokens_here = seq_count * LEN
    own_rows = block_input.shape[0]
    qkv_offset = 4 * D + member * heads_here * 3 * HD
    up_offset = 8 * D + member * hidden_here
    gain_one = vectors[0:D]
    shift_one = vectors[D : 2 * D]
    gain_two = vectors[2 * D : 3 * D]
    shift_two = vectors[3 * D : 4 * D]
    bias_qkv = lax.dynamic_slice_in_dim(vectors, qkv_offset, heads_here * 3 * HD).reshape(
        heads_here, 3, HD
    )
    bias_out = vectors[7 * D : 8 * D]
    bias_up = lax.dynamic_slice_in_dim(vectors, up_offset, hidden_here)
    bias_down = vectors[8 * D + FF : 9 * D + FF]
    gathered = lax.all_gather(matrices.astype(jnp.bfloat16), "dp", axis=1, tiled=True)[0]
    w_qkv, w_out, w_up, w_down = unpack_blocks(gathered, heads_here, row_blocks, hidden_blocks)
    normed_one, unit_one, inverse_one = layer_norm(block_input, gain_one, shift_one)
    normed_two, unit_two, inverse_two = layer_norm(block_input, gain_two, shift_two)
    grad_own = cotangent.astype(jnp.bfloat16)
    norm_one, norm_two, grad_rows = (
        lax.all_gather(normed_one.astype(jnp.bfloat16), ("heads", "tensor"), axis=0, tiled=True),
        lax.all_gather(normed_two.astype(jnp.bfloat16), ("heads", "tensor"), axis=0, tiled=True),
        lax.all_gather(grad_own, ("heads", "tensor"), axis=0, tiled=True),
    )
    norm_one3 = norm_one.reshape(tokens_here, row_blocks, HD)
    norm_two3 = norm_two.reshape(tokens_here, row_blocks, HD)
    projected = (
        jnp.einsum("tbr,hqbrc->thqc", norm_one3, w_qkv, preferred_element_type=jnp.float32)
        + bias_qkv
    )
    shaped = projected.reshape(seq_count, LEN, heads_here, 3, HD)
    cosine, sine = angles(segments)
    queries = rotate(shaped[:, :, :, 0], cosine, sine).astype(jnp.bfloat16)
    keys_rot = rotate(shaped[:, :, :, 1], cosine, sine).astype(jnp.bfloat16)
    values = shaped[:, :, :, 2].astype(jnp.bfloat16)
    attended, log_total = lax.map(seq_forward, (queries, keys_rot, values, segments))
    attend_low = attended.astype(jnp.bfloat16).reshape(tokens_here, heads_here, HD)
    pre_act = (
        jnp.einsum("tbr,kbrc->tkc", norm_two3, w_up, preferred_element_type=jnp.float32).reshape(
            tokens_here, hidden_here
        )
        + bias_up
    )
    act_low = gelu_exact(pre_act).astype(jnp.bfloat16)
    rows_act = act_low.reshape(lax.axis_size(("heads", "tensor")) * own_rows, hidden_blocks, HD)
    first_term = jnp.einsum("thr,hbrc->tbc", attend_low, w_out, preferred_element_type=jnp.float32)
    second_term = jnp.einsum("tkr,kbrc->tbc", rows_act, w_down, preferred_element_type=jnp.float32)
    summed = lax.psum_scatter(
        (first_term + second_term).reshape(lax.axis_size(("heads", "tensor")) * own_rows, D),
        ("heads", "tensor"),
        scatter_dimension=0,
        tiled=True,
    )
    output = block_input + summed + bias_out + bias_down
    regathered = lax.all_gather(matrices.astype(jnp.bfloat16), "dp", axis=1, tiled=True)[0]
    w_qkv, w_out, w_up, w_down = unpack_blocks(regathered, heads_here, row_blocks, hidden_blocks)
    grad_rows3 = grad_rows.reshape(tokens_here, row_blocks, HD)
    act_low3 = act_low.reshape(tokens_here, hidden_blocks, HD)
    grad_act = jnp.einsum(
        "tbc,kbrc->tkr", grad_rows3, w_down, preferred_element_type=jnp.float32
    ).reshape(tokens_here, hidden_here)
    gelu_pull = jax.vjp(gelu_exact, pre_act)[1]
    grad_pre = gelu_pull(grad_act)[0].astype(jnp.bfloat16)
    grad_pre3 = grad_pre.reshape(tokens_here, hidden_blocks, HD)
    grad_attend = jnp.einsum(
        "tbc,hbrc->thr", grad_rows3, w_out, preferred_element_type=jnp.float32
    ).astype(jnp.bfloat16)
    grad_attend = grad_attend.reshape(seq_count, LEN, heads_here, HD)
    grad_queries, grad_keys, grad_values = lax.map(
        seq_backward, (queries, keys_rot, values, segments, log_total, grad_attend)
    )
    grad_raw = jnp.stack(
        [rotate(grad_queries, cosine, -sine), rotate(grad_keys, cosine, -sine), grad_values], axis=3
    )
    grad_raw = grad_raw.astype(jnp.bfloat16).reshape(tokens_here, heads_here, 3, HD)
    rows_up = grad_pre.reshape(lax.axis_size(("heads", "tensor")) * own_rows, hidden_blocks, HD)
    back_one = jnp.einsum(
        "thqc,hqbrc->tbr", grad_raw, w_qkv, preferred_element_type=jnp.float32
    ).reshape(lax.axis_size(("heads", "tensor")) * own_rows, D)
    back_two = jnp.einsum(
        "tkc,kbrc->tbr", rows_up, w_up, preferred_element_type=jnp.float32
    ).reshape(lax.axis_size(("heads", "tensor")) * own_rows, D)
    grad_norms = lax.psum_scatter(
        jnp.stack([back_one, back_two], axis=1),
        ("heads", "tensor"),
        scatter_dimension=0,
        tiled=True,
    )
    grad_norm_one = grad_norms[:, 0]
    grad_norm_two = grad_norms[:, 1]
    grad_input = (
        cotangent
        + norm_back(grad_norm_one, unit_one, inverse_one, gain_one)
        + norm_back(grad_norm_two, unit_two, inverse_two, gain_two)
    )
    grad_bias_rows = jnp.sum(grad_own, axis=0, dtype=jnp.float32)
    pieces = jnp.concatenate(
        [
            jnp.sum(grad_norm_one * unit_one, axis=0),
            jnp.sum(grad_norm_one, axis=0),
            jnp.sum(grad_norm_two * unit_two, axis=0),
            jnp.sum(grad_norm_two, axis=0),
            jnp.zeros((3 * D,), jnp.float32),
            grad_bias_rows,
            jnp.zeros((FF,), jnp.float32),
            grad_bias_rows,
        ]
    )
    pieces = lax.dynamic_update_slice_in_dim(
        pieces, jnp.sum(grad_raw, axis=0, dtype=jnp.float32).reshape(-1), qkv_offset, 0
    )
    pieces = lax.dynamic_update_slice_in_dim(
        pieces, jnp.sum(grad_pre, axis=0, dtype=jnp.float32), up_offset, 0
    )
    grad_vectors = lax.psum(pieces, ("dp", "heads", "tensor"))
    grad_down = jnp.einsum(
        "tkr,tbc->kbrc", act_low3, grad_rows3, preferred_element_type=jnp.float32
    )
    grad_up = jnp.einsum("tbr,tkc->kbrc", norm_two3, grad_pre3, preferred_element_type=jnp.float32)
    grad_out = jnp.einsum(
        "thr,tbc->hbrc", attend_low, grad_rows3, preferred_element_type=jnp.float32
    )
    grad_qkv = jnp.einsum(
        "tbr,thqc->hqbrc", norm_one3, grad_raw, preferred_element_type=jnp.float32
    )
    attn_grads = jnp.concatenate([grad_qkv, grad_out[:, None]], axis=1).reshape(-1, HD, HD)
    all_grads = jnp.concatenate(
        [attn_grads, grad_up.reshape(-1, HD, HD), grad_down.reshape(-1, HD, HD)], axis=0
    )[None]
    owned = lax.psum_scatter(all_grads, "dp", scatter_dimension=1, tiled=True)
    blocks = [a[0] for a in (matrices, first_moment, second_moment, left_stat, right_stat, left_basis, right_basis)]
    updated = [u[None] for u in soap_part(jnp.zeros((1,), jnp.int32), owned[0], blocks, None)]
    new_vectors, new_vec_first, new_vec_second = adam_vector(
        grad_vectors, vectors, vec_first, vec_second
    )
    return (
        output,
        grad_input,
        updated[0],
        updated[1],
        updated[2],
        updated[3],
        updated[4],
        updated[5],
        updated[6],
        updated[7],
        new_vectors,
        new_vec_first,
        new_vec_second,
    )


def solution(mesh):
    in_specs = (
        P(("dp", "heads", "tensor"), None),
        P(("dp", "heads", "tensor"), None),
        P("dp", None),
        P(("heads", "tensor"), "dp", None, None),
        P(("heads", "tensor"), "dp", None, None),
        P(("heads", "tensor"), "dp", None, None),
        P(("heads", "tensor"), "dp", None, None),
        P(("heads", "tensor"), "dp", None, None),
        P(("heads", "tensor"), "dp", None, None),
        P(("heads", "tensor"), "dp", None, None),
        P(),
        P(),
        P(),
    )
    out_specs = (
        P(("dp", "heads", "tensor"), None),
        P(("dp", "heads", "tensor"), None),
        P(("heads", "tensor"), "dp", None, None),
        P(("heads", "tensor"), "dp", None, None),
        P(("heads", "tensor"), "dp", None, None),
        P(("heads", "tensor"), "dp", None, None),
        P(("heads", "tensor"), "dp", None, None),
        P(("heads", "tensor"), "dp", None, None),
        P(("heads", "tensor"), "dp", None, None),
        P(("heads", "tensor"), "dp", None, None),
        P(),
        P(),
        P(),
    )
    plane = dict(mesh.shape) == {"dp": 8, "heads": 2, "tensor": 2}
    shards = plane_shards if plane else generic_shards
    return jax.shard_map(shards, mesh=mesh, in_specs=in_specs, out_specs=out_specs, check_vma=False)
```

```python
import functools

import jax
import jax.numpy as jnp
from jax import lax
from jax.experimental import pallas as pl
from jax.experimental.pallas import tpu as pltpu
from jax.sharding import PartitionSpec as P

D = 2048
H = 8
HD = 256
RD = 64
FF = 8192
LEN = 1024
STEP = 10


epsilon_norm = 1e-05
epsilon_adam = 1e-08
rope_base = 10000.0
beta_one = 0.9
beta_two = 0.95
beta_stat = 0.95
rate_matrix = 0.05
rate_vector = 0.1
weight_decay = 0.01
PAN = 32
UNROLL = 8
GROUP = 2


def layer_norm(rows, gain, shift):
    middle = jnp.mean(rows, axis=-1, keepdims=True)
    centered = rows - middle
    spread = jnp.mean(centered * centered, axis=-1, keepdims=True)
    inverse = lax.rsqrt(spread + epsilon_norm)
    unit = centered * inverse
    return (unit * gain + shift, unit, inverse)


def norm_back(grad, unit, inverse, gain):
    scaled = grad * gain
    return inverse * (
        scaled
        - jnp.mean(scaled, axis=-1, keepdims=True)
        - unit * jnp.mean(scaled * unit, axis=-1, keepdims=True)
    )


def angles(segments):
    seq_count = segments.shape[0]
    column = jnp.arange(LEN, dtype=jnp.int32)[None, :]
    border = jnp.concatenate(
        [jnp.ones((seq_count, 1), jnp.bool_), segments[:, 1:] != segments[:, :-1]], axis=1
    )
    starts = lax.cummax(jnp.where(border, column, 0), axis=1)
    places = (column - starts).astype(jnp.float32)
    frequency = 1.0 / rope_base ** (jnp.arange(0, RD, 2).astype(jnp.float32) / RD)
    turns = places[:, :, None] * frequency[None, None, :]
    return (jnp.cos(turns)[:, :, None, :], jnp.sin(turns)[:, :, None, :])


def rotate(part, cosine, sine):
    half_dims = RD // 2
    first_half = part[..., :half_dims]
    second_half = part[..., half_dims:RD]
    return jnp.concatenate(
        [
            first_half * cosine - second_half * sine,
            second_half * cosine + first_half * sine,
            part[..., RD:],
        ],
        axis=-1,
    )


def unpack_blocks(blocks, heads_here, row_blocks, hidden_blocks):
    attn_count = heads_here * 4 * row_blocks
    up_count = hidden_blocks * row_blocks
    attn_part = blocks[:attn_count].reshape(heads_here, 4, row_blocks, HD, HD)
    w_up = blocks[attn_count : attn_count + up_count].reshape(hidden_blocks, row_blocks, HD, HD)
    w_down = blocks[attn_count + up_count :].reshape(hidden_blocks, row_blocks, HD, HD)
    return (attn_part[:, :3], attn_part[:, 3], w_up, w_down)


def masked_scores(queries, keys_rot, segment_row):
    column = jnp.arange(LEN)
    allowed = (segment_row[:, None] == segment_row[None, :]) & (column[None, :] <= column[:, None])
    scores = jnp.einsum(
        "qhd,khd->hqk", queries, keys_rot, preferred_element_type=jnp.float32
    ) * HD ** (-0.5)
    return jnp.where(allowed[None], scores, -1e30)


def seq_forward(items):
    queries, keys_rot, values, segment_row = items
    scores = masked_scores(queries, keys_rot, segment_row)
    row_max = jnp.max(scores, axis=-1, keepdims=True)
    powers = jnp.exp(scores - row_max)
    row_total = jnp.sum(powers, axis=-1, keepdims=True)
    probs_low = (powers / row_total).astype(jnp.bfloat16)
    attended = jnp.einsum("hqk,khd->qhd", probs_low, values, preferred_element_type=jnp.float32)
    return (attended, (row_max + jnp.log(row_total))[..., 0])


def seq_backward(items):
    queries, keys_rot, values, segment_row, log_total, grad_attend = items
    scores = masked_scores(queries, keys_rot, segment_row)
    probs = jnp.exp(scores - log_total[..., None])
    grad_probs = jnp.einsum("qhd,khd->hqk", grad_attend, values, preferred_element_type=jnp.float32)
    inner = jnp.sum(probs * grad_probs, axis=-1, keepdims=True)
    grad_scores = (probs * (grad_probs - inner)).astype(jnp.bfloat16)
    grad_queries = jnp.einsum(
        "hqk,khd->qhd", grad_scores, keys_rot, preferred_element_type=jnp.float32
    ) * HD ** (-0.5)
    grad_keys = jnp.einsum(
        "hqk,qhd->khd", grad_scores, queries, preferred_element_type=jnp.float32
    ) * HD ** (-0.5)
    grad_values = jnp.einsum(
        "hqk,qhd->khd", probs.astype(jnp.bfloat16), grad_attend, preferred_element_type=jnp.float32
    )
    return (grad_queries, grad_keys, grad_values)


def gelu_exact(inputs):
    return jax.nn.gelu(inputs, approximate=False)


def dot_nn(a, b):
    return lax.dot_general(a, b, (((1,), (0,)), ((), ())), preferred_element_type=jnp.float32)


def dot_nt(a, b):
    return lax.dot_general(a, b, (((1,), (1,)), ((), ())), preferred_element_type=jnp.float32)


def dot_tn(a, b):
    return lax.dot_general(a, b, (((0,), (0,)), ((), ())), preferred_element_type=jnp.float32)


def split(x):
    high = x.astype(jnp.bfloat16)
    return high, (x - high.astype(jnp.float32)).astype(jnp.bfloat16)


def three(dot, a, b):
    return dot(a[0], b[0]) + (dot(a[0], b[1]) + dot(a[1], b[0]))


def eliminate(diag, mats):
    lane = lax.broadcasted_iota(jnp.int32, (mats, 128), 1)
    rows = []
    for i in range(PAN):
        row = diag[pl.ds(i * mats, mats), :]
        rows.append(jnp.where(lane < PAN, jnp.where(lane == i, 1.0, 0.0), row))

    def entry(row, j):
        return jnp.broadcast_to(row[:, PAN + j : PAN + j + 1], (mats, 128))

    for k in range(0, PAN, 2):
        one, two = rows[k], rows[k + 1]
        cross = entry(one, k + 1)
        inverse = lax.rsqrt(entry(one, k))
        ratio = cross * (inverse * inverse)
        inverse_two = lax.rsqrt(entry(two, k + 1) - ratio * cross)
        two = two - ratio * one
        first, second = one * inverse, two * inverse_two
        diag[pl.ds(k * mats, mats), :] = first
        diag[pl.ds((k + 1) * mats, mats), :] = second
        for i in range(k + 2, PAN):
            of_one = entry(rows[k], i)
            of_two = entry(rows[k + 1], i) - ratio * of_one
            rows[i] = rows[i] - (of_one * inverse) * first - (of_two * inverse_two) * second


def soap_kernel(count, g, w, f, s, ls, rs, lb, rb, ow, owl, of, os, ols, ors, olb, orb, aug, diag):
    step = pl.program_id(0)
    mats = 2 * count
    unroll = UNROLL if mats % UNROLL == 0 else 4
    blocks = range(GROUP)
    grad = [g[i].astype(jnp.bfloat16) for i in blocks]
    left, right = [split(lb[i]) for i in blocks], [split(rb[i]) for i in blocks]
    left_t = [(x.T, y.T) for x, y in left]
    right_t = [(x.T, y.T) for x, y in right]
    grad_t = [x.T for x in grad]
    lnew = [beta_stat * ls[i] + (1.0 - beta_stat) * dot_nn(grad[i], grad_t[i]) for i in blocks]
    rnew = [beta_stat * rs[i] + (1.0 - beta_stat) * dot_nn(grad_t[i], grad[i]) for i in blocks]
    turned = [dot_nn(left_t[i][0], grad[i]) + dot_nn(left_t[i][1], grad[i]) for i in blocks]
    for i in blocks:
        ols[i] = lnew[i]
        ors[i] = rnew[i]
    turned = [three(dot_nn, split(turned[i]), right[i]) for i in blocks]
    sides = [
        three(dot_nn, basis_t, split(stat))
        for i in blocks
        for basis_t, stat in ((left_t[i], lnew[i]), (right_t[i], rnew[i]))
    ]
    first_new = [beta_one * f[i] + (1.0 - beta_one) * turned[i] for i in blocks]
    second_new = [beta_two * s[i] + (1.0 - beta_two) * turned[i] * turned[i] for i in blocks]
    direction = [
        x / (1.0 - beta_one**STEP) / (jnp.sqrt(y / (1.0 - beta_two**STEP)) + epsilon_adam)
        for x, y in zip(first_new, second_new)
    ]
    for i in blocks:
        of[i] = first_new[i]
        os[i] = second_new[i]
    stepped = [three(dot_nn, left[i], split(direction[i])) for i in blocks]
    for i, side in enumerate(sides):
        aug[2 * GROUP * step + i, :, HD:] = side
    grams = [three(dot_nt, x, x) for x in map(split, sides)]
    stepped = [three(dot_nn, split(stepped[i]), right_t[i]) for i in blocks]
    for i, gram in enumerate(grams):
        aug[2 * GROUP * step + i, :, :HD] = gram
    for i in blocks:
        weight = w[i]
        weight_new = weight - rate_matrix * (stepped[i] + weight_decay * weight)
        ow[i] = weight_new
        owl[i] = weight_new.astype(jnp.bfloat16)

    @pl.when(step == count // GROUP - 1)
    def _():
        half = HD // 2

        def place(p, i):
            low = pl.multiple_of(p * PAN, PAN)
            base = pl.multiple_of(p // 4 * 128, 128)
            for u in range(unroll):
                m = i * unroll + u
                own = aug[m, pl.ds(low, PAN), pl.ds(base, 128)]
                diag[pl.ds(m, PAN, stride=mats), :] = pltpu.roll(own, (PAN - p % 4 * PAN) % 128, 1)

        def update(p, i, late):
            low = pl.multiple_of(p * PAN, PAN)
            edge = half if late else 0
            start = edge + PAN
            mine = [i * unroll + u for u in range(unroll)]
            factors = [split(diag[pl.ds(m, PAN, stride=mats), :][:, :PAN]) for m in mine]
            panels = [split(aug[m, pl.ds(low, PAN), edge:]) for m in mine]
            panels = [three(dot_nn, x, y) for x, y in zip(factors, panels)]
            lane = lax.broadcasted_iota(jnp.int32, (PAN, HD - edge), 1) + edge
            heads = [split(jnp.where(lane >= low + PAN, panel[:, : HD - edge], 0.0)) for panel in panels]
            parts = [split(panel) for panel in panels]
            lhs = [jnp.concatenate([x, x, y], axis=0).T for x, y in heads]
            rhs = [jnp.concatenate([x, y, x], axis=0) for x, y in parts]
            rest = [aug[m, start:, edge:] - dot_nn(x[PAN:], y) for m, x, y in zip(mine, lhs, rhs)]
            for m, panel, left in zip(mine, panels, rest):
                aug[m, start:, edge:] = left
                aug[m, pl.ds(low, PAN), HD:] = panel[:, HD - edge :]

        def panel_step(p, carry):
            lax.fori_loop(0, mats // unroll, lambda i, n: (place(p, i), n)[1], 0)
            eliminate(diag, mats)

            @pl.when(p < 4)
            def _():
                lax.fori_loop(0, mats // unroll, lambda i, n: (update(p, i, False), n)[1], 0)

            @pl.when(p >= 4)
            def _():
                lax.fori_loop(0, mats // unroll, lambda i, n: (update(p, i, True), n)[1], 0)

            return carry

        lax.fori_loop(0, HD // PAN, panel_step, 0)

        def finish(b, carry):
            for side, out in enumerate((olb, orb)):
                out[b] = aug[2 * b + side, :, HD:].T
            return carry

        lax.fori_loop(0, count, finish, 0)


LIMIT = 56 * 2**20
SHRINK = 1


def cost(flops, moved, trans=0):
    return pl.CostEstimate(flops=int(flops) // SHRINK, bytes_accessed=int(moved) // SHRINK, transcendentals=0)


def turn(rows, cosine, sine):
    head = rows[:, :128]
    lane = lax.broadcasted_iota(jnp.int32, head.shape, 1)
    partner = jnp.where(lane < RD // 2, pltpu.roll(head, 128 - RD // 2, 1), pltpu.roll(head, RD // 2, 1))
    return jnp.concatenate([head * cosine + partner * sine, rows[:, 128:]], axis=1)


MESH = pl.DeviceIdType.MESH
RIGHT = (
    {0: 0, 1: 3, 2: 6},
    {0: 1, 1: 4, 2: 3},
    {0: 2, 1: 0, 2: 4},
    {1: 1, 2: 0},
    {1: 2, 2: 1},
    {1: 5, 2: 2},
    {2: 7},
    {2: 8},
    {2: 5},
)
LEFT = (
    {3: 9, 2: 6, 1: 3},
    {3: 10, 2: 9, 1: 6},
    {3: 11, 2: 10, 1: 9},
    {2: 7, 1: 4},
    {2: 11, 1: 10},
    {2: 8, 1: 7},
    {1: 11},
    {1: 8},
    {1: 5},
)
SWAPS = ((3, 9), (4, 0), (10, 11), (11, 8))
ROLES = {
    "q": (0, 1),
    "k": (1, 2),
    "v": (2, 12),
    "out": (13, 13),
    "up": ((6, 3), (7, 7), (8, 4), (5, 5)),
    "down": ((9, 6), (12, 10), (14, 14), (15, 15)),
}


def layer_kernel(
    rows_in, cotangent, segs, matrices, vectors, waves,
    held, units_out, grads_out, sum_0, sum_1, sum_2, extra, rows_out, sums, biases,
    units, grads, weight, act, pre, flipped, column, q, k, v, ga, att, dq, dk, dv, kseq, vseq, keys, vals, stage,
    raw, lines, cosine, sine, seg_row, seg_col,
    right_send, right_recv, left_send, left_recv, swap_send, swap_recv, row_send, row_recv, local,
):
    d, y, c = lax.axis_index("dp"), lax.axis_index("heads"), lax.axis_index("tensor")
    z, x = d // 2, d % 2
    by_x, by_y, by_core = {"dp": d + 1 - 2 * x}, {"heads": 1 - y}, {"tensor": 1 - c}
    shard = 2 * y + c
    block = rows_in.shape[0]
    tokens = units.shape[0]
    head = 32 + (shard * 2 + x) * 3

    barrier = pltpu.get_barrier_semaphore()
    for near in (by_x, by_y, by_core):
        pl.semaphore_signal(barrier, inc=1, device_id=near, device_id_type=MESH)

    @pl.when(z < 3)
    def _():
        pl.semaphore_signal(barrier, inc=1, device_id={"dp": d + 2}, device_id_type=MESH)

    @pl.when(z > 0)
    def _():
        pl.semaphore_signal(barrier, inc=1, device_id={"dp": d - 2}, device_id_type=MESH)

    pl.semaphore_wait(barrier, 4 + (z + 1) // 2 % 2)

    def remote(source, target, send, recv, device):
        return pltpu.make_async_remote_copy(
            src_ref=source, dst_ref=target, send_sem=send, recv_sem=recv, device_id=device, device_id_type=MESH
        )

    def hop(table, step, sends, recvs, shift, at):
        place = table[step][at]
        source = weight.at[0] if step == 0 else held.at[place]
        return remote(source, held.at[place], sends.at[step], recvs.at[step], {"dp": d + 2 * shift})

    ways = ((RIGHT, right_send, right_recv, 1), (LEFT, left_send, left_recv, -1))

    def start(step):
        for table, sends, recvs, shift in ways:
            for at in table[step]:

                @pl.when(z == at)
                def _():
                    hop(table, step, sends, recvs, shift, at).start()

    def arrived(step):
        for table, sends, recvs, shift in ways:
            for at in table[step]:

                @pl.when(z == at + shift)
                def _():
                    hop(table, step, sends, recvs, shift, at).wait_recv()

    def sent(step):
        for table, sends, recvs, shift in ways:
            for at in table[step]:

                @pl.when(z == at)
                def _():
                    hop(table, step, sends, recvs, shift, at).wait_send()

    def pump(step):
        arrived(step)
        if step + 1 < len(RIGHT):
            start(step + 1)

    def swap(i, side):
        return remote(held.at[SWAPS[i][side]], held.at[12 + i], swap_send.at[i], swap_recv.at[i], by_x)

    def start_swap(i):
        for side in range(2):

            @pl.when(x == side)
            def _():
                swap(i, side).start()

    def fetch(role, slot):
        for side in range(2):

            @pl.when(x == side)
            def _():
                pltpu.make_async_copy(held.at[role[side]], weight.at[slot], local.at[slot]).start()

    def fetched(slot):
        pltpu.make_async_copy(held.at[0], weight.at[slot], local.at[slot]).wait()

    def load(j, at):
        def begin(which):
            pltpu.make_async_copy(matrices.at[0, which * 8 : which * 8 + 8], raw.at[at], local.at[at]).start()

        usual = d < 5
        pl.when(usual)(lambda: begin(j))
        pl.when((d == 5) | (d == 6))(lambda: begin((j + 2) % 3))
        pl.when(d == 7)(lambda: begin((3 - j) % 3))

    def loaded(j, at):
        pltpu.make_async_copy(matrices.at[0, :8], raw.at[at], local.at[at]).wait()
        weight[j] = raw[at].astype(jnp.bfloat16)

    def keep_own(j):
        for at in range(4):

            @pl.when(z == at)
            def _():
                pltpu.make_async_copy(weight.at[j], held.at[3 * at + j], local.at[8 + j]).start()

    load(0, 0)
    load(1, 1)
    loaded(0, 0)
    start(0)
    load(2, 0)
    keep_own(0)
    rows = rows_in[...]
    centered = rows - jnp.mean(rows, axis=-1, keepdims=True)
    inverse = lax.rsqrt(jnp.mean(centered * centered, axis=-1, keepdims=True) + epsilon_norm)
    units[:block, :] = (centered * inverse).astype(jnp.bfloat16)
    grads[:block, :] = cotangent[...].astype(jnp.bfloat16)
    seg_row[x] = segs[...].astype(jnp.float32)

    def send_rows(kind, i, low, high, there, device):
        array = (units, grads)[kind]
        at = kind * 8 + i
        return remote(
            array.at[low:high], array.at[there : there + high - low], row_send.at[at], row_recv.at[at], device
        )

    half = block // 2

    def row_plan(kind):
        return (
            send_rows(kind, 0, 0, block, block, by_x),
            send_rows(kind, 1, 0, block, 2 * block, by_y),
            send_rows(kind, 2, block, block + half, 3 * block, by_y),
            send_rows(kind, 3, 2 * block + half, 3 * block, 3 * block + half, by_x),
            send_rows(kind, 4, 0, block, 4 * block, by_core),
            send_rows(kind, 5, block, 2 * block, 5 * block, by_core),
            send_rows(kind, 6, 2 * block, 3 * block, 6 * block, by_core),
            send_rows(kind, 7, 3 * block, 4 * block, 7 * block, by_core),
        )

    plans = [row_plan(kind) for kind in range(2)]
    for plan in plans:
        plan[0].start()
        plan[1].start()
        plan[4].start()
    segments = remote(seg_row.at[x], seg_row.at[x], swap_send.at[5], swap_recv.at[5], by_x)
    segments.start()
    loaded(1, 1)
    keep_own(1)
    loaded(2, 0)
    keep_own(2)
    for j in range(3):
        pltpu.make_async_copy(weight.at[j], held.at[j], local.at[8 + j]).wait()
    for i in range(4):
        lines[i : i + 1, :] = jnp.concatenate([vectors[8 * i + b : 8 * i + b + 1, :] for b in range(8)], axis=1)
    pump(0)
    segments.wait()
    for s in range(tokens // LEN):
        row = seg_row[s]
        wide = jnp.broadcast_to(row, (128, LEN)).T
        seg_col[s] = wide
        lane = lax.broadcasted_iota(jnp.int32, (LEN, 128), 1)
        token = lax.broadcasted_iota(jnp.int32, (LEN, 128), 0).astype(jnp.float32)
        first = jnp.sum(jnp.where(row < wide[:, 0:1], 1.0, 0.0), axis=1, keepdims=True)
        turns = (token - first) * waves[...]
        here = slice(s * LEN, (s + 1) * LEN)
        cosine[here, :] = jnp.where(lane < RD, jnp.cos(turns), 1.0)
        flips = jnp.where(lane < RD // 2, -1.0, jnp.where(lane < RD, 1.0, 0.0))
        sine[here, :] = jnp.sin(turns) * flips
    for plan in plans:
        plan[0].wait_recv()
        plan[2].start()
        plan[5].start()
        plan[1].wait_recv()
        plan[3].start()
        plan[6].start()
    pump(1)
    for plan in plans:
        plan[2].wait_recv()
        plan[3].wait_recv()
        plan[7].start()
    pump(2)
    start_swap(0)
    sent(0)
    fetch(ROLES["up"][0], 0)
    fetch(ROLES["down"][0], 1)
    for plan in plans:
        for i in range(4, 8):
            plan[i].wait_recv()
        for i in range(8):
            plan[i].wait_send()
    keep = [pltpu.make_async_copy(units, units_out, local.at[6]), pltpu.make_async_copy(grads, grads_out, local.at[7])]
    for copy in keep:
        copy.start()

    tile = 512

    def run_mlp(slot):
        hidden = SLOTS[0][slot] + (SLOTS[1][slot] - SLOTS[0][slot]) * x
        wu, wd = weight.at[0], weight.at[1]

        def body(i, carry):
            here = pl.ds(pl.multiple_of(i * tile, tile), tile)
            norm = (units[here, :].astype(jnp.float32) * lines[2:3, :] + lines[3:4, :]).astype(jnp.bfloat16)
            inner = dot_nn(norm, wu[...].reshape(D, HD)) + vectors[pl.ds(64 + shard * 8 + hidden, 1), :]
            pull = dot_nt(grads[here, :HD], wd[0])
            for b in range(1, D // HD):
                pull = pull + dot_nt(grads[here, b * HD : (b + 1) * HD], wd[b])
            share = 0.5 + 0.5 * lax.erf(inner * (0.5**0.5))
            act[here, :] = (inner * share).astype(jnp.bfloat16)
            slope = share + inner * jnp.exp(-0.5 * inner * inner) * ((2.0 * 3.141592653589793) ** (-0.5))
            pre[here, :] = (slope * pull).astype(jnp.bfloat16)
            return carry

        lax.fori_loop(0, tokens // tile, body, 0)

    def save_rows(source, i):
        copy = pltpu.make_async_copy(source, rows_out.at[i], local.at[8 + i])
        copy.start()
        return copy

    def put(i, to_0, to_1, sem):
        for side, target in ((0, to_0), (1, to_1)):
            if target is not None:

                @pl.when(x == side)
                def _():
                    pltpu.make_async_copy(stage.at[i], target, local.at[16 + sem]).start()

        def finish():
            for side, target in ((0, to_0), (1, to_1)):
                if target is not None:

                    @pl.when(x == side)
                    def _():
                        pltpu.make_async_copy(stage.at[i], target, local.at[16 + sem]).wait()

        return finish

    def run_down(source, at):
        flipped[:HD, :] = source[...].T

        def body(b, carry):
            here = pl.ds(pl.multiple_of(b * HD, HD), HD)
            stage[at, b] = dot_nn(flipped[:HD, :], grads[:, here]).astype(jnp.bfloat16)
            return carry

        lax.fori_loop(0, D // HD, body, 0)

    def run_up(sources, places, slots, gain, row, offset):
        for i, source in enumerate(sources):
            wide = source[...]
            flipped[i * HD : (i + 1) * HD, :] = wide.T
            total = jnp.sum(wide.astype(jnp.float32), axis=0, keepdims=True)
            biases[:, offset + i * HD : offset + (i + 1) * HD] = total
            column[i] = jnp.broadcast_to(total, (128, HD)).T

        def body(b, carry):
            here = pl.ds(pl.multiple_of(b * HD, HD), HD)
            gains = shifts = 0.0
            for i, (place, slot) in enumerate(zip(places, slots)):
                turned = dot_nn(flipped[i * HD : (i + 1) * HD, :], units[:, here])
                w = weight[slot, b].T.astype(jnp.float32)
                bias = column[i][:, 0:1]
                gains = gains + jnp.sum(w * turned, axis=0, keepdims=True)
                shifts = shifts + jnp.sum(w * bias, axis=0, keepdims=True)
                result = turned * lines[gain : gain + 1, here] + bias * lines[gain + 1 : gain + 2, here]
                stage[place, b] = result.T.astype(jnp.bfloat16)
            sums[row : row + 1, here] = gains
            sums[row + 1 : row + 2, here] = shifts
            return carry

        lax.fori_loop(0, D // HD, body, 0)

    fetched(0)
    fetched(1)
    run_mlp(0)
    saves = [save_rows(act, 0), save_rows(pre, 1)]
    run_down(act, 0)
    done = put(0, sum_0.at[3], sum_0.at[2], 0)
    pump(3)
    start_swap(1)
    run_up([pre], [1], [0], 2, 2, 3 * HD)
    done_up = put(1, sum_0.at[2], sum_0.at[1], 1)
    pump(4)
    pump(5)

    swap(0, 0).wait_recv()
    swap(1, 0).wait_recv()
    for i, role in enumerate(("q", "k", "v", "out")):
        fetch(ROLES[role], 2 + i)
    for i in range(4):
        fetched(2 + i)

    def project_rows(i, carry):
        here = pl.ds(pl.multiple_of(i * tile, tile), tile)
        turns = []
        for u in range(tile // block):
            r = i * (tile // block) + u
            a = (((x + r % 2) % 2) * 2 + (y + r // 2 % 2) % 2) * 2 + (c + r // 4) % 2
            turns.append(pl.ds(pl.multiple_of(a * block, block), block))
        cos_here = jnp.concatenate([cosine[t, :] for t in turns], axis=0)
        sin_here = jnp.concatenate([sine[t, :] for t in turns], axis=0)
        norm = (units[here, :].astype(jnp.float32) * lines[0:1, :] + lines[1:2, :]).astype(jnp.bfloat16)
        q[here, :] = turn(
            dot_nn(norm, weight[2].reshape(D, HD)) + vectors[pl.ds(head + 0, 1), :], cos_here, sin_here
        ).astype(jnp.bfloat16)
        k[here, :] = turn(
            dot_nn(norm, weight[3].reshape(D, HD)) + vectors[pl.ds(head + 1, 1), :], cos_here, sin_here
        ).astype(jnp.bfloat16)
        v[here, :] = (dot_nn(norm, weight[4].reshape(D, HD)) + vectors[pl.ds(head + 2, 1), :]).astype(jnp.bfloat16)
        total = dot_nt(grads[here, :HD], weight[5, 0])
        for b in range(1, D // HD):
            total = total + dot_nt(grads[here, b * HD : (b + 1) * HD], weight[5, b])
        ga[here, :] = total.astype(jnp.bfloat16)
        return carry

    lax.fori_loop(0, tokens // tile, project_rows, 0)
    pieces = LEN // block

    def attend(s, carry):
        scale = HD ** (-0.5)
        spots = []
        for i in range(pieces):
            a = s * pieces + i
            r = ((c + a % 2) % 2) * 4 + (x + a // 4) % 2 + 2 * ((y + a // 2 % 2) % 2)
            spots.append(pl.ds(pl.multiple_of(r * block, block), block))
        for i in range(pieces):
            kseq[i * block : (i + 1) * block, :] = k[spots[i], :]
            vseq[i * block : (i + 1) * block, :] = v[spots[i], :]
        keys[...] = jnp.zeros_like(keys)
        vals[...] = jnp.zeros_like(vals)
        for i in range(pieces):
            upto = (i + 1) * block
            angle = pl.ds(pl.multiple_of(s * LEN + i * block, block), block)
            mine, pulled = q[spots[i], :], ga[spots[i], :]
            scores = dot_nt(mine, kseq[:upto, :]) * scale
            to = lax.broadcasted_iota(jnp.int32, (block, upto), 0) + i * block
            of = lax.broadcasted_iota(jnp.int32, (block, upto), 1)
            allowed = (seg_col[s, i * block : upto, 0:1] == seg_row[s, :, :upto]) & (of <= to)
            scores = jnp.where(allowed, scores, -1e30)
            powers = jnp.exp(scores - jnp.max(scores, axis=-1, keepdims=True))
            probs = powers / jnp.sum(powers, axis=-1, keepdims=True)
            low = probs.astype(jnp.bfloat16)
            att[spots[i], :] = dot_nn(low, vseq[:upto, :]).astype(jnp.bfloat16)
            pull = dot_nt(pulled, vseq[:upto, :])
            inner = jnp.sum(probs * pull, axis=-1, keepdims=True)
            gs = (probs * (pull - inner)).astype(jnp.bfloat16)
            turned = turn(dot_nn(gs, kseq[:upto, :]) * scale, cosine[angle, :], -sine[angle, :])
            dq[spots[i], :] = turned.astype(jnp.bfloat16)
            keys[:upto, :] = keys[:upto, :] + dot_tn(gs, mine)
            vals[:upto, :] = vals[:upto, :] + dot_tn(low, pulled)
        for i in range(pieces):
            here = slice(i * block, (i + 1) * block)
            angle = pl.ds(pl.multiple_of(s * LEN + i * block, block), block)
            turned = turn(keys[here, :] * scale, cosine[angle, :], -sine[angle, :])
            dk[spots[i], :] = turned.astype(jnp.bfloat16)
            dv[spots[i], :] = vals[here, :].astype(jnp.bfloat16)
        return carry

    lax.fori_loop(0, tokens // LEN, attend, 0)
    pump(6)
    start_swap(2)
    fetch(ROLES["up"][1], 0)
    fetch(ROLES["down"][1], 1)
    for copy in saves:
        copy.wait()
    saves = [save_rows(a, 4 + i) for i, a in enumerate((att, dq, dk, dv))]
    run_up([dq, dk, dv], [2, 3, 4], [2, 3, 4], 0, 0, 0)
    done_qkv = [
        put(2, sum_1.at[0], sum_0.at[0], 2),
        put(3, sum_0.at[0], sum_2.at[0], 3),
        put(4, sum_2.at[0], None, 4),
    ]
    done()
    run_down(att, 0)
    done = put(0, None, extra, 5)
    pump(7)
    start_swap(3)

    back = [
        remote(stage.at[0], sum_1.at[0], swap_send.at[4], swap_recv.at[4], by_x),
        remote(stage.at[4], sum_0.at[1], swap_send.at[4], swap_recv.at[4], by_x),
    ]
    for side in range(2):
        pl.when(x == side)(back[side].start)

    fetched(0)
    fetched(1)
    run_mlp(1)
    saves += [save_rows(act, 2), save_rows(pre, 3)]
    done_up()
    run_down(act, 1)
    done_up = put(1, extra, sum_0.at[3], 6)
    arrived(8)
    for step in range(1, len(RIGHT)):
        sent(step)
    for i in range(4):
        swap(i, 0).wait_send()
    for i in range(2, 4):
        swap(i, 0).wait_recv()
    back[0].wait()
    for copy in saves + keep:
        copy.wait()
    for finish in done_qkv + [done, done_up]:
        finish()


def layer(rows, cotangent, segments, matrices, vectors, waves):
    block = rows.shape[0]
    tokens = 8 * block
    count = tokens // LEN
    anywhere, near = pl.BlockSpec(memory_space=pl.ANY), pl.BlockSpec(memory_space=pltpu.VMEM)
    low, full = jnp.bfloat16, jnp.float32
    group = (D // HD, HD, HD)
    narrow = pltpu.VMEM((tokens, HD), low)
    return pl.pallas_call(
        layer_kernel,
        in_specs=[near] * 3 + [anywhere] + [near] * 2,
        out_specs=[anywhere] * 8 + [near] * 2,
        out_shape=[
            jax.ShapeDtypeStruct((16,) + group, low),
            jax.ShapeDtypeStruct((tokens, D), low),
            jax.ShapeDtypeStruct((tokens, D), low),
        ]
        + [jax.ShapeDtypeStruct((4,) + group, low)] * 3
        + [
            jax.ShapeDtypeStruct(group, low),
            jax.ShapeDtypeStruct((8, tokens, HD), low),
            jax.ShapeDtypeStruct((4, D), full),
            jax.ShapeDtypeStruct((1, 4 * HD), full),
        ],
        scratch_shapes=[
            pltpu.VMEM((tokens, D), low),
            pltpu.VMEM((tokens, D), low),
            pltpu.VMEM((6,) + group, low),
            narrow,
            narrow,
            pltpu.VMEM((3 * HD, tokens), low),
            pltpu.VMEM((3, HD, 128), full),
        ]
        + [narrow] * 8
        + [pltpu.VMEM((LEN, HD), low)] * 2
        + [pltpu.VMEM((LEN, HD), full)] * 2
        + [
            pltpu.VMEM((5,) + group, low),
            pltpu.VMEM((2,) + group, full),
            pltpu.VMEM((4, D), full),
            pltpu.VMEM((tokens, 128), full),
            pltpu.VMEM((tokens, 128), full),
            pltpu.VMEM((count, 1, LEN), full),
            pltpu.VMEM((count, LEN, 128), full),
        ]
        + [pltpu.SemaphoreType.DMA((9,))] * 4
        + [pltpu.SemaphoreType.DMA((6,))] * 2
        + [pltpu.SemaphoreType.DMA((16,))] * 2
        + [pltpu.SemaphoreType.DMA((24,))],
        compiler_params=pltpu.CompilerParams(
            vmem_limit_bytes=63 * 2**20, collective_id=0, has_side_effects=True
        ),
        cost_estimate=cost(6e10, 1e8),
        name="layer",
    )(rows, cotangent, segments, matrices, vectors, waves)


def rest_kernel(
    held, units_in, grads_in, rows_in, vectors, early, early_bias, extra, sum_1_in, sum_2_in,
    sum_1, sum_2, rows_out, total,
    units, grads, weight, acts, pres, flipped, column, stage, lines, added, current, received,
    swap_send, swap_recv, hop_send, hop_recv, loads, local,
):
    d, y, c = lax.axis_index("dp"), lax.axis_index("heads"), lax.axis_index("tensor")
    z, x = d // 2, d % 2
    shard = 2 * y + c
    tokens = units.shape[0]
    block = tokens // 8
    by_x, by_y, by_core = {"dp": d + 1 - 2 * x}, {"heads": 1 - y}, {"tensor": 1 - c}
    by_z = [{"dp": d + 2 - 4 * (z % 2)}, {"dp": d + 4 - 8 * (z // 2)}]
    peers = [by_core, by_y, by_x] + by_z
    barrier = pltpu.get_barrier_semaphore()
    for near in peers:
        pl.semaphore_signal(barrier, inc=1, device_id=near, device_id_type=MESH)
    pl.semaphore_wait(barrier, len(peers))

    def remote(source, target, send, recv, device):
        return pltpu.make_async_remote_copy(
            src_ref=source, dst_ref=target, send_sem=send, recv_sem=recv, device_id=device, device_id_type=MESH
        )

    def back(source, i, to_0, to_1):
        copies = [remote(source, there, swap_send.at[i], swap_recv.at[i], by_x) for there in (to_0, to_1)]
        for side in range(2):
            pl.when(x == side)(copies[side].start)
        return copies[0]

    swaps = [back(extra, 0, sum_1.at[3], sum_1.at[1])]

    def fetch(role, slot):
        for side in range(2):

            @pl.when(x == side)
            def _():
                pltpu.make_async_copy(held.at[role[side]], weight.at[slot], local.at[slot]).start()

    tile = 512
    for slot, role in enumerate((ROLES["up"][1], ROLES["up"][2], ROLES["up"][3], ROLES["down"][2], ROLES["down"][3])):
        fetch(role, slot)
    pltpu.make_async_copy(rows_in.at[3], pres.at[0], local.at[5]).start()

    def row_loads(i):
        here = pl.ds(pl.multiple_of(i * tile, tile), tile)
        return [
            pltpu.make_async_copy(source.at[here], target.at[here], loads.at[2 * i + j])
            for j, (source, target) in enumerate(((units_in, units), (grads_in, grads)))
        ]

    for i in range(tokens // tile):
        for copy in row_loads(i):
            copy.start()
    for i in range(4):
        lines[i : i + 1, :] = jnp.concatenate([vectors[8 * i + b : 8 * i + b + 1, :] for b in range(8)], axis=1)
    for slot in range(5):
        pltpu.make_async_copy(held.at[0], weight.at[slot], local.at[slot]).wait()
    hidden = [SLOTS[0][s] + (SLOTS[1][s] - SLOTS[0][s]) * x for s in range(4)]

    def run_mlp(i, carry):
        here = pl.ds(pl.multiple_of(i * tile, tile), tile)
        for copy in row_loads(i):
            copy.wait()
        norm = (units[here, :].astype(jnp.float32) * lines[2:3, :] + lines[3:4, :]).astype(jnp.bfloat16)
        for s in range(2):
            bias = vectors[pl.ds(64 + shard * 8 + hidden[2 + s], 1), :]
            inner = dot_nn(norm, weight[1 + s].reshape(D, HD)) + bias
            pull = dot_nt(grads[here, :HD], weight[3 + s, 0])
            for b in range(1, D // HD):
                pull = pull + dot_nt(grads[here, b * HD : (b + 1) * HD], weight[3 + s, b])
            share = 0.5 + 0.5 * lax.erf(inner * (0.5**0.5))
            acts[s, here, :] = (inner * share).astype(jnp.bfloat16)
            slope = share + inner * jnp.exp(-0.5 * inner * inner) * ((2.0 * 3.141592653589793) ** (-0.5))
            pres[1 + s, here, :] = (slope * pull).astype(jnp.bfloat16)
        return carry

    lax.fori_loop(0, tokens // tile, run_mlp, 0)
    saves = []
    for s in range(2):
        for j, source in enumerate((acts.at[s], pres.at[1 + s])):
            copy = pltpu.make_async_copy(source, rows_out.at[2 * s + j], local.at[6 + 2 * s + j])
            copy.start()
            saves.append(copy)
    for s in range(2):
        flipped[s * HD : (s + 1) * HD, :] = acts[s].T

    def run_down(b, carry):
        here = pl.ds(pl.multiple_of(b * HD, HD), HD)
        for s in range(2):
            stage[s, b] = dot_nn(flipped[s * HD : (s + 1) * HD, :], grads[:, here]).astype(jnp.bfloat16)
        return carry

    lax.fori_loop(0, D // HD, run_down, 0)
    swaps.append(back(stage.at[0], 1, sum_2.at[3], sum_1.at[3]))
    swaps.append(back(stage.at[1], 2, sum_2.at[2], sum_2.at[3]))
    pltpu.make_async_copy(rows_in.at[3], pres.at[0], local.at[5]).wait()
    current[0] = jnp.zeros(current.shape[1:], jnp.float32)
    for i in range(3):
        wide = pres[i]
        flipped[i * HD : (i + 1) * HD, :] = wide.T
        bias = jnp.sum(wide.astype(jnp.float32), axis=0, keepdims=True)
        current[0, pl.ds(64 + shard * 8 + hidden[1 + i], 1), :] = bias
        column[i] = jnp.broadcast_to(bias, (128, HD)).T

    def run_up(b, carry):
        here = pl.ds(pl.multiple_of(b * HD, HD), HD)
        gains, shifts = early[2:3, here], early[3:4, here]
        for i in range(3):
            turned = dot_nn(flipped[i * HD : (i + 1) * HD, :], units[:, here])
            w = weight[i, b].T.astype(jnp.float32)
            bias = column[i][:, 0:1]
            gains = gains + jnp.sum(w * turned, axis=0, keepdims=True)
            shifts = shifts + jnp.sum(w * bias, axis=0, keepdims=True)
            result = turned * lines[2:3, here] + bias * lines[3:4, here]
            stage[2 + i, b] = result.T.astype(jnp.bfloat16)
        added[0:1, here] = gains
        added[1:2, here] = shifts
        return carry

    lax.fori_loop(0, D // HD, run_up, 0)
    places = ((sum_1.at[2], sum_1.at[2]), (sum_2.at[2], sum_1.at[1]), (sum_2.at[1], sum_2.at[1]))
    puts = [[pltpu.make_async_copy(stage.at[2 + i], places[i][side], local.at[10 + i]) for side in range(2)] for i in range(3)]
    for pair in puts:
        for side in range(2):
            pl.when(x == side)(pair[side].start)

    own = jnp.sum(grads[:block, :].astype(jnp.float32), axis=0, keepdims=True)
    for i, line in enumerate((early[0:1, :], early[1:2, :], added[0:1, :], added[1:2, :])):
        for b in range(8):
            current[0, 8 * i + b : 8 * i + b + 1, :] = line[:, b * HD : (b + 1) * HD]
    for b in range(8):
        current[0, 56 + b : 57 + b, :] = own[:, b * HD : (b + 1) * HD]
        current[0, 96 + b : 97 + b, :] = own[:, b * HD : (b + 1) * HD]
    for i in range(3):
        at = 32 + (shard * 2 + x) * 3 + i
        current[0, pl.ds(at, 1), :] = early_bias[:, i * HD : (i + 1) * HD]
    current[0, pl.ds(64 + shard * 8 + hidden[0], 1), :] = early_bias[:, 3 * HD :]
    for i, near in enumerate(peers):
        copy = remote(current.at[i], received.at[i], hop_send.at[i], hop_recv.at[i], near)
        copy.start()
        copy.wait()
        result = current[i] + received[i]
        if i + 1 < len(peers):
            current[i + 1] = result
        else:
            total[...] = result
    for copy in swaps + saves:
        copy.wait()
    for pair in puts:
        for side in range(2):
            pl.when(x == side)(pair[side].wait)


def rest(held, units, grads, rows, vectors, sums, biases, extra, sum_1, sum_2):
    tokens = units.shape[0]
    anywhere, near = pl.BlockSpec(memory_space=pl.ANY), pl.BlockSpec(memory_space=pltpu.VMEM)
    low, full = jnp.bfloat16, jnp.float32
    group = (D // HD, HD, HD)
    table = vectors.shape
    return pl.pallas_call(
        rest_kernel,
        in_specs=[anywhere] * 4 + [near] * 3 + [anywhere] * 3,
        out_specs=[anywhere] * 3 + [near],
        out_shape=[jax.ShapeDtypeStruct((4,) + group, low)] * 2
        + [jax.ShapeDtypeStruct((4, tokens, HD), low), jax.ShapeDtypeStruct(table, full)],
        input_output_aliases={8: 0, 9: 1},
        scratch_shapes=[
            pltpu.VMEM((tokens, D), low),
            pltpu.VMEM((tokens, D), low),
            pltpu.VMEM((5,) + group, low),
            pltpu.VMEM((2, tokens, HD), low),
            pltpu.VMEM((3, tokens, HD), low),
            pltpu.VMEM((3 * HD, tokens), low),
            pltpu.VMEM((3, HD, 128), full),
            pltpu.VMEM((5,) + group, low),
            pltpu.VMEM((4, D), full),
            pltpu.VMEM((2, D), full),
            pltpu.VMEM((5,) + table, full),
            pltpu.VMEM((5,) + table, full),
            pltpu.SemaphoreType.DMA((3,)),
            pltpu.SemaphoreType.DMA((3,)),
            pltpu.SemaphoreType.DMA((5,)),
            pltpu.SemaphoreType.DMA((5,)),
            pltpu.SemaphoreType.DMA((8,)),
            pltpu.SemaphoreType.DMA((13,)),
        ],
        compiler_params=pltpu.CompilerParams(
            vmem_limit_bytes=60 * 2**20, collective_id=1, has_side_effects=True
        ),
        cost_estimate=cost(4e10, 6e7),
        name="rest",
    )(held, units, grads, rows, vectors, sums, biases, extra, sum_1, sum_2)


def rows_kernel(roles, groups, x_at, held, *refs):
    many = len(roles)
    rows, gains, out, weight, sems = refs[:many], refs[many:-3], refs[-3], refs[-2], refs[-1]

    @pl.when(pl.program_id(0) == 0)
    def _():
        for i, role in enumerate(roles):
            for side in range(2):

                @pl.when(x_at[0] == side)
                def _():
                    pltpu.make_async_copy(held.at[role[side]], weight.at[i], sems.at[i]).start()

        for i in range(many):
            pltpu.make_async_copy(held.at[0], weight.at[i], sems.at[i]).wait()

    dot = dot_nt if gains else dot_nn
    for b in range(D // HD):
        here = slice(b * HD, (b + 1) * HD)
        total = None
        for j, (low, high) in enumerate(groups):
            part = dot(rows[low][0], weight[low, b])
            for i in range(low + 1, high):
                part = part + dot(rows[i][0], weight[i, b])
            if gains:
                part = part * gains[j][:, here]
            total = part if total is None else total + part
        out[:, here] = total.astype(jnp.bfloat16)


def rows_times(x, held, roles, groups, rows, gains):
    tokens, many = rows[0][0].shape[1], len(roles)
    tile = 512
    return pl.pallas_call(
        functools.partial(rows_kernel, roles, groups),
        grid=(tokens // tile,),
        in_specs=[pl.BlockSpec(memory_space=pltpu.SMEM), pl.BlockSpec(memory_space=pl.ANY)]
        + [pl.BlockSpec((1, tile, HD), lambda i, at=at: (at, i, 0)) for _, at in rows]
        + [pl.BlockSpec((1, D), lambda i: (0, 0))] * len(gains),
        out_specs=pl.BlockSpec((tile, D), lambda i: (i, 0)),
        out_shape=jax.ShapeDtypeStruct((tokens, D), jnp.bfloat16),
        scratch_shapes=[pltpu.VMEM((many, D // HD, HD, HD), jnp.bfloat16), pltpu.SemaphoreType.DMA((many,))],
        compiler_params=pltpu.CompilerParams(vmem_limit_bytes=LIMIT),
        cost_estimate=cost(2 * many * tokens * D * HD, 2 * tokens * D + many * 2 * D * HD),
        name="rows_times",
    )(x.reshape(1), held, *[array for array, _ in rows], *gains)


def soap_part(places, grad, blocks, previous):
    total, count = blocks[0].shape[0], grad.shape[0]
    mats = 2 * count
    own = pl.BlockSpec((GROUP, HD, HD), lambda i, at: (i, 0, 0))
    some = pl.BlockSpec((GROUP, HD, HD), lambda i, at: (at[0] * (count // GROUP) + i, 0, 0))
    whole = pl.BlockSpec((count, HD, HD), lambda i, at: (at[0], 0, 0))
    full = jax.ShapeDtypeStruct((total, HD, HD), jnp.float32)
    shapes = [full, jax.ShapeDtypeStruct((total, HD, HD), jnp.bfloat16)] + [full] * 6
    extra = [] if previous is None else list(previous)

    def body(at, *refs):
        soap_kernel(count, *refs[:8], *refs[8 + len(extra) :])

    return pl.pallas_call(
        body,
        grid_spec=pltpu.PrefetchScalarGridSpec(
            num_scalar_prefetch=1,
            grid=(count // GROUP,),
            in_specs=[own] + [some] * 7 + [pl.BlockSpec(memory_space=pl.ANY)] * len(extra),
            out_specs=[some] * 6 + [whole] * 2,
            scratch_shapes=[
                pltpu.VMEM((mats, HD, 2 * HD), jnp.float32),
                pltpu.VMEM((PAN * mats, 128), jnp.float32),
            ],
        ),
        out_shape=shapes,
        input_output_aliases={9 + i: i for i in range(len(extra))},
        compiler_params=pltpu.CompilerParams(vmem_limit_bytes=LIMIT),
        cost_estimate=cost(count * 40 * 2 * HD**3 * 3, count * 16 * 4 * HD * HD),
        name="soap",
    )(places, grad, *blocks, *extra)


def adam_vector(grad, params, first, second):
    first_new = beta_one * first + (1.0 - beta_one) * grad
    second_new = beta_two * second + (1.0 - beta_two) * grad * grad
    direction = (
        first_new
        / (1.0 - beta_one**STEP)
        / (jnp.sqrt(second_new / (1.0 - beta_two**STEP)) + epsilon_adam)
    )
    return (params - rate_vector * direction, first_new, second_new)


ALL = ("dp", "heads", "tensor")
SUMMED = ((1, 0, 2), (1, 0, 2), (0, 1, 2), (0, 1, 2), (0, 1, 2), (2, 0, 1), (2, 0, 1), (2, 0, 1))
SLOTS = ((4, 5, 6, 0), (1, 7, 2, 3))


def places():
    for z in range(4):
        for x in range(2):
            for y in range(2):
                for c in range(2):
                    yield z, x, y, c


def index_of(z, x, y, c):
    return ((z * 2 + x) * 2 + y) * 2 + c


def move(array, target):
    return lax.ppermute(array, ALL, [(index_of(*at), index_of(*target(*at))) for at in places()])


LINES = [[index_of(z, x, y, c) for z in range(4)] for x in range(2) for y in range(2) for c in range(2)]


def over_core(array):
    return move(array, lambda z, x, y, c: (z, x, y, 1 - c))


def over_y(array):
    return move(array, lambda z, x, y, c: (z, x, 1 - y, c))


def over_x(array):
    return move(array, lambda z, x, y, c: (z, 1 - x, y, c))


def over_xy(array):
    return move(array, lambda z, x, y, c: (z, 1 - x, 1 - y, c))


def after(array, *earlier):
    return lax.optimization_barrier((array, *earlier))[0]


def scatter_rows(partial, *earlier):
    half = partial.shape[0] // 2
    here, there = partial[:half], partial[half:]
    pair = (here.astype(jnp.float32) + over_core(there).astype(jnp.float32)).astype(jnp.bfloat16)
    own, by_x, by_y, by_xy = (pair[i * half // 4 : (i + 1) * half // 4] for i in range(4))
    return (
        after(own, *earlier).astype(jnp.float32)
        + over_x(by_x).astype(jnp.float32)
        + over_y(by_y).astype(jnp.float32)
        + over_xy(by_xy).astype(jnp.float32)
    )


def plane_shards(
    block_input,
    cotangent,
    segments,
    matrices,
    first_moment,
    second_moment,
    left_stat,
    right_stat,
    left_basis,
    right_basis,
    vectors,
    vec_first,
    vec_second,
):
    d = lax.axis_index("dp")
    x = d % 2
    gain_one, gain_two = vectors[:D].reshape(1, D), vectors[2 * D : 3 * D].reshape(1, D)
    bias_out, bias_down = vectors[7 * D : 8 * D], vectors[8 * D + FF : 9 * D + FF]
    table = vectors.reshape(-1, HD)
    frequency = 1.0 / rope_base ** (jnp.arange(0, RD, 2).astype(jnp.float32) / RD)
    turns = jnp.concatenate([frequency, frequency, jnp.zeros((128 - RD,), jnp.float32)]).reshape(1, 128)
    held, units, grads, sum_0, sum_1, sum_2, extra, rows, sums, biases = layer(
        block_input, cotangent, segments, matrices, table, turns
    )
    sum_1, sum_2, late, grad_table = rest(held, units, grads, rows, table, sums, biases, extra, sum_1, sum_2)
    owned = []
    for send in (sum_0, sum_1, sum_2):
        owned.append(lax.psum_scatter(send, ALL, scatter_dimension=0, tiled=False, axis_index_groups=LINES))

    ups, downs = ROLES["up"], ROLES["down"]
    out_share = rows_times(
        x,
        held,
        (downs[0], downs[1], ROLES["out"], downs[2], downs[3]),
        ((0, 5),),
        ((rows, 0), (rows, 2), (rows, 4), (late, 0), (late, 2)),
        (),
    )
    in_share = rows_times(
        x,
        held,
        (ROLES["q"], ROLES["k"], ROLES["v"]) + ups,
        ((0, 3), (3, 7)),
        ((rows, 5), (rows, 6), (rows, 7), (rows, 1), (rows, 3), (late, 1), (late, 3)),
        (gain_one, gain_two),
    )
    blocks = [a[0] for a in (matrices, first_moment, second_moment, left_stat, right_stat, left_basis, right_basis)]
    summed_order = jnp.array(SUMMED, jnp.int32)[d]
    updated = soap_part(summed_order[0:1], after(owned[0], in_share, out_share), blocks, None)
    output = block_input + scatter_rows(out_share, updated[1]) + bias_out + bias_down
    e = scatter_rows(in_share, updated[1])
    middle = jnp.mean(block_input, axis=-1, keepdims=True)
    centered = block_input - middle
    inverse = lax.rsqrt(jnp.mean(centered * centered, axis=-1, keepdims=True) + epsilon_norm)
    unit = centered * inverse
    grad_input = cotangent + inverse * (
        e - jnp.mean(e, axis=-1, keepdims=True) - unit * jnp.mean(e * unit, axis=-1, keepdims=True)
    )
    grad_vectors = grad_table.reshape(-1)
    updated = soap_part(summed_order[1:2], after(owned[1], output, grad_input), blocks, updated)
    updated = soap_part(summed_order[2:3], owned[2], blocks, updated)

    new_vectors, new_vec_first, new_vec_second = adam_vector(grad_vectors, vectors, vec_first, vec_second)
    return (output, grad_input, *[u[None] for u in updated], new_vectors, new_vec_first, new_vec_second)


def generic_shards(
    block_input,
    cotangent,
    segments,
    matrices,
    first_moment,
    second_moment,
    left_stat,
    right_stat,
    left_basis,
    right_basis,
    vectors,
    vec_first,
    vec_second,
):
    group_size = lax.axis_size(("heads", "tensor"))
    member = lax.axis_index(("heads", "tensor"))
    heads_here = H // group_size
    hidden_here = FF // group_size
    row_blocks = D // HD
    hidden_blocks = hidden_here // HD
    seq_count = segments.shape[0]
    tokens_here = seq_count * LEN
    own_rows = block_input.shape[0]
    qkv_offset = 4 * D + member * heads_here * 3 * HD
    up_offset = 8 * D + member * hidden_here
    gain_one = vectors[0:D]
    shift_one = vectors[D : 2 * D]
    gain_two = vectors[2 * D : 3 * D]
    shift_two = vectors[3 * D : 4 * D]
    bias_qkv = lax.dynamic_slice_in_dim(vectors, qkv_offset, heads_here * 3 * HD).reshape(
        heads_here, 3, HD
    )
    bias_out = vectors[7 * D : 8 * D]
    bias_up = lax.dynamic_slice_in_dim(vectors, up_offset, hidden_here)
    bias_down = vectors[8 * D + FF : 9 * D + FF]
    gathered = lax.all_gather(matrices.astype(jnp.bfloat16), "dp", axis=1, tiled=True)[0]
    w_qkv, w_out, w_up, w_down = unpack_blocks(gathered, heads_here, row_blocks, hidden_blocks)
    normed_one, unit_one, inverse_one = layer_norm(block_input, gain_one, shift_one)
    normed_two, unit_two, inverse_two = layer_norm(block_input, gain_two, shift_two)
    grad_own = cotangent.astype(jnp.bfloat16)
    norm_one, norm_two, grad_rows = (
        lax.all_gather(normed_one.astype(jnp.bfloat16), ("heads", "tensor"), axis=0, tiled=True),
        lax.all_gather(normed_two.astype(jnp.bfloat16), ("heads", "tensor"), axis=0, tiled=True),
        lax.all_gather(grad_own, ("heads", "tensor"), axis=0, tiled=True),
    )
    norm_one3 = norm_one.reshape(tokens_here, row_blocks, HD)
    norm_two3 = norm_two.reshape(tokens_here, row_blocks, HD)
    projected = (
        jnp.einsum("tbr,hqbrc->thqc", norm_one3, w_qkv, preferred_element_type=jnp.float32)
        + bias_qkv
    )
    shaped = projected.reshape(seq_count, LEN, heads_here, 3, HD)
    cosine, sine = angles(segments)
    queries = rotate(shaped[:, :, :, 0], cosine, sine).astype(jnp.bfloat16)
    keys_rot = rotate(shaped[:, :, :, 1], cosine, sine).astype(jnp.bfloat16)
    values = shaped[:, :, :, 2].astype(jnp.bfloat16)
    attended, log_total = lax.map(seq_forward, (queries, keys_rot, values, segments))
    attend_low = attended.astype(jnp.bfloat16).reshape(tokens_here, heads_here, HD)
    pre_act = (
        jnp.einsum("tbr,kbrc->tkc", norm_two3, w_up, preferred_element_type=jnp.float32).reshape(
            tokens_here, hidden_here
        )
        + bias_up
    )
    act_low = gelu_exact(pre_act).astype(jnp.bfloat16)
    rows_act = act_low.reshape(lax.axis_size(("heads", "tensor")) * own_rows, hidden_blocks, HD)
    first_term = jnp.einsum("thr,hbrc->tbc", attend_low, w_out, preferred_element_type=jnp.float32)
    second_term = jnp.einsum("tkr,kbrc->tbc", rows_act, w_down, preferred_element_type=jnp.float32)
    summed = lax.psum_scatter(
        (first_term + second_term).reshape(lax.axis_size(("heads", "tensor")) * own_rows, D),
        ("heads", "tensor"),
        scatter_dimension=0,
        tiled=True,
    )
    output = block_input + summed + bias_out + bias_down
    regathered = lax.all_gather(matrices.astype(jnp.bfloat16), "dp", axis=1, tiled=True)[0]
    w_qkv, w_out, w_up, w_down = unpack_blocks(regathered, heads_here, row_blocks, hidden_blocks)
    grad_rows3 = grad_rows.reshape(tokens_here, row_blocks, HD)
    act_low3 = act_low.reshape(tokens_here, hidden_blocks, HD)
    grad_act = jnp.einsum(
        "tbc,kbrc->tkr", grad_rows3, w_down, preferred_element_type=jnp.float32
    ).reshape(tokens_here, hidden_here)
    gelu_pull = jax.vjp(gelu_exact, pre_act)[1]
    grad_pre = gelu_pull(grad_act)[0].astype(jnp.bfloat16)
    grad_pre3 = grad_pre.reshape(tokens_here, hidden_blocks, HD)
    grad_attend = jnp.einsum(
        "tbc,hbrc->thr", grad_rows3, w_out, preferred_element_type=jnp.float32
    ).astype(jnp.bfloat16)
    grad_attend = grad_attend.reshape(seq_count, LEN, heads_here, HD)
    grad_queries, grad_keys, grad_values = lax.map(
        seq_backward, (queries, keys_rot, values, segments, log_total, grad_attend)
    )
    grad_raw = jnp.stack(
        [rotate(grad_queries, cosine, -sine), rotate(grad_keys, cosine, -sine), grad_values], axis=3
    )
    grad_raw = grad_raw.astype(jnp.bfloat16).reshape(tokens_here, heads_here, 3, HD)
    rows_up = grad_pre.reshape(lax.axis_size(("heads", "tensor")) * own_rows, hidden_blocks, HD)
    back_one = jnp.einsum(
        "thqc,hqbrc->tbr", grad_raw, w_qkv, preferred_element_type=jnp.float32
    ).reshape(lax.axis_size(("heads", "tensor")) * own_rows, D)
    back_two = jnp.einsum(
        "tkc,kbrc->tbr", rows_up, w_up, preferred_element_type=jnp.float32
    ).reshape(lax.axis_size(("heads", "tensor")) * own_rows, D)
    grad_norms = lax.psum_scatter(
        jnp.stack([back_one, back_two], axis=1),
        ("heads", "tensor"),
        scatter_dimension=0,
        tiled=True,
    )
    grad_norm_one = grad_norms[:, 0]
    grad_norm_two = grad_norms[:, 1]
    grad_input = (
        cotangent
        + norm_back(grad_norm_one, unit_one, inverse_one, gain_one)
        + norm_back(grad_norm_two, unit_two, inverse_two, gain_two)
    )
    grad_bias_rows = jnp.sum(grad_own, axis=0, dtype=jnp.float32)
    pieces = jnp.concatenate(
        [
            jnp.sum(grad_norm_one * unit_one, axis=0),
            jnp.sum(grad_norm_one, axis=0),
            jnp.sum(grad_norm_two * unit_two, axis=0),
            jnp.sum(grad_norm_two, axis=0),
            jnp.zeros((3 * D,), jnp.float32),
            grad_bias_rows,
            jnp.zeros((FF,), jnp.float32),
            grad_bias_rows,
        ]
    )
    pieces = lax.dynamic_update_slice_in_dim(
        pieces, jnp.sum(grad_raw, axis=0, dtype=jnp.float32).reshape(-1), qkv_offset, 0
    )
    pieces = lax.dynamic_update_slice_in_dim(
        pieces, jnp.sum(grad_pre, axis=0, dtype=jnp.float32), up_offset, 0
    )
    grad_vectors = lax.psum(pieces, ("dp", "heads", "tensor"))
    grad_down = jnp.einsum(
        "tkr,tbc->kbrc", act_low3, grad_rows3, preferred_element_type=jnp.float32
    )
    grad_up = jnp.einsum("tbr,tkc->kbrc", norm_two3, grad_pre3, preferred_element_type=jnp.float32)
    grad_out = jnp.einsum(
        "thr,tbc->hbrc", attend_low, grad_rows3, preferred_element_type=jnp.float32
    )
    grad_qkv = jnp.einsum(
        "tbr,thqc->hqbrc", norm_one3, grad_raw, preferred_element_type=jnp.float32
    )
    attn_grads = jnp.concatenate([grad_qkv, grad_out[:, None]], axis=1).reshape(-1, HD, HD)
    all_grads = jnp.concatenate(
        [attn_grads, grad_up.reshape(-1, HD, HD), grad_down.reshape(-1, HD, HD)], axis=0
    )[None]
    owned = lax.psum_scatter(all_grads, "dp", scatter_dimension=1, tiled=True)
    blocks = [a[0] for a in (matrices, first_moment, second_moment, left_stat, right_stat, left_basis, right_basis)]
    updated = [u[None] for u in soap_part(jnp.zeros((1,), jnp.int32), owned[0], blocks, None)]
    new_vectors, new_vec_first, new_vec_second = adam_vector(
        grad_vectors, vectors, vec_first, vec_second
    )
    return (
        output,
        grad_input,
        updated[0],
        updated[1],
        updated[2],
        updated[3],
        updated[4],
        updated[5],
        updated[6],
        updated[7],
        new_vectors,
        new_vec_first,
        new_vec_second,
    )


def solution(mesh):
    in_specs = (
        P(("dp", "heads", "tensor"), None),
        P(("dp", "heads", "tensor"), None),
        P("dp", None),
        P(("heads", "tensor"), "dp", None, None),
        P(("heads", "tensor"), "dp", None, None),
        P(("heads", "tensor"), "dp", None, None),
        P(("heads", "tensor"), "dp", None, None),
        P(("heads", "tensor"), "dp", None, None),
        P(("heads", "tensor"), "dp", None, None),
        P(("heads", "tensor"), "dp", None, None),
        P(),
        P(),
        P(),
    )
    out_specs = (
        P(("dp", "heads", "tensor"), None),
        P(("dp", "heads", "tensor"), None),
        P(("heads", "tensor"), "dp", None, None),
        P(("heads", "tensor"), "dp", None, None),
        P(("heads", "tensor"), "dp", None, None),
        P(("heads", "tensor"), "dp", None, None),
        P(("heads", "tensor"), "dp", None, None),
        P(("heads", "tensor"), "dp", None, None),
        P(("heads", "tensor"), "dp", None, None),
        P(("heads", "tensor"), "dp", None, None),
        P(),
        P(),
        P(),
    )
    plane = dict(mesh.shape) == {"dp": 8, "heads": 2, "tensor": 2}
    shards = plane_shards if plane else generic_shards
    return jax.shard_map(shards, mesh=mesh, in_specs=in_specs, out_specs=out_specs, check_vma=False)
```

```python
import functools

import jax
import jax.numpy as jnp
from jax import lax
from jax.experimental import pallas as pl
from jax.experimental.pallas import tpu as pltpu
from jax.sharding import PartitionSpec as P

D = 2048
H = 8
HD = 256
RD = 64
FF = 8192
LEN = 1024
STEP = 10


epsilon_norm = 1e-05
epsilon_adam = 1e-08
rope_base = 10000.0
beta_one = 0.9
beta_two = 0.95
beta_stat = 0.95
rate_matrix = 0.05
rate_vector = 0.1
weight_decay = 0.01
PAN = 32
PACK = 16
WIDE = 8
UNROLL = 8
GROUP = 2


def layer_norm(rows, gain, shift):
    middle = jnp.mean(rows, axis=-1, keepdims=True)
    centered = rows - middle
    spread = jnp.mean(centered * centered, axis=-1, keepdims=True)
    inverse = lax.rsqrt(spread + epsilon_norm)
    unit = centered * inverse
    return (unit * gain + shift, unit, inverse)


def norm_back(grad, unit, inverse, gain):
    scaled = grad * gain
    return inverse * (
        scaled
        - jnp.mean(scaled, axis=-1, keepdims=True)
        - unit * jnp.mean(scaled * unit, axis=-1, keepdims=True)
    )


def angles(segments):
    seq_count = segments.shape[0]
    column = jnp.arange(LEN, dtype=jnp.int32)[None, :]
    border = jnp.concatenate(
        [jnp.ones((seq_count, 1), jnp.bool_), segments[:, 1:] != segments[:, :-1]], axis=1
    )
    starts = lax.cummax(jnp.where(border, column, 0), axis=1)
    places = (column - starts).astype(jnp.float32)
    frequency = 1.0 / rope_base ** (jnp.arange(0, RD, 2).astype(jnp.float32) / RD)
    turns = places[:, :, None] * frequency[None, None, :]
    return (jnp.cos(turns)[:, :, None, :], jnp.sin(turns)[:, :, None, :])


def rotate(part, cosine, sine):
    half_dims = RD // 2
    first_half = part[..., :half_dims]
    second_half = part[..., half_dims:RD]
    return jnp.concatenate(
        [
            first_half * cosine - second_half * sine,
            second_half * cosine + first_half * sine,
            part[..., RD:],
        ],
        axis=-1,
    )


def unpack_blocks(blocks, heads_here, row_blocks, hidden_blocks):
    attn_count = heads_here * 4 * row_blocks
    up_count = hidden_blocks * row_blocks
    attn_part = blocks[:attn_count].reshape(heads_here, 4, row_blocks, HD, HD)
    w_up = blocks[attn_count : attn_count + up_count].reshape(hidden_blocks, row_blocks, HD, HD)
    w_down = blocks[attn_count + up_count :].reshape(hidden_blocks, row_blocks, HD, HD)
    return (attn_part[:, :3], attn_part[:, 3], w_up, w_down)


def masked_scores(queries, keys_rot, segment_row):
    column = jnp.arange(LEN)
    allowed = (segment_row[:, None] == segment_row[None, :]) & (column[None, :] <= column[:, None])
    scores = jnp.einsum(
        "qhd,khd->hqk", queries, keys_rot, preferred_element_type=jnp.float32
    ) * HD ** (-0.5)
    return jnp.where(allowed[None], scores, -1e30)


def seq_forward(items):
    queries, keys_rot, values, segment_row = items
    scores = masked_scores(queries, keys_rot, segment_row)
    row_max = jnp.max(scores, axis=-1, keepdims=True)
    powers = jnp.exp(scores - row_max)
    row_total = jnp.sum(powers, axis=-1, keepdims=True)
    probs_low = (powers / row_total).astype(jnp.bfloat16)
    attended = jnp.einsum("hqk,khd->qhd", probs_low, values, preferred_element_type=jnp.float32)
    return (attended, (row_max + jnp.log(row_total))[..., 0])


def seq_backward(items):
    queries, keys_rot, values, segment_row, log_total, grad_attend = items
    scores = masked_scores(queries, keys_rot, segment_row)
    probs = jnp.exp(scores - log_total[..., None])
    grad_probs = jnp.einsum("qhd,khd->hqk", grad_attend, values, preferred_element_type=jnp.float32)
    inner = jnp.sum(probs * grad_probs, axis=-1, keepdims=True)
    grad_scores = (probs * (grad_probs - inner)).astype(jnp.bfloat16)
    grad_queries = jnp.einsum(
        "hqk,khd->qhd", grad_scores, keys_rot, preferred_element_type=jnp.float32
    ) * HD ** (-0.5)
    grad_keys = jnp.einsum(
        "hqk,qhd->khd", grad_scores, queries, preferred_element_type=jnp.float32
    ) * HD ** (-0.5)
    grad_values = jnp.einsum(
        "hqk,qhd->khd", probs.astype(jnp.bfloat16), grad_attend, preferred_element_type=jnp.float32
    )
    return (grad_queries, grad_keys, grad_values)


def gelu_exact(inputs):
    return jax.nn.gelu(inputs, approximate=False)


def dot_nn(a, b):
    return lax.dot_general(a, b, (((1,), (0,)), ((), ())), preferred_element_type=jnp.float32)


def dot_nt(a, b):
    return lax.dot_general(a, b, (((1,), (1,)), ((), ())), preferred_element_type=jnp.float32)


def dot_tn(a, b):
    return lax.dot_general(a, b, (((0,), (0,)), ((), ())), preferred_element_type=jnp.float32)


def split(x):
    high = x.astype(jnp.bfloat16)
    return high, (x - high.astype(jnp.float32)).astype(jnp.bfloat16)


def three(dot, a, b):
    return dot(a[0], b[0]) + (dot(a[0], b[1]) + dot(a[1], b[0]))


def eliminate(diag):
    tiles = PAN * PACK // 128
    per = 128 // PACK
    flat = diag[...].T[:PAN]
    full = [flat[:, t * 128 : (t + 1) * 128] for t in range(tiles)]
    row = lax.broadcasted_iota(jnp.int32, (PAN, 128), 0)
    lane = lax.broadcasted_iota(jnp.int32, (PAN, 128), 1)
    inverse = [jnp.where(row == lane // PACK + t * per, 1.0, 0.0) for t in range(tiles)]

    def column(k):
        return jnp.take_along_axis(full[k // per], lane % PACK + k % per * PACK, axis=1)

    for k in range(0, PAN, WIDE):
        columns, scales, crosses = [column(k + i) for i in range(WIDE)], [], []
        for i in range(WIDE):
            for j in range(i):
                columns[i] = columns[i] - columns[j] * crosses[j][i]
            scales.append(lax.rsqrt(columns[i][k + i : k + i + 1]))
            columns[i] = columns[i] * scales[i]
            crosses.append([columns[i][k + n : k + n + 1] for n in range(WIDE)])
        columns = [jnp.where(row >= k + WIDE, c, 0.0) for c in columns]

        def step(tile):
            tops = []
            for i in range(WIDE):
                top = tile[k + i : k + i + 1]
                for j in range(i):
                    top = top - crosses[j][i] * tops[j]
                tops.append(top * scales[i])
            for c, top in zip(columns, tops):
                tile = tile - c * top
            return tops, tile

        for t in range(tiles):
            if (t + 1) * per > k + WIDE:
                full[t] = step(full[t])[1]
            if t * per < k + WIDE:
                tops, tile = step(inverse[t])
                for i, top in enumerate(tops):
                    tile = jnp.where(row == k + i, top, tile)
                inverse[t] = tile
    diag[:, :PAN] = jnp.concatenate(inverse, axis=1).T


def soap_kernel(count, g, w, f, s, ls, rs, lb, rb, ow, owl, of, os, ols, ors, olb, orb, aug, diag):
    step = pl.program_id(0)
    mats = 2 * count
    unroll = UNROLL if mats % UNROLL == 0 else 4
    blocks = range(GROUP)
    grad = [g[i].astype(jnp.bfloat16) for i in blocks]
    left, right = [split(lb[i]) for i in blocks], [split(rb[i]) for i in blocks]
    left_t = [(x.T, y.T) for x, y in left]
    right_t = [(x.T, y.T) for x, y in right]
    grad_t = [x.T for x in grad]
    lnew = [beta_stat * ls[i] + (1.0 - beta_stat) * dot_nn(grad[i], grad_t[i]) for i in blocks]
    rnew = [beta_stat * rs[i] + (1.0 - beta_stat) * dot_nn(grad_t[i], grad[i]) for i in blocks]
    turned = [dot_nn(left_t[i][0], grad[i]) + dot_nn(left_t[i][1], grad[i]) for i in blocks]
    for i in blocks:
        ols[i] = lnew[i]
        ors[i] = rnew[i]
    turned = [three(dot_nn, split(turned[i]), right[i]) for i in blocks]
    sides = [
        three(dot_nn, basis_t, split(stat))
        for i in blocks
        for basis_t, stat in ((left_t[i], lnew[i]), (right_t[i], rnew[i]))
    ]
    first_new = [beta_one * f[i] + (1.0 - beta_one) * turned[i] for i in blocks]
    second_new = [beta_two * s[i] + (1.0 - beta_two) * turned[i] * turned[i] for i in blocks]
    direction = [
        x / (1.0 - beta_one**STEP) / (jnp.sqrt(y / (1.0 - beta_two**STEP)) + epsilon_adam)
        for x, y in zip(first_new, second_new)
    ]
    for i in blocks:
        of[i] = first_new[i]
        os[i] = second_new[i]
    stepped = [three(dot_nn, left[i], split(direction[i])) for i in blocks]
    for i, side in enumerate(sides):
        aug[2 * GROUP * step + i, :, HD:] = side
    grams = [three(dot_nt, x, x) for x in map(split, sides)]
    stepped = [three(dot_nn, split(stepped[i]), right_t[i]) for i in blocks]
    for i, gram in enumerate(grams):
        aug[2 * GROUP * step + i, :, :HD] = gram
    for i in blocks:
        weight = w[i]
        weight_new = weight - rate_matrix * (stepped[i] + weight_decay * weight)
        ow[i] = weight_new
        owl[i] = weight_new.astype(jnp.bfloat16)

    @pl.when(step == count // GROUP - 1)
    def _():
        half = HD // 2

        def place(p, i):
            low = pl.multiple_of(p * PAN, PAN)
            base = pl.multiple_of(p // 4 * 128, 128)
            for u in range(unroll):
                m = i * unroll + u
                own = aug[m, pl.ds(low, PAN), pl.ds(base, 128)]
                diag[pl.ds(m, PAN, stride=PACK), :] = pltpu.roll(own, (128 - p % 4 * PAN) % 128, 1)

        def update(p, i, late):
            low = pl.multiple_of(p * PAN, PAN)
            edge = half if late else 0
            start = edge + PAN
            mine = [i * unroll + u for u in range(unroll)]
            factors = [split(diag[pl.ds(m, PAN, stride=PACK), :][:, :PAN]) for m in mine]
            panels = [split(aug[m, pl.ds(low, PAN), edge:]) for m in mine]
            panels = [three(dot_tn, x, y) for x, y in zip(factors, panels)]
            lane = lax.broadcasted_iota(jnp.int32, (PAN, HD - edge), 1) + edge
            heads = [split(jnp.where(lane >= low + PAN, panel[:, : HD - edge], 0.0)) for panel in panels]
            parts = [split(panel) for panel in panels]
            lhs = [jnp.concatenate([x, x, y], axis=0).T for x, y in heads]
            rhs = [jnp.concatenate([x, y, x], axis=0) for x, y in parts]
            rest = [aug[m, start:, edge:] - dot_nn(x[PAN:], y) for m, x, y in zip(mine, lhs, rhs)]
            for m, panel, left in zip(mine, panels, rest):
                aug[m, start:, edge:] = left
                aug[m, pl.ds(low, PAN), HD:] = panel[:, HD - edge :]

        def panel_step(p, carry):
            lax.fori_loop(0, mats // unroll, lambda i, n: (place(p, i), n)[1], 0)
            eliminate(diag)

            @pl.when(p < 4)
            def _():
                lax.fori_loop(0, mats // unroll, lambda i, n: (update(p, i, False), n)[1], 0)

            @pl.when(p >= 4)
            def _():
                lax.fori_loop(0, mats // unroll, lambda i, n: (update(p, i, True), n)[1], 0)

            return carry

        lax.fori_loop(0, HD // PAN, panel_step, 0)

        def finish(b, carry):
            for side, out in enumerate((olb, orb)):
                out[b] = aug[2 * b + side, :, HD:].T
            return carry

        lax.fori_loop(0, count, finish, 0)


LIMIT = 56 * 2**20
SHRINK = 1


def cost(flops, moved, trans=0):
    return pl.CostEstimate(flops=int(flops) // SHRINK, bytes_accessed=int(moved) // SHRINK, transcendentals=0)


def turn(rows, cosine, sine):
    head = rows[:, :128]
    lane = lax.broadcasted_iota(jnp.int32, head.shape, 1)
    partner = jnp.where(lane < RD // 2, pltpu.roll(head, 128 - RD // 2, 1), pltpu.roll(head, RD // 2, 1))
    return jnp.concatenate([head * cosine + partner * sine, rows[:, 128:]], axis=1)


MESH = pl.DeviceIdType.MESH
LAST = 9
RIGHT = (
    {0: 0, 1: 3, 2: 6},
    {0: 1, 1: 4, 2: 3},
    {0: 2, 1: 0, 2: 4},
    {1: 1, 2: 0},
    {1: 2, 2: 1},
    {1: 5, 2: 2},
    {2: 7},
    {2: 8},
    {2: 5},
)
LEFT = (
    {3: 9, 2: 6, 1: 3},
    {3: 10, 2: 9, 1: 6},
    {3: 11, 2: 10, 1: 9},
    {2: 7, 1: 4},
    {2: 11, 1: 10},
    {2: 8, 1: 7},
    {1: 11},
    {1: 8},
    {1: 5},
)
SWAPS = ((3, 9), (4, 0), (10, 10), (11, 7))
ROLES = {
    "q": (0, 1),
    "k": (1, 2),
    "v": (2, 12),
    "out": (13, 13),
    "up": ((6, 3), (7, 8), (8, 4), (5, 5)),
    "down": ((9, 6), (12, 11), (14, 14), (15, 15)),
}


def layer_kernel(
    rows_in, cotangent, segs, matrices, vectors, waves,
    held, units_out, grads_out, sum_0, sum_1, sum_2, extra, rows_out, sums, biases,
    units, grads, weight, act, pre, flipped, column, q, k, v, ga, att, dq, dk, dv, kseq, vseq, keys, vals, stage,
    raw, lines, cosine, sine, seg_row, seg_col,
    right_send, right_recv, left_send, left_recv, swap_send, swap_recv, row_send, row_recv, local,
):
    d, y, c = lax.axis_index("dp"), lax.axis_index("heads"), lax.axis_index("tensor")
    z, x = d // 2, d % 2
    by_x, by_y, by_core = {"dp": d + 1 - 2 * x}, {"heads": 1 - y}, {"tensor": 1 - c}
    shard = 2 * y + c
    block = rows_in.shape[0]
    tokens = units.shape[0]
    head = 32 + (shard * 2 + x) * 3

    barrier = pltpu.get_barrier_semaphore()
    for near in (by_x, by_y, by_core):
        pl.semaphore_signal(barrier, inc=1, device_id=near, device_id_type=MESH)

    @pl.when(z < 3)
    def _():
        pl.semaphore_signal(barrier, inc=1, device_id={"dp": d + 2}, device_id_type=MESH)

    @pl.when(z > 0)
    def _():
        pl.semaphore_signal(barrier, inc=1, device_id={"dp": d - 2}, device_id_type=MESH)

    pl.semaphore_wait(barrier, 4 + (z + 1) // 2 % 2)

    def remote(source, target, send, recv, device):
        return pltpu.make_async_remote_copy(
            src_ref=source, dst_ref=target, send_sem=send, recv_sem=recv, device_id=device, device_id_type=MESH
        )

    def hop(table, step, half, sends, recvs, shift, at):
        place, part, sem = table[step][at], pl.ds(half * 4, 4), 2 * step + half
        source = weight.at[0, part] if step == 0 else held.at[place, part]
        return remote(source, held.at[place, part], sends.at[sem], recvs.at[sem], {"dp": d + 2 * shift})

    ways = ((RIGHT, right_send, right_recv, 1), (LEFT, left_send, left_recv, -1))

    def start(step, half):
        for table, sends, recvs, shift in ways:
            for at in table[step]:

                @pl.when(z == at)
                def _():
                    hop(table, step, half, sends, recvs, shift, at).start()

    def arrived(step, half):
        for table, sends, recvs, shift in ways:
            for at in table[step]:

                @pl.when(z == at + shift)
                def _():
                    hop(table, step, half, sends, recvs, shift, at).wait_recv()

    def sent(step):
        for table, sends, recvs, shift in ways:
            for at in table[step]:

                @pl.when(z == at)
                def _():
                    for half in range(2):
                        hop(table, step, half, sends, recvs, shift, at).wait_send()

    def pass_on(step, half):
        arrived(step, half)
        if step + 1 < LAST:
            start(step + 1, half)

    def pump(step):
        pass_on(step, 0)
        pass_on(step, 1)

    def swap(i, side):
        return remote(held.at[SWAPS[i][side]], held.at[12 + i], swap_send.at[i], swap_recv.at[i], by_x)

    def start_swap(i):
        for side in range(2):

            @pl.when(x == side)
            def _():
                swap(i, side).start()

    def fetch(role, slot):
        for side in range(2):

            @pl.when(x == side)
            def _():
                pltpu.make_async_copy(held.at[role[side]], weight.at[slot], local.at[slot]).start()

    def fetched(slot):
        pltpu.make_async_copy(held.at[0], weight.at[slot], local.at[slot]).wait()

    def load(j, at):
        def begin(which):
            pltpu.make_async_copy(matrices.at[0, which * 8 : which * 8 + 8], raw.at[at], local.at[at]).start()

        pl.when((d < 5) | (d == 7))(lambda: begin(j))
        pl.when(d == 5)(lambda: begin(2 - j))
        pl.when(d == 6)(lambda: begin((j + 2) % 3))

    def loaded(j, at):
        pltpu.make_async_copy(matrices.at[0, :8], raw.at[at], local.at[at]).wait()
        weight[j] = raw[at].astype(jnp.bfloat16)

    def keep_own(j):
        for at in range(4):

            @pl.when(z == at)
            def _():
                pltpu.make_async_copy(weight.at[j], held.at[3 * at + j], local.at[8 + j]).start()

    load(0, 0)
    load(1, 1)
    loaded(0, 0)
    start(0, 0)
    start(0, 1)
    load(2, 0)
    keep_own(0)
    rows = rows_in[...]
    centered = rows - jnp.mean(rows, axis=-1, keepdims=True)
    inverse = lax.rsqrt(jnp.mean(centered * centered, axis=-1, keepdims=True) + epsilon_norm)
    units[:block, :] = (centered * inverse).astype(jnp.bfloat16)
    grads[:block, :] = cotangent[...].astype(jnp.bfloat16)
    seg_row[x] = segs[...].astype(jnp.float32)

    def send_rows(kind, i, low, high, there, device):
        array = (units, grads)[kind]
        at = kind * 8 + i
        return remote(
            array.at[low:high], array.at[there : there + high - low], row_send.at[at], row_recv.at[at], device
        )

    half = block // 2

    def row_plan(kind):
        return (
            send_rows(kind, 0, 0, block, block, by_x),
            send_rows(kind, 1, 0, block, 2 * block, by_y),
            send_rows(kind, 2, block, block + half, 3 * block, by_y),
            send_rows(kind, 3, 2 * block + half, 3 * block, 3 * block + half, by_x),
            send_rows(kind, 4, 0, block, 4 * block, by_core),
            send_rows(kind, 5, block, 2 * block, 5 * block, by_core),
            send_rows(kind, 6, 2 * block, 3 * block, 6 * block, by_core),
            send_rows(kind, 7, 3 * block, 4 * block, 7 * block, by_core),
        )

    plans = [row_plan(kind) for kind in range(2)]
    for plan in plans:
        plan[0].start()
        plan[1].start()
        plan[4].start()
    segments = remote(seg_row.at[x], seg_row.at[x], swap_send.at[5], swap_recv.at[5], by_x)
    segments.start()
    loaded(1, 1)
    keep_own(1)
    loaded(2, 0)
    keep_own(2)
    for j in range(3):
        pltpu.make_async_copy(weight.at[j], held.at[j], local.at[8 + j]).wait()
    for i in range(4):
        lines[i : i + 1, :] = jnp.concatenate([vectors[8 * i + b : 8 * i + b + 1, :] for b in range(8)], axis=1)
    pump(0)
    segments.wait()
    for s in range(tokens // LEN):
        row = seg_row[s]
        wide = jnp.broadcast_to(row, (128, LEN)).T
        seg_col[s] = wide
        lane = lax.broadcasted_iota(jnp.int32, (LEN, 128), 1)
        token = lax.broadcasted_iota(jnp.int32, (LEN, 128), 0).astype(jnp.float32)
        first = jnp.sum(jnp.where(row < wide[:, 0:1], 1.0, 0.0), axis=1, keepdims=True)
        turns = (token - first) * waves[...]
        here = slice(s * LEN, (s + 1) * LEN)
        cosine[here, :] = jnp.where(lane < RD, jnp.cos(turns), 1.0)
        flips = jnp.where(lane < RD // 2, -1.0, jnp.where(lane < RD, 1.0, 0.0))
        sine[here, :] = jnp.sin(turns) * flips
    for plan in plans:
        plan[0].wait_recv()
        plan[2].start()
        plan[5].start()
        plan[1].wait_recv()
        plan[3].start()
        plan[6].start()
    pump(1)
    for plan in plans:
        plan[2].wait_recv()
        plan[3].wait_recv()
        plan[7].start()
    pump(2)
    start_swap(0)
    sent(0)
    fetch(ROLES["up"][0], 0)
    fetch(ROLES["down"][0], 1)
    for plan in plans:
        for i in range(4, 8):
            plan[i].wait_recv()
        for i in range(8):
            plan[i].wait_send()
    keep = [pltpu.make_async_copy(units, units_out, local.at[6]), pltpu.make_async_copy(grads, grads_out, local.at[7])]
    for copy in keep:
        copy.start()

    tile = 512

    def run_mlp(slot):
        hidden = SLOTS[0][slot] + (SLOTS[1][slot] - SLOTS[0][slot]) * x
        wu, wd = weight.at[0], weight.at[1]

        def body(i, carry):
            here = pl.ds(pl.multiple_of(i * tile, tile), tile)
            norm = (units[here, :].astype(jnp.float32) * lines[2:3, :] + lines[3:4, :]).astype(jnp.bfloat16)
            inner = dot_nn(norm, wu[...].reshape(D, HD)) + vectors[pl.ds(64 + shard * 8 + hidden, 1), :]
            pull = dot_nt(grads[here, :HD], wd[0])
            for b in range(1, D // HD):
                pull = pull + dot_nt(grads[here, b * HD : (b + 1) * HD], wd[b])
            share = 0.5 + 0.5 * lax.erf(inner * (0.5**0.5))
            act[here, :] = (inner * share).astype(jnp.bfloat16)
            slope = share + inner * jnp.exp(-0.5 * inner * inner) * ((2.0 * 3.141592653589793) ** (-0.5))
            pre[here, :] = (slope * pull).astype(jnp.bfloat16)
            return carry

        lax.fori_loop(0, tokens // tile, body, 0)

    def save_rows(source, i):
        copy = pltpu.make_async_copy(source, rows_out.at[i], local.at[8 + i])
        copy.start()
        return copy

    def put(i, to_0, to_1, sem):
        for side, target in ((0, to_0), (1, to_1)):
            if target is not None:

                @pl.when(x == side)
                def _():
                    pltpu.make_async_copy(stage.at[i], target, local.at[16 + sem]).start()

        def finish():
            for side, target in ((0, to_0), (1, to_1)):
                if target is not None:

                    @pl.when(x == side)
                    def _():
                        pltpu.make_async_copy(stage.at[i], target, local.at[16 + sem]).wait()

        return finish

    def run_down(source, at):
        flipped[:HD, :] = source[...].T

        def body(b, carry):
            here = pl.ds(pl.multiple_of(b * HD, HD), HD)
            stage[at, b] = dot_nn(flipped[:HD, :], grads[:, here]).astype(jnp.bfloat16)
            return carry

        lax.fori_loop(0, D // HD, body, 0)

    def run_up(sources, places, slots, gain, row, offset, more=False):
        for i, source in enumerate(sources):
            wide = source[...]
            flipped[i * HD : (i + 1) * HD, :] = wide.T
            total = jnp.sum(wide.astype(jnp.float32), axis=0, keepdims=True)
            biases[:, offset + i * HD : offset + (i + 1) * HD] = total
            column[i] = jnp.broadcast_to(total, (128, HD)).T

        def body(b, carry):
            here = pl.ds(pl.multiple_of(b * HD, HD), HD)
            gains, shifts = (sums[row : row + 1, here], sums[row + 1 : row + 2, here]) if more else (0.0, 0.0)
            for i, (place, slot) in enumerate(zip(places, slots)):
                turned = dot_nn(flipped[i * HD : (i + 1) * HD, :], units[:, here])
                w = weight[slot, b].T.astype(jnp.float32)
                bias = column[i][:, 0:1]
                gains = gains + jnp.sum(w * turned, axis=0, keepdims=True)
                shifts = shifts + jnp.sum(w * bias, axis=0, keepdims=True)
                result = turned * lines[gain : gain + 1, here] + bias * lines[gain + 1 : gain + 2, here]
                stage[place, b] = result.T.astype(jnp.bfloat16)
            sums[row : row + 1, here] = gains
            sums[row + 1 : row + 2, here] = shifts
            return carry

        lax.fori_loop(0, D // HD, body, 0)

    fetched(0)
    fetched(1)
    run_mlp(0)
    saves = [save_rows(act, 0), save_rows(pre, 1)]
    pass_on(3, 0)
    run_down(act, 0)
    done = put(0, sum_0.at[3], sum_0.at[2], 0)
    pass_on(3, 1)
    start_swap(1)
    run_up([pre], [1], [0], 2, 2, 3 * HD)
    done_up = put(1, sum_0.at[2], sum_0.at[1], 1)
    pump(4)
    start_swap(2)
    pump(5)

    swap(0, 0).wait_recv()
    swap(1, 0).wait_recv()
    for i, role in enumerate(("q", "k", "v", "out")):
        fetch(ROLES[role], 2 + i)
    for i in range(4):
        fetched(2 + i)

    def project_rows(i, carry):
        here = pl.ds(pl.multiple_of(i * tile, tile), tile)
        turns = []
        for u in range(tile // block):
            r = i * (tile // block) + u
            a = (((x + r % 2) % 2) * 2 + (y + r // 2 % 2) % 2) * 2 + (c + r // 4) % 2
            turns.append(pl.ds(pl.multiple_of(a * block, block), block))
        cos_here = jnp.concatenate([cosine[t, :] for t in turns], axis=0)
        sin_here = jnp.concatenate([sine[t, :] for t in turns], axis=0)
        norm = (units[here, :].astype(jnp.float32) * lines[0:1, :] + lines[1:2, :]).astype(jnp.bfloat16)
        q[here, :] = turn(
            dot_nn(norm, weight[2].reshape(D, HD)) + vectors[pl.ds(head + 0, 1), :], cos_here, sin_here
        ).astype(jnp.bfloat16)
        k[here, :] = turn(
            dot_nn(norm, weight[3].reshape(D, HD)) + vectors[pl.ds(head + 1, 1), :], cos_here, sin_here
        ).astype(jnp.bfloat16)
        v[here, :] = (dot_nn(norm, weight[4].reshape(D, HD)) + vectors[pl.ds(head + 2, 1), :]).astype(jnp.bfloat16)
        total = dot_nt(grads[here, :HD], weight[5, 0])
        for b in range(1, D // HD):
            total = total + dot_nt(grads[here, b * HD : (b + 1) * HD], weight[5, b])
        ga[here, :] = total.astype(jnp.bfloat16)
        return carry

    lax.fori_loop(0, tokens // tile, project_rows, 0)
    pass_on(6, 0)
    pieces = LEN // block

    def attend(s, carry):
        scale = HD ** (-0.5)
        spots = []
        for i in range(pieces):
            a = s * pieces + i
            r = ((c + a % 2) % 2) * 4 + (x + a // 4) % 2 + 2 * ((y + a // 2 % 2) % 2)
            spots.append(pl.ds(pl.multiple_of(r * block, block), block))
        for i in range(pieces):
            kseq[i * block : (i + 1) * block, :] = k[spots[i], :]
            vseq[i * block : (i + 1) * block, :] = v[spots[i], :]
        keys[...] = jnp.zeros_like(keys)
        vals[...] = jnp.zeros_like(vals)
        for i in range(pieces):
            upto = (i + 1) * block
            angle = pl.ds(pl.multiple_of(s * LEN + i * block, block), block)
            mine, pulled = q[spots[i], :], ga[spots[i], :]
            scores = dot_nt(mine, kseq[:upto, :]) * scale
            to = lax.broadcasted_iota(jnp.int32, (block, upto), 0) + i * block
            of = lax.broadcasted_iota(jnp.int32, (block, upto), 1)
            allowed = (seg_col[s, i * block : upto, 0:1] == seg_row[s, :, :upto]) & (of <= to)
            scores = jnp.where(allowed, scores, -1e30)
            powers = jnp.exp(scores - jnp.max(scores, axis=-1, keepdims=True))
            probs = powers / jnp.sum(powers, axis=-1, keepdims=True)
            low = probs.astype(jnp.bfloat16)
            att[spots[i], :] = dot_nn(low, vseq[:upto, :]).astype(jnp.bfloat16)
            pull = dot_nt(pulled, vseq[:upto, :])
            inner = jnp.sum(probs * pull, axis=-1, keepdims=True)
            gs = (probs * (pull - inner)).astype(jnp.bfloat16)
            turned = turn(dot_nn(gs, kseq[:upto, :]) * scale, cosine[angle, :], -sine[angle, :])
            dq[spots[i], :] = turned.astype(jnp.bfloat16)
            keys[:upto, :] = keys[:upto, :] + dot_tn(gs, mine)
            vals[:upto, :] = vals[:upto, :] + dot_tn(low, pulled)
        for i in range(pieces):
            here = slice(i * block, (i + 1) * block)
            angle = pl.ds(pl.multiple_of(s * LEN + i * block, block), block)
            turned = turn(keys[here, :] * scale, cosine[angle, :], -sine[angle, :])
            dk[spots[i], :] = turned.astype(jnp.bfloat16)
            dv[spots[i], :] = vals[here, :].astype(jnp.bfloat16)

        @pl.when(s == 0)
        def _():
            pass_on(6, 1)

        return carry

    lax.fori_loop(0, tokens // LEN, attend, 0)
    start_swap(3)
    for copy in saves:
        copy.wait()
    saves = [save_rows(a, 4 + i) for i, a in enumerate((att, dq, dk, dv))]
    run_up([dv], [4], [4], 0, 0, 2 * HD, False)

    back_v = remote(stage.at[4], sum_0.at[1], swap_send.at[6], swap_recv.at[6], by_x)
    pl.when(x == 1)(back_v.start)
    done_v = put(4, sum_2.at[0], None, 4)
    pass_on(7, 0)
    done()
    run_down(att, 0)
    done = put(0, None, extra, 5)
    back_out = remote(stage.at[0], sum_1.at[0], swap_send.at[4], swap_recv.at[4], by_x)
    pl.when(x == 0)(back_out.start)
    run_up([dq, dk], [2, 3], [2, 3], 0, 0, 0, True)
    done_qk = [put(2, sum_1.at[0], sum_0.at[0], 2), put(3, sum_0.at[0], sum_2.at[0], 3)]
    pass_on(7, 1)
    fetch(ROLES["up"][1], 0)
    fetch(ROLES["down"][1], 1)

    fetched(0)
    fetched(1)
    run_mlp(1)
    saves += [save_rows(act, 2), save_rows(pre, 3)]
    done_up()
    run_down(act, 1)
    done_up = put(1, extra, sum_0.at[3], 6)
    pl.when(x == 0)(back_v.wait_recv)
    pl.when(x == 1)(back_v.wait_send)
    pl.when(x == 1)(back_out.wait_recv)
    pl.when(x == 0)(back_out.wait_send)
    arrived(8, 0)
    arrived(8, 1)
    for step in range(1, LAST):
        sent(step)
    for i in range(4):
        swap(i, 0).wait_send()
    for i in range(2, 4):
        swap(i, 0).wait_recv()
    for copy in saves + keep:
        copy.wait()
    for finish in done_qk + [done_v, done, done_up]:
        finish()


def layer(rows, cotangent, segments, matrices, vectors, waves):
    block = rows.shape[0]
    tokens = 8 * block
    count = tokens // LEN
    anywhere, near = pl.BlockSpec(memory_space=pl.ANY), pl.BlockSpec(memory_space=pltpu.VMEM)
    low, full = jnp.bfloat16, jnp.float32
    group = (D // HD, HD, HD)
    narrow = pltpu.VMEM((tokens, HD), low)
    return pl.pallas_call(
        layer_kernel,
        in_specs=[near] * 3 + [anywhere] + [near] * 2,
        out_specs=[anywhere] * 8 + [near] * 2,
        out_shape=[
            jax.ShapeDtypeStruct((16,) + group, low),
            jax.ShapeDtypeStruct((tokens, D), low),
            jax.ShapeDtypeStruct((tokens, D), low),
        ]
        + [jax.ShapeDtypeStruct((4,) + group, low)] * 3
        + [
            jax.ShapeDtypeStruct(group, low),
            jax.ShapeDtypeStruct((8, tokens, HD), low),
            jax.ShapeDtypeStruct((4, D), full),
            jax.ShapeDtypeStruct((1, 4 * HD), full),
        ],
        scratch_shapes=[
            pltpu.VMEM((tokens, D), low),
            pltpu.VMEM((tokens, D), low),
            pltpu.VMEM((6,) + group, low),
            narrow,
            narrow,
            pltpu.VMEM((3 * HD, tokens), low),
            pltpu.VMEM((3, HD, 128), full),
        ]
        + [narrow] * 8
        + [pltpu.VMEM((LEN, HD), low)] * 2
        + [pltpu.VMEM((LEN, HD), full)] * 2
        + [
            pltpu.VMEM((5,) + group, low),
            pltpu.VMEM((2,) + group, full),
            pltpu.VMEM((4, D), full),
            pltpu.VMEM((tokens, 128), full),
            pltpu.VMEM((tokens, 128), full),
            pltpu.VMEM((count, 1, LEN), full),
            pltpu.VMEM((count, LEN, 128), full),
        ]
        + [pltpu.SemaphoreType.DMA((2 * LAST,))] * 4
        + [pltpu.SemaphoreType.DMA((7,))] * 2
        + [pltpu.SemaphoreType.DMA((16,))] * 2
        + [pltpu.SemaphoreType.DMA((24,))],
        compiler_params=pltpu.CompilerParams(
            vmem_limit_bytes=63 * 2**20, collective_id=0, has_side_effects=True
        ),
        cost_estimate=cost(6e10, 1e8),
        name="layer",
    )(rows, cotangent, segments, matrices, vectors, waves)


def rest_kernel(
    held, units_in, grads_in, rows_in, vectors, early, early_bias, extra, sum_1_in, sum_2_in,
    sum_1, sum_2, rows_out, total, by_x_out, by_y_out, by_xy_out, own_out,
    units, grads, weight, acts, pres, flipped, column, stage, lines, added, current, received, shares, other,
    swap_send, swap_recv, hop_send, hop_recv, loads, local, share_send, share_recv,
):
    d, y, c = lax.axis_index("dp"), lax.axis_index("heads"), lax.axis_index("tensor")
    z, x = d // 2, d % 2
    shard = 2 * y + c
    tokens = units.shape[0]
    block = tokens // 8
    by_x, by_y, by_core = {"dp": d + 1 - 2 * x}, {"heads": 1 - y}, {"tensor": 1 - c}
    by_z = [{"dp": d + 2 - 4 * (z % 2)}, {"dp": d + 4 - 8 * (z // 2)}]
    peers = [by_core, by_y, by_x] + by_z
    barrier = pltpu.get_barrier_semaphore()
    for near in peers:
        pl.semaphore_signal(barrier, inc=1, device_id=near, device_id_type=MESH)
    pl.semaphore_wait(barrier, len(peers))

    def remote(source, target, send, recv, device):
        return pltpu.make_async_remote_copy(
            src_ref=source, dst_ref=target, send_sem=send, recv_sem=recv, device_id=device, device_id_type=MESH
        )

    def back(source, i, to_0, to_1):
        copies = [remote(source, there, swap_send.at[i], swap_recv.at[i], by_x) for there in (to_0, to_1)]
        for side in range(2):
            pl.when(x == side)(copies[side].start)
        return copies[0]

    swaps = [back(extra, 0, sum_1.at[3], sum_1.at[1])]

    def fetch(role, slot, sem):
        for side in range(2):

            @pl.when(x == side)
            def _():
                pltpu.make_async_copy(held.at[role[side]], weight.at[slot], local.at[sem]).start()

    tile = 512
    fetch(ROLES["up"][2], 1, 1)
    fetch(ROLES["down"][2], 3, 3)
    def row_loads(i):
        here = pl.ds(pl.multiple_of(i * tile, tile), tile)
        return [
            pltpu.make_async_copy(source.at[here], target.at[here], loads.at[2 * i + j])
            for j, (source, target) in enumerate(((units_in, units), (grads_in, grads)))
        ]

    for i in range(tokens // tile):
        for copy in row_loads(i):
            copy.start()
    fetch(ROLES["up"][3], 2, 2)
    fetch(ROLES["down"][3], 4, 4)
    fetch(ROLES["up"][1], 0, 0)
    pltpu.make_async_copy(rows_in.at[3], pres.at[0], local.at[5]).start()
    out_roles = (ROLES["down"][0], ROLES["down"][1], ROLES["out"])
    for i, (role, spot) in enumerate(zip(out_roles, (0, 2, 4))):
        fetch(role, 5 + i, 13 + i)
        pltpu.make_async_copy(rows_in.at[spot], acts.at[i], local.at[16 + i]).start()
    for i in range(4):
        lines[i : i + 1, :] = jnp.concatenate([vectors[8 * i + b : 8 * i + b + 1, :] for b in range(8)], axis=1)
    for slot in (1, 3):
        pltpu.make_async_copy(held.at[0], weight.at[slot], local.at[slot]).wait()
    hidden = [SLOTS[0][s] + (SLOTS[1][s] - SLOTS[0][s]) * x for s in range(4)]

    saves = []
    for s in range(2):
        bias = vectors[pl.ds(64 + shard * 8 + hidden[2 + s], 1), :]
        if s == 1:
            pltpu.make_async_copy(held.at[0], weight.at[2], local.at[2]).wait()
            pltpu.make_async_copy(held.at[0], weight.at[4], local.at[4]).wait()

        def run_mlp(i, carry):
            here = pl.ds(pl.multiple_of(i * tile, tile), tile)
            if s == 0:
                for copy in row_loads(i):
                    copy.wait()
            norm = (units[here, :].astype(jnp.float32) * lines[2:3, :] + lines[3:4, :]).astype(jnp.bfloat16)
            inner = dot_nn(norm, weight[1 + s].reshape(D, HD)) + bias
            pull = dot_nt(grads[here, :HD], weight[3 + s, 0])
            for b in range(1, D // HD):
                pull = pull + dot_nt(grads[here, b * HD : (b + 1) * HD], weight[3 + s, b])
            share = 0.5 + 0.5 * lax.erf(inner * (0.5**0.5))
            acts[3 + s, here, :] = (inner * share).astype(jnp.bfloat16)
            slope = share + inner * jnp.exp(-0.5 * inner * inner) * ((2.0 * 3.141592653589793) ** (-0.5))
            pres[1 + s, here, :] = (slope * pull).astype(jnp.bfloat16)
            return carry

        lax.fori_loop(0, tokens // tile, run_mlp, 0)
        copy = pltpu.make_async_copy(pres.at[1 + s], rows_out.at[s], local.at[6 + s])
        copy.start()
        saves.append(copy)
        flipped[:HD, :] = acts[3 + s].T

        def run_down(b, carry):
            here = pl.ds(pl.multiple_of(b * HD, HD), HD)
            stage[s, b] = dot_nn(flipped[:HD, :], grads[:, here]).astype(jnp.bfloat16)
            return carry

        lax.fori_loop(0, D // HD, run_down, 0)
        swaps.append(back(stage.at[s], 1 + s, sum_2.at[3 - s], (sum_1, sum_2)[s].at[3]))
    pltpu.make_async_copy(rows_in.at[3], pres.at[0], local.at[5]).wait()
    pltpu.make_async_copy(held.at[0], weight.at[0], local.at[0]).wait()
    current[0] = jnp.zeros(current.shape[1:], jnp.float32)
    for i in range(3):
        wide = pres[i]
        flipped[i * HD : (i + 1) * HD, :] = wide.T
        bias = jnp.sum(wide.astype(jnp.float32), axis=0, keepdims=True)
        current[0, pl.ds(64 + shard * 8 + hidden[1 + i], 1), :] = bias
        column[i] = jnp.broadcast_to(bias, (128, HD)).T

    def run_up(b, carry):
        here = pl.ds(pl.multiple_of(b * HD, HD), HD)
        gains, shifts = early[2:3, here], early[3:4, here]
        for i in range(3):
            turned = dot_nn(flipped[i * HD : (i + 1) * HD, :], units[:, here])
            w = weight[i, b].T.astype(jnp.float32)
            bias = column[i][:, 0:1]
            gains = gains + jnp.sum(w * turned, axis=0, keepdims=True)
            shifts = shifts + jnp.sum(w * bias, axis=0, keepdims=True)
            result = turned * lines[2:3, here] + bias * lines[3:4, here]
            stage[2 + i, b] = result.T.astype(jnp.bfloat16)
        added[0:1, here] = gains
        added[1:2, here] = shifts
        return carry

    lax.fori_loop(0, D // HD, run_up, 0)
    places = ((sum_1.at[2], sum_1.at[2]), (sum_2.at[2], sum_1.at[1]), (sum_2.at[1], sum_2.at[1]))
    puts = [[pltpu.make_async_copy(stage.at[2 + i], places[i][side], local.at[10 + i]) for side in range(2)] for i in range(3)]
    for pair in puts:
        for side in range(2):
            pl.when(x == side)(pair[side].start)

    for i in range(3):
        pltpu.make_async_copy(held.at[0], weight.at[5 + i], local.at[13 + i]).wait()
        pltpu.make_async_copy(rows_in.at[0], acts.at[i], local.at[16 + i]).wait()
    by_slot = (5, 6, 7, 3, 4)

    def share_rows(i):
        here = pl.ds(pl.multiple_of(i * tile, tile), tile)
        for b in range(D // HD):
            result = dot_nn(acts[0, here, :], weight[by_slot[0], b])
            for j in range(1, 5):
                result = result + dot_nn(acts[j, here, :], weight[by_slot[j], b])
            yield slice(b * HD, (b + 1) * HD), result

    own = jnp.sum(grads[:block, :].astype(jnp.float32), axis=0, keepdims=True)
    for i, line in enumerate((early[0:1, :], early[1:2, :], added[0:1, :], added[1:2, :])):
        for b in range(8):
            current[0, 8 * i + b : 8 * i + b + 1, :] = line[:, b * HD : (b + 1) * HD]
    for b in range(8):
        current[0, 56 + b : 57 + b, :] = own[:, b * HD : (b + 1) * HD]
        current[0, 96 + b : 97 + b, :] = own[:, b * HD : (b + 1) * HD]
    for i in range(3):
        at = 32 + (shard * 2 + x) * 3 + i
        current[0, pl.ds(at, 1), :] = early_bias[:, i * HD : (i + 1) * HD]
    current[0, pl.ds(64 + shard * 8 + hidden[0], 1), :] = early_bias[:, 3 * HD :]
    hops = [remote(current.at[i], received.at[i], hop_send.at[i], hop_recv.at[i], near) for i, near in enumerate(peers)]

    def finish_hop(i):
        hops[i].wait()
        result = current[i] + received[i]
        if i + 1 < len(peers):
            current[i + 1] = result
            hops[i + 1].start()
        else:
            total[...] = result

    hops[0].start()
    for i in range(2):
        for columns, result in share_rows(2 + i):
            shares[i * tile : (i + 1) * tile, columns] = result.astype(jnp.bfloat16)
        copy = remote(shares.at[i * tile : (i + 1) * tile], other.at[i * tile : (i + 1) * tile], share_send.at[i], share_recv.at[i], by_core)
        copy.start()
        finish_hop(i)
    sends = [
        remote(shares.at[i * tile : (i + 1) * tile], other.at[i * tile : (i + 1) * tile], share_send.at[i], share_recv.at[i], by_core)
        for i in range(2)
    ]
    for copy in sends:
        copy.wait_send()
    for i in range(2):
        sends[i].wait_recv()
        for columns, result in share_rows(i):
            theirs = other[i * tile : (i + 1) * tile, columns].astype(jnp.float32)
            shares[i * tile : (i + 1) * tile, columns] = (result + theirs).astype(jnp.bfloat16)
        finish_hop(2 + i)
    outs = []
    for i, target in enumerate((own_out, by_x_out, by_y_out, by_xy_out)):
        copy = pltpu.make_async_copy(shares.at[i * block : (i + 1) * block], target.at[0], local.at[19 + i])
        copy.start()
        outs.append(copy)

    finish_hop(4)
    for copy in swaps + saves + outs:
        copy.wait()
    for pair in puts:
        for side in range(2):
            pl.when(x == side)(pair[side].wait)


def rest(held, units, grads, rows, vectors, sums, biases, extra, sum_1, sum_2):
    tokens = units.shape[0]
    anywhere, near = pl.BlockSpec(memory_space=pl.ANY), pl.BlockSpec(memory_space=pltpu.VMEM)
    low, full = jnp.bfloat16, jnp.float32
    group = (D // HD, HD, HD)
    table = vectors.shape
    return pl.pallas_call(
        rest_kernel,
        in_specs=[anywhere] * 4 + [near] * 3 + [anywhere] * 3,
        out_specs=[anywhere] * 3 + [near] + [anywhere] * 4,
        out_shape=[jax.ShapeDtypeStruct((4,) + group, low)] * 2
        + [jax.ShapeDtypeStruct((2, tokens, HD), low), jax.ShapeDtypeStruct(table, full)]
        + [jax.ShapeDtypeStruct((2, tokens // 8, D), low)] * 4,
        input_output_aliases={8: 0, 9: 1},
        scratch_shapes=[
            pltpu.VMEM((tokens, D), low),
            pltpu.VMEM((tokens, D), low),
            pltpu.VMEM((8,) + group, low),
            pltpu.VMEM((5, tokens, HD), low),
            pltpu.VMEM((3, tokens, HD), low),
            pltpu.VMEM((3 * HD, tokens), low),
            pltpu.VMEM((3, HD, 128), full),
            pltpu.VMEM((5,) + group, low),
            pltpu.VMEM((4, D), full),
            pltpu.VMEM((2, D), full),
            pltpu.VMEM((5,) + table, full),
            pltpu.VMEM((5,) + table, full),
            pltpu.VMEM((tokens // 2, D), low),
            pltpu.VMEM((tokens // 2, D), low),
            pltpu.SemaphoreType.DMA((4,)),
            pltpu.SemaphoreType.DMA((4,)),
            pltpu.SemaphoreType.DMA((5,)),
            pltpu.SemaphoreType.DMA((5,)),
            pltpu.SemaphoreType.DMA((8,)),
            pltpu.SemaphoreType.DMA((23,)),
            pltpu.SemaphoreType.DMA((2,)),
            pltpu.SemaphoreType.DMA((2,)),
        ],
        compiler_params=pltpu.CompilerParams(
            vmem_limit_bytes=60 * 2**20, collective_id=1, has_side_effects=True
        ),
        cost_estimate=cost(4e10, 6e7),
        name="rest",
    )(held, units, grads, rows, vectors, sums, biases, extra, sum_1, sum_2)


def input_kernel(
    held, rows_in, late, gains, by_x_in, by_y_in, by_xy_in, own_in,
    by_x_out, by_y_out, by_xy_out, own_out,
    weight, rows, shares, other,
    local, share_send, share_recv,
):
    x, c = lax.axis_index("dp") % 2, lax.axis_index("tensor")
    by_core = {"tensor": 1 - c}
    barrier = pltpu.get_barrier_semaphore()
    pl.semaphore_signal(barrier, inc=1, device_id=by_core, device_id_type=MESH)
    pl.semaphore_wait(barrier, 1)
    tokens = rows.shape[1]
    block, tile = tokens // 8, 512
    roles = (ROLES["q"], ROLES["k"], ROLES["v"]) + ROLES["up"]
    sources = [rows_in.at[i] for i in (5, 6, 7, 1, 3)] + [late.at[i] for i in range(2)]
    for i, (role, source) in enumerate(zip(roles, sources)):
        for side in range(2):

            @pl.when(x == side)
            def _():
                pltpu.make_async_copy(held.at[role[side]], weight.at[i], local.at[i]).start()

        pltpu.make_async_copy(source, rows.at[i], local.at[7 + i]).start()
    for i, source in enumerate(sources):
        pltpu.make_async_copy(held.at[0], weight.at[i], local.at[i]).wait()
        pltpu.make_async_copy(source, rows.at[i], local.at[7 + i]).wait()

    def share_rows(i):
        here = pl.ds(i * tile, tile)
        for b in range(D // HD):
            columns = slice(b * HD, (b + 1) * HD)
            parts = []
            for j, (low, high) in enumerate(((0, 3), (3, 7))):
                part = dot_nt(rows[low, here, :], weight[low, b])
                for r in range(low + 1, high):
                    part = part + dot_nt(rows[r, here, :], weight[r, b])
                parts.append(part * gains[j : j + 1, columns])
            yield columns, parts[0] + parts[1]

    sends = [
        pltpu.make_async_remote_copy(
            src_ref=shares.at[i * tile : (i + 1) * tile],
            dst_ref=other.at[i * tile : (i + 1) * tile],
            send_sem=share_send.at[i],
            recv_sem=share_recv.at[i],
            device_id=by_core,
            device_id_type=MESH,
        )
        for i in range(2)
    ]
    for i in range(2):
        for columns, result in share_rows(2 + i):
            shares[i * tile : (i + 1) * tile, columns] = result.astype(jnp.bfloat16)
        sends[i].start()
    for copy in sends:
        copy.wait_send()
    for i in range(2):
        sends[i].wait_recv()
        for columns, result in share_rows(i):
            theirs = other[i * tile : (i + 1) * tile, columns].astype(jnp.float32)
            shares[i * tile : (i + 1) * tile, columns] = (result + theirs).astype(jnp.bfloat16)
    for i, target in enumerate((own_out, by_x_out, by_y_out, by_xy_out)):
        pltpu.make_async_copy(shares.at[i * block : (i + 1) * block], target.at[1], local.at[14 + i]).start()
    for i, target in enumerate((own_out, by_x_out, by_y_out, by_xy_out)):
        pltpu.make_async_copy(shares.at[i * block : (i + 1) * block], target.at[1], local.at[14 + i]).wait()


def input_share(held, rows, late, gains, parts):
    tokens = rows.shape[1]
    anywhere = pl.BlockSpec(memory_space=pl.ANY)
    low = jnp.bfloat16
    return pl.pallas_call(
        input_kernel,
        in_specs=[anywhere] * 3 + [pl.BlockSpec(memory_space=pltpu.VMEM)] + [anywhere] * 4,
        out_specs=[anywhere] * 4,
        out_shape=[jax.ShapeDtypeStruct((2, tokens // 8, D), low)] * 4,
        input_output_aliases={4 + i: i for i in range(4)},
        scratch_shapes=[
            pltpu.VMEM((7, D // HD, HD, HD), low),
            pltpu.VMEM((7, tokens, HD), low),
            pltpu.VMEM((tokens // 2, D), low),
            pltpu.VMEM((tokens // 2, D), low),
            pltpu.SemaphoreType.DMA((18,)),
            pltpu.SemaphoreType.DMA((2,)),
            pltpu.SemaphoreType.DMA((2,)),
        ],
        compiler_params=pltpu.CompilerParams(vmem_limit_bytes=LIMIT, collective_id=2, has_side_effects=True),
        cost_estimate=cost(2 * 7 * tokens * D * HD, 5e7),
        name="input_share",
    )(held, rows, late, gains, *parts)


def soap_part(places, grad, blocks, previous):
    total, count = blocks[0].shape[0], grad.shape[0]
    mats = 2 * count
    own = pl.BlockSpec((GROUP, HD, HD), lambda i, at: (i, 0, 0))
    some = pl.BlockSpec((GROUP, HD, HD), lambda i, at: (at[0] * (count // GROUP) + i, 0, 0))
    whole = pl.BlockSpec((count, HD, HD), lambda i, at: (at[0], 0, 0))
    full = jax.ShapeDtypeStruct((total, HD, HD), jnp.float32)
    shapes = [full, jax.ShapeDtypeStruct((total, HD, HD), jnp.bfloat16)] + [full] * 6
    extra = [] if previous is None else list(previous)

    def body(at, *refs):
        soap_kernel(count, *refs[:8], *refs[8 + len(extra) :])

    return pl.pallas_call(
        body,
        grid_spec=pltpu.PrefetchScalarGridSpec(
            num_scalar_prefetch=1,
            grid=(count // GROUP,),
            in_specs=[own] + [some] * 7 + [pl.BlockSpec(memory_space=pl.ANY)] * len(extra),
            out_specs=[some] * 6 + [whole] * 2,
            scratch_shapes=[
                pltpu.VMEM((mats, HD, 2 * HD), jnp.float32),
                pltpu.VMEM((PAN * PACK, 128), jnp.float32),
            ],
        ),
        out_shape=shapes,
        input_output_aliases={9 + i: i for i in range(len(extra))},
        compiler_params=pltpu.CompilerParams(vmem_limit_bytes=LIMIT),
        cost_estimate=cost(count * 40 * 2 * HD**3 * 3, count * 16 * 4 * HD * HD),
        name="soap",
    )(places, grad, *blocks, *extra)


def adam_vector(grad, params, first, second):
    first_new = beta_one * first + (1.0 - beta_one) * grad
    second_new = beta_two * second + (1.0 - beta_two) * grad * grad
    direction = (
        first_new
        / (1.0 - beta_one**STEP)
        / (jnp.sqrt(second_new / (1.0 - beta_two**STEP)) + epsilon_adam)
    )
    return (params - rate_vector * direction, first_new, second_new)


ALL = ("dp", "heads", "tensor")
SUMMED = ((1, 0, 2), (1, 0, 2), (0, 1, 2), (0, 1, 2), (0, 1, 2), (2, 0, 1), (2, 0, 1), (2, 0, 1))
SLOTS = ((4, 5, 6, 0), (1, 7, 2, 3))


def places():
    for z in range(4):
        for x in range(2):
            for y in range(2):
                for c in range(2):
                    yield z, x, y, c


def index_of(z, x, y, c):
    return ((z * 2 + x) * 2 + y) * 2 + c


def move(array, target):
    return lax.ppermute(array, ALL, [(index_of(*at), index_of(*target(*at))) for at in places()])


LINES = [[index_of(z, x, y, c) for z in range(4)] for x in range(2) for y in range(2) for c in range(2)]


def over_y(array):
    return move(array, lambda z, x, y, c: (z, x, 1 - y, c))


def over_x(array):
    return move(array, lambda z, x, y, c: (z, 1 - x, y, c))


def over_xy(array):
    return move(array, lambda z, x, y, c: (z, 1 - x, 1 - y, c))


def after(array, *earlier):
    return lax.optimization_barrier((array, *earlier))[0]


def plane_shards(
    block_input,
    cotangent,
    segments,
    matrices,
    first_moment,
    second_moment,
    left_stat,
    right_stat,
    left_basis,
    right_basis,
    vectors,
    vec_first,
    vec_second,
):
    d = lax.axis_index("dp")
    x = d % 2
    gain_one, gain_two = vectors[:D].reshape(1, D), vectors[2 * D : 3 * D].reshape(1, D)
    bias_out, bias_down = vectors[7 * D : 8 * D], vectors[8 * D + FF : 9 * D + FF]
    table = vectors.reshape(-1, HD)
    frequency = 1.0 / rope_base ** (jnp.arange(0, RD, 2).astype(jnp.float32) / RD)
    turns = jnp.concatenate([frequency, frequency, jnp.zeros((128 - RD,), jnp.float32)]).reshape(1, 128)
    held, units, grads, sum_0, sum_1, sum_2, extra, rows, sums, biases = layer(
        block_input, cotangent, segments, matrices, table, turns
    )
    sum_1, sum_2, late, grad_table, *parts = rest(
        held, units, grads, rows, table, sums, biases, extra, sum_1, sum_2
    )
    owned = []
    for send in (sum_0, sum_1, sum_2[:, :4], sum_2[:, 4:]):
        owned.append(lax.psum_scatter(send, ALL, scatter_dimension=0, tiled=False, axis_index_groups=LINES))

    parts = input_share(held, rows, late, jnp.concatenate([gain_one, gain_two]), parts)
    blocks = [a[0] for a in (matrices, first_moment, second_moment, left_stat, right_stat, left_basis, right_basis)]
    summed_order = jnp.array(SUMMED, jnp.int32)[d]
    updated = soap_part(summed_order[0:1], after(owned[0], parts[0]), blocks, None)
    updated = soap_part(summed_order[1:2], after(owned[1], updated[1]), blocks, updated)
    by_x, by_y, by_xy, own = parts
    totals = (
        after(own, updated[1]).astype(jnp.float32)
        + over_x(by_x).astype(jnp.float32)
        + over_y(by_y).astype(jnp.float32)
        + over_xy(by_xy).astype(jnp.float32)
    )
    output = block_input + totals[0] + bias_out + bias_down
    e = totals[1]
    middle = jnp.mean(block_input, axis=-1, keepdims=True)
    centered = block_input - middle
    inverse = lax.rsqrt(jnp.mean(centered * centered, axis=-1, keepdims=True) + epsilon_norm)
    unit = centered * inverse
    grad_input = cotangent + inverse * (
        e - jnp.mean(e, axis=-1, keepdims=True) - unit * jnp.mean(e * unit, axis=-1, keepdims=True)
    )
    grad_vectors = grad_table.reshape(-1)
    updated = soap_part(2 * summed_order[2:3], after(owned[2], output, grad_input), blocks, updated)
    updated = soap_part(2 * summed_order[2:3] + 1, owned[3], blocks, updated)
    new_vectors, new_vec_first, new_vec_second = adam_vector(grad_vectors, vectors, vec_first, vec_second)
    return (output, grad_input, *[u[None] for u in updated], new_vectors, new_vec_first, new_vec_second)


def generic_shards(
    block_input,
    cotangent,
    segments,
    matrices,
    first_moment,
    second_moment,
    left_stat,
    right_stat,
    left_basis,
    right_basis,
    vectors,
    vec_first,
    vec_second,
):
    group_size = lax.axis_size(("heads", "tensor"))
    member = lax.axis_index(("heads", "tensor"))
    heads_here = H // group_size
    hidden_here = FF // group_size
    row_blocks = D // HD
    hidden_blocks = hidden_here // HD
    seq_count = segments.shape[0]
    tokens_here = seq_count * LEN
    own_rows = block_input.shape[0]
    qkv_offset = 4 * D + member * heads_here * 3 * HD
    up_offset = 8 * D + member * hidden_here
    gain_one = vectors[0:D]
    shift_one = vectors[D : 2 * D]
    gain_two = vectors[2 * D : 3 * D]
    shift_two = vectors[3 * D : 4 * D]
    bias_qkv = lax.dynamic_slice_in_dim(vectors, qkv_offset, heads_here * 3 * HD).reshape(
        heads_here, 3, HD
    )
    bias_out = vectors[7 * D : 8 * D]
    bias_up = lax.dynamic_slice_in_dim(vectors, up_offset, hidden_here)
    bias_down = vectors[8 * D + FF : 9 * D + FF]
    gathered = lax.all_gather(matrices.astype(jnp.bfloat16), "dp", axis=1, tiled=True)[0]
    w_qkv, w_out, w_up, w_down = unpack_blocks(gathered, heads_here, row_blocks, hidden_blocks)
    normed_one, unit_one, inverse_one = layer_norm(block_input, gain_one, shift_one)
    normed_two, unit_two, inverse_two = layer_norm(block_input, gain_two, shift_two)
    grad_own = cotangent.astype(jnp.bfloat16)
    norm_one, norm_two, grad_rows = (
        lax.all_gather(normed_one.astype(jnp.bfloat16), ("heads", "tensor"), axis=0, tiled=True),
        lax.all_gather(normed_two.astype(jnp.bfloat16), ("heads", "tensor"), axis=0, tiled=True),
        lax.all_gather(grad_own, ("heads", "tensor"), axis=0, tiled=True),
    )
    norm_one3 = norm_one.reshape(tokens_here, row_blocks, HD)
    norm_two3 = norm_two.reshape(tokens_here, row_blocks, HD)
    projected = (
        jnp.einsum("tbr,hqbrc->thqc", norm_one3, w_qkv, preferred_element_type=jnp.float32)
        + bias_qkv
    )
    shaped = projected.reshape(seq_count, LEN, heads_here, 3, HD)
    cosine, sine = angles(segments)
    queries = rotate(shaped[:, :, :, 0], cosine, sine).astype(jnp.bfloat16)
    keys_rot = rotate(shaped[:, :, :, 1], cosine, sine).astype(jnp.bfloat16)
    values = shaped[:, :, :, 2].astype(jnp.bfloat16)
    attended, log_total = lax.map(seq_forward, (queries, keys_rot, values, segments))
    attend_low = attended.astype(jnp.bfloat16).reshape(tokens_here, heads_here, HD)
    pre_act = (
        jnp.einsum("tbr,kbrc->tkc", norm_two3, w_up, preferred_element_type=jnp.float32).reshape(
            tokens_here, hidden_here
        )
        + bias_up
    )
    act_low = gelu_exact(pre_act).astype(jnp.bfloat16)
    rows_act = act_low.reshape(lax.axis_size(("heads", "tensor")) * own_rows, hidden_blocks, HD)
    first_term = jnp.einsum("thr,hbrc->tbc", attend_low, w_out, preferred_element_type=jnp.float32)
    second_term = jnp.einsum("tkr,kbrc->tbc", rows_act, w_down, preferred_element_type=jnp.float32)
    summed = lax.psum_scatter(
        (first_term + second_term).reshape(lax.axis_size(("heads", "tensor")) * own_rows, D),
        ("heads", "tensor"),
        scatter_dimension=0,
        tiled=True,
    )
    output = block_input + summed + bias_out + bias_down
    regathered = lax.all_gather(matrices.astype(jnp.bfloat16), "dp", axis=1, tiled=True)[0]
    w_qkv, w_out, w_up, w_down = unpack_blocks(regathered, heads_here, row_blocks, hidden_blocks)
    grad_rows3 = grad_rows.reshape(tokens_here, row_blocks, HD)
    act_low3 = act_low.reshape(tokens_here, hidden_blocks, HD)
    grad_act = jnp.einsum(
        "tbc,kbrc->tkr", grad_rows3, w_down, preferred_element_type=jnp.float32
    ).reshape(tokens_here, hidden_here)
    gelu_pull = jax.vjp(gelu_exact, pre_act)[1]
    grad_pre = gelu_pull(grad_act)[0].astype(jnp.bfloat16)
    grad_pre3 = grad_pre.reshape(tokens_here, hidden_blocks, HD)
    grad_attend = jnp.einsum(
        "tbc,hbrc->thr", grad_rows3, w_out, preferred_element_type=jnp.float32
    ).astype(jnp.bfloat16)
    grad_attend = grad_attend.reshape(seq_count, LEN, heads_here, HD)
    grad_queries, grad_keys, grad_values = lax.map(
        seq_backward, (queries, keys_rot, values, segments, log_total, grad_attend)
    )
    grad_raw = jnp.stack(
        [rotate(grad_queries, cosine, -sine), rotate(grad_keys, cosine, -sine), grad_values], axis=3
    )
    grad_raw = grad_raw.astype(jnp.bfloat16).reshape(tokens_here, heads_here, 3, HD)
    rows_up = grad_pre.reshape(lax.axis_size(("heads", "tensor")) * own_rows, hidden_blocks, HD)
    back_one = jnp.einsum(
        "thqc,hqbrc->tbr", grad_raw, w_qkv, preferred_element_type=jnp.float32
    ).reshape(lax.axis_size(("heads", "tensor")) * own_rows, D)
    back_two = jnp.einsum(
        "tkc,kbrc->tbr", rows_up, w_up, preferred_element_type=jnp.float32
    ).reshape(lax.axis_size(("heads", "tensor")) * own_rows, D)
    grad_norms = lax.psum_scatter(
        jnp.stack([back_one, back_two], axis=1),
        ("heads", "tensor"),
        scatter_dimension=0,
        tiled=True,
    )
    grad_norm_one = grad_norms[:, 0]
    grad_norm_two = grad_norms[:, 1]
    grad_input = (
        cotangent
        + norm_back(grad_norm_one, unit_one, inverse_one, gain_one)
        + norm_back(grad_norm_two, unit_two, inverse_two, gain_two)
    )
    grad_bias_rows = jnp.sum(grad_own, axis=0, dtype=jnp.float32)
    pieces = jnp.concatenate(
        [
            jnp.sum(grad_norm_one * unit_one, axis=0),
            jnp.sum(grad_norm_one, axis=0),
            jnp.sum(grad_norm_two * unit_two, axis=0),
            jnp.sum(grad_norm_two, axis=0),
            jnp.zeros((3 * D,), jnp.float32),
            grad_bias_rows,
            jnp.zeros((FF,), jnp.float32),
            grad_bias_rows,
        ]
    )
    pieces = lax.dynamic_update_slice_in_dim(
        pieces, jnp.sum(grad_raw, axis=0, dtype=jnp.float32).reshape(-1), qkv_offset, 0
    )
    pieces = lax.dynamic_update_slice_in_dim(
        pieces, jnp.sum(grad_pre, axis=0, dtype=jnp.float32), up_offset, 0
    )
    grad_vectors = lax.psum(pieces, ("dp", "heads", "tensor"))
    grad_down = jnp.einsum(
        "tkr,tbc->kbrc", act_low3, grad_rows3, preferred_element_type=jnp.float32
    )
    grad_up = jnp.einsum("tbr,tkc->kbrc", norm_two3, grad_pre3, preferred_element_type=jnp.float32)
    grad_out = jnp.einsum(
        "thr,tbc->hbrc", attend_low, grad_rows3, preferred_element_type=jnp.float32
    )
    grad_qkv = jnp.einsum(
        "tbr,thqc->hqbrc", norm_one3, grad_raw, preferred_element_type=jnp.float32
    )
    attn_grads = jnp.concatenate([grad_qkv, grad_out[:, None]], axis=1).reshape(-1, HD, HD)
    all_grads = jnp.concatenate(
        [attn_grads, grad_up.reshape(-1, HD, HD), grad_down.reshape(-1, HD, HD)], axis=0
    )[None]
    owned = lax.psum_scatter(all_grads, "dp", scatter_dimension=1, tiled=True)
    blocks = [a[0] for a in (matrices, first_moment, second_moment, left_stat, right_stat, left_basis, right_basis)]
    updated = [u[None] for u in soap_part(jnp.zeros((1,), jnp.int32), owned[0], blocks, None)]
    new_vectors, new_vec_first, new_vec_second = adam_vector(
        grad_vectors, vectors, vec_first, vec_second
    )
    return (
        output,
        grad_input,
        updated[0],
        updated[1],
        updated[2],
        updated[3],
        updated[4],
        updated[5],
        updated[6],
        updated[7],
        new_vectors,
        new_vec_first,
        new_vec_second,
    )


def solution(mesh):
    in_specs = (
        P(("dp", "heads", "tensor"), None),
        P(("dp", "heads", "tensor"), None),
        P("dp", None),
        P(("heads", "tensor"), "dp", None, None),
        P(("heads", "tensor"), "dp", None, None),
        P(("heads", "tensor"), "dp", None, None),
        P(("heads", "tensor"), "dp", None, None),
        P(("heads", "tensor"), "dp", None, None),
        P(("heads", "tensor"), "dp", None, None),
        P(("heads", "tensor"), "dp", None, None),
        P(),
        P(),
        P(),
    )
    out_specs = (
        P(("dp", "heads", "tensor"), None),
        P(("dp", "heads", "tensor"), None),
        P(("heads", "tensor"), "dp", None, None),
        P(("heads", "tensor"), "dp", None, None),
        P(("heads", "tensor"), "dp", None, None),
        P(("heads", "tensor"), "dp", None, None),
        P(("heads", "tensor"), "dp", None, None),
        P(("heads", "tensor"), "dp", None, None),
        P(("heads", "tensor"), "dp", None, None),
        P(("heads", "tensor"), "dp", None, None),
        P(),
        P(),
        P(),
    )
    plane = dict(mesh.shape) == {"dp": 8, "heads": 2, "tensor": 2}
    shards = plane_shards if plane else generic_shards
    return jax.shard_map(shards, mesh=mesh, in_specs=in_specs, out_specs=out_specs, check_vma=False)
```

```python
import functools

import jax
import jax.numpy as jnp
from jax import lax
from jax.experimental import pallas as pl
from jax.experimental.pallas import tpu as pltpu
from jax.sharding import PartitionSpec as P

D = 2048
H = 8
HD = 256
RD = 64
FF = 8192
LEN = 1024
STEP = 10


epsilon_norm = 1e-05
epsilon_adam = 1e-08
rope_base = 10000.0
beta_one = 0.9
beta_two = 0.95
beta_stat = 0.95
rate_matrix = 0.05
rate_vector = 0.1
weight_decay = 0.01
PAN = 32
PACK = 16
WIDE = 8
UNROLL = 16
GROUP = 2


def layer_norm(rows, gain, shift):
    middle = jnp.mean(rows, axis=-1, keepdims=True)
    centered = rows - middle
    spread = jnp.mean(centered * centered, axis=-1, keepdims=True)
    inverse = lax.rsqrt(spread + epsilon_norm)
    unit = centered * inverse
    return (unit * gain + shift, unit, inverse)


def norm_back(grad, unit, inverse, gain):
    scaled = grad * gain
    return inverse * (
        scaled
        - jnp.mean(scaled, axis=-1, keepdims=True)
        - unit * jnp.mean(scaled * unit, axis=-1, keepdims=True)
    )


def angles(segments):
    seq_count = segments.shape[0]
    column = jnp.arange(LEN, dtype=jnp.int32)[None, :]
    border = jnp.concatenate(
        [jnp.ones((seq_count, 1), jnp.bool_), segments[:, 1:] != segments[:, :-1]], axis=1
    )
    starts = lax.cummax(jnp.where(border, column, 0), axis=1)
    places = (column - starts).astype(jnp.float32)
    frequency = 1.0 / rope_base ** (jnp.arange(0, RD, 2).astype(jnp.float32) / RD)
    turns = places[:, :, None] * frequency[None, None, :]
    return (jnp.cos(turns)[:, :, None, :], jnp.sin(turns)[:, :, None, :])


def rotate(part, cosine, sine):
    half_dims = RD // 2
    first_half = part[..., :half_dims]
    second_half = part[..., half_dims:RD]
    return jnp.concatenate(
        [
            first_half * cosine - second_half * sine,
            second_half * cosine + first_half * sine,
            part[..., RD:],
        ],
        axis=-1,
    )


def unpack_blocks(blocks, heads_here, row_blocks, hidden_blocks):
    attn_count = heads_here * 4 * row_blocks
    up_count = hidden_blocks * row_blocks
    attn_part = blocks[:attn_count].reshape(heads_here, 4, row_blocks, HD, HD)
    w_up = blocks[attn_count : attn_count + up_count].reshape(hidden_blocks, row_blocks, HD, HD)
    w_down = blocks[attn_count + up_count :].reshape(hidden_blocks, row_blocks, HD, HD)
    return (attn_part[:, :3], attn_part[:, 3], w_up, w_down)


def masked_scores(queries, keys_rot, segment_row):
    column = jnp.arange(LEN)
    allowed = (segment_row[:, None] == segment_row[None, :]) & (column[None, :] <= column[:, None])
    scores = jnp.einsum(
        "qhd,khd->hqk", queries, keys_rot, preferred_element_type=jnp.float32
    ) * HD ** (-0.5)
    return jnp.where(allowed[None], scores, -1e30)


def seq_forward(items):
    queries, keys_rot, values, segment_row = items
    scores = masked_scores(queries, keys_rot, segment_row)
    row_max = jnp.max(scores, axis=-1, keepdims=True)
    powers = jnp.exp(scores - row_max)
    row_total = jnp.sum(powers, axis=-1, keepdims=True)
    probs_low = (powers / row_total).astype(jnp.bfloat16)
    attended = jnp.einsum("hqk,khd->qhd", probs_low, values, preferred_element_type=jnp.float32)
    return (attended, (row_max + jnp.log(row_total))[..., 0])


def seq_backward(items):
    queries, keys_rot, values, segment_row, log_total, grad_attend = items
    scores = masked_scores(queries, keys_rot, segment_row)
    probs = jnp.exp(scores - log_total[..., None])
    grad_probs = jnp.einsum("qhd,khd->hqk", grad_attend, values, preferred_element_type=jnp.float32)
    inner = jnp.sum(probs * grad_probs, axis=-1, keepdims=True)
    grad_scores = (probs * (grad_probs - inner)).astype(jnp.bfloat16)
    grad_queries = jnp.einsum(
        "hqk,khd->qhd", grad_scores, keys_rot, preferred_element_type=jnp.float32
    ) * HD ** (-0.5)
    grad_keys = jnp.einsum(
        "hqk,qhd->khd", grad_scores, queries, preferred_element_type=jnp.float32
    ) * HD ** (-0.5)
    grad_values = jnp.einsum(
        "hqk,qhd->khd", probs.astype(jnp.bfloat16), grad_attend, preferred_element_type=jnp.float32
    )
    return (grad_queries, grad_keys, grad_values)


def gelu_exact(inputs):
    return jax.nn.gelu(inputs, approximate=False)


def dot_nn(a, b):
    return lax.dot_general(a, b, (((1,), (0,)), ((), ())), preferred_element_type=jnp.float32)


def dot_nt(a, b):
    return lax.dot_general(a, b, (((1,), (1,)), ((), ())), preferred_element_type=jnp.float32)


def dot_tn(a, b):
    return lax.dot_general(a, b, (((0,), (0,)), ((), ())), preferred_element_type=jnp.float32)


def split(x):
    high = x.astype(jnp.bfloat16)
    return high, (x - high.astype(jnp.float32)).astype(jnp.bfloat16)


def three(dot, a, b):
    return dot(a[0], b[0]) + (dot(a[0], b[1]) + dot(a[1], b[0]))


def eliminate(diag):
    tiles = PAN * PACK // 128
    per = 128 // PACK
    flat = diag[...].T[:PAN]
    full = [flat[:, t * 128 : (t + 1) * 128] for t in range(tiles)]
    row = lax.broadcasted_iota(jnp.int32, (PAN, 128), 0)
    lane = lax.broadcasted_iota(jnp.int32, (PAN, 128), 1)
    inverse = [jnp.where(row == lane // PACK + t * per, 1.0, 0.0) for t in range(tiles)]

    def column(k):
        return jnp.take_along_axis(full[k // per], lane % PACK + k % per * PACK, axis=1)

    for k in range(0, PAN, WIDE):
        columns, scales, crosses = [column(k + i) for i in range(WIDE)], [], []
        for i in range(WIDE):
            for j in range(i):
                columns[i] = columns[i] - columns[j] * crosses[j][i]
            scales.append(lax.rsqrt(columns[i][k + i : k + i + 1]))
            columns[i] = columns[i] * scales[i]
            crosses.append([columns[i][k + n : k + n + 1] for n in range(WIDE)])
        columns = [jnp.where(row >= k + WIDE, c, 0.0) for c in columns]

        def step(tile):
            tops = []
            for i in range(WIDE):
                top = tile[k + i : k + i + 1]
                for j in range(i):
                    top = top - crosses[j][i] * tops[j]
                tops.append(top * scales[i])
            for c, top in zip(columns, tops):
                tile = tile - c * top
            return tops, tile

        for t in range(tiles):
            if (t + 1) * per > k + WIDE:
                full[t] = step(full[t])[1]
            if t * per < k + WIDE:
                tops, tile = step(inverse[t])
                for i, top in enumerate(tops):
                    tile = jnp.where(row == k + i, top, tile)
                inverse[t] = tile
    diag[:, :PAN] = jnp.concatenate(inverse, axis=1).T


def soap_kernel(count, g, w, f, s, ls, rs, lb, rb, ow, owl, of, os, ols, ors, olb, orb, aug, diag):
    step = pl.program_id(0)
    mats = 2 * count
    unroll = UNROLL if mats % UNROLL == 0 else 4
    blocks = range(GROUP)
    grad = [g[i].astype(jnp.bfloat16) for i in blocks]
    left, right = [split(lb[i]) for i in blocks], [split(rb[i]) for i in blocks]
    left_t = [(x.T, y.T) for x, y in left]
    right_t = [(x.T, y.T) for x, y in right]
    grad_t = [x.T for x in grad]
    lnew = [beta_stat * ls[i] + (1.0 - beta_stat) * dot_nn(grad[i], grad_t[i]) for i in blocks]
    rnew = [beta_stat * rs[i] + (1.0 - beta_stat) * dot_nn(grad_t[i], grad[i]) for i in blocks]
    turned = [dot_nn(left_t[i][0], grad[i]) + dot_nn(left_t[i][1], grad[i]) for i in blocks]
    for i in blocks:
        ols[i] = lnew[i]
        ors[i] = rnew[i]
    turned = [three(dot_nn, split(turned[i]), right[i]) for i in blocks]
    sides = [
        three(dot_nn, basis_t, split(stat))
        for i in blocks
        for basis_t, stat in ((left_t[i], lnew[i]), (right_t[i], rnew[i]))
    ]
    first_new = [beta_one * f[i] + (1.0 - beta_one) * turned[i] for i in blocks]
    second_new = [beta_two * s[i] + (1.0 - beta_two) * turned[i] * turned[i] for i in blocks]
    direction = [
        x / (1.0 - beta_one**STEP) / (jnp.sqrt(y / (1.0 - beta_two**STEP)) + epsilon_adam)
        for x, y in zip(first_new, second_new)
    ]
    for i in blocks:
        of[i] = first_new[i]
        os[i] = second_new[i]
    stepped = [three(dot_nn, left[i], split(direction[i])) for i in blocks]
    for i, side in enumerate(sides):
        aug[2 * GROUP * step + i, :, HD:] = side
    grams = [three(dot_nt, x, x) for x in map(split, sides)]
    stepped = [three(dot_nn, split(stepped[i]), right_t[i]) for i in blocks]
    for i, gram in enumerate(grams):
        aug[2 * GROUP * step + i, :, :HD] = gram
    for i in blocks:
        weight = w[i]
        weight_new = weight - rate_matrix * (stepped[i] + weight_decay * weight)
        ow[i] = weight_new
        owl[i] = weight_new.astype(jnp.bfloat16)

    @pl.when(step == count // GROUP - 1)
    def _():
        half = HD // 2

        def place(p, i):
            low = pl.multiple_of(p * PAN, PAN)
            base = pl.multiple_of(p // 4 * 128, 128)
            for u in range(unroll):
                m = i * unroll + u
                own = aug[m, pl.ds(low, PAN), pl.ds(base, 128)]
                diag[pl.ds(m, PAN, stride=PACK), :] = pltpu.roll(own, (128 - p % 4 * PAN) % 128, 1)

        def update(p, i, pair):
            low = pl.multiple_of(p * PAN, PAN)
            edge = pair // 2 * half
            start = pair * 2 * PAN + PAN
            mine = [i * unroll + u for u in range(unroll)]
            factors = [split(diag[pl.ds(m, PAN, stride=PACK), :][:, :PAN]) for m in mine]
            panels = [split(aug[m, pl.ds(low, PAN), edge:]) for m in mine]
            panels = [three(dot_tn, x, y) for x, y in zip(factors, panels)]
            lane = lax.broadcasted_iota(jnp.int32, (PAN, HD - edge), 1) + edge
            heads = [split(jnp.where(lane >= low + PAN, panel[:, : HD - edge], 0.0)) for panel in panels]
            parts = [split(panel) for panel in panels]
            lhs = [jnp.concatenate([x, x, y], axis=0).T for x, y in heads]
            rhs = [jnp.concatenate([x, y, x], axis=0) for x, y in parts]
            rest = [aug[m, start:, edge:] - dot_nn(x[start - edge :], y) for m, x, y in zip(mine, lhs, rhs)]
            for m, panel, left in zip(mine, panels, rest):
                aug[m, start:, edge:] = left
                aug[m, pl.ds(low, PAN), HD:] = panel[:, HD - edge :]

        def panel_step(p, carry):
            lax.fori_loop(0, mats // unroll, lambda i, n: (place(p, i), n)[1], 0)
            eliminate(diag)

            for pair in range(4):

                @pl.when(p // 2 == pair)
                def _():
                    lax.fori_loop(0, mats // unroll, lambda i, n: (update(p, i, pair), n)[1], 0)

            return carry

        lax.fori_loop(0, HD // PAN, panel_step, 0)

        def finish(b, carry):
            for side, out in enumerate((olb, orb)):
                out[b] = aug[2 * b + side, :, HD:].T
            return carry

        lax.fori_loop(0, count, finish, 0)


LIMIT = 56 * 2**20
SHRINK = 1


def cost(flops, moved, trans=0):
    return pl.CostEstimate(flops=int(flops) // SHRINK, bytes_accessed=int(moved) // SHRINK, transcendentals=0)


def turn(rows, cosine, sine):
    head = rows[:, :128]
    lane = lax.broadcasted_iota(jnp.int32, head.shape, 1)
    partner = jnp.where(lane < RD // 2, pltpu.roll(head, 128 - RD // 2, 1), pltpu.roll(head, RD // 2, 1))
    return jnp.concatenate([head * cosine + partner * sine, rows[:, 128:]], axis=1)


MESH = pl.DeviceIdType.MESH
RIGHT = (
    {0: 0, 1: 3, 2: 6},
    {0: 1, 1: 4, 2: 3},
    {0: 2, 1: 0, 2: 4},
    {1: 1, 2: 0},
    {1: 2, 2: 1},
    {1: 5, 2: 2},
    {2: 7},
    {2: 8},
    {2: 5},
)
LEFT = (
    {3: 9, 2: 6, 1: 3},
    {3: 10, 2: 9, 1: 6},
    {3: 11, 2: 10, 1: 9},
    {2: 7, 1: 4},
    {2: 11, 1: 10},
    {2: 8, 1: 7},
    {1: 11},
    {1: 8},
    {1: 5},
)
SWAPS = ((3, 9), (4, 0), (10, 10), (11, 7))
ROLES = {
    "q": (0, 1),
    "k": (1, 2),
    "v": (2, 12),
    "out": (13, 13),
    "up": ((6, 3), (7, 8), (8, 4), (5, 5)),
    "down": ((9, 6), (12, 11), (14, 14), (15, 15)),
}


def beside(blocks):
    return jnp.concatenate([blocks[b] for b in range(D // HD)], axis=1)


def layer_kernel(
    rows_in, cotangent, segs, matrices, vectors, waves,
    held, units_out, grads_out, sum_0, sum_1, sum_2, extra, rows_out, sums, biases,
    units, grads, weight, act, pre, flipped, column, q, k, v, ga, att, dq, dk, dv, kseq, vseq, keys, vals, stage,
    raw, lines, cosine, sine, seg_row, seg_col,
    right_send, right_recv, left_send, left_recv, swap_send, swap_recv, row_send, row_recv, local,
):
    d, y, c = lax.axis_index("dp"), lax.axis_index("heads"), lax.axis_index("tensor")
    z, x = d // 2, d % 2
    by_x, by_y, by_core = {"dp": d + 1 - 2 * x}, {"heads": 1 - y}, {"tensor": 1 - c}
    shard = 2 * y + c
    block = rows_in.shape[0]
    tokens = units.shape[0]
    head = 32 + (shard * 2 + x) * 3

    barrier = pltpu.get_barrier_semaphore()
    for near in (by_x, by_y, by_core):
        pl.semaphore_signal(barrier, inc=1, device_id=near, device_id_type=MESH)

    @pl.when(z < 3)
    def _():
        pl.semaphore_signal(barrier, inc=1, device_id={"dp": d + 2}, device_id_type=MESH)

    @pl.when(z > 0)
    def _():
        pl.semaphore_signal(barrier, inc=1, device_id={"dp": d - 2}, device_id_type=MESH)

    pl.semaphore_wait(barrier, 4 + (z + 1) // 2 % 2)

    def remote(source, target, send, recv, device):
        return pltpu.make_async_remote_copy(
            src_ref=source, dst_ref=target, send_sem=send, recv_sem=recv, device_id=device, device_id_type=MESH
        )

    def hop(table, step, half, sends, recvs, shift, at):
        place, part, sem = table[step][at], pl.ds(half * 4, 4), 2 * step + half
        source = weight.at[0, part] if step == 0 else held.at[place, part]
        return remote(source, held.at[place, part], sends.at[sem], recvs.at[sem], {"dp": d + 2 * shift})

    ways = ((RIGHT, right_send, right_recv, 1), (LEFT, left_send, left_recv, -1))

    def start(step, half):
        for table, sends, recvs, shift in ways:
            for at in table[step]:

                @pl.when(z == at)
                def _():
                    hop(table, step, half, sends, recvs, shift, at).start()

    def arrived(step, half):
        for table, sends, recvs, shift in ways:
            for at in table[step]:

                @pl.when(z == at + shift)
                def _():
                    hop(table, step, half, sends, recvs, shift, at).wait_recv()

    def sent(step):
        for table, sends, recvs, shift in ways:
            for at in table[step]:

                @pl.when(z == at)
                def _():
                    for half in range(2):
                        hop(table, step, half, sends, recvs, shift, at).wait_send()

    def pass_on(step, half):
        arrived(step, half)
        for later in {6: (7, 8), 7: ()}.get(step, (step + 1,)):
            start(later, half)

    def pump(step):
        pass_on(step, 0)
        pass_on(step, 1)

    def swap(i, side):
        return remote(held.at[SWAPS[i][side]], held.at[12 + i], swap_send.at[i], swap_recv.at[i], by_x)

    def start_swap(i):
        for side in range(2):

            @pl.when(x == side)
            def _():
                swap(i, side).start()

    def fetch(role, slot):
        for side in range(2):

            @pl.when(x == side)
            def _():
                pltpu.make_async_copy(held.at[role[side]], weight.at[slot], local.at[slot]).start()

    def fetched(slot):
        pltpu.make_async_copy(held.at[0], weight.at[slot], local.at[slot]).wait()

    def load(j, at):
        def begin(which):
            pltpu.make_async_copy(matrices.at[0, which * 8 : which * 8 + 8], raw.at[at], local.at[at]).start()

        pl.when((d < 5) | (d == 7))(lambda: begin(j))
        pl.when(d == 5)(lambda: begin(2 - j))
        pl.when(d == 6)(lambda: begin((j + 2) % 3))

    def loaded(j, at):
        pltpu.make_async_copy(matrices.at[0, :8], raw.at[at], local.at[at]).wait()
        weight[j] = raw[at].astype(jnp.bfloat16)

    def keep_own(j):
        for at in range(4):

            @pl.when(z == at)
            def _():
                pltpu.make_async_copy(weight.at[j], held.at[3 * at + j], local.at[8 + j]).start()

    load(0, 0)
    load(1, 1)
    loaded(0, 0)
    start(0, 0)
    start(0, 1)
    load(2, 0)
    keep_own(0)
    rows = rows_in[...]
    centered = rows - jnp.mean(rows, axis=-1, keepdims=True)
    inverse = lax.rsqrt(jnp.mean(centered * centered, axis=-1, keepdims=True) + epsilon_norm)
    units[:block, :] = (centered * inverse).astype(jnp.bfloat16)
    grads[:block, :] = cotangent[...].astype(jnp.bfloat16)
    seg_row[x] = segs[...].astype(jnp.float32)

    def send_rows(kind, i, low, high, there, device):
        array = (units, grads)[kind]
        at = kind * 8 + i
        return remote(
            array.at[low:high], array.at[there : there + high - low], row_send.at[at], row_recv.at[at], device
        )

    half = block // 2

    def row_plan(kind):
        return (
            send_rows(kind, 0, 0, block, block, by_x),
            send_rows(kind, 1, 0, block, 2 * block, by_y),
            send_rows(kind, 2, block, block + half, 3 * block, by_y),
            send_rows(kind, 3, 2 * block + half, 3 * block, 3 * block + half, by_x),
            send_rows(kind, 4, 0, block, 4 * block, by_core),
            send_rows(kind, 5, block, 2 * block, 5 * block, by_core),
            send_rows(kind, 6, 2 * block, 3 * block, 6 * block, by_core),
            send_rows(kind, 7, 3 * block, 4 * block, 7 * block, by_core),
        )

    plans = [row_plan(kind) for kind in range(2)]
    for plan in plans:
        plan[0].start()
        plan[1].start()
        plan[4].start()
    segments = remote(seg_row.at[x], seg_row.at[x], swap_send.at[5], swap_recv.at[5], by_x)
    segments.start()
    loaded(1, 1)
    keep_own(1)
    loaded(2, 0)
    keep_own(2)
    for j in range(3):
        pltpu.make_async_copy(weight.at[j], held.at[j], local.at[8 + j]).wait()
    for i in range(4):
        lines[i : i + 1, :] = jnp.concatenate([vectors[8 * i + b : 8 * i + b + 1, :] for b in range(8)], axis=1)
    pump(0)
    segments.wait()
    for s in range(tokens // LEN):
        row = seg_row[s]
        wide = jnp.broadcast_to(row, (128, LEN)).T
        seg_col[s] = wide
        lane = lax.broadcasted_iota(jnp.int32, (LEN, 128), 1)
        token = lax.broadcasted_iota(jnp.int32, (LEN, 128), 0).astype(jnp.float32)
        first = jnp.sum(jnp.where(row < wide[:, 0:1], 1.0, 0.0), axis=1, keepdims=True)
        turns = (token - first) * waves[...]
        here = slice(s * LEN, (s + 1) * LEN)
        cosine[here, :] = jnp.where(lane < RD, jnp.cos(turns), 1.0)
        flips = jnp.where(lane < RD // 2, -1.0, jnp.where(lane < RD, 1.0, 0.0))
        sine[here, :] = jnp.sin(turns) * flips
    for plan in plans:
        plan[0].wait_recv()
        plan[2].start()
        plan[5].start()
        plan[1].wait_recv()
        plan[3].start()
        plan[6].start()
    pump(1)
    for plan in plans:
        plan[2].wait_recv()
        plan[3].wait_recv()
        plan[7].start()
    pump(2)
    start_swap(0)
    sent(0)
    fetch(ROLES["up"][0], 0)
    fetch(ROLES["down"][0], 1)
    for plan in plans:
        for i in range(4, 8):
            plan[i].wait_recv()
        for i in range(8):
            plan[i].wait_send()
    keep = [pltpu.make_async_copy(units, units_out, local.at[6]), pltpu.make_async_copy(grads, grads_out, local.at[7])]
    for copy in keep:
        copy.start()

    tile = 512

    def run_mlp(slot):
        hidden = SLOTS[0][slot] + (SLOTS[1][slot] - SLOTS[0][slot]) * x
        wu, wd = weight.at[0], weight.at[1]

        def body(i, carry):
            here = pl.ds(pl.multiple_of(i * tile, tile), tile)
            norm = (units[here, :].astype(jnp.float32) * lines[2:3, :] + lines[3:4, :]).astype(jnp.bfloat16)
            inner = dot_nn(norm, wu[...].reshape(D, HD)) + vectors[pl.ds(64 + shard * 8 + hidden, 1), :]
            pull = dot_nt(grads[here, :], beside(wd))
            share = 0.5 + 0.5 * lax.erf(inner * (0.5**0.5))
            act[here, :] = (inner * share).astype(jnp.bfloat16)
            slope = share + inner * jnp.exp(-0.5 * inner * inner) * ((2.0 * 3.141592653589793) ** (-0.5))
            pre[here, :] = (slope * pull).astype(jnp.bfloat16)
            return carry

        lax.fori_loop(0, tokens // tile, body, 0)

    def save_rows(source, i):
        copy = pltpu.make_async_copy(source, rows_out.at[i], local.at[8 + i])
        copy.start()
        return copy

    def put(i, to_0, to_1, sem):
        for side, target in ((0, to_0), (1, to_1)):
            if target is not None:

                @pl.when(x == side)
                def _():
                    pltpu.make_async_copy(stage.at[i], target, local.at[16 + sem]).start()

        def finish():
            for side, target in ((0, to_0), (1, to_1)):
                if target is not None:

                    @pl.when(x == side)
                    def _():
                        pltpu.make_async_copy(stage.at[i], target, local.at[16 + sem]).wait()

        return finish

    def run_down(source, at):
        flipped[:HD, :] = source[...].T

        def body(b, carry):
            here = pl.ds(pl.multiple_of(b * HD, HD), HD)
            stage[at, b] = dot_nn(flipped[:HD, :], grads[:, here]).astype(jnp.bfloat16)
            return carry

        lax.fori_loop(0, D // HD, body, 0)

    def run_up(sources, places, slots, gain, row, offset, more=False):
        for i, source in enumerate(sources):
            wide = source[...]
            flipped[i * HD : (i + 1) * HD, :] = wide.T
            total = jnp.sum(wide.astype(jnp.float32), axis=0, keepdims=True)
            biases[:, offset + i * HD : offset + (i + 1) * HD] = total
            column[i] = jnp.broadcast_to(total, (128, HD)).T

        def body(b, carry):
            here = pl.ds(pl.multiple_of(b * HD, HD), HD)
            gains, shifts = (sums[row : row + 1, here], sums[row + 1 : row + 2, here]) if more else (0.0, 0.0)
            every = dot_nn(flipped[: len(sources) * HD, :], units[:, here])
            for i, (place, slot) in enumerate(zip(places, slots)):
                turned = every[i * HD : (i + 1) * HD, :]
                w = weight[slot, b].T.astype(jnp.float32)
                bias = column[i][:, 0:1]
                gains = gains + jnp.sum(w * turned, axis=0, keepdims=True)
                shifts = shifts + jnp.sum(w * bias, axis=0, keepdims=True)
                result = turned * lines[gain : gain + 1, here] + bias * lines[gain + 1 : gain + 2, here]
                stage[place, b] = result.T.astype(jnp.bfloat16)
            sums[row : row + 1, here] = gains
            sums[row + 1 : row + 2, here] = shifts
            return carry

        lax.fori_loop(0, D // HD, body, 0)

    fetched(0)
    fetched(1)
    run_mlp(0)
    saves = [save_rows(act, 0), save_rows(pre, 1)]
    pass_on(3, 0)
    run_down(act, 0)
    done = put(0, sum_0.at[3], sum_0.at[2], 0)
    pass_on(3, 1)
    start_swap(1)
    run_up([pre], [1], [0], 2, 2, 3 * HD)
    done_up = put(1, sum_0.at[2], sum_0.at[1], 1)
    pump(4)
    start_swap(2)
    pump(5)

    swap(0, 0).wait_recv()
    swap(1, 0).wait_recv()
    for i, role in enumerate(("q", "k", "v", "out")):
        fetch(ROLES[role], 2 + i)
    for i in range(4):
        fetched(2 + i)

    def project_rows(i, carry):
        here = pl.ds(pl.multiple_of(i * tile, tile), tile)
        turns = []
        for u in range(tile // block):
            r = i * (tile // block) + u
            a = (((x + r % 2) % 2) * 2 + (y + r // 2 % 2) % 2) * 2 + (c + r // 4) % 2
            turns.append(pl.ds(pl.multiple_of(a * block, block), block))
        cos_here = jnp.concatenate([cosine[t, :] for t in turns], axis=0)
        sin_here = jnp.concatenate([sine[t, :] for t in turns], axis=0)
        norm = (units[here, :].astype(jnp.float32) * lines[0:1, :] + lines[1:2, :]).astype(jnp.bfloat16)
        q[here, :] = turn(
            dot_nn(norm, weight[2].reshape(D, HD)) + vectors[pl.ds(head + 0, 1), :], cos_here, sin_here
        ).astype(jnp.bfloat16)
        k[here, :] = turn(
            dot_nn(norm, weight[3].reshape(D, HD)) + vectors[pl.ds(head + 1, 1), :], cos_here, sin_here
        ).astype(jnp.bfloat16)
        v[here, :] = (dot_nn(norm, weight[4].reshape(D, HD)) + vectors[pl.ds(head + 2, 1), :]).astype(jnp.bfloat16)
        ga[here, :] = dot_nt(grads[here, :], beside(weight.at[5])).astype(jnp.bfloat16)
        return carry

    lax.fori_loop(0, tokens // tile, project_rows, 0)
    pass_on(6, 0)
    pieces = LEN // block

    def attend(s, carry):
        scale = HD ** (-0.5)
        spots = []
        for i in range(pieces):
            a = s * pieces + i
            r = ((c + a % 2) % 2) * 4 + (x + a // 4) % 2 + 2 * ((y + a // 2 % 2) % 2)
            spots.append(pl.ds(pl.multiple_of(r * block, block), block))
        for i in range(pieces):
            kseq[i * block : (i + 1) * block, :] = k[spots[i], :]
            vseq[i * block : (i + 1) * block, :] = v[spots[i], :]
        keys[...] = jnp.zeros_like(keys)
        vals[...] = jnp.zeros_like(vals)
        for i in range(pieces):
            upto = (i + 1) * block
            angle = pl.ds(pl.multiple_of(s * LEN + i * block, block), block)
            mine, pulled = q[spots[i], :], ga[spots[i], :]
            scores = dot_nt(mine, kseq[:upto, :]) * scale
            to = lax.broadcasted_iota(jnp.int32, (block, upto), 0) + i * block
            of = lax.broadcasted_iota(jnp.int32, (block, upto), 1)
            allowed = (seg_col[s, i * block : upto, 0:1] == seg_row[s, :, :upto]) & (of <= to)
            scores = jnp.where(allowed, scores, -1e30)
            powers = jnp.exp(scores - jnp.max(scores, axis=-1, keepdims=True))
            probs = powers / jnp.sum(powers, axis=-1, keepdims=True)
            low = probs.astype(jnp.bfloat16)
            att[spots[i], :] = dot_nn(low, vseq[:upto, :]).astype(jnp.bfloat16)
            pull = dot_nt(pulled, vseq[:upto, :])
            inner = jnp.sum(probs * pull, axis=-1, keepdims=True)
            gs = (probs * (pull - inner)).astype(jnp.bfloat16)
            turned = turn(dot_nn(gs, kseq[:upto, :]) * scale, cosine[angle, :], -sine[angle, :])
            dq[spots[i], :] = turned.astype(jnp.bfloat16)
            keys[:upto, :] = keys[:upto, :] + dot_tn(gs, mine)
            vals[:upto, :] = vals[:upto, :] + dot_tn(low, pulled)
        for i in range(pieces):
            here = slice(i * block, (i + 1) * block)
            angle = pl.ds(pl.multiple_of(s * LEN + i * block, block), block)
            turned = turn(keys[here, :] * scale, cosine[angle, :], -sine[angle, :])
            dk[spots[i], :] = turned.astype(jnp.bfloat16)
            dv[spots[i], :] = vals[here, :].astype(jnp.bfloat16)

        @pl.when(s == 0)
        def _():
            pass_on(6, 1)
            start_swap(3)

        return carry

    lax.fori_loop(0, tokens // LEN, attend, 0)
    for copy in saves:
        copy.wait()
    saves = [save_rows(a, 4 + i) for i, a in enumerate((att, dq, dk, dv))]
    run_up([dv], [4], [4], 0, 0, 2 * HD, False)

    back_v = remote(stage.at[4], sum_0.at[1], swap_send.at[6], swap_recv.at[6], by_x)
    pl.when(x == 1)(back_v.start)
    done_v = put(4, sum_2.at[0], None, 4)
    pass_on(7, 0)
    done()
    run_down(att, 0)
    done = put(0, None, extra, 5)
    back_out = remote(stage.at[0], sum_1.at[0], swap_send.at[4], swap_recv.at[4], by_x)
    pl.when(x == 0)(back_out.start)
    run_up([dq, dk], [2, 3], [2, 3], 0, 0, 0, True)
    done_qk = [put(2, sum_1.at[0], sum_0.at[0], 2), put(3, sum_0.at[0], sum_2.at[0], 3)]
    pass_on(7, 1)
    fetch(ROLES["up"][1], 0)
    fetch(ROLES["down"][1], 1)

    fetched(0)
    fetched(1)
    run_mlp(1)
    saves += [save_rows(act, 2), save_rows(pre, 3)]
    done_up()
    run_down(act, 1)
    done_up = put(1, extra, sum_0.at[3], 6)
    pl.when(x == 0)(back_v.wait_recv)
    pl.when(x == 1)(back_v.wait_send)
    pl.when(x == 1)(back_out.wait_recv)
    pl.when(x == 0)(back_out.wait_send)
    arrived(8, 0)
    arrived(8, 1)
    for step in range(1, len(RIGHT)):
        sent(step)
    for i in range(4):
        swap(i, 0).wait_send()
    for i in range(2, 4):
        swap(i, 0).wait_recv()
    for copy in saves + keep:
        copy.wait()
    for finish in done_qk + [done_v, done, done_up]:
        finish()


def layer(rows, cotangent, segments, matrices, vectors, waves):
    block = rows.shape[0]
    tokens = 8 * block
    count = tokens // LEN
    anywhere, near = pl.BlockSpec(memory_space=pl.ANY), pl.BlockSpec(memory_space=pltpu.VMEM)
    low, full = jnp.bfloat16, jnp.float32
    group = (D // HD, HD, HD)
    narrow = pltpu.VMEM((tokens, HD), low)
    return pl.pallas_call(
        layer_kernel,
        in_specs=[near] * 3 + [anywhere] + [near] * 2,
        out_specs=[anywhere] * 8 + [near] * 2,
        out_shape=[
            jax.ShapeDtypeStruct((16,) + group, low),
            jax.ShapeDtypeStruct((tokens, D), low),
            jax.ShapeDtypeStruct((tokens, D), low),
        ]
        + [jax.ShapeDtypeStruct((4,) + group, low)] * 3
        + [
            jax.ShapeDtypeStruct(group, low),
            jax.ShapeDtypeStruct((8, tokens, HD), low),
            jax.ShapeDtypeStruct((4, D), full),
            jax.ShapeDtypeStruct((1, 4 * HD), full),
        ],
        scratch_shapes=[
            pltpu.VMEM((tokens, D), low),
            pltpu.VMEM((tokens, D), low),
            pltpu.VMEM((6,) + group, low),
            narrow,
            narrow,
            pltpu.VMEM((3 * HD, tokens), low),
            pltpu.VMEM((3, HD, 128), full),
        ]
        + [narrow] * 8
        + [pltpu.VMEM((LEN, HD), low)] * 2
        + [pltpu.VMEM((LEN, HD), full)] * 2
        + [
            pltpu.VMEM((5,) + group, low),
            pltpu.VMEM((2,) + group, full),
            pltpu.VMEM((4, D), full),
            pltpu.VMEM((tokens, 128), full),
            pltpu.VMEM((tokens, 128), full),
            pltpu.VMEM((count, 1, LEN), full),
            pltpu.VMEM((count, LEN, 128), full),
        ]
        + [pltpu.SemaphoreType.DMA((18,))] * 4
        + [pltpu.SemaphoreType.DMA((7,))] * 2
        + [pltpu.SemaphoreType.DMA((16,))] * 2
        + [pltpu.SemaphoreType.DMA((24,))],
        compiler_params=pltpu.CompilerParams(
            vmem_limit_bytes=63 * 2**20, collective_id=0, has_side_effects=True
        ),
        cost_estimate=cost(6e10, 1e8),
        name="layer",
    )(rows, cotangent, segments, matrices, vectors, waves)


def remote_copy(source, target, send, recv, device):
    return pltpu.make_async_remote_copy(
        src_ref=source, dst_ref=target, send_sem=send, recv_sem=recv, device_id=device, device_id_type=MESH
    )


def greet(peers):
    barrier = pltpu.get_barrier_semaphore()
    for near in peers:
        pl.semaphore_signal(barrier, inc=1, device_id=near, device_id_type=MESH)
    pl.semaphore_wait(barrier, len(peers))


def swap_with(source, send, recv, x, device, to_0, to_1):
    copies = [remote_copy(source, there, send, recv, device) for there in (to_0, to_1)]
    for side in range(2):
        pl.when(x == side)(copies[side].start)
    return copies[0]


def fetch_role(held, role, target, sem, x):
    for side in range(2):

        @pl.when(x == side)
        def _():
            pltpu.make_async_copy(held.at[role[side]], target, sem).start()


def hidden_rows(units, grads, lines, bias, wu, wd, act, pre, before):
    tile = 512

    def body(i, carry):
        here = pl.ds(pl.multiple_of(i * tile, tile), tile)
        before(i)
        norm = (units[here, :].astype(jnp.float32) * lines[2:3, :] + lines[3:4, :]).astype(jnp.bfloat16)
        inner = dot_nn(norm, wu[...].reshape(D, HD)) + bias
        pull = dot_nt(grads[here, :], beside(wd))
        share = 0.5 + 0.5 * lax.erf(inner * (0.5**0.5))
        act[here, :] = (inner * share).astype(jnp.bfloat16)
        slope = share + inner * jnp.exp(-0.5 * inner * inner) * ((2.0 * 3.141592653589793) ** (-0.5))
        pre[here, :] = (slope * pull).astype(jnp.bfloat16)
        return carry

    lax.fori_loop(0, units.shape[0] // tile, body, 0)


def down_blocks(flipped, act, grads, stage):
    flipped[:HD, :] = act[...].T

    def body(b, carry):
        here = pl.ds(pl.multiple_of(b * HD, HD), HD)
        stage[b] = dot_nn(flipped[:HD, :], grads[:, here]).astype(jnp.bfloat16)
        return carry

    lax.fori_loop(0, D // HD, body, 0)


def up_blocks(flipped, column, pres, biases, units, weight, lines, stage, gains_out, shifts_out, early):
    parts = len(pres)
    for i, pre in enumerate(pres):
        wide = pre[...]
        flipped[i * HD : (i + 1) * HD, :] = wide.T
        bias = jnp.sum(wide.astype(jnp.float32), axis=0, keepdims=True)
        biases[i] = bias
        column[i] = jnp.broadcast_to(bias, (128, HD)).T

    def body(b, carry):
        here = pl.ds(pl.multiple_of(b * HD, HD), HD)
        gains, shifts = early[2:3, here], early[3:4, here]
        every = dot_nn(flipped[: parts * HD, :], units[:, here])
        for i in range(parts):
            turned = every[i * HD : (i + 1) * HD, :]
            w = weight[i, b].T.astype(jnp.float32)
            bias = column[i][:, 0:1]
            gains = gains + jnp.sum(w * turned, axis=0, keepdims=True)
            shifts = shifts + jnp.sum(w * bias, axis=0, keepdims=True)
            result = turned * lines[2:3, here] + bias * lines[3:4, here]
            stage[i, b] = result.T.astype(jnp.bfloat16)
        gains_out[:, here] = gains
        shifts_out[:, here] = shifts
        return carry

    lax.fori_loop(0, D // HD, body, 0)


def spread(vectors, lines):
    for i in range(4):
        lines[i : i + 1, :] = jnp.concatenate([vectors[8 * i + b : 8 * i + b + 1, :] for b in range(8)], axis=1)


def third_kernel(
    held, units_in, grads_in, rows_in, vectors, early, extra, sum_1_in, sum_2_in,
    sum_1, sum_2, rows_out, sums, biases,
    units, grads, weight, act, pres, flipped, column, stage, lines,
    swap_send, swap_recv, loads, local,
):
    d, y, c = lax.axis_index("dp"), lax.axis_index("heads"), lax.axis_index("tensor")
    x = d % 2
    shard = 2 * y + c
    tokens = units.shape[0]
    tile = 512
    by_x = {"dp": d + 1 - 2 * x}
    greet([by_x])
    swaps = [swap_with(extra, swap_send.at[0], swap_recv.at[0], x, by_x, sum_1.at[3], sum_1.at[1])]
    for slot, role in ((1, ROLES["up"][2]), (2, ROLES["down"][2])):
        fetch_role(held, role, weight.at[slot], local.at[slot], x)

    def row_loads(i):
        here = pl.ds(pl.multiple_of(i * tile, tile), tile)
        return [
            pltpu.make_async_copy(source.at[here], target.at[here], loads.at[2 * i + j])
            for j, (source, target) in enumerate(((units_in, units), (grads_in, grads)))
        ]

    for i in range(tokens // tile):
        for copy in row_loads(i):
            copy.start()
    fetch_role(held, ROLES["up"][1], weight.at[0], local.at[0], x)
    second = pltpu.make_async_copy(rows_in.at[3], pres.at[0], local.at[3])
    second.start()
    spread(vectors, lines)
    for slot in (1, 2):
        pltpu.make_async_copy(held.at[0], weight.at[slot], local.at[slot]).wait()

    def ready(i):
        for copy in row_loads(i):
            copy.wait()

    hidden = SLOTS[0][2] + (SLOTS[1][2] - SLOTS[0][2]) * x
    bias = vectors[pl.ds(64 + shard * 8 + hidden, 1), :]
    hidden_rows(units, grads, lines, bias, weight.at[1], weight.at[2], act, pres.at[1], ready)
    saves = [
        pltpu.make_async_copy(act, rows_out.at[0], local.at[4]),
        pltpu.make_async_copy(pres.at[1], rows_out.at[1], local.at[5]),
    ]
    for copy in saves:
        copy.start()
    down_blocks(flipped, act, grads, stage.at[2])
    swaps.append(swap_with(stage.at[2], swap_send.at[1], swap_recv.at[1], x, by_x, sum_2.at[3], sum_1.at[3]))
    second.wait()
    pltpu.make_async_copy(held.at[0], weight.at[0], local.at[0]).wait()
    up_blocks(
        flipped, column, [pres.at[0], pres.at[1]], biases, units, weight, lines, stage,
        sums.at[0], sums.at[1], early,
    )
    puts = [
        [pltpu.make_async_copy(stage.at[i], place, local.at[6 + i]) for place in places]
        for i, places in enumerate(((sum_1.at[2], sum_1.at[2]), (sum_2.at[2], sum_1.at[1])))
    ]
    for pair in puts:
        for side in range(2):
            pl.when(x == side)(pair[side].start)
    for copy in swaps + saves:
        copy.wait()
    for pair in puts:
        for side in range(2):
            pl.when(x == side)(pair[side].wait)


def third(held, units, grads, rows, vectors, sums, extra, sum_1, sum_2):
    tokens = units.shape[0]
    anywhere, near = pl.BlockSpec(memory_space=pl.ANY), pl.BlockSpec(memory_space=pltpu.VMEM)
    low, full = jnp.bfloat16, jnp.float32
    group = (D // HD, HD, HD)
    return pl.pallas_call(
        third_kernel,
        in_specs=[anywhere] * 4 + [near] * 2 + [anywhere] * 3,
        out_specs=[anywhere] * 3 + [near] * 2,
        out_shape=[
            jax.ShapeDtypeStruct((4,) + group, low),
            jax.ShapeDtypeStruct((4,) + group, low),
            jax.ShapeDtypeStruct((2, tokens, HD), low),
            jax.ShapeDtypeStruct((2, 1, D), full),
            jax.ShapeDtypeStruct((2, 1, HD), full),
        ],
        input_output_aliases={7: 0, 8: 1},
        scratch_shapes=[
            pltpu.VMEM((tokens, D), low),
            pltpu.VMEM((tokens, D), low),
            pltpu.VMEM((3,) + group, low),
            pltpu.VMEM((tokens, HD), low),
            pltpu.VMEM((2, tokens, HD), low),
            pltpu.VMEM((2 * HD, tokens), low),
            pltpu.VMEM((2, HD, 128), full),
            pltpu.VMEM((3,) + group, low),
            pltpu.VMEM((4, D), full),
            pltpu.SemaphoreType.DMA((2,)),
            pltpu.SemaphoreType.DMA((2,)),
            pltpu.SemaphoreType.DMA((8,)),
            pltpu.SemaphoreType.DMA((8,)),
        ],
        compiler_params=pltpu.CompilerParams(
            vmem_limit_bytes=56 * 2**20, collective_id=1, has_side_effects=True
        ),
        cost_estimate=cost(2e10, 6e7),
        name="third",
    )(held, units, grads, rows, vectors, sums, extra, sum_1, sum_2)


def rest_kernel(
    held, units_in, grads_in, rows_in, third_rows, vectors, early, early_bias, third_sums, third_bias, sum_2_in,
    sum_2, rows_out, total, by_x_out, by_y_out, by_xy_out, own_out,
    units, grads, weight, acts, pre, flipped, column, stage, lines, more, added, biases, current, received, shares, other,
    swap_send, swap_recv, hop_send, hop_recv, loads, local, share_send, share_recv,
):
    d, y, c = lax.axis_index("dp"), lax.axis_index("heads"), lax.axis_index("tensor")
    z, x = d // 2, d % 2
    shard = 2 * y + c
    tokens = units.shape[0]
    block, tile = tokens // 8, 512
    by_x, by_y, by_core = {"dp": d + 1 - 2 * x}, {"heads": 1 - y}, {"tensor": 1 - c}
    by_z = [{"dp": d + 2 - 4 * (z % 2)}, {"dp": d + 4 - 8 * (z // 2)}]
    peers = [by_core, by_y] + by_z + [by_x]
    greet(peers)
    fetch_role(held, ROLES["up"][3], weight.at[0], local.at[0], x)
    fetch_role(held, ROLES["down"][3], weight.at[1], local.at[1], x)

    def row_loads(i):
        here = pl.ds(pl.multiple_of(i * tile, tile), tile)
        return [
            pltpu.make_async_copy(source.at[here], target.at[here], loads.at[2 * i + j])
            for j, (source, target) in enumerate(((units_in, units), (grads_in, grads)))
        ]

    for i in range(tokens // tile):
        for copy in row_loads(i):
            copy.start()
    out_roles = (ROLES["down"][0], ROLES["down"][1], ROLES["out"], ROLES["down"][2])
    out_rows = [rows_in.at[i] for i in (0, 2, 4)] + [third_rows.at[0]]
    for i in range(4):
        fetch_role(held, out_roles[i], weight.at[2 + i], local.at[2 + i], x)
        pltpu.make_async_copy(out_rows[i], acts.at[i], local.at[6 + i]).start()
    spread(vectors, lines)
    more[0:2, :] = early[0:2, :]
    more[2:3, :] = third_sums[0]
    more[3:4, :] = third_sums[1]
    for slot in (0, 1):
        pltpu.make_async_copy(held.at[0], weight.at[slot], local.at[slot]).wait()

    def ready(i):
        for copy in row_loads(i):
            copy.wait()

    hidden = [SLOTS[0][s] + (SLOTS[1][s] - SLOTS[0][s]) * x for s in range(4)]
    bias = vectors[pl.ds(64 + shard * 8 + hidden[3], 1), :]
    hidden_rows(units, grads, lines, bias, weight.at[0], weight.at[1], acts.at[4], pre, ready)
    saves = [pltpu.make_async_copy(pre, rows_out, local.at[10])]
    saves[0].start()
    down_blocks(flipped, acts.at[4], grads, stage.at[1])
    saves.append(swap_with(stage.at[1], swap_send.at[0], swap_recv.at[0], x, by_x, sum_2.at[2], sum_2.at[3]))
    up_blocks(
        flipped, column, [pre], biases, units, weight, lines, stage, added.at[0], added.at[1], more
    )
    put = pltpu.make_async_copy(stage.at[0], sum_2.at[1], local.at[11])
    put.start()
    saves.append(put)

    current[0] = jnp.zeros(current.shape[1:], jnp.float32)
    own = jnp.sum(grads[:block, :].astype(jnp.float32), axis=0, keepdims=True)
    for i, line in enumerate((more[0:1, :], more[1:2, :], added[0], added[1])):
        for b in range(8):
            current[0, 8 * i + b : 8 * i + b + 1, :] = line[:, b * HD : (b + 1) * HD]
    for b in range(8):
        current[0, 56 + b : 57 + b, :] = own[:, b * HD : (b + 1) * HD]
        current[0, 96 + b : 97 + b, :] = own[:, b * HD : (b + 1) * HD]
    for i in range(3):
        at = 32 + (shard * 2 + x) * 3 + i
        current[0, pl.ds(at, 1), :] = early_bias[:, i * HD : (i + 1) * HD]
    for i, line in enumerate((early_bias[:, 3 * HD :], third_bias[0], third_bias[1], biases[0])):
        current[0, pl.ds(64 + shard * 8 + hidden[i], 1), :] = line
    hops = [
        remote_copy(current.at[i], received.at[i], hop_send.at[i], hop_recv.at[i], near) for i, near in enumerate(peers)
    ]

    def finish_hop(i):
        hops[i].wait()
        result = current[i] + received[i]
        if i + 1 < len(peers):
            current[i + 1] = result
            hops[i + 1].start()
        else:
            total[...] = result

    hops[0].start()

    for i in range(4):
        pltpu.make_async_copy(held.at[0], weight.at[2 + i], local.at[2 + i]).wait()
        pltpu.make_async_copy(rows_in.at[0], acts.at[i], local.at[6 + i]).wait()
    by_slot = (2, 3, 4, 5, 1)

    def share_rows(i):
        here = slice(i * tile, (i + 1) * tile)
        left = jnp.concatenate([acts[j, here, :] for j in range(5)], axis=1)
        for b in range(D // HD):
            right = jnp.concatenate([weight[slot, b] for slot in by_slot], axis=0)
            yield slice(b * HD, (b + 1) * HD), dot_nn(left, right)

    sends = [
        remote_copy(
            shares.at[i * tile : (i + 1) * tile],
            other.at[i * tile : (i + 1) * tile],
            share_send.at[i],
            share_recv.at[i],
            by_core,
        )
        for i in range(2)
    ]
    for i in range(2):
        for columns, result in share_rows(2 + i):
            shares[i * tile : (i + 1) * tile, columns] = result.astype(jnp.bfloat16)
        sends[i].start()
        finish_hop(i)
    for copy in sends:
        copy.wait_send()
    for i in range(2):
        sends[i].wait_recv()
        for columns, result in share_rows(i):
            theirs = other[i * tile : (i + 1) * tile, columns].astype(jnp.float32)
            shares[i * tile : (i + 1) * tile, columns] = (result + theirs).astype(jnp.bfloat16)
        finish_hop(2 + i)
    for i, target in enumerate((own_out, by_x_out, by_y_out, by_xy_out)):
        copy = pltpu.make_async_copy(shares.at[i * block : (i + 1) * block], target.at[0], local.at[12 + i])
        copy.start()
        saves.append(copy)
    finish_hop(4)
    for copy in saves:
        copy.wait()


def rest(held, units, grads, rows, third_rows, vectors, sums, biases, third_sums, third_bias, sum_2):
    tokens = units.shape[0]
    anywhere, near = pl.BlockSpec(memory_space=pl.ANY), pl.BlockSpec(memory_space=pltpu.VMEM)
    low, full = jnp.bfloat16, jnp.float32
    group = (D // HD, HD, HD)
    table = vectors.shape
    return pl.pallas_call(
        rest_kernel,
        in_specs=[anywhere] * 5 + [near] * 5 + [anywhere],
        out_specs=[anywhere] * 2 + [near] + [anywhere] * 4,
        out_shape=[
            jax.ShapeDtypeStruct((4,) + group, low),
            jax.ShapeDtypeStruct((tokens, HD), low),
            jax.ShapeDtypeStruct(table, full),
        ]
        + [jax.ShapeDtypeStruct((2, tokens // 8, D), low)] * 4,
        input_output_aliases={10: 0},
        scratch_shapes=[
            pltpu.VMEM((tokens, D), low),
            pltpu.VMEM((tokens, D), low),
            pltpu.VMEM((6,) + group, low),
            pltpu.VMEM((5, tokens, HD), low),
            pltpu.VMEM((tokens, HD), low),
            pltpu.VMEM((HD, tokens), low),
            pltpu.VMEM((1, HD, 128), full),
            pltpu.VMEM((2,) + group, low),
            pltpu.VMEM((4, D), full),
            pltpu.VMEM((4, D), full),
            pltpu.VMEM((2, 1, D), full),
            pltpu.VMEM((1, 1, HD), full),
            pltpu.VMEM((5,) + table, full),
            pltpu.VMEM((5,) + table, full),
            pltpu.VMEM((tokens // 2, D), low),
            pltpu.VMEM((tokens // 2, D), low),
            pltpu.SemaphoreType.DMA((1,)),
            pltpu.SemaphoreType.DMA((1,)),
            pltpu.SemaphoreType.DMA((5,)),
            pltpu.SemaphoreType.DMA((5,)),
            pltpu.SemaphoreType.DMA((8,)),
            pltpu.SemaphoreType.DMA((16,)),
            pltpu.SemaphoreType.DMA((2,)),
            pltpu.SemaphoreType.DMA((2,)),
        ],
        compiler_params=pltpu.CompilerParams(
            vmem_limit_bytes=60 * 2**20, collective_id=3, has_side_effects=True
        ),
        cost_estimate=cost(4e10, 6e7),
        name="rest",
    )(held, units, grads, rows, third_rows, vectors, sums, biases, third_sums, third_bias, sum_2)


def input_kernel(
    held, rows_in, third_rows, late, gains, by_x_in, by_y_in, by_xy_in, own_in,
    by_x_out, by_y_out, by_xy_out, own_out,
    weight, rows, shares, other,
    local, share_send, share_recv,
):
    x, c = lax.axis_index("dp") % 2, lax.axis_index("tensor")
    by_core = {"tensor": 1 - c}
    barrier = pltpu.get_barrier_semaphore()
    pl.semaphore_signal(barrier, inc=1, device_id=by_core, device_id_type=MESH)
    pl.semaphore_wait(barrier, 1)
    tokens = rows.shape[1]
    block, tile = tokens // 8, 512
    roles = (ROLES["q"], ROLES["k"], ROLES["v"]) + ROLES["up"]
    sources = [rows_in.at[i] for i in (5, 6, 7, 1, 3)] + [third_rows.at[1], late]
    for i, (role, source) in enumerate(zip(roles, sources)):
        for side in range(2):

            @pl.when(x == side)
            def _():
                pltpu.make_async_copy(held.at[role[side]], weight.at[i], local.at[i]).start()

        pltpu.make_async_copy(source, rows.at[i], local.at[7 + i]).start()
    for i, source in enumerate(sources):
        pltpu.make_async_copy(held.at[0], weight.at[i], local.at[i]).wait()
        pltpu.make_async_copy(source, rows.at[i], local.at[7 + i]).wait()

    def share_rows(i):
        here = pl.ds(i * tile, tile)
        sides = ((0, 3), (3, 7))
        lefts = [jnp.concatenate([rows[r, here, :] for r in range(*side)], axis=1) for side in sides]
        for b in range(D // HD):
            columns = slice(b * HD, (b + 1) * HD)
            parts = []
            for j, side in enumerate(sides):
                right = jnp.concatenate([weight[r, b] for r in range(*side)], axis=1)
                parts.append(dot_nt(lefts[j], right) * gains[j : j + 1, columns])
            yield columns, parts[0] + parts[1]

    sends = [
        pltpu.make_async_remote_copy(
            src_ref=shares.at[i * tile : (i + 1) * tile],
            dst_ref=other.at[i * tile : (i + 1) * tile],
            send_sem=share_send.at[i],
            recv_sem=share_recv.at[i],
            device_id=by_core,
            device_id_type=MESH,
        )
        for i in range(2)
    ]
    for i in range(2):
        for columns, result in share_rows(2 + i):
            shares[i * tile : (i + 1) * tile, columns] = result.astype(jnp.bfloat16)
        sends[i].start()
    for copy in sends:
        copy.wait_send()
    for i in range(2):
        sends[i].wait_recv()
        for columns, result in share_rows(i):
            theirs = other[i * tile : (i + 1) * tile, columns].astype(jnp.float32)
            shares[i * tile : (i + 1) * tile, columns] = (result + theirs).astype(jnp.bfloat16)
    for i, target in enumerate((own_out, by_x_out, by_y_out, by_xy_out)):
        pltpu.make_async_copy(shares.at[i * block : (i + 1) * block], target.at[1], local.at[14 + i]).start()
    for i, target in enumerate((own_out, by_x_out, by_y_out, by_xy_out)):
        pltpu.make_async_copy(shares.at[i * block : (i + 1) * block], target.at[1], local.at[14 + i]).wait()


def input_share(held, rows, third_rows, late, gains, parts):
    tokens = rows.shape[1]
    anywhere = pl.BlockSpec(memory_space=pl.ANY)
    low = jnp.bfloat16
    return pl.pallas_call(
        input_kernel,
        in_specs=[anywhere] * 4 + [pl.BlockSpec(memory_space=pltpu.VMEM)] + [anywhere] * 4,
        out_specs=[anywhere] * 4,
        out_shape=[jax.ShapeDtypeStruct((2, tokens // 8, D), low)] * 4,
        input_output_aliases={5 + i: i for i in range(4)},
        scratch_shapes=[
            pltpu.VMEM((7, D // HD, HD, HD), low),
            pltpu.VMEM((7, tokens, HD), low),
            pltpu.VMEM((tokens // 2, D), low),
            pltpu.VMEM((tokens // 2, D), low),
            pltpu.SemaphoreType.DMA((18,)),
            pltpu.SemaphoreType.DMA((2,)),
            pltpu.SemaphoreType.DMA((2,)),
        ],
        compiler_params=pltpu.CompilerParams(vmem_limit_bytes=LIMIT, collective_id=2, has_side_effects=True),
        cost_estimate=cost(2 * 7 * tokens * D * HD, 5e7),
        name="input_share",
    )(held, rows, third_rows, late, gains, *parts)


def soap_part(places, grad, blocks, previous):
    total, count = blocks[0].shape[0], grad.shape[0]
    mats = 2 * count
    own = pl.BlockSpec((GROUP, HD, HD), lambda i, at: (i, 0, 0))
    some = pl.BlockSpec((GROUP, HD, HD), lambda i, at: (at[0] * (count // GROUP) + i, 0, 0))
    whole = pl.BlockSpec((count, HD, HD), lambda i, at: (at[0], 0, 0))
    full = jax.ShapeDtypeStruct((total, HD, HD), jnp.float32)
    shapes = [full, jax.ShapeDtypeStruct((total, HD, HD), jnp.bfloat16)] + [full] * 6
    extra = [] if previous is None else list(previous)

    def body(at, *refs):
        soap_kernel(count, *refs[:8], *refs[8 + len(extra) :])

    return pl.pallas_call(
        body,
        grid_spec=pltpu.PrefetchScalarGridSpec(
            num_scalar_prefetch=1,
            grid=(count // GROUP,),
            in_specs=[own] + [some] * 7 + [pl.BlockSpec(memory_space=pl.ANY)] * len(extra),
            out_specs=[some] * 6 + [whole] * 2,
            scratch_shapes=[
                pltpu.VMEM((mats, HD, 2 * HD), jnp.float32),
                pltpu.VMEM((PAN * PACK, 128), jnp.float32),
            ],
        ),
        out_shape=shapes,
        input_output_aliases={9 + i: i for i in range(len(extra))},
        compiler_params=pltpu.CompilerParams(vmem_limit_bytes=LIMIT),
        cost_estimate=cost(count * 40 * 2 * HD**3 * 3, count * 16 * 4 * HD * HD),
        name="soap",
    )(places, grad, *blocks, *extra)


def adam_vector(grad, params, first, second):
    first_new = beta_one * first + (1.0 - beta_one) * grad
    second_new = beta_two * second + (1.0 - beta_two) * grad * grad
    direction = (
        first_new
        / (1.0 - beta_one**STEP)
        / (jnp.sqrt(second_new / (1.0 - beta_two**STEP)) + epsilon_adam)
    )
    return (params - rate_vector * direction, first_new, second_new)


ALL = ("dp", "heads", "tensor")
SUMMED = ((1, 0, 2), (1, 0, 2), (0, 1, 2), (0, 1, 2), (0, 1, 2), (2, 0, 1), (2, 0, 1), (2, 0, 1))
SLOTS = ((4, 5, 6, 0), (1, 7, 2, 3))


def places():
    for z in range(4):
        for x in range(2):
            for y in range(2):
                for c in range(2):
                    yield z, x, y, c


def index_of(z, x, y, c):
    return ((z * 2 + x) * 2 + y) * 2 + c


def move(array, target):
    return lax.ppermute(array, ALL, [(index_of(*at), index_of(*target(*at))) for at in places()])


LINES = [[index_of(z, x, y, c) for z in range(4)] for x in range(2) for y in range(2) for c in range(2)]


def over_y(array):
    return move(array, lambda z, x, y, c: (z, x, 1 - y, c))


def over_x(array):
    return move(array, lambda z, x, y, c: (z, 1 - x, y, c))


def over_xy(array):
    return move(array, lambda z, x, y, c: (z, 1 - x, 1 - y, c))


def after(array, *earlier):
    return lax.optimization_barrier((array, *earlier))[0]


def plane_shards(
    block_input,
    cotangent,
    segments,
    matrices,
    first_moment,
    second_moment,
    left_stat,
    right_stat,
    left_basis,
    right_basis,
    vectors,
    vec_first,
    vec_second,
):
    d = lax.axis_index("dp")
    x = d % 2
    gain_one, gain_two = vectors[:D].reshape(1, D), vectors[2 * D : 3 * D].reshape(1, D)
    bias_out, bias_down = vectors[7 * D : 8 * D], vectors[8 * D + FF : 9 * D + FF]
    table = vectors.reshape(-1, HD)
    frequency = 1.0 / rope_base ** (jnp.arange(0, RD, 2).astype(jnp.float32) / RD)
    turns = jnp.concatenate([frequency, frequency, jnp.zeros((128 - RD,), jnp.float32)]).reshape(1, 128)
    held, units, grads, sum_0, sum_1, sum_2, extra, rows, sums, biases = layer(
        block_input, cotangent, segments, matrices, table, turns
    )
    sum_1, sum_2, third_rows, third_sums, third_bias = third(
        held, units, grads, rows, table, sums, extra, sum_1, sum_2
    )
    sum_2, late, grad_table, *parts = rest(
        held, units, grads, rows, third_rows, table, sums, biases, third_sums, third_bias, sum_2
    )
    owned = []
    for send in (sum_0, sum_1, sum_2):
        owned.append(lax.psum_scatter(send, ALL, scatter_dimension=0, tiled=False, axis_index_groups=LINES))

    parts = input_share(held, rows, third_rows, late, jnp.concatenate([gain_one, gain_two]), parts)
    blocks = [a[0] for a in (matrices, first_moment, second_moment, left_stat, right_stat, left_basis, right_basis)]
    summed_order = jnp.array(SUMMED, jnp.int32)[d]
    updated = soap_part(summed_order[0:1], after(owned[0], parts[0]), blocks, None)
    updated = soap_part(summed_order[1:2], after(owned[1], updated[1]), blocks, updated)
    by_x, by_y, by_xy, own = parts
    totals = (
        after(own, updated[1]).astype(jnp.float32)
        + over_x(by_x).astype(jnp.float32)
        + over_y(by_y).astype(jnp.float32)
        + over_xy(by_xy).astype(jnp.float32)
    )
    output = block_input + totals[0] + bias_out + bias_down
    e = totals[1]
    middle = jnp.mean(block_input, axis=-1, keepdims=True)
    centered = block_input - middle
    inverse = lax.rsqrt(jnp.mean(centered * centered, axis=-1, keepdims=True) + epsilon_norm)
    unit = centered * inverse
    grad_input = cotangent + inverse * (
        e - jnp.mean(e, axis=-1, keepdims=True) - unit * jnp.mean(e * unit, axis=-1, keepdims=True)
    )
    grad_vectors = grad_table.reshape(-1)
    updated = soap_part(summed_order[2:3], after(owned[2], output, grad_input), blocks, updated)
    new_vectors, new_vec_first, new_vec_second = adam_vector(grad_vectors, vectors, vec_first, vec_second)
    return (output, grad_input, *[u[None] for u in updated], new_vectors, new_vec_first, new_vec_second)


def generic_shards(
    block_input,
    cotangent,
    segments,
    matrices,
    first_moment,
    second_moment,
    left_stat,
    right_stat,
    left_basis,
    right_basis,
    vectors,
    vec_first,
    vec_second,
):
    group_size = lax.axis_size(("heads", "tensor"))
    member = lax.axis_index(("heads", "tensor"))
    heads_here = H // group_size
    hidden_here = FF // group_size
    row_blocks = D // HD
    hidden_blocks = hidden_here // HD
    seq_count = segments.shape[0]
    tokens_here = seq_count * LEN
    own_rows = block_input.shape[0]
    qkv_offset = 4 * D + member * heads_here * 3 * HD
    up_offset = 8 * D + member * hidden_here
    gain_one = vectors[0:D]
    shift_one = vectors[D : 2 * D]
    gain_two = vectors[2 * D : 3 * D]
    shift_two = vectors[3 * D : 4 * D]
    bias_qkv = lax.dynamic_slice_in_dim(vectors, qkv_offset, heads_here * 3 * HD).reshape(
        heads_here, 3, HD
    )
    bias_out = vectors[7 * D : 8 * D]
    bias_up = lax.dynamic_slice_in_dim(vectors, up_offset, hidden_here)
    bias_down = vectors[8 * D + FF : 9 * D + FF]
    gathered = lax.all_gather(matrices.astype(jnp.bfloat16), "dp", axis=1, tiled=True)[0]
    w_qkv, w_out, w_up, w_down = unpack_blocks(gathered, heads_here, row_blocks, hidden_blocks)
    normed_one, unit_one, inverse_one = layer_norm(block_input, gain_one, shift_one)
    normed_two, unit_two, inverse_two = layer_norm(block_input, gain_two, shift_two)
    grad_own = cotangent.astype(jnp.bfloat16)
    norm_one, norm_two, grad_rows = (
        lax.all_gather(normed_one.astype(jnp.bfloat16), ("heads", "tensor"), axis=0, tiled=True),
        lax.all_gather(normed_two.astype(jnp.bfloat16), ("heads", "tensor"), axis=0, tiled=True),
        lax.all_gather(grad_own, ("heads", "tensor"), axis=0, tiled=True),
    )
    norm_one3 = norm_one.reshape(tokens_here, row_blocks, HD)
    norm_two3 = norm_two.reshape(tokens_here, row_blocks, HD)
    projected = (
        jnp.einsum("tbr,hqbrc->thqc", norm_one3, w_qkv, preferred_element_type=jnp.float32)
        + bias_qkv
    )
    shaped = projected.reshape(seq_count, LEN, heads_here, 3, HD)
    cosine, sine = angles(segments)
    queries = rotate(shaped[:, :, :, 0], cosine, sine).astype(jnp.bfloat16)
    keys_rot = rotate(shaped[:, :, :, 1], cosine, sine).astype(jnp.bfloat16)
    values = shaped[:, :, :, 2].astype(jnp.bfloat16)
    attended, log_total = lax.map(seq_forward, (queries, keys_rot, values, segments))
    attend_low = attended.astype(jnp.bfloat16).reshape(tokens_here, heads_here, HD)
    pre_act = (
        jnp.einsum("tbr,kbrc->tkc", norm_two3, w_up, preferred_element_type=jnp.float32).reshape(
            tokens_here, hidden_here
        )
        + bias_up
    )
    act_low = gelu_exact(pre_act).astype(jnp.bfloat16)
    rows_act = act_low.reshape(lax.axis_size(("heads", "tensor")) * own_rows, hidden_blocks, HD)
    first_term = jnp.einsum("thr,hbrc->tbc", attend_low, w_out, preferred_element_type=jnp.float32)
    second_term = jnp.einsum("tkr,kbrc->tbc", rows_act, w_down, preferred_element_type=jnp.float32)
    summed = lax.psum_scatter(
        (first_term + second_term).reshape(lax.axis_size(("heads", "tensor")) * own_rows, D),
        ("heads", "tensor"),
        scatter_dimension=0,
        tiled=True,
    )
    output = block_input + summed + bias_out + bias_down
    regathered = lax.all_gather(matrices.astype(jnp.bfloat16), "dp", axis=1, tiled=True)[0]
    w_qkv, w_out, w_up, w_down = unpack_blocks(regathered, heads_here, row_blocks, hidden_blocks)
    grad_rows3 = grad_rows.reshape(tokens_here, row_blocks, HD)
    act_low3 = act_low.reshape(tokens_here, hidden_blocks, HD)
    grad_act = jnp.einsum(
        "tbc,kbrc->tkr", grad_rows3, w_down, preferred_element_type=jnp.float32
    ).reshape(tokens_here, hidden_here)
    gelu_pull = jax.vjp(gelu_exact, pre_act)[1]
    grad_pre = gelu_pull(grad_act)[0].astype(jnp.bfloat16)
    grad_pre3 = grad_pre.reshape(tokens_here, hidden_blocks, HD)
    grad_attend = jnp.einsum(
        "tbc,hbrc->thr", grad_rows3, w_out, preferred_element_type=jnp.float32
    ).astype(jnp.bfloat16)
    grad_attend = grad_attend.reshape(seq_count, LEN, heads_here, HD)
    grad_queries, grad_keys, grad_values = lax.map(
        seq_backward, (queries, keys_rot, values, segments, log_total, grad_attend)
    )
    grad_raw = jnp.stack(
        [rotate(grad_queries, cosine, -sine), rotate(grad_keys, cosine, -sine), grad_values], axis=3
    )
    grad_raw = grad_raw.astype(jnp.bfloat16).reshape(tokens_here, heads_here, 3, HD)
    rows_up = grad_pre.reshape(lax.axis_size(("heads", "tensor")) * own_rows, hidden_blocks, HD)
    back_one = jnp.einsum(
        "thqc,hqbrc->tbr", grad_raw, w_qkv, preferred_element_type=jnp.float32
    ).reshape(lax.axis_size(("heads", "tensor")) * own_rows, D)
    back_two = jnp.einsum(
        "tkc,kbrc->tbr", rows_up, w_up, preferred_element_type=jnp.float32
    ).reshape(lax.axis_size(("heads", "tensor")) * own_rows, D)
    grad_norms = lax.psum_scatter(
        jnp.stack([back_one, back_two], axis=1),
        ("heads", "tensor"),
        scatter_dimension=0,
        tiled=True,
    )
    grad_norm_one = grad_norms[:, 0]
    grad_norm_two = grad_norms[:, 1]
    grad_input = (
        cotangent
        + norm_back(grad_norm_one, unit_one, inverse_one, gain_one)
        + norm_back(grad_norm_two, unit_two, inverse_two, gain_two)
    )
    grad_bias_rows = jnp.sum(grad_own, axis=0, dtype=jnp.float32)
    pieces = jnp.concatenate(
        [
            jnp.sum(grad_norm_one * unit_one, axis=0),
            jnp.sum(grad_norm_one, axis=0),
            jnp.sum(grad_norm_two * unit_two, axis=0),
            jnp.sum(grad_norm_two, axis=0),
            jnp.zeros((3 * D,), jnp.float32),
            grad_bias_rows,
            jnp.zeros((FF,), jnp.float32),
            grad_bias_rows,
        ]
    )
    pieces = lax.dynamic_update_slice_in_dim(
        pieces, jnp.sum(grad_raw, axis=0, dtype=jnp.float32).reshape(-1), qkv_offset, 0
    )
    pieces = lax.dynamic_update_slice_in_dim(
        pieces, jnp.sum(grad_pre, axis=0, dtype=jnp.float32), up_offset, 0
    )
    grad_vectors = lax.psum(pieces, ("dp", "heads", "tensor"))
    grad_down = jnp.einsum(
        "tkr,tbc->kbrc", act_low3, grad_rows3, preferred_element_type=jnp.float32
    )
    grad_up = jnp.einsum("tbr,tkc->kbrc", norm_two3, grad_pre3, preferred_element_type=jnp.float32)
    grad_out = jnp.einsum(
        "thr,tbc->hbrc", attend_low, grad_rows3, preferred_element_type=jnp.float32
    )
    grad_qkv = jnp.einsum(
        "tbr,thqc->hqbrc", norm_one3, grad_raw, preferred_element_type=jnp.float32
    )
    attn_grads = jnp.concatenate([grad_qkv, grad_out[:, None]], axis=1).reshape(-1, HD, HD)
    all_grads = jnp.concatenate(
        [attn_grads, grad_up.reshape(-1, HD, HD), grad_down.reshape(-1, HD, HD)], axis=0
    )[None]
    owned = lax.psum_scatter(all_grads, "dp", scatter_dimension=1, tiled=True)
    blocks = [a[0] for a in (matrices, first_moment, second_moment, left_stat, right_stat, left_basis, right_basis)]
    updated = [u[None] for u in soap_part(jnp.zeros((1,), jnp.int32), owned[0], blocks, None)]
    new_vectors, new_vec_first, new_vec_second = adam_vector(
        grad_vectors, vectors, vec_first, vec_second
    )
    return (
        output,
        grad_input,
        updated[0],
        updated[1],
        updated[2],
        updated[3],
        updated[4],
        updated[5],
        updated[6],
        updated[7],
        new_vectors,
        new_vec_first,
        new_vec_second,
    )


def solution(mesh):
    in_specs = (
        P(("dp", "heads", "tensor"), None),
        P(("dp", "heads", "tensor"), None),
        P("dp", None),
        P(("heads", "tensor"), "dp", None, None),
        P(("heads", "tensor"), "dp", None, None),
        P(("heads", "tensor"), "dp", None, None),
        P(("heads", "tensor"), "dp", None, None),
        P(("heads", "tensor"), "dp", None, None),
        P(("heads", "tensor"), "dp", None, None),
        P(("heads", "tensor"), "dp", None, None),
        P(),
        P(),
        P(),
    )
    out_specs = (
        P(("dp", "heads", "tensor"), None),
        P(("dp", "heads", "tensor"), None),
        P(("heads", "tensor"), "dp", None, None),
        P(("heads", "tensor"), "dp", None, None),
        P(("heads", "tensor"), "dp", None, None),
        P(("heads", "tensor"), "dp", None, None),
        P(("heads", "tensor"), "dp", None, None),
        P(("heads", "tensor"), "dp", None, None),
        P(("heads", "tensor"), "dp", None, None),
        P(("heads", "tensor"), "dp", None, None),
        P(),
        P(),
        P(),
    )
    plane = dict(mesh.shape) == {"dp": 8, "heads": 2, "tensor": 2}
    shards = plane_shards if plane else generic_shards
    return jax.shard_map(shards, mesh=mesh, in_specs=in_specs, out_specs=out_specs, check_vma=False)
```

```python
import functools

import jax
import jax.numpy as jnp
from jax import lax
from jax.experimental import pallas as pl
from jax.experimental.pallas import tpu as pltpu
from jax.sharding import PartitionSpec as P

D = 2048
H = 8
HD = 256
RD = 64
FF = 8192
LEN = 1024
STEP = 10


epsilon_norm = 1e-05
epsilon_adam = 1e-08
rope_base = 10000.0
beta_one = 0.9
beta_two = 0.95
beta_stat = 0.95
rate_matrix = 0.05
rate_vector = 0.1
weight_decay = 0.01
PAN = 32
PACK = 16
WIDE = 8
UNROLL = 16
GROUP = 2


def layer_norm(rows, gain, shift):
    middle = jnp.mean(rows, axis=-1, keepdims=True)
    centered = rows - middle
    spread = jnp.mean(centered * centered, axis=-1, keepdims=True)
    inverse = lax.rsqrt(spread + epsilon_norm)
    unit = centered * inverse
    return (unit * gain + shift, unit, inverse)


def norm_back(grad, unit, inverse, gain):
    scaled = grad * gain
    return inverse * (
        scaled
        - jnp.mean(scaled, axis=-1, keepdims=True)
        - unit * jnp.mean(scaled * unit, axis=-1, keepdims=True)
    )


def angles(segments):
    seq_count = segments.shape[0]
    column = jnp.arange(LEN, dtype=jnp.int32)[None, :]
    border = jnp.concatenate(
        [jnp.ones((seq_count, 1), jnp.bool_), segments[:, 1:] != segments[:, :-1]], axis=1
    )
    starts = lax.cummax(jnp.where(border, column, 0), axis=1)
    places = (column - starts).astype(jnp.float32)
    frequency = 1.0 / rope_base ** (jnp.arange(0, RD, 2).astype(jnp.float32) / RD)
    turns = places[:, :, None] * frequency[None, None, :]
    return (jnp.cos(turns)[:, :, None, :], jnp.sin(turns)[:, :, None, :])


def rotate(part, cosine, sine):
    half_dims = RD // 2
    first_half = part[..., :half_dims]
    second_half = part[..., half_dims:RD]
    return jnp.concatenate(
        [
            first_half * cosine - second_half * sine,
            second_half * cosine + first_half * sine,
            part[..., RD:],
        ],
        axis=-1,
    )


def unpack_blocks(blocks, heads_here, row_blocks, hidden_blocks):
    attn_count = heads_here * 4 * row_blocks
    up_count = hidden_blocks * row_blocks
    attn_part = blocks[:attn_count].reshape(heads_here, 4, row_blocks, HD, HD)
    w_up = blocks[attn_count : attn_count + up_count].reshape(hidden_blocks, row_blocks, HD, HD)
    w_down = blocks[attn_count + up_count :].reshape(hidden_blocks, row_blocks, HD, HD)
    return (attn_part[:, :3], attn_part[:, 3], w_up, w_down)


def masked_scores(queries, keys_rot, segment_row):
    column = jnp.arange(LEN)
    allowed = (segment_row[:, None] == segment_row[None, :]) & (column[None, :] <= column[:, None])
    scores = jnp.einsum(
        "qhd,khd->hqk", queries, keys_rot, preferred_element_type=jnp.float32
    ) * HD ** (-0.5)
    return jnp.where(allowed[None], scores, -1e30)


def seq_forward(items):
    queries, keys_rot, values, segment_row = items
    scores = masked_scores(queries, keys_rot, segment_row)
    row_max = jnp.max(scores, axis=-1, keepdims=True)
    powers = jnp.exp(scores - row_max)
    row_total = jnp.sum(powers, axis=-1, keepdims=True)
    probs_low = (powers / row_total).astype(jnp.bfloat16)
    attended = jnp.einsum("hqk,khd->qhd", probs_low, values, preferred_element_type=jnp.float32)
    return (attended, (row_max + jnp.log(row_total))[..., 0])


def seq_backward(items):
    queries, keys_rot, values, segment_row, log_total, grad_attend = items
    scores = masked_scores(queries, keys_rot, segment_row)
    probs = jnp.exp(scores - log_total[..., None])
    grad_probs = jnp.einsum("qhd,khd->hqk", grad_attend, values, preferred_element_type=jnp.float32)
    inner = jnp.sum(probs * grad_probs, axis=-1, keepdims=True)
    grad_scores = (probs * (grad_probs - inner)).astype(jnp.bfloat16)
    grad_queries = jnp.einsum(
        "hqk,khd->qhd", grad_scores, keys_rot, preferred_element_type=jnp.float32
    ) * HD ** (-0.5)
    grad_keys = jnp.einsum(
        "hqk,qhd->khd", grad_scores, queries, preferred_element_type=jnp.float32
    ) * HD ** (-0.5)
    grad_values = jnp.einsum(
        "hqk,qhd->khd", probs.astype(jnp.bfloat16), grad_attend, preferred_element_type=jnp.float32
    )
    return (grad_queries, grad_keys, grad_values)


def gelu_exact(inputs):
    return jax.nn.gelu(inputs, approximate=False)


def dot_nn(a, b):
    return lax.dot_general(a, b, (((1,), (0,)), ((), ())), preferred_element_type=jnp.float32)


def dot_nt(a, b):
    return lax.dot_general(a, b, (((1,), (1,)), ((), ())), preferred_element_type=jnp.float32)


def dot_tn(a, b):
    return lax.dot_general(a, b, (((0,), (0,)), ((), ())), preferred_element_type=jnp.float32)


def split(x):
    high = x.astype(jnp.bfloat16)
    return high, (x - high.astype(jnp.float32)).astype(jnp.bfloat16)


def three(dot, a, b):
    return dot(a[0], b[0]) + (dot(a[0], b[1]) + dot(a[1], b[0]))


def eliminate(diag):
    tiles = PAN * PACK // 128
    per = 128 // PACK
    flat = diag[: PAN * PACK, :].T[:PAN]
    full = [flat[:, t * 128 : (t + 1) * 128] for t in range(tiles)]
    row = lax.broadcasted_iota(jnp.int32, (PAN, 128), 0)
    lane = lax.broadcasted_iota(jnp.int32, (PAN, 128), 1)
    inverse = [jnp.where(row == lane // PACK + t * per, 1.0, 0.0) for t in range(tiles)]

    def column(k):
        return jnp.take_along_axis(full[k // per], lane % PACK + k % per * PACK, axis=1)

    for k in range(0, PAN, WIDE):
        columns, scales, crosses = [column(k + i) for i in range(WIDE)], [], []
        for i in range(WIDE):
            for j in range(i):
                columns[i] = columns[i] - columns[j] * crosses[j][i]
            scales.append(lax.rsqrt(columns[i][k + i : k + i + 1]))
            columns[i] = columns[i] * scales[i]
            crosses.append([columns[i][k + n : k + n + 1] for n in range(WIDE)])
        columns = [jnp.where(row >= k + WIDE, c, 0.0) for c in columns]

        def step(tile):
            tops = []
            for i in range(WIDE):
                top = tile[k + i : k + i + 1]
                for j in range(i):
                    top = top - crosses[j][i] * tops[j]
                tops.append(top * scales[i])
            for c, top in zip(columns, tops):
                tile = tile - c * top
            return tops, tile

        for t in range(tiles):
            if (t + 1) * per > k + WIDE:
                full[t] = step(full[t])[1]
            if t * per < k + WIDE:
                tops, tile = step(inverse[t])
                for i, top in enumerate(tops):
                    tile = jnp.where(row == k + i, top, tile)
                inverse[t] = tile
    diag[: PAN * PACK, :PAN] = jnp.concatenate(inverse, axis=1).T


def soap_kernel(count, g, w, f, s, ls, rs, lb, rb, ow, owl, of, os, ols, ors, olb, orb, aug, diag):
    step = pl.program_id(0)
    mats = 2 * count
    unroll = UNROLL if mats % UNROLL == 0 else 4
    blocks = range(GROUP)
    grad = [g[i].astype(jnp.bfloat16) for i in blocks]
    left, right = [split(lb[i]) for i in blocks], [split(rb[i]) for i in blocks]
    left_t = [(x.T, y.T) for x, y in left]
    right_t = [(x.T, y.T) for x, y in right]
    grad_t = [x.T for x in grad]
    lnew = [beta_stat * ls[i] + (1.0 - beta_stat) * dot_nn(grad[i], grad_t[i]) for i in blocks]
    rnew = [beta_stat * rs[i] + (1.0 - beta_stat) * dot_nn(grad_t[i], grad[i]) for i in blocks]
    turned = [dot_nn(left_t[i][0], grad[i]) + dot_nn(left_t[i][1], grad[i]) for i in blocks]
    for i in blocks:
        ols[i] = lnew[i]
        ors[i] = rnew[i]
    turned = [three(dot_nn, split(turned[i]), right[i]) for i in blocks]
    sides = [
        three(dot_nn, basis_t, split(stat))
        for i in blocks
        for basis_t, stat in ((left_t[i], lnew[i]), (right_t[i], rnew[i]))
    ]
    first_new = [beta_one * f[i] + (1.0 - beta_one) * turned[i] for i in blocks]
    second_new = [beta_two * s[i] + (1.0 - beta_two) * turned[i] * turned[i] for i in blocks]
    direction = [
        x / (1.0 - beta_one**STEP) / (jnp.sqrt(y / (1.0 - beta_two**STEP)) + epsilon_adam)
        for x, y in zip(first_new, second_new)
    ]
    for i in blocks:
        of[i] = first_new[i]
        os[i] = second_new[i]
    stepped = [three(dot_nn, left[i], split(direction[i])) for i in blocks]
    for i, side in enumerate(sides):
        aug[2 * GROUP * step + i, :, HD:] = side
    grams = [three(dot_nt, x, x) for x in map(split, sides)]
    stepped = [three(dot_nn, split(stepped[i]), right_t[i]) for i in blocks]
    for i, gram in enumerate(grams):
        aug[2 * GROUP * step + i, :, :HD] = gram
    for i in blocks:
        weight = w[i]
        weight_new = weight - rate_matrix * (stepped[i] + weight_decay * weight)
        ow[i] = weight_new
        owl[i] = weight_new.astype(jnp.bfloat16)

    @pl.when(step == count // GROUP - 1)
    def _():
        half = HD // 2

        def place(p, i):
            low = pl.multiple_of(p * PAN, PAN)
            base = pl.multiple_of(p // 4 * 128, 128)
            for u in range(unroll):
                m = i * unroll + u
                own = aug[m, pl.ds(low, PAN), pl.ds(base, 128)]
                diag[pl.ds(m, PAN, stride=PACK), :] = pltpu.roll(own, (128 - p % 4 * PAN) % 128, 1)

        def update(p, i, pair):
            low = pl.multiple_of(p * PAN, PAN)
            edge = pair // 2 * half
            start = pair * 2 * PAN + PAN
            mine = [i * unroll + u for u in range(unroll)]
            factors = [split(diag[pl.ds(m, PAN, stride=PACK), :][:, :PAN]) for m in mine]
            panels = [split(aug[m, pl.ds(low, PAN), edge:]) for m in mine]
            panels = [three(dot_tn, x, y) for x, y in zip(factors, panels)]
            lane = lax.broadcasted_iota(jnp.int32, (PAN, HD - edge), 1) + edge
            heads = [split(jnp.where(lane >= low + PAN, panel[:, : HD - edge], 0.0)) for panel in panels]
            parts = [split(panel) for panel in panels]
            lhs = [jnp.concatenate([x, x, y], axis=0).T for x, y in heads]
            rhs = [jnp.concatenate([x, y, x], axis=0) for x, y in parts]
            rest = [aug[m, start:, edge:] - dot_nn(x[start - edge :], y) for m, x, y in zip(mine, lhs, rhs)]
            for m, panel, left in zip(mine, panels, rest):
                aug[m, start:, edge:] = left
                aug[m, pl.ds(low, PAN), HD:] = panel[:, HD - edge :]

        def panel_step(p, carry):
            lax.fori_loop(0, mats // unroll, lambda i, n: (place(p, i), n)[1], 0)
            eliminate(diag)

            for pair in range(4):

                @pl.when(p // 2 == pair)
                def _():
                    lax.fori_loop(0, mats // unroll, lambda i, n: (update(p, i, pair), n)[1], 0)

            return carry

        lax.fori_loop(0, HD // PAN, panel_step, 0)

        def finish(b, carry):
            for side, out in enumerate((olb, orb)):
                out[b] = aug[2 * b + side, :, HD:].T
            return carry

        lax.fori_loop(0, count, finish, 0)


LIMIT = 56 * 2**20
SHRINK = 1


def cost(flops, moved, trans=0):
    return pl.CostEstimate(flops=int(flops) // SHRINK, bytes_accessed=int(moved) // SHRINK, transcendentals=0)


def turn(rows, cosine, sine):
    head = rows[:, :128]
    lane = lax.broadcasted_iota(jnp.int32, head.shape, 1)
    partner = jnp.where(lane < RD // 2, pltpu.roll(head, 128 - RD // 2, 1), pltpu.roll(head, RD // 2, 1))
    return jnp.concatenate([head * cosine + partner * sine, rows[:, 128:]], axis=1)


MESH = pl.DeviceIdType.MESH
RIGHT = (
    {0: 0, 1: 3, 2: 6},
    {0: 1, 1: 4, 2: 3},
    {0: 2, 1: 0, 2: 4},
    {1: 1, 2: 0},
    {1: 2, 2: 1},
    {1: 5, 2: 2},
    {2: 7},
    {2: 8},
    {2: 5},
)
LEFT = (
    {3: 9, 2: 6, 1: 3},
    {3: 10, 2: 9, 1: 6},
    {3: 11, 2: 10, 1: 9},
    {2: 7, 1: 4},
    {2: 11, 1: 10},
    {2: 8, 1: 7},
    {1: 11},
    {1: 8},
    {1: 5},
)
SWAPS = ((3, 9), (4, 0), (10, 10), (11, 7))
ROLES = {
    "q": (0, 1),
    "k": (1, 2),
    "v": (2, 12),
    "out": (13, 13),
    "up": ((6, 3), (7, 8), (8, 4), (5, 5)),
    "down": ((9, 6), (12, 11), (14, 14), (15, 15)),
}


def beside(blocks):
    return jnp.concatenate([blocks[b] for b in range(D // HD)], axis=1)


def layer_kernel(
    rows_in, cotangent, segs, matrices, vectors, waves,
    held, units_out, grads_out, sum_0, sum_1, sum_2, extra, rows_out, sums, biases,
    units, grads, weight, act, pre, flipped, column, q, k, v, ga, att, dq, dk, dv, kseq, vseq, keys, vals, stage,
    raw, lines, cosine, sine, seg_row, seg_col,
    right_send, right_recv, left_send, left_recv, swap_send, swap_recv, row_send, row_recv, local,
):
    d, y, c = lax.axis_index("dp"), lax.axis_index("heads"), lax.axis_index("tensor")
    z, x = d // 2, d % 2
    by_x, by_y, by_core = {"dp": d + 1 - 2 * x}, {"heads": 1 - y}, {"tensor": 1 - c}
    shard = 2 * y + c
    block = rows_in.shape[0]
    tokens = units.shape[0]
    head = 32 + (shard * 2 + x) * 3

    barrier = pltpu.get_barrier_semaphore()
    for near in (by_x, by_y, by_core):
        pl.semaphore_signal(barrier, inc=1, device_id=near, device_id_type=MESH)

    @pl.when(z < 3)
    def _():
        pl.semaphore_signal(barrier, inc=1, device_id={"dp": d + 2}, device_id_type=MESH)

    @pl.when(z > 0)
    def _():
        pl.semaphore_signal(barrier, inc=1, device_id={"dp": d - 2}, device_id_type=MESH)

    def remote(source, target, send, recv, device):
        return pltpu.make_async_remote_copy(
            src_ref=source, dst_ref=target, send_sem=send, recv_sem=recv, device_id=device, device_id_type=MESH
        )

    def hop(table, step, half, sends, recvs, shift, at):
        place, part, sem = table[step][at], pl.ds(half * 4, 4), 2 * step + half
        source = weight.at[0, part] if step == 0 else held.at[place, part]
        return remote(source, held.at[place, part], sends.at[sem], recvs.at[sem], {"dp": d + 2 * shift})

    ways = ((RIGHT, right_send, right_recv, 1), (LEFT, left_send, left_recv, -1))

    def start(step, half):
        for table, sends, recvs, shift in ways:
            for at in table[step]:

                @pl.when(z == at)
                def _():
                    hop(table, step, half, sends, recvs, shift, at).start()

    def arrived(step, half):
        for table, sends, recvs, shift in ways:
            for at in table[step]:

                @pl.when(z == at + shift)
                def _():
                    hop(table, step, half, sends, recvs, shift, at).wait_recv()

    def sent(step):
        for table, sends, recvs, shift in ways:
            for at in table[step]:

                @pl.when(z == at)
                def _():
                    for half in range(2):
                        hop(table, step, half, sends, recvs, shift, at).wait_send()

    def pass_on(step, half):
        arrived(step, half)
        for later in {6: (7, 8), 7: ()}.get(step, (step + 1,)):
            start(later, half)

    def pump(step):
        pass_on(step, 0)
        pass_on(step, 1)

    def swap(i, side):
        return remote(held.at[SWAPS[i][side]], held.at[12 + i], swap_send.at[i], swap_recv.at[i], by_x)

    def start_swap(i):
        for side in range(2):

            @pl.when(x == side)
            def _():
                swap(i, side).start()

    def fetch(role, slot):
        for side in range(2):

            @pl.when(x == side)
            def _():
                pltpu.make_async_copy(held.at[role[side]], weight.at[slot], local.at[slot]).start()

    def fetched(slot):
        pltpu.make_async_copy(held.at[0], weight.at[slot], local.at[slot]).wait()

    def load(j, at):
        def begin(which):
            pltpu.make_async_copy(matrices.at[0, which * 8 : which * 8 + 8], raw.at[at], local.at[at]).start()

        pl.when((d < 5) | (d == 7))(lambda: begin(j))
        pl.when(d == 5)(lambda: begin(2 - j))
        pl.when(d == 6)(lambda: begin((j + 2) % 3))

    def loaded(j, at):
        pltpu.make_async_copy(matrices.at[0, :8], raw.at[at], local.at[at]).wait()
        weight[j] = raw[at].astype(jnp.bfloat16)

    def keep_own(j):
        for at in range(4):

            @pl.when(z == at)
            def _():
                pltpu.make_async_copy(weight.at[j], held.at[3 * at + j], local.at[8 + j]).start()

    load(0, 0)
    load(1, 1)
    loaded(0, 0)
    pl.semaphore_wait(barrier, 4 + (z + 1) // 2 % 2)
    start(0, 0)
    start(0, 1)
    load(2, 0)
    keep_own(0)
    rows = rows_in[...]
    centered = rows - jnp.mean(rows, axis=-1, keepdims=True)
    inverse = lax.rsqrt(jnp.mean(centered * centered, axis=-1, keepdims=True) + epsilon_norm)
    units[:block, :] = (centered * inverse).astype(jnp.bfloat16)
    grads[:block, :] = cotangent[...].astype(jnp.bfloat16)
    seg_row[x] = segs[...].astype(jnp.float32)

    def send_rows(kind, i, low, high, there, device):
        array = (units, grads)[kind]
        at = kind * 8 + i
        return remote(
            array.at[low:high], array.at[there : there + high - low], row_send.at[at], row_recv.at[at], device
        )

    half = block // 2

    def row_plan(kind):
        return (
            send_rows(kind, 0, 0, block, block, by_x),
            send_rows(kind, 1, 0, block, 2 * block, by_y),
            send_rows(kind, 2, block, block + half, 3 * block, by_y),
            send_rows(kind, 3, 2 * block + half, 3 * block, 3 * block + half, by_x),
            send_rows(kind, 4, 0, block, 4 * block, by_core),
            send_rows(kind, 5, block, 2 * block, 5 * block, by_core),
            send_rows(kind, 6, 2 * block, 3 * block, 6 * block, by_core),
            send_rows(kind, 7, 3 * block, 4 * block, 7 * block, by_core),
        )

    plans = [row_plan(kind) for kind in range(2)]
    for plan in plans:
        plan[0].start()
        plan[1].start()
        plan[4].start()
    segments = remote(seg_row.at[x], seg_row.at[x], swap_send.at[5], swap_recv.at[5], by_x)
    segments.start()
    loaded(1, 1)
    keep_own(1)
    loaded(2, 0)
    keep_own(2)
    for j in range(3):
        pltpu.make_async_copy(weight.at[j], held.at[j], local.at[8 + j]).wait()
    for i in range(4):
        lines[i : i + 1, :] = jnp.concatenate([vectors[8 * i + b : 8 * i + b + 1, :] for b in range(8)], axis=1)
    pump(0)
    segments.wait()
    for s in range(tokens // LEN):
        row = seg_row[s]
        wide = jnp.broadcast_to(row, (128, LEN)).T
        seg_col[s] = wide
        lane = lax.broadcasted_iota(jnp.int32, (LEN, 128), 1)
        token = lax.broadcasted_iota(jnp.int32, (LEN, 128), 0).astype(jnp.float32)
        first = jnp.sum(jnp.where(row < wide[:, 0:1], 1.0, 0.0), axis=1, keepdims=True)
        turns = (token - first) * waves[...]
        here = slice(s * LEN, (s + 1) * LEN)
        cosine[here, :] = jnp.where(lane < RD, jnp.cos(turns), 1.0)
        flips = jnp.where(lane < RD // 2, -1.0, jnp.where(lane < RD, 1.0, 0.0))
        sine[here, :] = jnp.sin(turns) * flips
    for plan in plans:
        plan[0].wait_recv()
        plan[2].start()
        plan[5].start()
        plan[1].wait_recv()
        plan[3].start()
        plan[6].start()
    pump(1)
    for plan in plans:
        plan[2].wait_recv()
        plan[3].wait_recv()
        plan[7].start()
    pump(2)
    start_swap(0)
    sent(0)
    fetch(ROLES["up"][0], 0)
    fetch(ROLES["down"][0], 1)
    for plan in plans:
        for i in range(4, 8):
            plan[i].wait_recv()
        for i in range(8):
            plan[i].wait_send()
    keep = [pltpu.make_async_copy(units, units_out, local.at[6]), pltpu.make_async_copy(grads, grads_out, local.at[7])]
    for copy in keep:
        copy.start()

    tile = 512

    def run_mlp(slot):
        hidden = SLOTS[0][slot] + (SLOTS[1][slot] - SLOTS[0][slot]) * x
        wu, wd = weight.at[0], weight.at[1]

        def body(i, carry):
            here = pl.ds(pl.multiple_of(i * tile, tile), tile)
            norm = (units[here, :].astype(jnp.float32) * lines[2:3, :] + lines[3:4, :]).astype(jnp.bfloat16)
            inner = dot_nn(norm, wu[...].reshape(D, HD)) + vectors[pl.ds(64 + shard * 8 + hidden, 1), :]
            pull = dot_nt(grads[here, :], beside(wd))
            share = 0.5 + 0.5 * lax.erf(inner * (0.5**0.5))
            act[here, :] = (inner * share).astype(jnp.bfloat16)
            slope = share + inner * jnp.exp(-0.5 * inner * inner) * ((2.0 * 3.141592653589793) ** (-0.5))
            pre[here, :] = (slope * pull).astype(jnp.bfloat16)
            return carry

        lax.fori_loop(0, tokens // tile, body, 0)

    def save_rows(source, i):
        copy = pltpu.make_async_copy(source, rows_out.at[i], local.at[8 + i])
        copy.start()
        return copy

    def put(i, to_0, to_1, sem):
        for side, target in ((0, to_0), (1, to_1)):
            if target is not None:

                @pl.when(x == side)
                def _():
                    pltpu.make_async_copy(stage.at[i], target, local.at[16 + sem]).start()

        def finish():
            for side, target in ((0, to_0), (1, to_1)):
                if target is not None:

                    @pl.when(x == side)
                    def _():
                        pltpu.make_async_copy(stage.at[i], target, local.at[16 + sem]).wait()

        return finish

    def run_down(source, at):
        flipped[:HD, :] = source[...].T

        def body(b, carry):
            here = pl.ds(pl.multiple_of(b * HD, HD), HD)
            stage[at, b] = dot_nn(flipped[:HD, :], grads[:, here]).astype(jnp.bfloat16)
            return carry

        lax.fori_loop(0, D // HD, body, 0)

    def run_up(sources, places, slots, gain, row, offset, more=False):
        for i, source in enumerate(sources):
            wide = source[...]
            flipped[i * HD : (i + 1) * HD, :] = wide.T
            total = jnp.sum(wide.astype(jnp.float32), axis=0, keepdims=True)
            biases[:, offset + i * HD : offset + (i + 1) * HD] = total
            column[i] = jnp.broadcast_to(total, (128, HD)).T

        def body(b, carry):
            here = pl.ds(pl.multiple_of(b * HD, HD), HD)
            gains, shifts = (sums[row : row + 1, here], sums[row + 1 : row + 2, here]) if more else (0.0, 0.0)
            every = dot_nn(flipped[: len(sources) * HD, :], units[:, here])
            for i, (place, slot) in enumerate(zip(places, slots)):
                turned = every[i * HD : (i + 1) * HD, :]
                w = weight[slot, b].T.astype(jnp.float32)
                bias = column[i][:, 0:1]
                gains = gains + jnp.sum(w * turned, axis=0, keepdims=True)
                shifts = shifts + jnp.sum(w * bias, axis=0, keepdims=True)
                result = turned * lines[gain : gain + 1, here] + bias * lines[gain + 1 : gain + 2, here]
                stage[place, b] = result.T.astype(jnp.bfloat16)
            sums[row : row + 1, here] = gains
            sums[row + 1 : row + 2, here] = shifts
            return carry

        lax.fori_loop(0, D // HD, body, 0)

    fetched(0)
    fetched(1)
    run_mlp(0)
    saves = [save_rows(act, 0), save_rows(pre, 1)]
    pass_on(3, 0)
    run_down(act, 0)
    done = put(0, sum_0.at[3], sum_0.at[2], 0)
    pass_on(3, 1)
    start_swap(1)
    run_up([pre], [1], [0], 2, 2, 3 * HD)
    done_up = put(1, sum_0.at[2], sum_0.at[1], 1)
    pump(4)
    start_swap(2)
    pump(5)

    swap(0, 0).wait_recv()
    swap(1, 0).wait_recv()
    for i, role in enumerate(("q", "k", "v", "out")):
        fetch(ROLES[role], 2 + i)
    for i in range(4):
        fetched(2 + i)

    def project_rows(i, carry):
        here = pl.ds(pl.multiple_of(i * tile, tile), tile)
        turns = []
        for u in range(tile // block):
            r = i * (tile // block) + u
            a = (((x + r % 2) % 2) * 2 + (y + r // 2 % 2) % 2) * 2 + (c + r // 4) % 2
            turns.append(pl.ds(pl.multiple_of(a * block, block), block))
        cos_here = jnp.concatenate([cosine[t, :] for t in turns], axis=0)
        sin_here = jnp.concatenate([sine[t, :] for t in turns], axis=0)
        norm = (units[here, :].astype(jnp.float32) * lines[0:1, :] + lines[1:2, :]).astype(jnp.bfloat16)
        q[here, :] = turn(
            dot_nn(norm, weight[2].reshape(D, HD)) + vectors[pl.ds(head + 0, 1), :], cos_here, sin_here
        ).astype(jnp.bfloat16)
        k[here, :] = turn(
            dot_nn(norm, weight[3].reshape(D, HD)) + vectors[pl.ds(head + 1, 1), :], cos_here, sin_here
        ).astype(jnp.bfloat16)
        v[here, :] = (dot_nn(norm, weight[4].reshape(D, HD)) + vectors[pl.ds(head + 2, 1), :]).astype(jnp.bfloat16)
        ga[here, :] = dot_nt(grads[here, :], beside(weight.at[5])).astype(jnp.bfloat16)
        return carry

    lax.fori_loop(0, tokens // tile, project_rows, 0)
    pass_on(6, 0)
    pieces = LEN // block

    def attend(s, carry):
        scale = HD ** (-0.5)
        spots = []
        for i in range(pieces):
            a = s * pieces + i
            r = ((c + a % 2) % 2) * 4 + (x + a // 4) % 2 + 2 * ((y + a // 2 % 2) % 2)
            spots.append(pl.ds(pl.multiple_of(r * block, block), block))
        for i in range(pieces):
            kseq[i * block : (i + 1) * block, :] = k[spots[i], :]
            vseq[i * block : (i + 1) * block, :] = v[spots[i], :]
        keys[...] = jnp.zeros_like(keys)
        vals[...] = jnp.zeros_like(vals)
        for i in range(pieces):
            upto = (i + 1) * block
            angle = pl.ds(pl.multiple_of(s * LEN + i * block, block), block)
            mine, pulled = q[spots[i], :], ga[spots[i], :]
            scores = dot_nt(mine, kseq[:upto, :]) * scale
            to = lax.broadcasted_iota(jnp.int32, (block, upto), 0) + i * block
            of = lax.broadcasted_iota(jnp.int32, (block, upto), 1)
            allowed = (seg_col[s, i * block : upto, 0:1] == seg_row[s, :, :upto]) & (of <= to)
            scores = jnp.where(allowed, scores, -1e30)
            powers = jnp.exp(scores - jnp.max(scores, axis=-1, keepdims=True))
            probs = powers / jnp.sum(powers, axis=-1, keepdims=True)
            low = probs.astype(jnp.bfloat16)
            att[spots[i], :] = dot_nn(low, vseq[:upto, :]).astype(jnp.bfloat16)
            pull = dot_nt(pulled, vseq[:upto, :])
            inner = jnp.sum(probs * pull, axis=-1, keepdims=True)
            gs = (probs * (pull - inner)).astype(jnp.bfloat16)
            turned = turn(dot_nn(gs, kseq[:upto, :]) * scale, cosine[angle, :], -sine[angle, :])
            dq[spots[i], :] = turned.astype(jnp.bfloat16)
            keys[:upto, :] = keys[:upto, :] + dot_tn(gs, mine)
            vals[:upto, :] = vals[:upto, :] + dot_tn(low, pulled)
        for i in range(pieces):
            here = slice(i * block, (i + 1) * block)
            angle = pl.ds(pl.multiple_of(s * LEN + i * block, block), block)
            turned = turn(keys[here, :] * scale, cosine[angle, :], -sine[angle, :])
            dk[spots[i], :] = turned.astype(jnp.bfloat16)
            dv[spots[i], :] = vals[here, :].astype(jnp.bfloat16)

        @pl.when(s == 0)
        def _():
            pass_on(6, 1)
            start_swap(3)

        return carry

    lax.fori_loop(0, tokens // LEN, attend, 0)
    for copy in saves:
        copy.wait()
    saves = [save_rows(a, 4 + i) for i, a in enumerate((att, dq, dk, dv))]
    run_up([dv], [4], [4], 0, 0, 2 * HD, False)

    back_v = remote(stage.at[4], sum_0.at[1], swap_send.at[6], swap_recv.at[6], by_x)
    pl.when(x == 1)(back_v.start)
    done_v = put(4, sum_2.at[0], None, 4)
    pass_on(7, 0)
    done()
    run_down(att, 0)
    done = put(0, None, extra, 5)
    back_out = remote(stage.at[0], sum_1.at[0], swap_send.at[4], swap_recv.at[4], by_x)
    pl.when(x == 0)(back_out.start)
    run_up([dq, dk], [2, 3], [2, 3], 0, 0, 0, True)
    done_qk = [put(2, sum_1.at[0], sum_0.at[0], 2), put(3, sum_0.at[0], sum_2.at[0], 3)]
    pass_on(7, 1)
    fetch(ROLES["up"][1], 0)
    fetch(ROLES["down"][1], 1)

    fetched(0)
    fetched(1)
    run_mlp(1)
    saves += [save_rows(act, 2), save_rows(pre, 3)]
    done_up()
    run_down(act, 1)
    done_up = put(1, extra, sum_0.at[3], 6)
    pl.when(x == 0)(back_v.wait_recv)
    pl.when(x == 1)(back_v.wait_send)
    pl.when(x == 1)(back_out.wait_recv)
    pl.when(x == 0)(back_out.wait_send)
    arrived(8, 0)
    arrived(8, 1)
    for step in range(1, len(RIGHT)):
        sent(step)
    for i in range(4):
        swap(i, 0).wait_send()
    for i in range(2, 4):
        swap(i, 0).wait_recv()
    for copy in saves + keep:
        copy.wait()
    for finish in done_qk + [done_v, done, done_up]:
        finish()


def layer(rows, cotangent, segments, matrices, vectors, waves):
    block = rows.shape[0]
    tokens = 8 * block
    count = tokens // LEN
    anywhere, near = pl.BlockSpec(memory_space=pl.ANY), pl.BlockSpec(memory_space=pltpu.VMEM)
    low, full = jnp.bfloat16, jnp.float32
    group = (D // HD, HD, HD)
    narrow = pltpu.VMEM((tokens, HD), low)
    return pl.pallas_call(
        layer_kernel,
        in_specs=[near] * 3 + [anywhere] + [near] * 2,
        out_specs=[anywhere] * 8 + [near] * 2,
        out_shape=[
            jax.ShapeDtypeStruct((16,) + group, low),
            jax.ShapeDtypeStruct((tokens, D), low),
            jax.ShapeDtypeStruct((tokens, D), low),
        ]
        + [jax.ShapeDtypeStruct((4,) + group, low)] * 3
        + [
            jax.ShapeDtypeStruct(group, low),
            jax.ShapeDtypeStruct((8, tokens, HD), low),
            jax.ShapeDtypeStruct((4, D), full),
            jax.ShapeDtypeStruct((1, 4 * HD), full),
        ],
        scratch_shapes=[
            pltpu.VMEM((tokens, D), low),
            pltpu.VMEM((tokens, D), low),
            pltpu.VMEM((6,) + group, low),
            narrow,
            narrow,
            pltpu.VMEM((3 * HD, tokens), low),
            pltpu.VMEM((3, HD, 128), full),
        ]
        + [narrow] * 8
        + [pltpu.VMEM((LEN, HD), low)] * 2
        + [pltpu.VMEM((LEN, HD), full)] * 2
        + [
            pltpu.VMEM((5,) + group, low),
            pltpu.VMEM((2,) + group, full),
            pltpu.VMEM((4, D), full),
            pltpu.VMEM((tokens, 128), full),
            pltpu.VMEM((tokens, 128), full),
            pltpu.VMEM((count, 1, LEN), full),
            pltpu.VMEM((count, LEN, 128), full),
        ]
        + [pltpu.SemaphoreType.DMA((18,))] * 4
        + [pltpu.SemaphoreType.DMA((7,))] * 2
        + [pltpu.SemaphoreType.DMA((16,))] * 2
        + [pltpu.SemaphoreType.DMA((24,))],
        compiler_params=pltpu.CompilerParams(
            vmem_limit_bytes=63 * 2**20, collective_id=0, has_side_effects=True
        ),
        cost_estimate=cost(6e10, 1e8),
        name="layer",
    )(rows, cotangent, segments, matrices, vectors, waves)


def remote_copy(source, target, send, recv, device):
    return pltpu.make_async_remote_copy(
        src_ref=source, dst_ref=target, send_sem=send, recv_sem=recv, device_id=device, device_id_type=MESH
    )


def greet(peers):
    barrier = pltpu.get_barrier_semaphore()
    for near in peers:
        pl.semaphore_signal(barrier, inc=1, device_id=near, device_id_type=MESH)
    pl.semaphore_wait(barrier, len(peers))


def swap_with(source, send, recv, x, device, to_0, to_1):
    copies = [remote_copy(source, there, send, recv, device) for there in (to_0, to_1)]
    for side in range(2):
        pl.when(x == side)(copies[side].start)
    return copies[0]


def fetch_role(held, role, target, sem, x):
    for side in range(2):

        @pl.when(x == side)
        def _():
            pltpu.make_async_copy(held.at[role[side]], target, sem).start()


def hidden_rows(units, grads, lines, bias, wu, wd, act, pre, before):
    tile = 512

    def body(i, carry):
        here = pl.ds(pl.multiple_of(i * tile, tile), tile)
        before(i)
        norm = (units[here, :].astype(jnp.float32) * lines[2:3, :] + lines[3:4, :]).astype(jnp.bfloat16)
        inner = dot_nn(norm, wu[...].reshape(D, HD)) + bias
        pull = dot_nt(grads[here, :], beside(wd))
        share = 0.5 + 0.5 * lax.erf(inner * (0.5**0.5))
        act[here, :] = (inner * share).astype(jnp.bfloat16)
        slope = share + inner * jnp.exp(-0.5 * inner * inner) * ((2.0 * 3.141592653589793) ** (-0.5))
        pre[here, :] = (slope * pull).astype(jnp.bfloat16)
        return carry

    lax.fori_loop(0, units.shape[0] // tile, body, 0)


def down_blocks(flipped, act, grads, stage):
    flipped[:HD, :] = act[...].T

    def body(b, carry):
        here = pl.ds(pl.multiple_of(b * HD, HD), HD)
        stage[b] = dot_nn(flipped[:HD, :], grads[:, here]).astype(jnp.bfloat16)
        return carry

    lax.fori_loop(0, D // HD, body, 0)


def up_blocks(flipped, column, pres, biases, units, weight, lines, stage, gains_out, shifts_out, early):
    parts = len(pres)
    for i, pre in enumerate(pres):
        wide = pre[...]
        flipped[i * HD : (i + 1) * HD, :] = wide.T
        bias = jnp.sum(wide.astype(jnp.float32), axis=0, keepdims=True)
        biases[i] = bias
        column[i] = jnp.broadcast_to(bias, (128, HD)).T

    def body(b, carry):
        here = pl.ds(pl.multiple_of(b * HD, HD), HD)
        gains, shifts = early[2:3, here], early[3:4, here]
        every = dot_nn(flipped[: parts * HD, :], units[:, here])
        for i in range(parts):
            turned = every[i * HD : (i + 1) * HD, :]
            w = weight[i, b].T.astype(jnp.float32)
            bias = column[i][:, 0:1]
            gains = gains + jnp.sum(w * turned, axis=0, keepdims=True)
            shifts = shifts + jnp.sum(w * bias, axis=0, keepdims=True)
            result = turned * lines[2:3, here] + bias * lines[3:4, here]
            stage[i, b] = result.T.astype(jnp.bfloat16)
        gains_out[:, here] = gains
        shifts_out[:, here] = shifts
        return carry

    lax.fori_loop(0, D // HD, body, 0)


def spread(vectors, lines):
    for i in range(4):
        lines[i : i + 1, :] = jnp.concatenate([vectors[8 * i + b : 8 * i + b + 1, :] for b in range(8)], axis=1)


def third_kernel(
    held, units_in, grads_in, rows_in, vectors, early, extra, sum_1_in, sum_2_in,
    sum_1, sum_2, rows_out, sums, biases,
    units, grads, weight, act, pres, flipped, column, stage, lines,
    swap_send, swap_recv, loads, local,
):
    d, y, c = lax.axis_index("dp"), lax.axis_index("heads"), lax.axis_index("tensor")
    x = d % 2
    shard = 2 * y + c
    tokens = units.shape[0]
    tile = 512
    by_x = {"dp": d + 1 - 2 * x}
    greet([by_x])
    swaps = [swap_with(extra, swap_send.at[0], swap_recv.at[0], x, by_x, sum_1.at[3], sum_1.at[1])]
    for slot, role in ((1, ROLES["up"][2]), (2, ROLES["down"][2])):
        fetch_role(held, role, weight.at[slot], local.at[slot], x)

    def row_loads(i):
        here = pl.ds(pl.multiple_of(i * tile, tile), tile)
        return [
            pltpu.make_async_copy(source.at[here], target.at[here], loads.at[2 * i + j])
            for j, (source, target) in enumerate(((units_in, units), (grads_in, grads)))
        ]

    for i in range(tokens // tile):
        for copy in row_loads(i):
            copy.start()
    fetch_role(held, ROLES["up"][1], weight.at[0], local.at[0], x)
    second = pltpu.make_async_copy(rows_in.at[3], pres.at[0], local.at[3])
    second.start()
    spread(vectors, lines)
    for slot in (1, 2):
        pltpu.make_async_copy(held.at[0], weight.at[slot], local.at[slot]).wait()

    def ready(i):
        for copy in row_loads(i):
            copy.wait()

    hidden = SLOTS[0][2] + (SLOTS[1][2] - SLOTS[0][2]) * x
    bias = vectors[pl.ds(64 + shard * 8 + hidden, 1), :]
    hidden_rows(units, grads, lines, bias, weight.at[1], weight.at[2], act, pres.at[1], ready)
    saves = [
        pltpu.make_async_copy(act, rows_out.at[0], local.at[4]),
        pltpu.make_async_copy(pres.at[1], rows_out.at[1], local.at[5]),
    ]
    for copy in saves:
        copy.start()
    down_blocks(flipped, act, grads, stage.at[2])
    swaps.append(swap_with(stage.at[2], swap_send.at[1], swap_recv.at[1], x, by_x, sum_2.at[3], sum_1.at[3]))
    second.wait()
    pltpu.make_async_copy(held.at[0], weight.at[0], local.at[0]).wait()
    up_blocks(
        flipped, column, [pres.at[0], pres.at[1]], biases, units, weight, lines, stage,
        sums.at[0], sums.at[1], early,
    )
    puts = [
        [pltpu.make_async_copy(stage.at[i], place, local.at[6 + i]) for place in places]
        for i, places in enumerate(((sum_1.at[2], sum_1.at[2]), (sum_2.at[2], sum_1.at[1])))
    ]
    for pair in puts:
        for side in range(2):
            pl.when(x == side)(pair[side].start)
    for copy in swaps + saves:
        copy.wait()
    for pair in puts:
        for side in range(2):
            pl.when(x == side)(pair[side].wait)


def third(held, units, grads, rows, vectors, sums, extra, sum_1, sum_2):
    tokens = units.shape[0]
    anywhere, near = pl.BlockSpec(memory_space=pl.ANY), pl.BlockSpec(memory_space=pltpu.VMEM)
    low, full = jnp.bfloat16, jnp.float32
    group = (D // HD, HD, HD)
    return pl.pallas_call(
        third_kernel,
        in_specs=[anywhere] * 4 + [near] * 2 + [anywhere] * 3,
        out_specs=[anywhere] * 3 + [near] * 2,
        out_shape=[
            jax.ShapeDtypeStruct((4,) + group, low),
            jax.ShapeDtypeStruct((4,) + group, low),
            jax.ShapeDtypeStruct((2, tokens, HD), low),
            jax.ShapeDtypeStruct((2, 1, D), full),
            jax.ShapeDtypeStruct((2, 1, HD), full),
        ],
        input_output_aliases={7: 0, 8: 1},
        scratch_shapes=[
            pltpu.VMEM((tokens, D), low),
            pltpu.VMEM((tokens, D), low),
            pltpu.VMEM((3,) + group, low),
            pltpu.VMEM((tokens, HD), low),
            pltpu.VMEM((2, tokens, HD), low),
            pltpu.VMEM((2 * HD, tokens), low),
            pltpu.VMEM((2, HD, 128), full),
            pltpu.VMEM((3,) + group, low),
            pltpu.VMEM((4, D), full),
            pltpu.SemaphoreType.DMA((2,)),
            pltpu.SemaphoreType.DMA((2,)),
            pltpu.SemaphoreType.DMA((8,)),
            pltpu.SemaphoreType.DMA((8,)),
        ],
        compiler_params=pltpu.CompilerParams(
            vmem_limit_bytes=56 * 2**20, collective_id=1, has_side_effects=True
        ),
        cost_estimate=cost(2e10, 6e7),
        name="third",
    )(held, units, grads, rows, vectors, sums, extra, sum_1, sum_2)


def rest_kernel(
    held, units_in, grads_in, rows_in, third_rows, vectors, early, early_bias, third_sums, third_bias, sum_2_in,
    sum_2, rows_out, total, by_x_out, by_y_out, by_xy_out, own_out,
    units, grads, weight, acts, pre, flipped, column, stage, lines, more, added, biases, current, received, shares, other,
    swap_send, swap_recv, hop_send, hop_recv, loads, local, share_send, share_recv,
):
    d, y, c = lax.axis_index("dp"), lax.axis_index("heads"), lax.axis_index("tensor")
    z, x = d // 2, d % 2
    shard = 2 * y + c
    tokens = units.shape[0]
    block, tile = tokens // 8, 512
    by_x, by_y, by_core = {"dp": d + 1 - 2 * x}, {"heads": 1 - y}, {"tensor": 1 - c}
    by_z = [{"dp": d + 2 - 4 * (z % 2)}, {"dp": d + 4 - 8 * (z // 2)}]
    peers = [by_core, by_y] + by_z + [by_x]
    greet(peers)
    fetch_role(held, ROLES["up"][3], weight.at[0], local.at[0], x)
    fetch_role(held, ROLES["down"][3], weight.at[1], local.at[1], x)

    def row_loads(i):
        here = pl.ds(pl.multiple_of(i * tile, tile), tile)
        return [
            pltpu.make_async_copy(source.at[here], target.at[here], loads.at[2 * i + j])
            for j, (source, target) in enumerate(((units_in, units), (grads_in, grads)))
        ]

    for i in range(tokens // tile):
        for copy in row_loads(i):
            copy.start()
    out_roles = (ROLES["down"][0], ROLES["down"][1], ROLES["out"], ROLES["down"][2])
    out_rows = [rows_in.at[i] for i in (0, 2, 4)] + [third_rows.at[0]]
    for i in range(4):
        fetch_role(held, out_roles[i], weight.at[2 + i], local.at[2 + i], x)
        pltpu.make_async_copy(out_rows[i], acts.at[i], local.at[6 + i]).start()
    spread(vectors, lines)
    more[0:2, :] = early[0:2, :]
    more[2:3, :] = third_sums[0]
    more[3:4, :] = third_sums[1]
    for slot in (0, 1):
        pltpu.make_async_copy(held.at[0], weight.at[slot], local.at[slot]).wait()

    def ready(i):
        for copy in row_loads(i):
            copy.wait()

    hidden = [SLOTS[0][s] + (SLOTS[1][s] - SLOTS[0][s]) * x for s in range(4)]
    bias = vectors[pl.ds(64 + shard * 8 + hidden[3], 1), :]
    hidden_rows(units, grads, lines, bias, weight.at[0], weight.at[1], acts.at[4], pre, ready)
    saves = [pltpu.make_async_copy(pre, rows_out, local.at[10])]
    saves[0].start()
    down_blocks(flipped, acts.at[4], grads, stage.at[1])
    saves.append(swap_with(stage.at[1], swap_send.at[0], swap_recv.at[0], x, by_x, sum_2.at[2], sum_2.at[3]))
    up_blocks(
        flipped, column, [pre], biases, units, weight, lines, stage, added.at[0], added.at[1], more
    )
    put = pltpu.make_async_copy(stage.at[0], sum_2.at[1], local.at[11])
    put.start()
    saves.append(put)

    current[0] = jnp.zeros(current.shape[1:], jnp.float32)
    own = jnp.sum(grads[:block, :].astype(jnp.float32), axis=0, keepdims=True)
    for i, line in enumerate((more[0:1, :], more[1:2, :], added[0], added[1])):
        for b in range(8):
            current[0, 8 * i + b : 8 * i + b + 1, :] = line[:, b * HD : (b + 1) * HD]
    for b in range(8):
        current[0, 56 + b : 57 + b, :] = own[:, b * HD : (b + 1) * HD]
        current[0, 96 + b : 97 + b, :] = own[:, b * HD : (b + 1) * HD]
    for i in range(3):
        at = 32 + (shard * 2 + x) * 3 + i
        current[0, pl.ds(at, 1), :] = early_bias[:, i * HD : (i + 1) * HD]
    for i, line in enumerate((early_bias[:, 3 * HD :], third_bias[0], third_bias[1], biases[0])):
        current[0, pl.ds(64 + shard * 8 + hidden[i], 1), :] = line
    hops = [
        remote_copy(current.at[i], received.at[i], hop_send.at[i], hop_recv.at[i], near) for i, near in enumerate(peers)
    ]

    def finish_hop(i):
        hops[i].wait()
        result = current[i] + received[i]
        if i + 1 < len(peers):
            current[i + 1] = result
            hops[i + 1].start()
        else:
            total[...] = result

    hops[0].start()

    for i in range(4):
        pltpu.make_async_copy(held.at[0], weight.at[2 + i], local.at[2 + i]).wait()
        pltpu.make_async_copy(rows_in.at[0], acts.at[i], local.at[6 + i]).wait()
    by_slot = (2, 3, 4, 5, 1)

    def share_rows(i):
        here = slice(i * tile, (i + 1) * tile)
        left = jnp.concatenate([acts[j, here, :] for j in range(5)], axis=1)
        for b in range(D // HD):
            right = jnp.concatenate([weight[slot, b] for slot in by_slot], axis=0)
            yield slice(b * HD, (b + 1) * HD), dot_nn(left, right)

    sends = [
        remote_copy(
            shares.at[i * tile : (i + 1) * tile],
            other.at[i * tile : (i + 1) * tile],
            share_send.at[i],
            share_recv.at[i],
            by_core,
        )
        for i in range(2)
    ]
    for i in range(2):
        for columns, result in share_rows(2 + i):
            shares[i * tile : (i + 1) * tile, columns] = result.astype(jnp.bfloat16)
        sends[i].start()
        finish_hop(i)
    for copy in sends:
        copy.wait_send()
    for i in range(2):
        sends[i].wait_recv()
        for columns, result in share_rows(i):
            theirs = other[i * tile : (i + 1) * tile, columns].astype(jnp.float32)
            shares[i * tile : (i + 1) * tile, columns] = (result + theirs).astype(jnp.bfloat16)
        finish_hop(2 + i)
    for i, target in enumerate((own_out, by_x_out, by_y_out, by_xy_out)):
        copy = pltpu.make_async_copy(shares.at[i * block : (i + 1) * block], target.at[0], local.at[12 + i])
        copy.start()
        saves.append(copy)
    finish_hop(4)
    for copy in saves:
        copy.wait()


def rest(held, units, grads, rows, third_rows, vectors, sums, biases, third_sums, third_bias, sum_2):
    tokens = units.shape[0]
    anywhere, near = pl.BlockSpec(memory_space=pl.ANY), pl.BlockSpec(memory_space=pltpu.VMEM)
    low, full = jnp.bfloat16, jnp.float32
    group = (D // HD, HD, HD)
    table = vectors.shape
    return pl.pallas_call(
        rest_kernel,
        in_specs=[anywhere] * 5 + [near] * 5 + [anywhere],
        out_specs=[anywhere] * 2 + [near] + [anywhere] * 4,
        out_shape=[
            jax.ShapeDtypeStruct((4,) + group, low),
            jax.ShapeDtypeStruct((tokens, HD), low),
            jax.ShapeDtypeStruct(table, full),
        ]
        + [jax.ShapeDtypeStruct((2, tokens // 8, D), low)] * 4,
        input_output_aliases={10: 0},
        scratch_shapes=[
            pltpu.VMEM((tokens, D), low),
            pltpu.VMEM((tokens, D), low),
            pltpu.VMEM((6,) + group, low),
            pltpu.VMEM((5, tokens, HD), low),
            pltpu.VMEM((tokens, HD), low),
            pltpu.VMEM((HD, tokens), low),
            pltpu.VMEM((1, HD, 128), full),
            pltpu.VMEM((2,) + group, low),
            pltpu.VMEM((4, D), full),
            pltpu.VMEM((4, D), full),
            pltpu.VMEM((2, 1, D), full),
            pltpu.VMEM((1, 1, HD), full),
            pltpu.VMEM((5,) + table, full),
            pltpu.VMEM((5,) + table, full),
            pltpu.VMEM((tokens // 2, D), low),
            pltpu.VMEM((tokens // 2, D), low),
            pltpu.SemaphoreType.DMA((1,)),
            pltpu.SemaphoreType.DMA((1,)),
            pltpu.SemaphoreType.DMA((5,)),
            pltpu.SemaphoreType.DMA((5,)),
            pltpu.SemaphoreType.DMA((8,)),
            pltpu.SemaphoreType.DMA((16,)),
            pltpu.SemaphoreType.DMA((2,)),
            pltpu.SemaphoreType.DMA((2,)),
        ],
        compiler_params=pltpu.CompilerParams(
            vmem_limit_bytes=60 * 2**20, collective_id=3, has_side_effects=True
        ),
        cost_estimate=cost(4e10, 6e7),
        name="rest",
    )(held, units, grads, rows, third_rows, vectors, sums, biases, third_sums, third_bias, sum_2)


def input_kernel(
    held, rows_in, third_rows, late, gains, by_x_in, by_y_in, by_xy_in, own_in,
    by_x_out, by_y_out, by_xy_out, own_out,
    weight, rows, shares, other,
    local, share_send, share_recv,
):
    x, c = lax.axis_index("dp") % 2, lax.axis_index("tensor")
    by_core = {"tensor": 1 - c}
    barrier = pltpu.get_barrier_semaphore()
    pl.semaphore_signal(barrier, inc=1, device_id=by_core, device_id_type=MESH)
    pl.semaphore_wait(barrier, 1)
    tokens = rows.shape[1]
    block, tile = tokens // 8, 512
    roles = (ROLES["q"], ROLES["k"], ROLES["v"]) + ROLES["up"]
    sources = [rows_in.at[i] for i in (5, 6, 7, 1, 3)] + [third_rows.at[1], late]
    for i, (role, source) in enumerate(zip(roles, sources)):
        for side in range(2):

            @pl.when(x == side)
            def _():
                pltpu.make_async_copy(held.at[role[side]], weight.at[i], local.at[i]).start()

        pltpu.make_async_copy(source, rows.at[i], local.at[7 + i]).start()
    for i, source in enumerate(sources):
        pltpu.make_async_copy(held.at[0], weight.at[i], local.at[i]).wait()
        pltpu.make_async_copy(source, rows.at[i], local.at[7 + i]).wait()

    def share_rows(i):
        here = pl.ds(i * tile, tile)
        sides = ((0, 3), (3, 7))
        lefts = [jnp.concatenate([rows[r, here, :] for r in range(*side)], axis=1) for side in sides]
        for b in range(D // HD):
            columns = slice(b * HD, (b + 1) * HD)
            parts = []
            for j, side in enumerate(sides):
                right = jnp.concatenate([weight[r, b] for r in range(*side)], axis=1)
                parts.append(dot_nt(lefts[j], right) * gains[j : j + 1, columns])
            yield columns, parts[0] + parts[1]

    sends = [
        pltpu.make_async_remote_copy(
            src_ref=shares.at[i * tile : (i + 1) * tile],
            dst_ref=other.at[i * tile : (i + 1) * tile],
            send_sem=share_send.at[i],
            recv_sem=share_recv.at[i],
            device_id=by_core,
            device_id_type=MESH,
        )
        for i in range(2)
    ]
    for i in range(2):
        for columns, result in share_rows(2 + i):
            shares[i * tile : (i + 1) * tile, columns] = result.astype(jnp.bfloat16)
        sends[i].start()
    for copy in sends:
        copy.wait_send()
    for i in range(2):
        sends[i].wait_recv()
        for columns, result in share_rows(i):
            theirs = other[i * tile : (i + 1) * tile, columns].astype(jnp.float32)
            shares[i * tile : (i + 1) * tile, columns] = (result + theirs).astype(jnp.bfloat16)
    for i, target in enumerate((own_out, by_x_out, by_y_out, by_xy_out)):
        pltpu.make_async_copy(shares.at[i * block : (i + 1) * block], target.at[1], local.at[14 + i]).start()
    for i, target in enumerate((own_out, by_x_out, by_y_out, by_xy_out)):
        pltpu.make_async_copy(shares.at[i * block : (i + 1) * block], target.at[1], local.at[14 + i]).wait()


def input_share(held, rows, third_rows, late, gains, parts):
    tokens = rows.shape[1]
    anywhere = pl.BlockSpec(memory_space=pl.ANY)
    low = jnp.bfloat16
    return pl.pallas_call(
        input_kernel,
        in_specs=[anywhere] * 4 + [pl.BlockSpec(memory_space=pltpu.VMEM)] + [anywhere] * 4,
        out_specs=[anywhere] * 4,
        out_shape=[jax.ShapeDtypeStruct((2, tokens // 8, D), low)] * 4,
        input_output_aliases={5 + i: i for i in range(4)},
        scratch_shapes=[
            pltpu.VMEM((7, D // HD, HD, HD), low),
            pltpu.VMEM((7, tokens, HD), low),
            pltpu.VMEM((tokens // 2, D), low),
            pltpu.VMEM((tokens // 2, D), low),
            pltpu.SemaphoreType.DMA((18,)),
            pltpu.SemaphoreType.DMA((2,)),
            pltpu.SemaphoreType.DMA((2,)),
        ],
        compiler_params=pltpu.CompilerParams(vmem_limit_bytes=LIMIT, collective_id=2, has_side_effects=True),
        cost_estimate=cost(2 * 7 * tokens * D * HD, 5e7),
        name="input_share",
    )(held, rows, third_rows, late, gains, *parts)


def soap_part(places, grad, blocks, previous):
    total, count = blocks[0].shape[0], grad.shape[0]
    mats = 2 * count
    own = pl.BlockSpec((GROUP, HD, HD), lambda i, at: (i, 0, 0))
    some = pl.BlockSpec((GROUP, HD, HD), lambda i, at: (at[0] * (count // GROUP) + i, 0, 0))
    whole = pl.BlockSpec((count, HD, HD), lambda i, at: (at[0], 0, 0))
    full = jax.ShapeDtypeStruct((total, HD, HD), jnp.float32)
    shapes = [full, jax.ShapeDtypeStruct((total, HD, HD), jnp.bfloat16)] + [full] * 6
    extra = [] if previous is None else list(previous)

    def body(at, *refs):
        soap_kernel(count, *refs[:8], *refs[8 + len(extra) :])

    return pl.pallas_call(
        body,
        grid_spec=pltpu.PrefetchScalarGridSpec(
            num_scalar_prefetch=1,
            grid=(count // GROUP,),
            in_specs=[own] + [some] * 7 + [pl.BlockSpec(memory_space=pl.ANY)] * len(extra),
            out_specs=[some] * 6 + [whole] * 2,
            scratch_shapes=[
                pltpu.VMEM((mats, HD, 2 * HD), jnp.float32),
                pltpu.VMEM((PAN * PACK + PACK, 128), jnp.float32),
            ],
        ),
        out_shape=shapes,
        input_output_aliases={9 + i: i for i in range(len(extra))},
        compiler_params=pltpu.CompilerParams(vmem_limit_bytes=LIMIT),
        cost_estimate=cost(count * 40 * 2 * HD**3 * 3, count * 16 * 4 * HD * HD),
        name="soap",
    )(places, grad, *blocks, *extra)


def adam_vector(grad, params, first, second):
    first_new = beta_one * first + (1.0 - beta_one) * grad
    second_new = beta_two * second + (1.0 - beta_two) * grad * grad
    direction = (
        first_new
        / (1.0 - beta_one**STEP)
        / (jnp.sqrt(second_new / (1.0 - beta_two**STEP)) + epsilon_adam)
    )
    return (params - rate_vector * direction, first_new, second_new)


ALL = ("dp", "heads", "tensor")
SUMMED = ((1, 0, 2), (1, 0, 2), (0, 1, 2), (0, 1, 2), (0, 1, 2), (2, 0, 1), (2, 0, 1), (2, 0, 1))
SLOTS = ((4, 5, 6, 0), (1, 7, 2, 3))


def places():
    for z in range(4):
        for x in range(2):
            for y in range(2):
                for c in range(2):
                    yield z, x, y, c


def index_of(z, x, y, c):
    return ((z * 2 + x) * 2 + y) * 2 + c


def move(array, target):
    return lax.ppermute(array, ALL, [(index_of(*at), index_of(*target(*at))) for at in places()])


LINES = [[index_of(z, x, y, c) for z in range(4)] for x in range(2) for y in range(2) for c in range(2)]


def over_y(array):
    return move(array, lambda z, x, y, c: (z, x, 1 - y, c))


def over_x(array):
    return move(array, lambda z, x, y, c: (z, 1 - x, y, c))


def over_xy(array):
    return move(array, lambda z, x, y, c: (z, 1 - x, 1 - y, c))


def after(array, *earlier):
    return lax.optimization_barrier((array, *earlier))[0]


def plane_shards(
    block_input,
    cotangent,
    segments,
    matrices,
    first_moment,
    second_moment,
    left_stat,
    right_stat,
    left_basis,
    right_basis,
    vectors,
    vec_first,
    vec_second,
):
    d = lax.axis_index("dp")
    x = d % 2
    gain_one, gain_two = vectors[:D].reshape(1, D), vectors[2 * D : 3 * D].reshape(1, D)
    bias_out, bias_down = vectors[7 * D : 8 * D], vectors[8 * D + FF : 9 * D + FF]
    table = vectors.reshape(-1, HD)
    frequency = 1.0 / rope_base ** (jnp.arange(0, RD, 2).astype(jnp.float32) / RD)
    turns = jnp.concatenate([frequency, frequency, jnp.zeros((128 - RD,), jnp.float32)]).reshape(1, 128)
    held, units, grads, sum_0, sum_1, sum_2, extra, rows, sums, biases = layer(
        block_input, cotangent, segments, matrices, table, turns
    )
    sum_1, sum_2, third_rows, third_sums, third_bias = third(
        held, units, grads, rows, table, sums, extra, sum_1, sum_2
    )
    sum_2, late, grad_table, *parts = rest(
        held, units, grads, rows, third_rows, table, sums, biases, third_sums, third_bias, sum_2
    )
    owned = []
    for send in (sum_0, sum_1, sum_2):
        owned.append(lax.psum_scatter(send, ALL, scatter_dimension=0, tiled=False, axis_index_groups=LINES))

    parts = input_share(held, rows, third_rows, late, jnp.concatenate([gain_one, gain_two]), parts)
    blocks = [a[0] for a in (matrices, first_moment, second_moment, left_stat, right_stat, left_basis, right_basis)]
    summed_order = jnp.array(SUMMED, jnp.int32)[d]
    updated = soap_part(summed_order[0:1], after(owned[0], parts[0]), blocks, None)
    updated = soap_part(summed_order[1:2], after(owned[1], updated[1]), blocks, updated)
    by_x, by_y, by_xy, own = parts
    totals = (
        after(own, updated[1]).astype(jnp.float32)
        + over_x(by_x).astype(jnp.float32)
        + over_y(by_y).astype(jnp.float32)
        + over_xy(by_xy).astype(jnp.float32)
    )
    output = block_input + totals[0] + bias_out + bias_down
    e = totals[1]
    middle = jnp.mean(block_input, axis=-1, keepdims=True)
    centered = block_input - middle
    inverse = lax.rsqrt(jnp.mean(centered * centered, axis=-1, keepdims=True) + epsilon_norm)
    unit = centered * inverse
    grad_input = cotangent + inverse * (
        e - jnp.mean(e, axis=-1, keepdims=True) - unit * jnp.mean(e * unit, axis=-1, keepdims=True)
    )
    grad_vectors = grad_table.reshape(-1)
    updated = soap_part(summed_order[2:3], after(owned[2], output, grad_input), blocks, updated)
    new_vectors, new_vec_first, new_vec_second = adam_vector(grad_vectors, vectors, vec_first, vec_second)
    return (output, grad_input, *[u[None] for u in updated], new_vectors, new_vec_first, new_vec_second)


def generic_shards(
    block_input,
    cotangent,
    segments,
    matrices,
    first_moment,
    second_moment,
    left_stat,
    right_stat,
    left_basis,
    right_basis,
    vectors,
    vec_first,
    vec_second,
):
    group_size = lax.axis_size(("heads", "tensor"))
    member = lax.axis_index(("heads", "tensor"))
    heads_here = H // group_size
    hidden_here = FF // group_size
    row_blocks = D // HD
    hidden_blocks = hidden_here // HD
    seq_count = segments.shape[0]
    tokens_here = seq_count * LEN
    own_rows = block_input.shape[0]
    qkv_offset = 4 * D + member * heads_here * 3 * HD
    up_offset = 8 * D + member * hidden_here
    gain_one = vectors[0:D]
    shift_one = vectors[D : 2 * D]
    gain_two = vectors[2 * D : 3 * D]
    shift_two = vectors[3 * D : 4 * D]
    bias_qkv = lax.dynamic_slice_in_dim(vectors, qkv_offset, heads_here * 3 * HD).reshape(
        heads_here, 3, HD
    )
    bias_out = vectors[7 * D : 8 * D]
    bias_up = lax.dynamic_slice_in_dim(vectors, up_offset, hidden_here)
    bias_down = vectors[8 * D + FF : 9 * D + FF]
    gathered = lax.all_gather(matrices.astype(jnp.bfloat16), "dp", axis=1, tiled=True)[0]
    w_qkv, w_out, w_up, w_down = unpack_blocks(gathered, heads_here, row_blocks, hidden_blocks)
    normed_one, unit_one, inverse_one = layer_norm(block_input, gain_one, shift_one)
    normed_two, unit_two, inverse_two = layer_norm(block_input, gain_two, shift_two)
    grad_own = cotangent.astype(jnp.bfloat16)
    norm_one, norm_two, grad_rows = (
        lax.all_gather(normed_one.astype(jnp.bfloat16), ("heads", "tensor"), axis=0, tiled=True),
        lax.all_gather(normed_two.astype(jnp.bfloat16), ("heads", "tensor"), axis=0, tiled=True),
        lax.all_gather(grad_own, ("heads", "tensor"), axis=0, tiled=True),
    )
    norm_one3 = norm_one.reshape(tokens_here, row_blocks, HD)
    norm_two3 = norm_two.reshape(tokens_here, row_blocks, HD)
    projected = (
        jnp.einsum("tbr,hqbrc->thqc", norm_one3, w_qkv, preferred_element_type=jnp.float32)
        + bias_qkv
    )
    shaped = projected.reshape(seq_count, LEN, heads_here, 3, HD)
    cosine, sine = angles(segments)
    queries = rotate(shaped[:, :, :, 0], cosine, sine).astype(jnp.bfloat16)
    keys_rot = rotate(shaped[:, :, :, 1], cosine, sine).astype(jnp.bfloat16)
    values = shaped[:, :, :, 2].astype(jnp.bfloat16)
    attended, log_total = lax.map(seq_forward, (queries, keys_rot, values, segments))
    attend_low = attended.astype(jnp.bfloat16).reshape(tokens_here, heads_here, HD)
    pre_act = (
        jnp.einsum("tbr,kbrc->tkc", norm_two3, w_up, preferred_element_type=jnp.float32).reshape(
            tokens_here, hidden_here
        )
        + bias_up
    )
    act_low = gelu_exact(pre_act).astype(jnp.bfloat16)
    rows_act = act_low.reshape(lax.axis_size(("heads", "tensor")) * own_rows, hidden_blocks, HD)
    first_term = jnp.einsum("thr,hbrc->tbc", attend_low, w_out, preferred_element_type=jnp.float32)
    second_term = jnp.einsum("tkr,kbrc->tbc", rows_act, w_down, preferred_element_type=jnp.float32)
    summed = lax.psum_scatter(
        (first_term + second_term).reshape(lax.axis_size(("heads", "tensor")) * own_rows, D),
        ("heads", "tensor"),
        scatter_dimension=0,
        tiled=True,
    )
    output = block_input + summed + bias_out + bias_down
    regathered = lax.all_gather(matrices.astype(jnp.bfloat16), "dp", axis=1, tiled=True)[0]
    w_qkv, w_out, w_up, w_down = unpack_blocks(regathered, heads_here, row_blocks, hidden_blocks)
    grad_rows3 = grad_rows.reshape(tokens_here, row_blocks, HD)
    act_low3 = act_low.reshape(tokens_here, hidden_blocks, HD)
    grad_act = jnp.einsum(
        "tbc,kbrc->tkr", grad_rows3, w_down, preferred_element_type=jnp.float32
    ).reshape(tokens_here, hidden_here)
    gelu_pull = jax.vjp(gelu_exact, pre_act)[1]
    grad_pre = gelu_pull(grad_act)[0].astype(jnp.bfloat16)
    grad_pre3 = grad_pre.reshape(tokens_here, hidden_blocks, HD)
    grad_attend = jnp.einsum(
        "tbc,hbrc->thr", grad_rows3, w_out, preferred_element_type=jnp.float32
    ).astype(jnp.bfloat16)
    grad_attend = grad_attend.reshape(seq_count, LEN, heads_here, HD)
    grad_queries, grad_keys, grad_values = lax.map(
        seq_backward, (queries, keys_rot, values, segments, log_total, grad_attend)
    )
    grad_raw = jnp.stack(
        [rotate(grad_queries, cosine, -sine), rotate(grad_keys, cosine, -sine), grad_values], axis=3
    )
    grad_raw = grad_raw.astype(jnp.bfloat16).reshape(tokens_here, heads_here, 3, HD)
    rows_up = grad_pre.reshape(lax.axis_size(("heads", "tensor")) * own_rows, hidden_blocks, HD)
    back_one = jnp.einsum(
        "thqc,hqbrc->tbr", grad_raw, w_qkv, preferred_element_type=jnp.float32
    ).reshape(lax.axis_size(("heads", "tensor")) * own_rows, D)
    back_two = jnp.einsum(
        "tkc,kbrc->tbr", rows_up, w_up, preferred_element_type=jnp.float32
    ).reshape(lax.axis_size(("heads", "tensor")) * own_rows, D)
    grad_norms = lax.psum_scatter(
        jnp.stack([back_one, back_two], axis=1),
        ("heads", "tensor"),
        scatter_dimension=0,
        tiled=True,
    )
    grad_norm_one = grad_norms[:, 0]
    grad_norm_two = grad_norms[:, 1]
    grad_input = (
        cotangent
        + norm_back(grad_norm_one, unit_one, inverse_one, gain_one)
        + norm_back(grad_norm_two, unit_two, inverse_two, gain_two)
    )
    grad_bias_rows = jnp.sum(grad_own, axis=0, dtype=jnp.float32)
    pieces = jnp.concatenate(
        [
            jnp.sum(grad_norm_one * unit_one, axis=0),
            jnp.sum(grad_norm_one, axis=0),
            jnp.sum(grad_norm_two * unit_two, axis=0),
            jnp.sum(grad_norm_two, axis=0),
            jnp.zeros((3 * D,), jnp.float32),
            grad_bias_rows,
            jnp.zeros((FF,), jnp.float32),
            grad_bias_rows,
        ]
    )
    pieces = lax.dynamic_update_slice_in_dim(
        pieces, jnp.sum(grad_raw, axis=0, dtype=jnp.float32).reshape(-1), qkv_offset, 0
    )
    pieces = lax.dynamic_update_slice_in_dim(
        pieces, jnp.sum(grad_pre, axis=0, dtype=jnp.float32), up_offset, 0
    )
    grad_vectors = lax.psum(pieces, ("dp", "heads", "tensor"))
    grad_down = jnp.einsum(
        "tkr,tbc->kbrc", act_low3, grad_rows3, preferred_element_type=jnp.float32
    )
    grad_up = jnp.einsum("tbr,tkc->kbrc", norm_two3, grad_pre3, preferred_element_type=jnp.float32)
    grad_out = jnp.einsum(
        "thr,tbc->hbrc", attend_low, grad_rows3, preferred_element_type=jnp.float32
    )
    grad_qkv = jnp.einsum(
        "tbr,thqc->hqbrc", norm_one3, grad_raw, preferred_element_type=jnp.float32
    )
    attn_grads = jnp.concatenate([grad_qkv, grad_out[:, None]], axis=1).reshape(-1, HD, HD)
    all_grads = jnp.concatenate(
        [attn_grads, grad_up.reshape(-1, HD, HD), grad_down.reshape(-1, HD, HD)], axis=0
    )[None]
    owned = lax.psum_scatter(all_grads, "dp", scatter_dimension=1, tiled=True)
    blocks = [a[0] for a in (matrices, first_moment, second_moment, left_stat, right_stat, left_basis, right_basis)]
    updated = [u[None] for u in soap_part(jnp.zeros((1,), jnp.int32), owned[0], blocks, None)]
    new_vectors, new_vec_first, new_vec_second = adam_vector(
        grad_vectors, vectors, vec_first, vec_second
    )
    return (
        output,
        grad_input,
        updated[0],
        updated[1],
        updated[2],
        updated[3],
        updated[4],
        updated[5],
        updated[6],
        updated[7],
        new_vectors,
        new_vec_first,
        new_vec_second,
    )


def solution(mesh):
    in_specs = (
        P(("dp", "heads", "tensor"), None),
        P(("dp", "heads", "tensor"), None),
        P("dp", None),
        P(("heads", "tensor"), "dp", None, None),
        P(("heads", "tensor"), "dp", None, None),
        P(("heads", "tensor"), "dp", None, None),
        P(("heads", "tensor"), "dp", None, None),
        P(("heads", "tensor"), "dp", None, None),
        P(("heads", "tensor"), "dp", None, None),
        P(("heads", "tensor"), "dp", None, None),
        P(),
        P(),
        P(),
    )
    out_specs = (
        P(("dp", "heads", "tensor"), None),
        P(("dp", "heads", "tensor"), None),
        P(("heads", "tensor"), "dp", None, None),
        P(("heads", "tensor"), "dp", None, None),
        P(("heads", "tensor"), "dp", None, None),
        P(("heads", "tensor"), "dp", None, None),
        P(("heads", "tensor"), "dp", None, None),
        P(("heads", "tensor"), "dp", None, None),
        P(("heads", "tensor"), "dp", None, None),
        P(("heads", "tensor"), "dp", None, None),
        P(),
        P(),
        P(),
    )
    plane = dict(mesh.shape) == {"dp": 8, "heads": 2, "tensor": 2}
    shards = plane_shards if plane else generic_shards
    return jax.shard_map(shards, mesh=mesh, in_specs=in_specs, out_specs=out_specs, check_vma=False)
```

```python
import functools

import jax
import jax.numpy as jnp
from jax import lax
from jax.experimental import pallas as pl
from jax.experimental.pallas import tpu as pltpu
from jax.sharding import PartitionSpec as P

D = 2048
H = 8
HD = 256
RD = 64
FF = 8192
LEN = 1024
STEP = 10


epsilon_norm = 1e-05
epsilon_adam = 1e-08
rope_base = 10000.0
beta_one = 0.9
beta_two = 0.95
beta_stat = 0.95
rate_matrix = 0.05
rate_vector = 0.1
weight_decay = 0.01
PAN = 32
PACK = 16
WIDE = 8
UNROLL = 16
GROUP = 2


def layer_norm(rows, gain, shift):
    middle = jnp.mean(rows, axis=-1, keepdims=True)
    centered = rows - middle
    spread = jnp.mean(centered * centered, axis=-1, keepdims=True)
    inverse = lax.rsqrt(spread + epsilon_norm)
    unit = centered * inverse
    return (unit * gain + shift, unit, inverse)


def norm_back(grad, unit, inverse, gain):
    scaled = grad * gain
    return inverse * (
        scaled
        - jnp.mean(scaled, axis=-1, keepdims=True)
        - unit * jnp.mean(scaled * unit, axis=-1, keepdims=True)
    )


def angles(segments):
    seq_count = segments.shape[0]
    column = jnp.arange(LEN, dtype=jnp.int32)[None, :]
    border = jnp.concatenate(
        [jnp.ones((seq_count, 1), jnp.bool_), segments[:, 1:] != segments[:, :-1]], axis=1
    )
    starts = lax.cummax(jnp.where(border, column, 0), axis=1)
    places = (column - starts).astype(jnp.float32)
    frequency = 1.0 / rope_base ** (jnp.arange(0, RD, 2).astype(jnp.float32) / RD)
    turns = places[:, :, None] * frequency[None, None, :]
    return (jnp.cos(turns)[:, :, None, :], jnp.sin(turns)[:, :, None, :])


def rotate(part, cosine, sine):
    half_dims = RD // 2
    first_half = part[..., :half_dims]
    second_half = part[..., half_dims:RD]
    return jnp.concatenate(
        [
            first_half * cosine - second_half * sine,
            second_half * cosine + first_half * sine,
            part[..., RD:],
        ],
        axis=-1,
    )


def unpack_blocks(blocks, heads_here, row_blocks, hidden_blocks):
    attn_count = heads_here * 4 * row_blocks
    up_count = hidden_blocks * row_blocks
    attn_part = blocks[:attn_count].reshape(heads_here, 4, row_blocks, HD, HD)
    w_up = blocks[attn_count : attn_count + up_count].reshape(hidden_blocks, row_blocks, HD, HD)
    w_down = blocks[attn_count + up_count :].reshape(hidden_blocks, row_blocks, HD, HD)
    return (attn_part[:, :3], attn_part[:, 3], w_up, w_down)


def masked_scores(queries, keys_rot, segment_row):
    column = jnp.arange(LEN)
    allowed = (segment_row[:, None] == segment_row[None, :]) & (column[None, :] <= column[:, None])
    scores = jnp.einsum(
        "qhd,khd->hqk", queries, keys_rot, preferred_element_type=jnp.float32
    ) * HD ** (-0.5)
    return jnp.where(allowed[None], scores, -1e30)


def seq_forward(items):
    queries, keys_rot, values, segment_row = items
    scores = masked_scores(queries, keys_rot, segment_row)
    row_max = jnp.max(scores, axis=-1, keepdims=True)
    powers = jnp.exp(scores - row_max)
    row_total = jnp.sum(powers, axis=-1, keepdims=True)
    probs_low = (powers / row_total).astype(jnp.bfloat16)
    attended = jnp.einsum("hqk,khd->qhd", probs_low, values, preferred_element_type=jnp.float32)
    return (attended, (row_max + jnp.log(row_total))[..., 0])


def seq_backward(items):
    queries, keys_rot, values, segment_row, log_total, grad_attend = items
    scores = masked_scores(queries, keys_rot, segment_row)
    probs = jnp.exp(scores - log_total[..., None])
    grad_probs = jnp.einsum("qhd,khd->hqk", grad_attend, values, preferred_element_type=jnp.float32)
    inner = jnp.sum(probs * grad_probs, axis=-1, keepdims=True)
    grad_scores = (probs * (grad_probs - inner)).astype(jnp.bfloat16)
    grad_queries = jnp.einsum(
        "hqk,khd->qhd", grad_scores, keys_rot, preferred_element_type=jnp.float32
    ) * HD ** (-0.5)
    grad_keys = jnp.einsum(
        "hqk,qhd->khd", grad_scores, queries, preferred_element_type=jnp.float32
    ) * HD ** (-0.5)
    grad_values = jnp.einsum(
        "hqk,qhd->khd", probs.astype(jnp.bfloat16), grad_attend, preferred_element_type=jnp.float32
    )
    return (grad_queries, grad_keys, grad_values)


def gelu_exact(inputs):
    return jax.nn.gelu(inputs, approximate=False)


def dot_nn(a, b):
    return lax.dot_general(a, b, (((1,), (0,)), ((), ())), preferred_element_type=jnp.float32)


def dot_nt(a, b):
    return lax.dot_general(a, b, (((1,), (1,)), ((), ())), preferred_element_type=jnp.float32)


def dot_tn(a, b):
    return lax.dot_general(a, b, (((0,), (0,)), ((), ())), preferred_element_type=jnp.float32)


def split(x):
    high = x.astype(jnp.bfloat16)
    return high, (x - high.astype(jnp.float32)).astype(jnp.bfloat16)


def three(dot, a, b):
    return dot(a[0], b[0]) + (dot(a[0], b[1]) + dot(a[1], b[0]))


def eliminate(diag):
    tiles = PAN * PACK // 128
    per = 128 // PACK
    flat = diag[: PAN * PACK, :].T[:PAN]
    full = [flat[:, t * 128 : (t + 1) * 128] for t in range(tiles)]
    row = lax.broadcasted_iota(jnp.int32, (PAN, 128), 0)
    lane = lax.broadcasted_iota(jnp.int32, (PAN, 128), 1)
    inverse = [jnp.where(row == lane // PACK + t * per, 1.0, 0.0) for t in range(tiles)]

    def column(k):
        return jnp.take_along_axis(full[k // per], lane % PACK + k % per * PACK, axis=1)

    for k in range(0, PAN, WIDE):
        columns, scales, crosses = [column(k + i) for i in range(WIDE)], [], []
        for i in range(WIDE):
            for j in range(i):
                columns[i] = columns[i] - columns[j] * crosses[j][i]
            scales.append(lax.rsqrt(columns[i][k + i : k + i + 1]))
            columns[i] = columns[i] * scales[i]
            crosses.append([columns[i][k + n : k + n + 1] for n in range(WIDE)])
        columns = [jnp.where(row >= k + WIDE, c, 0.0) for c in columns]

        def step(tile):
            tops = []
            for i in range(WIDE):
                top = tile[k + i : k + i + 1]
                for j in range(i):
                    top = top - crosses[j][i] * tops[j]
                tops.append(top * scales[i])
            for c, top in zip(columns, tops):
                tile = tile - c * top
            return tops, tile

        for t in range(tiles):
            if (t + 1) * per > k + WIDE:
                full[t] = step(full[t])[1]
            if t * per < k + WIDE:
                tops, tile = step(inverse[t])
                for i, top in enumerate(tops):
                    tile = jnp.where(row == k + i, top, tile)
                inverse[t] = tile
    diag[: PAN * PACK, :PAN] = jnp.concatenate(inverse, axis=1).T


def soap_kernel(count, spot, g, w, f, s, ls, rs, lb, rb, ow, owl, of, os, ols, ors, olb, orb, aug, diag, bases, sems):
    step = pl.program_id(0)
    mats = 2 * count
    unroll = UNROLL if mats % UNROLL == 0 else 4
    blocks = range(GROUP)
    grad = [g[i].astype(jnp.bfloat16) for i in blocks]
    left, right = [split(lb[i]) for i in blocks], [split(rb[i]) for i in blocks]
    left_t = [(x.T, y.T) for x, y in left]
    right_t = [(x.T, y.T) for x, y in right]
    grad_t = [x.T for x in grad]
    lnew = [beta_stat * ls[i] + (1.0 - beta_stat) * dot_nn(grad[i], grad_t[i]) for i in blocks]
    rnew = [beta_stat * rs[i] + (1.0 - beta_stat) * dot_nn(grad_t[i], grad[i]) for i in blocks]
    turned = [dot_nn(left_t[i][0], grad[i]) + dot_nn(left_t[i][1], grad[i]) for i in blocks]
    for i in blocks:
        ols[i] = lnew[i]
        ors[i] = rnew[i]
    turned = [three(dot_nn, split(turned[i]), right[i]) for i in blocks]
    sides = [
        three(dot_nn, basis_t, split(stat))
        for i in blocks
        for basis_t, stat in ((left_t[i], lnew[i]), (right_t[i], rnew[i]))
    ]
    first_new = [beta_one * f[i] + (1.0 - beta_one) * turned[i] for i in blocks]
    second_new = [beta_two * s[i] + (1.0 - beta_two) * turned[i] * turned[i] for i in blocks]
    direction = [
        x / (1.0 - beta_one**STEP) / (jnp.sqrt(y / (1.0 - beta_two**STEP)) + epsilon_adam)
        for x, y in zip(first_new, second_new)
    ]
    for i in blocks:
        of[i] = first_new[i]
        os[i] = second_new[i]
    stepped = [three(dot_nn, left[i], split(direction[i])) for i in blocks]
    for i, side in enumerate(sides):
        aug[2 * GROUP * step + i, :, HD:] = side
    grams = [three(dot_nt, x, x) for x in map(split, sides)]
    stepped = [three(dot_nn, split(stepped[i]), right_t[i]) for i in blocks]
    for i, gram in enumerate(grams):
        aug[2 * GROUP * step + i, :, :HD] = gram
    for i in blocks:
        weight = w[i]
        weight_new = weight - rate_matrix * (stepped[i] + weight_decay * weight)
        ow[i] = weight_new
        owl[i] = weight_new.astype(jnp.bfloat16)

    @pl.when(step == count // GROUP - 1)
    def _():
        half = HD // 2

        def place(p, i):
            low = pl.multiple_of(p * PAN, PAN)
            base = pl.multiple_of(p // 4 * 128, 128)
            for u in range(unroll):
                m = i * unroll + u
                own = aug[m, pl.ds(low, PAN), pl.ds(base, 128)]
                diag[pl.ds(m, PAN, stride=PACK), :] = pltpu.roll(own, (128 - p % 4 * PAN) % 128, 1)

        def update(p, i, pair):
            low = pl.multiple_of(p * PAN, PAN)
            edge = pair // 2 * half
            start = pair * 2 * PAN + PAN
            mine = [i * unroll + u for u in range(unroll)]
            factors = [split(diag[pl.ds(m, PAN, stride=PACK), :][:, :PAN]) for m in mine]
            panels = [split(aug[m, pl.ds(low, PAN), edge:]) for m in mine]
            panels = [three(dot_tn, x, y) for x, y in zip(factors, panels)]
            lane = lax.broadcasted_iota(jnp.int32, (PAN, HD - edge), 1) + edge
            heads = [split(jnp.where(lane >= low + PAN, panel[:, : HD - edge], 0.0)) for panel in panels]
            parts = [split(panel) for panel in panels]
            lhs = [jnp.concatenate([x, x, y], axis=0).T for x, y in heads]
            rhs = [jnp.concatenate([x, y, x], axis=0) for x, y in parts]
            rest = [aug[m, start:, edge:] - dot_nn(x[start - edge :], y) for m, x, y in zip(mine, lhs, rhs)]
            for m, panel, left in zip(mine, panels, rest):
                aug[m, start:, edge:] = left
                aug[m, pl.ds(low, PAN), HD:] = panel[:, HD - edge :]

        def panel_step(p, carry):
            lax.fori_loop(0, mats // unroll, lambda i, n: (place(p, i), n)[1], 0)
            eliminate(diag)

            for pair in range(4):

                @pl.when(p // 2 == pair)
                def _():
                    lax.fori_loop(0, mats // unroll, lambda i, n: (update(p, i, pair), n)[1], 0)

            return carry

        lax.fori_loop(0, HD // PAN, panel_step, 0)

        def leave(side, b):
            out = (olb, orb)[side]
            return pltpu.make_async_copy(bases.at[side, b], out.at[spot[0] * GROUP + b], sems.at[side, b])

        for b in range(count):
            for side in range(2):
                bases[side, b] = aug[2 * b + side, :, HD:].T
                leave(side, b).start()
        for b in range(count):
            for side in range(2):
                leave(side, b).wait()


LIMIT = 56 * 2**20
SHRINK = 1


def cost(flops, moved, trans=0):
    return pl.CostEstimate(flops=int(flops) // SHRINK, bytes_accessed=int(moved) // SHRINK, transcendentals=0)


def turn(rows, cosine, sine):
    head = rows[:, :128]
    lane = lax.broadcasted_iota(jnp.int32, head.shape, 1)
    partner = jnp.where(lane < RD // 2, pltpu.roll(head, 128 - RD // 2, 1), pltpu.roll(head, RD // 2, 1))
    return jnp.concatenate([head * cosine + partner * sine, rows[:, 128:]], axis=1)


MESH = pl.DeviceIdType.MESH
RIGHT = (
    {0: 0, 1: 3, 2: 6},
    {0: 1, 1: 4, 2: 3},
    {0: 2, 1: 0, 2: 4},
    {1: 1, 2: 0},
    {1: 2, 2: 1},
    {1: 5, 2: 2},
    {2: 7},
    {2: 8},
    {2: 5},
)
LEFT = (
    {3: 9, 2: 6, 1: 3},
    {3: 10, 2: 9, 1: 6},
    {3: 11, 2: 10, 1: 9},
    {2: 7, 1: 4},
    {2: 11, 1: 10},
    {2: 8, 1: 7},
    {1: 11},
    {1: 8},
    {1: 5},
)
SWAPS = ((3, 9), (4, 0), (10, 10), (11, 7))
ROLES = {
    "q": (0, 1),
    "k": (1, 2),
    "v": (2, 12),
    "out": (13, 13),
    "up": ((6, 3), (7, 8), (8, 4), (5, 5)),
    "down": ((9, 6), (12, 11), (14, 14), (15, 15)),
}


def beside(blocks):
    return jnp.concatenate([blocks[b] for b in range(D // HD)], axis=1)


def layer_kernel(
    rows_in, cotangent, segs, matrices, vectors, waves,
    held, units_out, grads_out, sum_0, sum_1, sum_2, extra, rows_out, sums, biases,
    units, grads, weight, act, pre, flipped, column, q, k, v, ga, att, dq, dk, dv, kseq, vseq, keys, vals, stage,
    raw, lines, cosine, sine, seg_row, seg_col,
    right_send, right_recv, left_send, left_recv, swap_send, swap_recv, row_send, row_recv, local,
):
    d, y, c = lax.axis_index("dp"), lax.axis_index("heads"), lax.axis_index("tensor")
    z, x = d // 2, d % 2
    by_x, by_y, by_core = {"dp": d + 1 - 2 * x}, {"heads": 1 - y}, {"tensor": 1 - c}
    shard = 2 * y + c
    block = rows_in.shape[0]
    tokens = units.shape[0]
    head = 32 + (shard * 2 + x) * 3

    barrier = pltpu.get_barrier_semaphore()
    for near in (by_x, by_y, by_core):
        pl.semaphore_signal(barrier, inc=1, device_id=near, device_id_type=MESH)

    @pl.when(z < 3)
    def _():
        pl.semaphore_signal(barrier, inc=1, device_id={"dp": d + 2}, device_id_type=MESH)

    @pl.when(z > 0)
    def _():
        pl.semaphore_signal(barrier, inc=1, device_id={"dp": d - 2}, device_id_type=MESH)

    def remote(source, target, send, recv, device):
        return pltpu.make_async_remote_copy(
            src_ref=source, dst_ref=target, send_sem=send, recv_sem=recv, device_id=device, device_id_type=MESH
        )

    def hop(table, step, half, sends, recvs, shift, at):
        place, part, sem = table[step][at], pl.ds(half * 4, 4), 2 * step + half
        source = weight.at[0, part] if step == 0 else held.at[place, part]
        return remote(source, held.at[place, part], sends.at[sem], recvs.at[sem], {"dp": d + 2 * shift})

    ways = ((RIGHT, right_send, right_recv, 1), (LEFT, left_send, left_recv, -1))

    def start(step, half):
        for table, sends, recvs, shift in ways:
            for at in table[step]:

                @pl.when(z == at)
                def _():
                    hop(table, step, half, sends, recvs, shift, at).start()

    def arrived(step, half):
        for table, sends, recvs, shift in ways:
            for at in table[step]:

                @pl.when(z == at + shift)
                def _():
                    hop(table, step, half, sends, recvs, shift, at).wait_recv()

    def sent(step):
        for table, sends, recvs, shift in ways:
            for at in table[step]:

                @pl.when(z == at)
                def _():
                    for half in range(2):
                        hop(table, step, half, sends, recvs, shift, at).wait_send()

    def pass_on(step, half):
        arrived(step, half)
        for later in {6: (7, 8), 7: ()}.get(step, (step + 1,)):
            start(later, half)

    def pump(step):
        pass_on(step, 0)
        pass_on(step, 1)

    def swap(i, side):
        return remote(held.at[SWAPS[i][side]], held.at[12 + i], swap_send.at[i], swap_recv.at[i], by_x)

    def start_swap(i):
        for side in range(2):

            @pl.when(x == side)
            def _():
                swap(i, side).start()

    def fetch(role, slot):
        for side in range(2):

            @pl.when(x == side)
            def _():
                pltpu.make_async_copy(held.at[role[side]], weight.at[slot], local.at[slot]).start()

    def fetched(slot):
        pltpu.make_async_copy(held.at[0], weight.at[slot], local.at[slot]).wait()

    def load(j, at):
        def begin(which):
            pltpu.make_async_copy(matrices.at[0, which * 8 : which * 8 + 8], raw.at[at], local.at[at]).start()

        pl.when((d < 5) | (d == 7))(lambda: begin(j))
        pl.when(d == 5)(lambda: begin(2 - j))
        pl.when(d == 6)(lambda: begin((j + 2) % 3))

    def loaded(j, at):
        pltpu.make_async_copy(matrices.at[0, :8], raw.at[at], local.at[at]).wait()
        weight[j] = raw[at].astype(jnp.bfloat16)

    def keep_own(j):
        for at in range(4):

            @pl.when(z == at)
            def _():
                pltpu.make_async_copy(weight.at[j], held.at[3 * at + j], local.at[8 + j]).start()

    load(0, 0)
    load(1, 1)
    loaded(0, 0)
    pl.semaphore_wait(barrier, 4 + (z + 1) // 2 % 2)
    start(0, 0)
    start(0, 1)
    load(2, 0)
    keep_own(0)
    rows = rows_in[...]
    centered = rows - jnp.mean(rows, axis=-1, keepdims=True)
    inverse = lax.rsqrt(jnp.mean(centered * centered, axis=-1, keepdims=True) + epsilon_norm)
    units[:block, :] = (centered * inverse).astype(jnp.bfloat16)
    grads[:block, :] = cotangent[...].astype(jnp.bfloat16)
    seg_row[x] = segs[...].astype(jnp.float32)

    def send_rows(kind, i, low, high, there, device):
        array = (units, grads)[kind]
        at = kind * 8 + i
        return remote(
            array.at[low:high], array.at[there : there + high - low], row_send.at[at], row_recv.at[at], device
        )

    half = block // 2

    def row_plan(kind):
        return (
            send_rows(kind, 0, 0, block, block, by_x),
            send_rows(kind, 1, 0, block, 2 * block, by_y),
            send_rows(kind, 2, block, block + half, 3 * block, by_y),
            send_rows(kind, 3, 2 * block + half, 3 * block, 3 * block + half, by_x),
            send_rows(kind, 4, 0, block, 4 * block, by_core),
            send_rows(kind, 5, block, 2 * block, 5 * block, by_core),
            send_rows(kind, 6, 2 * block, 3 * block, 6 * block, by_core),
            send_rows(kind, 7, 3 * block, 4 * block, 7 * block, by_core),
        )

    plans = [row_plan(kind) for kind in range(2)]
    for plan in plans:
        plan[0].start()
        plan[1].start()
        plan[4].start()
    segments = remote(seg_row.at[x], seg_row.at[x], swap_send.at[5], swap_recv.at[5], by_x)
    segments.start()
    loaded(1, 1)
    keep_own(1)
    loaded(2, 0)
    keep_own(2)
    for j in range(3):
        pltpu.make_async_copy(weight.at[j], held.at[j], local.at[8 + j]).wait()
    for i in range(4):
        lines[i : i + 1, :] = jnp.concatenate([vectors[8 * i + b : 8 * i + b + 1, :] for b in range(8)], axis=1)
    pump(0)
    segments.wait()
    for s in range(tokens // LEN):
        row = seg_row[s]
        wide = jnp.broadcast_to(row, (128, LEN)).T
        seg_col[s] = wide
        lane = lax.broadcasted_iota(jnp.int32, (LEN, 128), 1)
        token = lax.broadcasted_iota(jnp.int32, (LEN, 128), 0).astype(jnp.float32)
        first = jnp.sum(jnp.where(row < wide[:, 0:1], 1.0, 0.0), axis=1, keepdims=True)
        turns = (token - first) * waves[...]
        here = slice(s * LEN, (s + 1) * LEN)
        cosine[here, :] = jnp.where(lane < RD, jnp.cos(turns), 1.0)
        flips = jnp.where(lane < RD // 2, -1.0, jnp.where(lane < RD, 1.0, 0.0))
        sine[here, :] = jnp.sin(turns) * flips
    for plan in plans:
        plan[0].wait_recv()
        plan[2].start()
        plan[5].start()
        plan[1].wait_recv()
        plan[3].start()
        plan[6].start()
    pump(1)
    for plan in plans:
        plan[2].wait_recv()
        plan[3].wait_recv()
        plan[7].start()
    pump(2)
    start_swap(0)
    sent(0)
    fetch(ROLES["up"][0], 0)
    fetch(ROLES["down"][0], 1)
    for plan in plans:
        for i in range(4, 8):
            plan[i].wait_recv()
        for i in range(8):
            plan[i].wait_send()
    keep = [pltpu.make_async_copy(units, units_out, local.at[6]), pltpu.make_async_copy(grads, grads_out, local.at[7])]
    for copy in keep:
        copy.start()

    tile = 512

    def run_mlp(slot):
        hidden = SLOTS[0][slot] + (SLOTS[1][slot] - SLOTS[0][slot]) * x
        wu, wd = weight.at[0], weight.at[1]

        def body(i, carry):
            here = pl.ds(pl.multiple_of(i * tile, tile), tile)
            norm = (units[here, :].astype(jnp.float32) * lines[2:3, :] + lines[3:4, :]).astype(jnp.bfloat16)
            inner = dot_nn(norm, wu[...].reshape(D, HD)) + vectors[pl.ds(64 + shard * 8 + hidden, 1), :]
            pull = dot_nt(grads[here, :], beside(wd))
            share = 0.5 + 0.5 * lax.erf(inner * (0.5**0.5))
            act[here, :] = (inner * share).astype(jnp.bfloat16)
            slope = share + inner * jnp.exp(-0.5 * inner * inner) * ((2.0 * 3.141592653589793) ** (-0.5))
            pre[here, :] = (slope * pull).astype(jnp.bfloat16)
            return carry

        lax.fori_loop(0, tokens // tile, body, 0)

    def save_rows(source, i):
        copy = pltpu.make_async_copy(source, rows_out.at[i], local.at[8 + i])
        copy.start()
        return copy

    def put(i, to_0, to_1, sem):
        for side, target in ((0, to_0), (1, to_1)):
            if target is not None:

                @pl.when(x == side)
                def _():
                    pltpu.make_async_copy(stage.at[i], target, local.at[16 + sem]).start()

        def finish():
            for side, target in ((0, to_0), (1, to_1)):
                if target is not None:

                    @pl.when(x == side)
                    def _():
                        pltpu.make_async_copy(stage.at[i], target, local.at[16 + sem]).wait()

        return finish

    def run_down(source, at):
        flipped[:HD, :] = source[...].T

        def body(b, carry):
            here = pl.ds(pl.multiple_of(b * HD, HD), HD)
            stage[at, b] = dot_nn(flipped[:HD, :], grads[:, here]).astype(jnp.bfloat16)
            return carry

        lax.fori_loop(0, D // HD, body, 0)

    def run_up(sources, places, slots, gain, row, offset, more=False):
        for i, source in enumerate(sources):
            wide = source[...]
            flipped[i * HD : (i + 1) * HD, :] = wide.T
            total = jnp.sum(wide.astype(jnp.float32), axis=0, keepdims=True)
            biases[:, offset + i * HD : offset + (i + 1) * HD] = total
            column[i] = jnp.broadcast_to(total, (128, HD)).T

        def body(b, carry):
            here = pl.ds(pl.multiple_of(b * HD, HD), HD)
            gains, shifts = (sums[row : row + 1, here], sums[row + 1 : row + 2, here]) if more else (0.0, 0.0)
            every = dot_nn(flipped[: len(sources) * HD, :], units[:, here])
            for i, (place, slot) in enumerate(zip(places, slots)):
                turned = every[i * HD : (i + 1) * HD, :]
                w = weight[slot, b].T.astype(jnp.float32)
                bias = column[i][:, 0:1]
                gains = gains + jnp.sum(w * turned, axis=0, keepdims=True)
                shifts = shifts + jnp.sum(w * bias, axis=0, keepdims=True)
                result = turned * lines[gain : gain + 1, here] + bias * lines[gain + 1 : gain + 2, here]
                stage[place, b] = result.T.astype(jnp.bfloat16)
            sums[row : row + 1, here] = gains
            sums[row + 1 : row + 2, here] = shifts
            return carry

        lax.fori_loop(0, D // HD, body, 0)

    fetched(0)
    fetched(1)
    run_mlp(0)
    saves = [save_rows(act, 0), save_rows(pre, 1)]
    pass_on(3, 0)
    run_down(act, 0)
    done = put(0, sum_0.at[3], sum_0.at[2], 0)
    pass_on(3, 1)
    start_swap(1)
    run_up([pre], [1], [0], 2, 2, 3 * HD)
    done_up = put(1, sum_0.at[2], sum_0.at[1], 1)
    pump(4)
    start_swap(2)
    pump(5)

    swap(0, 0).wait_recv()
    swap(1, 0).wait_recv()
    for i, role in enumerate(("q", "k", "v", "out")):
        fetch(ROLES[role], 2 + i)
    for i in range(4):
        fetched(2 + i)

    def project_rows(i, carry):
        here = pl.ds(pl.multiple_of(i * tile, tile), tile)
        turns = []
        for u in range(tile // block):
            r = i * (tile // block) + u
            a = (((x + r % 2) % 2) * 2 + (y + r // 2 % 2) % 2) * 2 + (c + r // 4) % 2
            turns.append(pl.ds(pl.multiple_of(a * block, block), block))
        cos_here = jnp.concatenate([cosine[t, :] for t in turns], axis=0)
        sin_here = jnp.concatenate([sine[t, :] for t in turns], axis=0)
        norm = (units[here, :].astype(jnp.float32) * lines[0:1, :] + lines[1:2, :]).astype(jnp.bfloat16)
        q[here, :] = turn(
            dot_nn(norm, weight[2].reshape(D, HD)) + vectors[pl.ds(head + 0, 1), :], cos_here, sin_here
        ).astype(jnp.bfloat16)
        k[here, :] = turn(
            dot_nn(norm, weight[3].reshape(D, HD)) + vectors[pl.ds(head + 1, 1), :], cos_here, sin_here
        ).astype(jnp.bfloat16)
        v[here, :] = (dot_nn(norm, weight[4].reshape(D, HD)) + vectors[pl.ds(head + 2, 1), :]).astype(jnp.bfloat16)
        ga[here, :] = dot_nt(grads[here, :], beside(weight.at[5])).astype(jnp.bfloat16)
        return carry

    lax.fori_loop(0, tokens // tile, project_rows, 0)
    pass_on(6, 0)
    pieces = LEN // block

    def attend(s, carry):
        scale = HD ** (-0.5)
        spots = []
        for i in range(pieces):
            a = s * pieces + i
            r = ((c + a % 2) % 2) * 4 + (x + a // 4) % 2 + 2 * ((y + a // 2 % 2) % 2)
            spots.append(pl.ds(pl.multiple_of(r * block, block), block))
        for i in range(pieces):
            kseq[i * block : (i + 1) * block, :] = k[spots[i], :]
            vseq[i * block : (i + 1) * block, :] = v[spots[i], :]
        keys[...] = jnp.zeros_like(keys)
        vals[...] = jnp.zeros_like(vals)
        for i in range(pieces):
            upto = (i + 1) * block
            angle = pl.ds(pl.multiple_of(s * LEN + i * block, block), block)
            mine, pulled = q[spots[i], :], ga[spots[i], :]
            scores = dot_nt(mine, kseq[:upto, :]) * scale
            to = lax.broadcasted_iota(jnp.int32, (block, upto), 0) + i * block
            of = lax.broadcasted_iota(jnp.int32, (block, upto), 1)
            allowed = (seg_col[s, i * block : upto, 0:1] == seg_row[s, :, :upto]) & (of <= to)
            scores = jnp.where(allowed, scores, -1e30)
            powers = jnp.exp(scores - jnp.max(scores, axis=-1, keepdims=True))
            probs = powers / jnp.sum(powers, axis=-1, keepdims=True)
            low = probs.astype(jnp.bfloat16)
            att[spots[i], :] = dot_nn(low, vseq[:upto, :]).astype(jnp.bfloat16)
            pull = dot_nt(pulled, vseq[:upto, :])
            inner = jnp.sum(probs * pull, axis=-1, keepdims=True)
            gs = (probs * (pull - inner)).astype(jnp.bfloat16)
            turned = turn(dot_nn(gs, kseq[:upto, :]) * scale, cosine[angle, :], -sine[angle, :])
            dq[spots[i], :] = turned.astype(jnp.bfloat16)
            keys[:upto, :] = keys[:upto, :] + dot_tn(gs, mine)
            vals[:upto, :] = vals[:upto, :] + dot_tn(low, pulled)
        for i in range(pieces):
            here = slice(i * block, (i + 1) * block)
            angle = pl.ds(pl.multiple_of(s * LEN + i * block, block), block)
            turned = turn(keys[here, :] * scale, cosine[angle, :], -sine[angle, :])
            dk[spots[i], :] = turned.astype(jnp.bfloat16)
            dv[spots[i], :] = vals[here, :].astype(jnp.bfloat16)

        @pl.when(s == 0)
        def _():
            pass_on(6, 1)
            start_swap(3)

        return carry

    lax.fori_loop(0, tokens // LEN, attend, 0)
    for copy in saves:
        copy.wait()
    saves = [save_rows(a, 4 + i) for i, a in enumerate((att, dq, dk, dv))]
    run_up([dv], [4], [4], 0, 0, 2 * HD, False)

    back_v = remote(stage.at[4], sum_0.at[1], swap_send.at[6], swap_recv.at[6], by_x)
    pl.when(x == 1)(back_v.start)
    done_v = put(4, sum_2.at[0], None, 4)
    pass_on(7, 0)
    done()
    run_down(att, 0)
    done = put(0, None, extra, 5)
    back_out = remote(stage.at[0], sum_1.at[0], swap_send.at[4], swap_recv.at[4], by_x)
    pl.when(x == 0)(back_out.start)
    run_up([dq, dk], [2, 3], [2, 3], 0, 0, 0, True)
    done_qk = [put(2, sum_1.at[0], sum_0.at[0], 2), put(3, sum_0.at[0], sum_2.at[0], 3)]
    pass_on(7, 1)
    fetch(ROLES["up"][1], 0)
    fetch(ROLES["down"][1], 1)

    fetched(0)
    fetched(1)
    run_mlp(1)
    saves += [save_rows(act, 2), save_rows(pre, 3)]
    done_up()
    run_down(act, 1)
    done_up = put(1, extra, sum_0.at[3], 6)
    pl.when(x == 0)(back_v.wait_recv)
    pl.when(x == 1)(back_v.wait_send)
    pl.when(x == 1)(back_out.wait_recv)
    pl.when(x == 0)(back_out.wait_send)
    arrived(8, 0)
    arrived(8, 1)
    for step in range(1, len(RIGHT)):
        sent(step)
    for i in range(4):
        swap(i, 0).wait_send()
    for i in range(2, 4):
        swap(i, 0).wait_recv()
    for copy in saves + keep:
        copy.wait()
    for finish in done_qk + [done_v, done, done_up]:
        finish()


def layer(rows, cotangent, segments, matrices, vectors, waves):
    block = rows.shape[0]
    tokens = 8 * block
    count = tokens // LEN
    anywhere, near = pl.BlockSpec(memory_space=pl.ANY), pl.BlockSpec(memory_space=pltpu.VMEM)
    low, full = jnp.bfloat16, jnp.float32
    group = (D // HD, HD, HD)
    narrow = pltpu.VMEM((tokens, HD), low)
    return pl.pallas_call(
        layer_kernel,
        in_specs=[near] * 3 + [anywhere] + [near] * 2,
        out_specs=[anywhere] * 8 + [near] * 2,
        out_shape=[
            jax.ShapeDtypeStruct((16,) + group, low),
            jax.ShapeDtypeStruct((tokens, D), low),
            jax.ShapeDtypeStruct((tokens, D), low),
        ]
        + [jax.ShapeDtypeStruct((4,) + group, low)] * 3
        + [
            jax.ShapeDtypeStruct(group, low),
            jax.ShapeDtypeStruct((8, tokens, HD), low),
            jax.ShapeDtypeStruct((4, D), full),
            jax.ShapeDtypeStruct((1, 4 * HD), full),
        ],
        scratch_shapes=[
            pltpu.VMEM((tokens, D), low),
            pltpu.VMEM((tokens, D), low),
            pltpu.VMEM((6,) + group, low),
            narrow,
            narrow,
            pltpu.VMEM((3 * HD, tokens), low),
            pltpu.VMEM((3, HD, 128), full),
        ]
        + [narrow] * 8
        + [pltpu.VMEM((LEN, HD), low)] * 2
        + [pltpu.VMEM((LEN, HD), full)] * 2
        + [
            pltpu.VMEM((5,) + group, low),
            pltpu.VMEM((2,) + group, full),
            pltpu.VMEM((4, D), full),
            pltpu.VMEM((tokens, 128), full),
            pltpu.VMEM((tokens, 128), full),
            pltpu.VMEM((count, 1, LEN), full),
            pltpu.VMEM((count, LEN, 128), full),
        ]
        + [pltpu.SemaphoreType.DMA((18,))] * 4
        + [pltpu.SemaphoreType.DMA((7,))] * 2
        + [pltpu.SemaphoreType.DMA((16,))] * 2
        + [pltpu.SemaphoreType.DMA((24,))],
        compiler_params=pltpu.CompilerParams(
            vmem_limit_bytes=63 * 2**20, collective_id=0, has_side_effects=True
        ),
        cost_estimate=cost(6e10, 1e8),
        name="layer",
    )(rows, cotangent, segments, matrices, vectors, waves)


def remote_copy(source, target, send, recv, device):
    return pltpu.make_async_remote_copy(
        src_ref=source, dst_ref=target, send_sem=send, recv_sem=recv, device_id=device, device_id_type=MESH
    )


def greet(peers):
    barrier = pltpu.get_barrier_semaphore()
    for near in peers:
        pl.semaphore_signal(barrier, inc=1, device_id=near, device_id_type=MESH)
    pl.semaphore_wait(barrier, len(peers))


def swap_with(source, send, recv, x, device, to_0, to_1):
    copies = [remote_copy(source, there, send, recv, device) for there in (to_0, to_1)]
    for side in range(2):
        pl.when(x == side)(copies[side].start)
    return copies[0]


def fetch_role(held, role, target, sem, x):
    for side in range(2):

        @pl.when(x == side)
        def _():
            pltpu.make_async_copy(held.at[role[side]], target, sem).start()


def hidden_rows(units, grads, lines, bias, wu, wd, act, pre, before):
    tile = 512

    def body(i, carry):
        here = pl.ds(pl.multiple_of(i * tile, tile), tile)
        before(i)
        norm = (units[here, :].astype(jnp.float32) * lines[2:3, :] + lines[3:4, :]).astype(jnp.bfloat16)
        inner = dot_nn(norm, wu[...].reshape(D, HD)) + bias
        pull = dot_nt(grads[here, :], beside(wd))
        share = 0.5 + 0.5 * lax.erf(inner * (0.5**0.5))
        act[here, :] = (inner * share).astype(jnp.bfloat16)
        slope = share + inner * jnp.exp(-0.5 * inner * inner) * ((2.0 * 3.141592653589793) ** (-0.5))
        pre[here, :] = (slope * pull).astype(jnp.bfloat16)
        return carry

    lax.fori_loop(0, units.shape[0] // tile, body, 0)


def down_blocks(flipped, act, grads, stage):
    flipped[:HD, :] = act[...].T

    def body(b, carry):
        here = pl.ds(pl.multiple_of(b * HD, HD), HD)
        stage[b] = dot_nn(flipped[:HD, :], grads[:, here]).astype(jnp.bfloat16)
        return carry

    lax.fori_loop(0, D // HD, body, 0)


def up_blocks(flipped, column, pres, biases, units, weight, lines, stage, gains_out, shifts_out, early):
    parts = len(pres)
    for i, pre in enumerate(pres):
        wide = pre[...]
        flipped[i * HD : (i + 1) * HD, :] = wide.T
        bias = jnp.sum(wide.astype(jnp.float32), axis=0, keepdims=True)
        biases[i] = bias
        column[i] = jnp.broadcast_to(bias, (128, HD)).T

    def body(b, carry):
        here = pl.ds(pl.multiple_of(b * HD, HD), HD)
        gains, shifts = early[2:3, here], early[3:4, here]
        every = dot_nn(flipped[: parts * HD, :], units[:, here])
        for i in range(parts):
            turned = every[i * HD : (i + 1) * HD, :]
            w = weight[i, b].T.astype(jnp.float32)
            bias = column[i][:, 0:1]
            gains = gains + jnp.sum(w * turned, axis=0, keepdims=True)
            shifts = shifts + jnp.sum(w * bias, axis=0, keepdims=True)
            result = turned * lines[2:3, here] + bias * lines[3:4, here]
            stage[i, b] = result.T.astype(jnp.bfloat16)
        gains_out[:, here] = gains
        shifts_out[:, here] = shifts
        return carry

    lax.fori_loop(0, D // HD, body, 0)


def spread(vectors, lines):
    for i in range(4):
        lines[i : i + 1, :] = jnp.concatenate([vectors[8 * i + b : 8 * i + b + 1, :] for b in range(8)], axis=1)


def third_kernel(
    held, units_in, grads_in, rows_in, vectors, early, extra, sum_1_in, sum_2_in,
    sum_1, sum_2, rows_out, sums, biases,
    units, grads, weight, act, pres, flipped, column, stage, lines,
    swap_send, swap_recv, loads, local,
):
    d, y, c = lax.axis_index("dp"), lax.axis_index("heads"), lax.axis_index("tensor")
    x = d % 2
    shard = 2 * y + c
    tokens = units.shape[0]
    tile = 512
    by_x = {"dp": d + 1 - 2 * x}
    greet([by_x])
    swaps = [swap_with(extra, swap_send.at[0], swap_recv.at[0], x, by_x, sum_1.at[3], sum_1.at[1])]
    for slot, role in ((1, ROLES["up"][2]), (2, ROLES["down"][2])):
        fetch_role(held, role, weight.at[slot], local.at[slot], x)

    def row_loads(i):
        here = pl.ds(pl.multiple_of(i * tile, tile), tile)
        return [
            pltpu.make_async_copy(source.at[here], target.at[here], loads.at[2 * i + j])
            for j, (source, target) in enumerate(((units_in, units), (grads_in, grads)))
        ]

    for i in range(tokens // tile):
        for copy in row_loads(i):
            copy.start()
    fetch_role(held, ROLES["up"][1], weight.at[0], local.at[0], x)
    second = pltpu.make_async_copy(rows_in.at[3], pres.at[0], local.at[3])
    second.start()
    spread(vectors, lines)
    for slot in (1, 2):
        pltpu.make_async_copy(held.at[0], weight.at[slot], local.at[slot]).wait()

    def ready(i):
        for copy in row_loads(i):
            copy.wait()

    hidden = SLOTS[0][2] + (SLOTS[1][2] - SLOTS[0][2]) * x
    bias = vectors[pl.ds(64 + shard * 8 + hidden, 1), :]
    hidden_rows(units, grads, lines, bias, weight.at[1], weight.at[2], act, pres.at[1], ready)
    saves = [
        pltpu.make_async_copy(act, rows_out.at[0], local.at[4]),
        pltpu.make_async_copy(pres.at[1], rows_out.at[1], local.at[5]),
    ]
    for copy in saves:
        copy.start()
    down_blocks(flipped, act, grads, stage.at[2])
    swaps.append(swap_with(stage.at[2], swap_send.at[1], swap_recv.at[1], x, by_x, sum_2.at[3], sum_1.at[3]))
    second.wait()
    pltpu.make_async_copy(held.at[0], weight.at[0], local.at[0]).wait()
    up_blocks(
        flipped, column, [pres.at[0], pres.at[1]], biases, units, weight, lines, stage,
        sums.at[0], sums.at[1], early,
    )
    puts = [
        [pltpu.make_async_copy(stage.at[i], place, local.at[6 + i]) for place in places]
        for i, places in enumerate(((sum_1.at[2], sum_1.at[2]), (sum_2.at[2], sum_1.at[1])))
    ]
    for pair in puts:
        for side in range(2):
            pl.when(x == side)(pair[side].start)
    for copy in swaps + saves:
        copy.wait()
    for pair in puts:
        for side in range(2):
            pl.when(x == side)(pair[side].wait)


def third(held, units, grads, rows, vectors, sums, extra, sum_1, sum_2):
    tokens = units.shape[0]
    anywhere, near = pl.BlockSpec(memory_space=pl.ANY), pl.BlockSpec(memory_space=pltpu.VMEM)
    low, full = jnp.bfloat16, jnp.float32
    group = (D // HD, HD, HD)
    return pl.pallas_call(
        third_kernel,
        in_specs=[anywhere] * 4 + [near] * 2 + [anywhere] * 3,
        out_specs=[anywhere] * 3 + [near] * 2,
        out_shape=[
            jax.ShapeDtypeStruct((4,) + group, low),
            jax.ShapeDtypeStruct((4,) + group, low),
            jax.ShapeDtypeStruct((2, tokens, HD), low),
            jax.ShapeDtypeStruct((2, 1, D), full),
            jax.ShapeDtypeStruct((2, 1, HD), full),
        ],
        input_output_aliases={7: 0, 8: 1},
        scratch_shapes=[
            pltpu.VMEM((tokens, D), low),
            pltpu.VMEM((tokens, D), low),
            pltpu.VMEM((3,) + group, low),
            pltpu.VMEM((tokens, HD), low),
            pltpu.VMEM((2, tokens, HD), low),
            pltpu.VMEM((2 * HD, tokens), low),
            pltpu.VMEM((2, HD, 128), full),
            pltpu.VMEM((3,) + group, low),
            pltpu.VMEM((4, D), full),
            pltpu.SemaphoreType.DMA((2,)),
            pltpu.SemaphoreType.DMA((2,)),
            pltpu.SemaphoreType.DMA((8,)),
            pltpu.SemaphoreType.DMA((8,)),
        ],
        compiler_params=pltpu.CompilerParams(
            vmem_limit_bytes=56 * 2**20, collective_id=1, has_side_effects=True
        ),
        cost_estimate=cost(2e10, 6e7),
        name="third",
    )(held, units, grads, rows, vectors, sums, extra, sum_1, sum_2)


def rest_kernel(
    held, units_in, grads_in, rows_in, third_rows, vectors, early, early_bias, third_sums, third_bias, sum_2_in,
    sum_2, rows_out, total, by_x_out, by_y_out, by_xy_out, own_out,
    units, grads, weight, acts, pre, flipped, column, stage, lines, more, added, biases, current, received, shares, other,
    swap_send, swap_recv, hop_send, hop_recv, loads, local, share_send, share_recv,
):
    d, y, c = lax.axis_index("dp"), lax.axis_index("heads"), lax.axis_index("tensor")
    z, x = d // 2, d % 2
    shard = 2 * y + c
    tokens = units.shape[0]
    block, tile = tokens // 8, 512
    by_x, by_y, by_core = {"dp": d + 1 - 2 * x}, {"heads": 1 - y}, {"tensor": 1 - c}
    by_z = [{"dp": d + 2 - 4 * (z % 2)}, {"dp": d + 4 - 8 * (z // 2)}]
    peers = [by_core, by_y] + by_z + [by_x]
    greet(peers)
    fetch_role(held, ROLES["up"][3], weight.at[0], local.at[0], x)
    fetch_role(held, ROLES["down"][3], weight.at[1], local.at[1], x)

    def row_loads(i):
        here = pl.ds(pl.multiple_of(i * tile, tile), tile)
        return [
            pltpu.make_async_copy(source.at[here], target.at[here], loads.at[2 * i + j])
            for j, (source, target) in enumerate(((units_in, units), (grads_in, grads)))
        ]

    for i in range(tokens // tile):
        for copy in row_loads(i):
            copy.start()
    out_roles = (ROLES["down"][0], ROLES["down"][1], ROLES["out"], ROLES["down"][2])
    out_rows = [rows_in.at[i] for i in (0, 2, 4)] + [third_rows.at[0]]
    for i in range(4):
        fetch_role(held, out_roles[i], weight.at[2 + i], local.at[2 + i], x)
        pltpu.make_async_copy(out_rows[i], acts.at[i], local.at[6 + i]).start()
    spread(vectors, lines)
    more[0:2, :] = early[0:2, :]
    more[2:3, :] = third_sums[0]
    more[3:4, :] = third_sums[1]
    for slot in (0, 1):
        pltpu.make_async_copy(held.at[0], weight.at[slot], local.at[slot]).wait()

    def ready(i):
        for copy in row_loads(i):
            copy.wait()

    hidden = [SLOTS[0][s] + (SLOTS[1][s] - SLOTS[0][s]) * x for s in range(4)]
    bias = vectors[pl.ds(64 + shard * 8 + hidden[3], 1), :]
    hidden_rows(units, grads, lines, bias, weight.at[0], weight.at[1], acts.at[4], pre, ready)
    saves = [pltpu.make_async_copy(pre, rows_out, local.at[10])]
    saves[0].start()
    down_blocks(flipped, acts.at[4], grads, stage.at[1])
    saves.append(swap_with(stage.at[1], swap_send.at[0], swap_recv.at[0], x, by_x, sum_2.at[2], sum_2.at[3]))
    up_blocks(
        flipped, column, [pre], biases, units, weight, lines, stage, added.at[0], added.at[1], more
    )
    put = pltpu.make_async_copy(stage.at[0], sum_2.at[1], local.at[11])
    put.start()
    saves.append(put)

    current[0] = jnp.zeros(current.shape[1:], jnp.float32)
    own = jnp.sum(grads[:block, :].astype(jnp.float32), axis=0, keepdims=True)
    for i, line in enumerate((more[0:1, :], more[1:2, :], added[0], added[1])):
        for b in range(8):
            current[0, 8 * i + b : 8 * i + b + 1, :] = line[:, b * HD : (b + 1) * HD]
    for b in range(8):
        current[0, 56 + b : 57 + b, :] = own[:, b * HD : (b + 1) * HD]
        current[0, 96 + b : 97 + b, :] = own[:, b * HD : (b + 1) * HD]
    for i in range(3):
        at = 32 + (shard * 2 + x) * 3 + i
        current[0, pl.ds(at, 1), :] = early_bias[:, i * HD : (i + 1) * HD]
    for i, line in enumerate((early_bias[:, 3 * HD :], third_bias[0], third_bias[1], biases[0])):
        current[0, pl.ds(64 + shard * 8 + hidden[i], 1), :] = line
    hops = [
        remote_copy(current.at[i], received.at[i], hop_send.at[i], hop_recv.at[i], near) for i, near in enumerate(peers)
    ]

    def finish_hop(i):
        hops[i].wait()
        result = current[i] + received[i]
        if i + 1 < len(peers):
            current[i + 1] = result
            hops[i + 1].start()
        else:
            total[...] = result

    hops[0].start()

    for i in range(4):
        pltpu.make_async_copy(held.at[0], weight.at[2 + i], local.at[2 + i]).wait()
        pltpu.make_async_copy(rows_in.at[0], acts.at[i], local.at[6 + i]).wait()
    by_slot = (2, 3, 4, 5, 1)

    def share_rows(i):
        here = slice(i * tile, (i + 1) * tile)
        left = jnp.concatenate([acts[j, here, :] for j in range(5)], axis=1)
        for b in range(D // HD):
            right = jnp.concatenate([weight[slot, b] for slot in by_slot], axis=0)
            yield slice(b * HD, (b + 1) * HD), dot_nn(left, right)

    sends = [
        remote_copy(
            shares.at[i * tile : (i + 1) * tile],
            other.at[i * tile : (i + 1) * tile],
            share_send.at[i],
            share_recv.at[i],
            by_core,
        )
        for i in range(2)
    ]
    for i in range(2):
        for columns, result in share_rows(2 + i):
            shares[i * tile : (i + 1) * tile, columns] = result.astype(jnp.bfloat16)
        sends[i].start()
        finish_hop(i)
    for copy in sends:
        copy.wait_send()
    for i in range(2):
        sends[i].wait_recv()
        for columns, result in share_rows(i):
            theirs = other[i * tile : (i + 1) * tile, columns].astype(jnp.float32)
            shares[i * tile : (i + 1) * tile, columns] = (result + theirs).astype(jnp.bfloat16)
        finish_hop(2 + i)
    for i, target in enumerate((own_out, by_x_out, by_y_out, by_xy_out)):
        copy = pltpu.make_async_copy(shares.at[i * block : (i + 1) * block], target.at[0], local.at[12 + i])
        copy.start()
        saves.append(copy)
    finish_hop(4)
    for copy in saves:
        copy.wait()


def rest(held, units, grads, rows, third_rows, vectors, sums, biases, third_sums, third_bias, sum_2):
    tokens = units.shape[0]
    anywhere, near = pl.BlockSpec(memory_space=pl.ANY), pl.BlockSpec(memory_space=pltpu.VMEM)
    low, full = jnp.bfloat16, jnp.float32
    group = (D // HD, HD, HD)
    table = vectors.shape
    return pl.pallas_call(
        rest_kernel,
        in_specs=[anywhere] * 5 + [near] * 5 + [anywhere],
        out_specs=[anywhere] * 2 + [near] + [anywhere] * 4,
        out_shape=[
            jax.ShapeDtypeStruct((4,) + group, low),
            jax.ShapeDtypeStruct((tokens, HD), low),
            jax.ShapeDtypeStruct(table, full),
        ]
        + [jax.ShapeDtypeStruct((2, tokens // 8, D), low)] * 4,
        input_output_aliases={10: 0},
        scratch_shapes=[
            pltpu.VMEM((tokens, D), low),
            pltpu.VMEM((tokens, D), low),
            pltpu.VMEM((6,) + group, low),
            pltpu.VMEM((5, tokens, HD), low),
            pltpu.VMEM((tokens, HD), low),
            pltpu.VMEM((HD, tokens), low),
            pltpu.VMEM((1, HD, 128), full),
            pltpu.VMEM((2,) + group, low),
            pltpu.VMEM((4, D), full),
            pltpu.VMEM((4, D), full),
            pltpu.VMEM((2, 1, D), full),
            pltpu.VMEM((1, 1, HD), full),
            pltpu.VMEM((5,) + table, full),
            pltpu.VMEM((5,) + table, full),
            pltpu.VMEM((tokens // 2, D), low),
            pltpu.VMEM((tokens // 2, D), low),
            pltpu.SemaphoreType.DMA((1,)),
            pltpu.SemaphoreType.DMA((1,)),
            pltpu.SemaphoreType.DMA((5,)),
            pltpu.SemaphoreType.DMA((5,)),
            pltpu.SemaphoreType.DMA((8,)),
            pltpu.SemaphoreType.DMA((16,)),
            pltpu.SemaphoreType.DMA((2,)),
            pltpu.SemaphoreType.DMA((2,)),
        ],
        compiler_params=pltpu.CompilerParams(
            vmem_limit_bytes=60 * 2**20, collective_id=3, has_side_effects=True
        ),
        cost_estimate=cost(4e10, 6e7),
        name="rest",
    )(held, units, grads, rows, third_rows, vectors, sums, biases, third_sums, third_bias, sum_2)


def input_kernel(
    held, rows_in, third_rows, late, gains, by_x_in, by_y_in, by_xy_in, own_in,
    by_x_out, by_y_out, by_xy_out, own_out,
    weight, rows, shares, other,
    local, share_send, share_recv,
):
    x, c = lax.axis_index("dp") % 2, lax.axis_index("tensor")
    by_core = {"tensor": 1 - c}
    barrier = pltpu.get_barrier_semaphore()
    pl.semaphore_signal(barrier, inc=1, device_id=by_core, device_id_type=MESH)
    pl.semaphore_wait(barrier, 1)
    tokens = rows.shape[1]
    block, tile = tokens // 8, 512
    roles = (ROLES["q"], ROLES["k"], ROLES["v"]) + ROLES["up"]
    sources = [rows_in.at[i] for i in (5, 6, 7, 1, 3)] + [third_rows.at[1], late]
    for i, (role, source) in enumerate(zip(roles, sources)):
        for side in range(2):

            @pl.when(x == side)
            def _():
                pltpu.make_async_copy(held.at[role[side]], weight.at[i], local.at[i]).start()

        pltpu.make_async_copy(source, rows.at[i], local.at[7 + i]).start()
    for i, source in enumerate(sources):
        pltpu.make_async_copy(held.at[0], weight.at[i], local.at[i]).wait()
        pltpu.make_async_copy(source, rows.at[i], local.at[7 + i]).wait()

    def share_rows(i):
        here = pl.ds(i * tile, tile)
        sides = ((0, 3), (3, 7))
        lefts = [jnp.concatenate([rows[r, here, :] for r in range(*side)], axis=1) for side in sides]
        for b in range(D // HD):
            columns = slice(b * HD, (b + 1) * HD)
            parts = []
            for j, side in enumerate(sides):
                right = jnp.concatenate([weight[r, b] for r in range(*side)], axis=1)
                parts.append(dot_nt(lefts[j], right) * gains[j : j + 1, columns])
            yield columns, parts[0] + parts[1]

    sends = [
        pltpu.make_async_remote_copy(
            src_ref=shares.at[i * tile : (i + 1) * tile],
            dst_ref=other.at[i * tile : (i + 1) * tile],
            send_sem=share_send.at[i],
            recv_sem=share_recv.at[i],
            device_id=by_core,
            device_id_type=MESH,
        )
        for i in range(2)
    ]
    for i in range(2):
        for columns, result in share_rows(2 + i):
            shares[i * tile : (i + 1) * tile, columns] = result.astype(jnp.bfloat16)
        sends[i].start()
    for copy in sends:
        copy.wait_send()
    for i in range(2):
        sends[i].wait_recv()
        for columns, result in share_rows(i):
            theirs = other[i * tile : (i + 1) * tile, columns].astype(jnp.float32)
            shares[i * tile : (i + 1) * tile, columns] = (result + theirs).astype(jnp.bfloat16)
    for i, target in enumerate((own_out, by_x_out, by_y_out, by_xy_out)):
        pltpu.make_async_copy(shares.at[i * block : (i + 1) * block], target.at[1], local.at[14 + i]).start()
    for i, target in enumerate((own_out, by_x_out, by_y_out, by_xy_out)):
        pltpu.make_async_copy(shares.at[i * block : (i + 1) * block], target.at[1], local.at[14 + i]).wait()


def input_share(held, rows, third_rows, late, gains, parts):
    tokens = rows.shape[1]
    anywhere = pl.BlockSpec(memory_space=pl.ANY)
    low = jnp.bfloat16
    return pl.pallas_call(
        input_kernel,
        in_specs=[anywhere] * 4 + [pl.BlockSpec(memory_space=pltpu.VMEM)] + [anywhere] * 4,
        out_specs=[anywhere] * 4,
        out_shape=[jax.ShapeDtypeStruct((2, tokens // 8, D), low)] * 4,
        input_output_aliases={5 + i: i for i in range(4)},
        scratch_shapes=[
            pltpu.VMEM((7, D // HD, HD, HD), low),
            pltpu.VMEM((7, tokens, HD), low),
            pltpu.VMEM((tokens // 2, D), low),
            pltpu.VMEM((tokens // 2, D), low),
            pltpu.SemaphoreType.DMA((18,)),
            pltpu.SemaphoreType.DMA((2,)),
            pltpu.SemaphoreType.DMA((2,)),
        ],
        compiler_params=pltpu.CompilerParams(vmem_limit_bytes=LIMIT, collective_id=2, has_side_effects=True),
        cost_estimate=cost(2 * 7 * tokens * D * HD, 5e7),
        name="input_share",
    )(held, rows, third_rows, late, gains, *parts)


def soap_part(places, grad, blocks, previous):
    total, count = blocks[0].shape[0], grad.shape[0]
    mats = 2 * count
    own = pl.BlockSpec((GROUP, HD, HD), lambda i, at: (i, 0, 0))
    some = pl.BlockSpec((GROUP, HD, HD), lambda i, at: (at[0] + i, 0, 0))
    anywhere = pl.BlockSpec(memory_space=pl.ANY)
    full = jax.ShapeDtypeStruct((total, HD, HD), jnp.float32)
    shapes = [full, jax.ShapeDtypeStruct((total, HD, HD), jnp.bfloat16)] + [full] * 6
    extra = [] if previous is None else list(previous)

    def body(at, *refs):
        soap_kernel(count, at, *refs[:8], *refs[8 + len(extra) :])

    return pl.pallas_call(
        body,
        grid_spec=pltpu.PrefetchScalarGridSpec(
            num_scalar_prefetch=1,
            grid=(count // GROUP,),
            in_specs=[own] + [some] * 7 + [anywhere] * len(extra),
            out_specs=[some] * 6 + [anywhere] * 2,
            scratch_shapes=[
                pltpu.VMEM((mats, HD, 2 * HD), jnp.float32),
                pltpu.VMEM((PAN * PACK + PACK, 128), jnp.float32),
                pltpu.VMEM((2, count, HD, HD), jnp.float32),
                pltpu.SemaphoreType.DMA((2, count)),
            ],
        ),
        out_shape=shapes,
        input_output_aliases={9 + i: i for i in range(len(extra))},
        compiler_params=pltpu.CompilerParams(vmem_limit_bytes=LIMIT),
        cost_estimate=cost(count * 40 * 2 * HD**3 * 3, count * 16 * 4 * HD * HD),
        name="soap",
    )(places, grad, *blocks, *extra)


def adam_vector(grad, params, first, second):
    first_new = beta_one * first + (1.0 - beta_one) * grad
    second_new = beta_two * second + (1.0 - beta_two) * grad * grad
    direction = (
        first_new
        / (1.0 - beta_one**STEP)
        / (jnp.sqrt(second_new / (1.0 - beta_two**STEP)) + epsilon_adam)
    )
    return (params - rate_vector * direction, first_new, second_new)


ALL = ("dp", "heads", "tensor")
SUMMED = ((1, 0, 2), (1, 0, 2), (0, 1, 2), (0, 1, 2), (0, 1, 2), (2, 0, 1), (2, 0, 1), (2, 0, 1))
SLOTS = ((4, 5, 6, 0), (1, 7, 2, 3))


def places():
    for z in range(4):
        for x in range(2):
            for y in range(2):
                for c in range(2):
                    yield z, x, y, c


def index_of(z, x, y, c):
    return ((z * 2 + x) * 2 + y) * 2 + c


def move(array, target):
    return lax.ppermute(array, ALL, [(index_of(*at), index_of(*target(*at))) for at in places()])


LINES = [[index_of(z, x, y, c) for z in range(4)] for x in range(2) for y in range(2) for c in range(2)]


def over_y(array):
    return move(array, lambda z, x, y, c: (z, x, 1 - y, c))


def over_x(array):
    return move(array, lambda z, x, y, c: (z, 1 - x, y, c))


def over_xy(array):
    return move(array, lambda z, x, y, c: (z, 1 - x, 1 - y, c))


def after(array, *earlier):
    return lax.optimization_barrier((array, *earlier))[0]


def plane_shards(
    block_input,
    cotangent,
    segments,
    matrices,
    first_moment,
    second_moment,
    left_stat,
    right_stat,
    left_basis,
    right_basis,
    vectors,
    vec_first,
    vec_second,
):
    d = lax.axis_index("dp")
    x = d % 2
    gain_one, gain_two = vectors[:D].reshape(1, D), vectors[2 * D : 3 * D].reshape(1, D)
    bias_out, bias_down = vectors[7 * D : 8 * D], vectors[8 * D + FF : 9 * D + FF]
    table = vectors.reshape(-1, HD)
    frequency = 1.0 / rope_base ** (jnp.arange(0, RD, 2).astype(jnp.float32) / RD)
    turns = jnp.concatenate([frequency, frequency, jnp.zeros((128 - RD,), jnp.float32)]).reshape(1, 128)
    held, units, grads, sum_0, sum_1, sum_2, extra, rows, sums, biases = layer(
        block_input, cotangent, segments, matrices, table, turns
    )
    sum_1, sum_2, third_rows, third_sums, third_bias = third(
        held, units, grads, rows, table, sums, extra, sum_1, sum_2
    )
    sum_2, late, grad_table, *parts = rest(
        held, units, grads, rows, third_rows, table, sums, biases, third_sums, third_bias, sum_2
    )
    owned = []
    for send in (sum_0, sum_1, sum_2):
        owned.append(lax.psum_scatter(send, ALL, scatter_dimension=0, tiled=False, axis_index_groups=LINES))

    parts = input_share(held, rows, third_rows, late, jnp.concatenate([gain_one, gain_two]), parts)
    blocks = [a[0] for a in (matrices, first_moment, second_moment, left_stat, right_stat, left_basis, right_basis)]
    summed_order = jnp.array(SUMMED, jnp.int32)[d] * (8 // GROUP)
    updated = soap_part(summed_order[0:1], after(owned[0], parts[0]), blocks, None)
    updated = soap_part(summed_order[1:2], after(owned[1], updated[1]), blocks, updated)
    by_x, by_y, by_xy, own = parts
    totals = (
        after(own, updated[1]).astype(jnp.float32)
        + over_x(by_x).astype(jnp.float32)
        + over_y(by_y).astype(jnp.float32)
        + over_xy(by_xy).astype(jnp.float32)
    )
    output = block_input + totals[0] + bias_out + bias_down
    e = totals[1]
    middle = jnp.mean(block_input, axis=-1, keepdims=True)
    centered = block_input - middle
    inverse = lax.rsqrt(jnp.mean(centered * centered, axis=-1, keepdims=True) + epsilon_norm)
    unit = centered * inverse
    grad_input = cotangent + inverse * (
        e - jnp.mean(e, axis=-1, keepdims=True) - unit * jnp.mean(e * unit, axis=-1, keepdims=True)
    )
    grad_vectors = grad_table.reshape(-1)
    updated = soap_part(summed_order[2:3], after(owned[2], output, grad_input), blocks, updated)
    new_vectors, new_vec_first, new_vec_second = adam_vector(grad_vectors, vectors, vec_first, vec_second)
    return (output, grad_input, *[u[None] for u in updated], new_vectors, new_vec_first, new_vec_second)


def generic_shards(
    block_input,
    cotangent,
    segments,
    matrices,
    first_moment,
    second_moment,
    left_stat,
    right_stat,
    left_basis,
    right_basis,
    vectors,
    vec_first,
    vec_second,
):
    group_size = lax.axis_size(("heads", "tensor"))
    member = lax.axis_index(("heads", "tensor"))
    heads_here = H // group_size
    hidden_here = FF // group_size
    row_blocks = D // HD
    hidden_blocks = hidden_here // HD
    seq_count = segments.shape[0]
    tokens_here = seq_count * LEN
    own_rows = block_input.shape[0]
    qkv_offset = 4 * D + member * heads_here * 3 * HD
    up_offset = 8 * D + member * hidden_here
    gain_one = vectors[0:D]
    shift_one = vectors[D : 2 * D]
    gain_two = vectors[2 * D : 3 * D]
    shift_two = vectors[3 * D : 4 * D]
    bias_qkv = lax.dynamic_slice_in_dim(vectors, qkv_offset, heads_here * 3 * HD).reshape(
        heads_here, 3, HD
    )
    bias_out = vectors[7 * D : 8 * D]
    bias_up = lax.dynamic_slice_in_dim(vectors, up_offset, hidden_here)
    bias_down = vectors[8 * D + FF : 9 * D + FF]
    gathered = lax.all_gather(matrices.astype(jnp.bfloat16), "dp", axis=1, tiled=True)[0]
    w_qkv, w_out, w_up, w_down = unpack_blocks(gathered, heads_here, row_blocks, hidden_blocks)
    normed_one, unit_one, inverse_one = layer_norm(block_input, gain_one, shift_one)
    normed_two, unit_two, inverse_two = layer_norm(block_input, gain_two, shift_two)
    grad_own = cotangent.astype(jnp.bfloat16)
    norm_one, norm_two, grad_rows = (
        lax.all_gather(normed_one.astype(jnp.bfloat16), ("heads", "tensor"), axis=0, tiled=True),
        lax.all_gather(normed_two.astype(jnp.bfloat16), ("heads", "tensor"), axis=0, tiled=True),
        lax.all_gather(grad_own, ("heads", "tensor"), axis=0, tiled=True),
    )
    norm_one3 = norm_one.reshape(tokens_here, row_blocks, HD)
    norm_two3 = norm_two.reshape(tokens_here, row_blocks, HD)
    projected = (
        jnp.einsum("tbr,hqbrc->thqc", norm_one3, w_qkv, preferred_element_type=jnp.float32)
        + bias_qkv
    )
    shaped = projected.reshape(seq_count, LEN, heads_here, 3, HD)
    cosine, sine = angles(segments)
    queries = rotate(shaped[:, :, :, 0], cosine, sine).astype(jnp.bfloat16)
    keys_rot = rotate(shaped[:, :, :, 1], cosine, sine).astype(jnp.bfloat16)
    values = shaped[:, :, :, 2].astype(jnp.bfloat16)
    attended, log_total = lax.map(seq_forward, (queries, keys_rot, values, segments))
    attend_low = attended.astype(jnp.bfloat16).reshape(tokens_here, heads_here, HD)
    pre_act = (
        jnp.einsum("tbr,kbrc->tkc", norm_two3, w_up, preferred_element_type=jnp.float32).reshape(
            tokens_here, hidden_here
        )
        + bias_up
    )
    act_low = gelu_exact(pre_act).astype(jnp.bfloat16)
    rows_act = act_low.reshape(lax.axis_size(("heads", "tensor")) * own_rows, hidden_blocks, HD)
    first_term = jnp.einsum("thr,hbrc->tbc", attend_low, w_out, preferred_element_type=jnp.float32)
    second_term = jnp.einsum("tkr,kbrc->tbc", rows_act, w_down, preferred_element_type=jnp.float32)
    summed = lax.psum_scatter(
        (first_term + second_term).reshape(lax.axis_size(("heads", "tensor")) * own_rows, D),
        ("heads", "tensor"),
        scatter_dimension=0,
        tiled=True,
    )
    output = block_input + summed + bias_out + bias_down
    regathered = lax.all_gather(matrices.astype(jnp.bfloat16), "dp", axis=1, tiled=True)[0]
    w_qkv, w_out, w_up, w_down = unpack_blocks(regathered, heads_here, row_blocks, hidden_blocks)
    grad_rows3 = grad_rows.reshape(tokens_here, row_blocks, HD)
    act_low3 = act_low.reshape(tokens_here, hidden_blocks, HD)
    grad_act = jnp.einsum(
        "tbc,kbrc->tkr", grad_rows3, w_down, preferred_element_type=jnp.float32
    ).reshape(tokens_here, hidden_here)
    gelu_pull = jax.vjp(gelu_exact, pre_act)[1]
    grad_pre = gelu_pull(grad_act)[0].astype(jnp.bfloat16)
    grad_pre3 = grad_pre.reshape(tokens_here, hidden_blocks, HD)
    grad_attend = jnp.einsum(
        "tbc,hbrc->thr", grad_rows3, w_out, preferred_element_type=jnp.float32
    ).astype(jnp.bfloat16)
    grad_attend = grad_attend.reshape(seq_count, LEN, heads_here, HD)
    grad_queries, grad_keys, grad_values = lax.map(
        seq_backward, (queries, keys_rot, values, segments, log_total, grad_attend)
    )
    grad_raw = jnp.stack(
        [rotate(grad_queries, cosine, -sine), rotate(grad_keys, cosine, -sine), grad_values], axis=3
    )
    grad_raw = grad_raw.astype(jnp.bfloat16).reshape(tokens_here, heads_here, 3, HD)
    rows_up = grad_pre.reshape(lax.axis_size(("heads", "tensor")) * own_rows, hidden_blocks, HD)
    back_one = jnp.einsum(
        "thqc,hqbrc->tbr", grad_raw, w_qkv, preferred_element_type=jnp.float32
    ).reshape(lax.axis_size(("heads", "tensor")) * own_rows, D)
    back_two = jnp.einsum(
        "tkc,kbrc->tbr", rows_up, w_up, preferred_element_type=jnp.float32
    ).reshape(lax.axis_size(("heads", "tensor")) * own_rows, D)
    grad_norms = lax.psum_scatter(
        jnp.stack([back_one, back_two], axis=1),
        ("heads", "tensor"),
        scatter_dimension=0,
        tiled=True,
    )
    grad_norm_one = grad_norms[:, 0]
    grad_norm_two = grad_norms[:, 1]
    grad_input = (
        cotangent
        + norm_back(grad_norm_one, unit_one, inverse_one, gain_one)
        + norm_back(grad_norm_two, unit_two, inverse_two, gain_two)
    )
    grad_bias_rows = jnp.sum(grad_own, axis=0, dtype=jnp.float32)
    pieces = jnp.concatenate(
        [
            jnp.sum(grad_norm_one * unit_one, axis=0),
            jnp.sum(grad_norm_one, axis=0),
            jnp.sum(grad_norm_two * unit_two, axis=0),
            jnp.sum(grad_norm_two, axis=0),
            jnp.zeros((3 * D,), jnp.float32),
            grad_bias_rows,
            jnp.zeros((FF,), jnp.float32),
            grad_bias_rows,
        ]
    )
    pieces = lax.dynamic_update_slice_in_dim(
        pieces, jnp.sum(grad_raw, axis=0, dtype=jnp.float32).reshape(-1), qkv_offset, 0
    )
    pieces = lax.dynamic_update_slice_in_dim(
        pieces, jnp.sum(grad_pre, axis=0, dtype=jnp.float32), up_offset, 0
    )
    grad_vectors = lax.psum(pieces, ("dp", "heads", "tensor"))
    grad_down = jnp.einsum(
        "tkr,tbc->kbrc", act_low3, grad_rows3, preferred_element_type=jnp.float32
    )
    grad_up = jnp.einsum("tbr,tkc->kbrc", norm_two3, grad_pre3, preferred_element_type=jnp.float32)
    grad_out = jnp.einsum(
        "thr,tbc->hbrc", attend_low, grad_rows3, preferred_element_type=jnp.float32
    )
    grad_qkv = jnp.einsum(
        "tbr,thqc->hqbrc", norm_one3, grad_raw, preferred_element_type=jnp.float32
    )
    attn_grads = jnp.concatenate([grad_qkv, grad_out[:, None]], axis=1).reshape(-1, HD, HD)
    all_grads = jnp.concatenate(
        [attn_grads, grad_up.reshape(-1, HD, HD), grad_down.reshape(-1, HD, HD)], axis=0
    )[None]
    owned = lax.psum_scatter(all_grads, "dp", scatter_dimension=1, tiled=True)
    blocks = [a[0] for a in (matrices, first_moment, second_moment, left_stat, right_stat, left_basis, right_basis)]
    updated = [u[None] for u in soap_part(jnp.zeros((1,), jnp.int32), owned[0], blocks, None)]
    new_vectors, new_vec_first, new_vec_second = adam_vector(
        grad_vectors, vectors, vec_first, vec_second
    )
    return (
        output,
        grad_input,
        updated[0],
        updated[1],
        updated[2],
        updated[3],
        updated[4],
        updated[5],
        updated[6],
        updated[7],
        new_vectors,
        new_vec_first,
        new_vec_second,
    )


def solution(mesh):
    in_specs = (
        P(("dp", "heads", "tensor"), None),
        P(("dp", "heads", "tensor"), None),
        P("dp", None),
        P(("heads", "tensor"), "dp", None, None),
        P(("heads", "tensor"), "dp", None, None),
        P(("heads", "tensor"), "dp", None, None),
        P(("heads", "tensor"), "dp", None, None),
        P(("heads", "tensor"), "dp", None, None),
        P(("heads", "tensor"), "dp", None, None),
        P(("heads", "tensor"), "dp", None, None),
        P(),
        P(),
        P(),
    )
    out_specs = (
        P(("dp", "heads", "tensor"), None),
        P(("dp", "heads", "tensor"), None),
        P(("heads", "tensor"), "dp", None, None),
        P(("heads", "tensor"), "dp", None, None),
        P(("heads", "tensor"), "dp", None, None),
        P(("heads", "tensor"), "dp", None, None),
        P(("heads", "tensor"), "dp", None, None),
        P(("heads", "tensor"), "dp", None, None),
        P(("heads", "tensor"), "dp", None, None),
        P(("heads", "tensor"), "dp", None, None),
        P(),
        P(),
        P(),
    )
    plane = dict(mesh.shape) == {"dp": 8, "heads": 2, "tensor": 2}
    shards = plane_shards if plane else generic_shards
    return jax.shard_map(shards, mesh=mesh, in_specs=in_specs, out_specs=out_specs, check_vma=False)
```
